32 devices in a mesh: ctx: 8 (over z, core), fsdp: 4 (over y, x).
Axes of the slice: x: 2, y: 2, z: 4, core: 2. Of those that a mesh axis runs over, the one named last changes fastest.
Arguments:
- streams: bfloat16 [4, 4, 1024, 2048], P('fsdp', None, 'ctx'), may hold values from -6 to 6
- w_attn: bfloat16 [2048, 4, 2048], P('fsdp'), may hold values from -2 to 2
- w_ffn: bfloat16 [8192, 3, 2048], P('fsdp'), may hold values from -2 to 2
- hc_dynamic: float32 [2, 6, 2048], replicated, may hold values from -0.125 to 0.125
- hc_static: float32 [2, 4, 6], replicated, may hold values from -3 to 3
- cotangent: bfloat16 [4, 4, 1024, 2048], P('fsdp', None, 'ctx'), may hold values from -6 to 6
- pair_order: int32 [8], replicated, may hold values from 0 to 7, each once
Outputs:
- streams_out: bfloat16 [4, 4, 1024, 2048], P('fsdp', None, 'ctx')
- streams_grad: float32 [4, 4, 1024, 2048], P('fsdp', None, 'ctx')
- w_attn_grad: float32 [2048, 4, 2048], P('fsdp', None, 'ctx')
- w_ffn_grad: float32 [8192, 3, 2048], P('fsdp', None, 'ctx')
- hc_dynamic_grad: float32 [2, 6, 2048], replicated
- hc_static_grad: float32 [2, 4, 6], replicated
The draws below stay inside these ranges and needn't reach their ends.
Inputs may be any that keep to these rules, and one draw needn't show every extreme that they name: `pair_order`: every pair index appears once.
All inputs are finite; a program needn't handle non-finite values.
Results may differ from the reference program's by a relative error of at most 0.019.
The reference program's roundings to bfloat16 on the way count: a program that leaves them out, or rounds other values in their place, can miss the bound.
Values may be sent and summed in bfloat16 or wider, within the bound.
A program may use at most 256 MiB of HBM per device.

```python
import jax
import jax.numpy as jnp
from jax import lax

D = 2048
HEADS = 16
HEAD_DIM = 128
FF = 8192
STREAMS = 4
TOK_DEV = 128
SEQ = 1024
SEQS = 4
N_CTX = 8


def draw_w_attn(key, part):
    key = jax.random.fold_in(key, 17)
    gaussian = jax.random.normal(key, (D, 4, D), jnp.float32)
    factors = jnp.array([1.5, 1.0, 1.0, float(SEQ) ** 0.25], jnp.float32)
    return (gaussian * factors[None, :, None] * float(D) ** (-0.5)).astype(jnp.bfloat16)


def draw_w_ffn(key, part):
    key = jax.random.fold_in(key, 29)
    gaussian = jax.random.normal(key, (FF, 3, D), jnp.float32)
    factors = jnp.array([float(D) ** (-0.5), float(D) ** (-0.5), float(FF) ** (-0.5)], jnp.float32)
    return (gaussian * factors[None, :, None]).astype(jnp.bfloat16)


def block_scale(own_key, dims, shards, low, high):
    def one(axis_at, blocks):
        heights = jax.random.uniform(jax.random.fold_in(jax.random.fold_in(own_key, 6), axis_at), (blocks,), jnp.float32, low / len(shards), high / len(shards))
        return jnp.repeat(jnp.exp(heights), dims[axis_at] // blocks).reshape((-1,) + (1,) * (len(dims) - axis_at - 1))

    factor_of = one(*shards[0])
    for cut in shards[1:]:
        factor_of = factor_of * one(*cut)
    return factor_of


def normal_values(stream_key, extent, scale, limit, cuts=(), kind=jnp.bfloat16):
    entries = scale * jax.random.normal(stream_key, extent, jnp.float32)
    if cuts:
        entries = entries * block_scale(stream_key, extent, cuts, -0.22, 0.18)
    return jnp.clip(entries, -limit, limit).astype(kind)


def setup_inputs(seed: int = 0) -> dict:
    splits = jax.random.split(jax.random.key(seed), 8)
    return {
        "streams": normal_values(splits[0], (SEQS, STREAMS, SEQ, D), 1.0, 6.0, ((0, 4), (2, 8))),
        "w_attn": draw_w_attn(jax.random.fold_in(splits[7], 71), 0),
        "w_ffn": draw_w_ffn(jax.random.fold_in(splits[7], 71), 0),
        "hc_dynamic": normal_values(splits[3], (2, 6, D), D ** -0.5, 0.125, (), jnp.float32),
        "hc_static": normal_values(splits[4], (2, STREAMS, 6), 0.5, 3.0, (), jnp.float32),
        "cotangent": normal_values(splits[5], (SEQS, STREAMS, SEQ, D), 1.0, 6.0, ((0, 4), (2, 8))),
        "pair_order": jax.random.permutation(splits[6], N_CTX).astype(jnp.int32),
    }


EPS = 1e-05
THETA = 10000.0
HIGH = lax.Precision.HIGHEST
MASKED = -1e+30

@jax.custom_vjp
def low(v):
    return lax.optimization_barrier(v.astype(jnp.bfloat16)).astype(jnp.float32)

@jax.custom_vjp
def low_back(v):
    return v

def low_keep(v):
    return (low(v), None)

def low_pass(kept, grad):
    return (grad,)

def back_keep(v):
    return (v, None)

def back_low(kept, grad):
    return (low(grad),)
low.defvjp(low_keep, low_pass)
low_back.defvjp(back_keep, back_low)

def normalize(values):
    centered = values - lax.optimization_barrier(jnp.mean(values, axis=-1, keepdims=True))
    return centered * lax.rsqrt(lax.optimization_barrier(jnp.mean(centered * centered, axis=-1, keepdims=True)) + EPS)

def block_positions(pair_order, length):
    half_size = length // 2
    offsets = jnp.arange(half_size, dtype=jnp.int32)
    mirror = 2 * pair_order.shape[0] - 1 - pair_order
    first_half = pair_order[:, None] * half_size + offsets[None, :]
    second_half = mirror[:, None] * half_size + offsets[None, :]
    return jnp.concatenate([first_half, second_half], axis=1).reshape(-1)

def rope_tables(positions, head_size):
    frequency = THETA ** (-(jnp.arange(head_size // 2, dtype=jnp.float32) * 2.0) / head_size)
    angles = positions.astype(jnp.float32)[:, None] * frequency[None, :]
    return (jnp.cos(angles), jnp.sin(angles))

def rotate(values, cosine_table, sine_table):
    half_size = values.shape[-1] // 2
    first_half = values[..., :half_size]
    second_half = values[..., half_size:]
    cosine_part = cosine_table[:, None, :]
    sine_part = sine_table[:, None, :]
    return jnp.concatenate([first_half * cosine_part - second_half * sine_part, second_half * cosine_part + first_half * sine_part], axis=-1)

def attention(inputs, w_attn, positions):
    length = inputs.shape[0]
    normed = low(normalize(inputs))
    qkv = low_back(jnp.einsum('td,dce->tce', normed, w_attn[:, 0:3], precision=HIGH))
    cosine_table, sine_table = rope_tables(positions, HEAD_DIM)
    queries = low(rotate(qkv[:, 0].reshape(length, HEADS, HEAD_DIM), cosine_table, sine_table))
    keys = low(rotate(qkv[:, 1].reshape(length, HEADS, HEAD_DIM), cosine_table, sine_table))
    values = low(qkv[:, 2]).reshape(length, HEADS, HEAD_DIM)
    causal_mask = positions[:, None] >= positions[None, :]

    def one_head(parts):
        query_head, key_head, value_head = parts
        scores = low_back(jnp.dot(query_head, key_head.T, precision=HIGH) * HEAD_DIM ** (-0.5))
        scores = jnp.where(causal_mask, scores, MASKED)
        exponent = jnp.exp(scores - lax.optimization_barrier(jnp.max(scores, axis=-1, keepdims=True)))
        probs = exponent / lax.optimization_barrier(jnp.sum(exponent, axis=-1, keepdims=True))
        return jnp.dot(low(probs), value_head, precision=HIGH)
    per_head = lax.map(jax.checkpoint(one_head), (queries.transpose(1, 0, 2), keys.transpose(1, 0, 2), values.transpose(1, 0, 2)))
    attended = low(low_back(per_head.transpose(1, 0, 2).reshape(length, HEADS * HEAD_DIM)))
    return low_back(jnp.dot(attended, w_attn[:, 3], precision=HIGH))

def feed_forward(inputs, w_ffn):
    normed = low(normalize(inputs))
    gate_up = low_back(jnp.einsum('td,ncd->tcn', normed, w_ffn[:, 0:2], precision=HIGH))
    hidden = low(jax.nn.silu(gate_up[:, 0]) * gate_up[:, 1])
    return low_back(jnp.dot(hidden, w_ffn[:, 2], precision=HIGH))

def connect(streams, dynamic, static, branch):
    normed = normalize(streams)
    coefficients = jnp.tanh(jnp.einsum('std,kd->stk', normed, dynamic, precision=HIGH)) + static[:, None, :]
    number = streams.shape[0]
    mixed = sum((coefficients[i, :, 1:2] * streams[i] for i in range(number)))
    branch_out = branch(mixed)
    return jnp.stack([sum((coefficients[i, :, 2 + j:3 + j] * streams[i] for i in range(number))) + coefficients[j, :, 0:1] * branch_out for j in range(number)])

def layer(streams, w_attn, w_ffn, hc_dynamic, hc_static, positions):
    first_out = connect(streams, hc_dynamic[0], hc_static[0], lambda v: attention(v, w_attn, positions))
    return connect(first_out, hc_dynamic[1], hc_static[1], lambda v: feed_forward(v, w_ffn))

def reference(streams, w_attn, w_ffn, hc_dynamic, hc_static, cotangent, pair_order):
    positions = block_positions(pair_order, TOK_DEV)
    params = (w_attn.astype(jnp.float32), w_ffn.astype(jnp.float32), hc_dynamic, hc_static)

    def one_sequence(totals, item):
        sequence_in, sequence_cot = item
        result, pullback = jax.vjp(lambda h, wa, wf, hd, hs: layer(h, wa, wf, hd, hs, positions), sequence_in.astype(jnp.float32), *params)
        grads = pullback(sequence_cot.astype(jnp.float32))
        totals = tuple((a + g for a, g in zip(totals, grads[1:])))
        return (totals, (result.astype(jnp.bfloat16), grads[0]))
    zeros = tuple((jnp.zeros_like(p) for p in params))
    totals, (outputs, input_grads) = lax.scan(one_sequence, zeros, (streams, cotangent))
    return (outputs, input_grads, totals[0], totals[1], totals[2], totals[3])
```

```python
import functools

import jax
import jax.numpy as jnp
from jax import lax
from jax.sharding import PartitionSpec as P

HEADS = 16
HEAD_DIM = 128


EPS = 1e-05
THETA = 10000.0
HIGH = lax.Precision.HIGHEST
MASKED = -1e30
CONTRACT_LAST = (((1,), (1,)), ((), ()))
CONTRACT_FIRST = (((0,), (0,)), ((), ()))


def normalize(values):
    centered = values - jnp.mean(values, axis=-1, keepdims=True)
    inverse = lax.rsqrt(jnp.mean(centered * centered, axis=-1, keepdims=True) + EPS)
    return (centered * inverse, inverse)


def normalize_back(normed, inverse, gradient):
    inner = jnp.mean(gradient * normed, axis=-1, keepdims=True)
    return inverse * (gradient - jnp.mean(gradient, axis=-1, keepdims=True) - normed * inner)


def block_positions(pair_order, length):
    half_size = length // 2
    offsets = jnp.arange(half_size, dtype=jnp.int32)
    mirror = 2 * pair_order.shape[0] - 1 - pair_order
    first_half = pair_order[:, None] * half_size + offsets[None, :]
    second_half = mirror[:, None] * half_size + offsets[None, :]
    return jnp.concatenate([first_half, second_half], axis=1).reshape(-1)


def rope_tables(positions, head_size):
    frequency = THETA ** (-(jnp.arange(head_size // 2, dtype=jnp.float32) * 2.0) / head_size)
    angles = positions.astype(jnp.float32)[:, None] * frequency[None, :]
    return (jnp.cos(angles), jnp.sin(angles))


def rotate(values, cosine_table, sine_table):
    half_size = values.shape[-1] // 2
    first_half = values[..., :half_size]
    second_half = values[..., half_size:]
    cosine_part = cosine_table[:, None, :]
    sine_part = sine_table[:, None, :]
    return jnp.concatenate(
        [
            first_half * cosine_part - second_half * sine_part,
            second_half * cosine_part + first_half * sine_part,
        ],
        axis=-1,
    )


def rotate_back(values, cosine_table, sine_table):
    half_size = values.shape[-1] // 2
    first_half = values[..., :half_size]
    second_half = values[..., half_size:]
    cosine_part = cosine_table[:, None, :]
    sine_part = sine_table[:, None, :]
    return jnp.concatenate(
        [
            first_half * cosine_part + second_half * sine_part,
            second_half * cosine_part - first_half * sine_part,
        ],
        axis=-1,
    )


def mixing(streams, dynamic, static):
    normed, inverse = normalize(streams)
    dynamic_part = jnp.tanh(jnp.einsum("std,kd->stk", normed, dynamic, precision=HIGH))
    return (normed, inverse, dynamic_part, dynamic_part + static[:, None, :])


def branch_input(streams, coefficients):
    return sum((coefficients[i, :, 1:2] * streams[i] for i in range(streams.shape[0])))


def mix_output(streams, coefficients, branch_out):
    number = streams.shape[0]
    return jnp.stack(
        [
            sum((coefficients[i, :, 2 + j : 3 + j] * streams[i] for i in range(number)))
            + coefficients[j, :, 0:1] * branch_out
            for j in range(number)
        ]
    )


def low(values):
    return values.astype(jnp.bfloat16)


def mm(a, b, dims=None):
    if dims is None:
        return jnp.dot(a, b, preferred_element_type=jnp.float32)
    return lax.dot_general(a, b, dims, preferred_element_type=jnp.float32)


def gather(values, axis, dim=0):
    return lax.all_gather(values, axis, axis=dim, tiled=True)


def scatter(values, axis, dim=0):
    return lax.psum_scatter(values, axis, scatter_dimension=dim, tiled=True)


def attend(query, key, value, allowed):
    scores = mm(query, key, CONTRACT_LAST) * HEAD_DIM ** (-0.5)
    scores = jnp.where(allowed, scores, MASKED)
    highest = jnp.max(scores, axis=-1, keepdims=True)
    exponent = jnp.exp(scores - highest)
    total = jnp.sum(exponent, axis=-1, keepdims=True)
    return (mm(low(exponent / total), value), highest + jnp.log(total))


def attend_back(query, key, value, grad_out, log_total, allowed):
    scale = HEAD_DIM ** (-0.5)
    scores = jnp.where(allowed, mm(query, key, CONTRACT_LAST) * scale, MASKED)
    probs = jnp.exp(scores - log_total)
    probs_grad = mm(grad_out, value, CONTRACT_LAST)
    centre = jnp.sum(probs * probs_grad, axis=-1, keepdims=True)
    scores_grad = low(probs * (probs_grad - centre))
    return (
        mm(scores_grad, key) * scale,
        mm(scores_grad, query, CONTRACT_FIRST) * scale,
        mm(low(probs), grad_out, CONTRACT_FIRST),
    )


def local(n_ctx, n_fsdp, streams, w_attn, w_ffn, hc_dynamic, hc_static, cotangent, pair_order):
    number = streams.shape[1]
    length = streams.shape[2]
    features = streams.shape[3]
    size = HEAD_DIM
    own = features // n_ctx
    heads = own // size
    rows = length * n_ctx
    own_rows = w_attn.shape[0]
    ctx = lax.axis_index("ctx")
    fsdp = lax.axis_index("fsdp")
    both = ("ctx", "fsdp")

    w_planes = jnp.moveaxis(w_attn, 1, 0)
    w_own = lax.dynamic_slice_in_dim(w_planes[0:3], ctx * own, own, 2)
    w_qkv = gather(jnp.moveaxis(w_own, 0, 1).reshape(own_rows, 3 * own), "fsdp")
    w_out = gather(w_planes[3], "fsdp")

    positions = block_positions(pair_order, length)
    cosine_table, sine_table = rope_tables(positions, size)
    allowed = positions[:, None] >= positions[None, :]

    inputs = streams[0].astype(jnp.float32)
    normed_one, inverse_one, dynamic_one, coef_one = mixing(inputs, hc_dynamic[0], hc_static[0])
    mixed_one = branch_input(inputs, coef_one)
    attn_normed, attn_inverse = normalize(mixed_one)
    attn_low = low(attn_normed)
    attn_all = gather(attn_low, "ctx")
    qkv = mm(attn_all, w_qkv).reshape(rows, 3, heads, size)
    query = low(rotate(qkv[:, 0], cosine_table, sine_table))
    key = low(rotate(qkv[:, 1], cosine_table, sine_table))
    value = low(qkv[:, 2])
    outs, logs = [], []
    for h in range(heads):
        out, log_total = attend(query[:, h], key[:, h], value[:, h], allowed)
        outs.append(out)
        logs.append(log_total)
    attended = low(jnp.concatenate(outs, axis=1))
    attended_rows = lax.all_to_all(attended, "ctx", 0, 1, tiled=True)
    attn_branch = mm(attended_rows, w_out)
    attended_cols = lax.all_to_all(attended_rows, "fsdp", 1, 0, tiled=True)

    first_out = mix_output(inputs, coef_one, attn_branch)
    normed_two, inverse_two, dynamic_two, coef_two = mixing(first_out, hc_dynamic[1], hc_static[1])
    mixed_two = branch_input(first_out, coef_two)
    ffn_normed, ffn_inverse = normalize(mixed_two)
    ffn_low = low(ffn_normed)
    grad_final = cotangent[0].astype(jnp.float32)
    grad_ffn = low(sum((coef_two[j, :, 0:1] * grad_final[j] for j in range(number))))

    ffn_rows = gather(ffn_low, "fsdp")
    grad_rows = gather(grad_ffn, "fsdp")
    gate = mm(ffn_rows, w_ffn[:, 0], CONTRACT_LAST)
    up_part = mm(ffn_rows, w_ffn[:, 1], CONTRACT_LAST)
    grad_hidden = mm(grad_rows, w_ffn[:, 2], CONTRACT_LAST)
    sigmoid_gate = jax.nn.sigmoid(gate)
    activated = gate * sigmoid_gate
    hidden_low = low(activated * up_part)
    grad_gate = low(grad_hidden * up_part * sigmoid_gate * (1.0 + gate * (1.0 - sigmoid_gate)))
    grad_up = low(grad_hidden * activated)
    ffn_branch = scatter(low(mm(hidden_low, w_ffn[:, 2])), "fsdp").astype(jnp.float32)
    grad_ffn_normed = scatter(
        low(mm(grad_gate, w_ffn[:, 0]) + mm(grad_up, w_ffn[:, 1])), "fsdp"
    ).astype(jnp.float32)

    def weight_part(left, right):
        blocks = right.reshape(right.shape[0], n_ctx, own)
        return scatter(low(jnp.einsum("tn,tke->kne", left, blocks, preferred_element_type=jnp.float32)), "ctx")[0]

    down_grad = weight_part(hidden_low, grad_rows)
    gate_grad = weight_part(grad_gate, ffn_rows)
    up_grad = weight_part(grad_up, ffn_rows)
    ffn_grad = jnp.stack([gate_grad, up_grad, down_grad], axis=1).astype(jnp.float32)

    second_out = mix_output(first_out, coef_two, ffn_branch)
    streams_out = low(second_out)[None]

    def connect_back(
        values, normed, inverse, dynamic_part, coefficients, dynamic, branch_out, grad_out, grad_mixed
    ):
        coef_rows = []
        grads = []
        for i in range(number):
            coef_rows.append(
                jnp.stack(
                    [
                        jnp.sum(grad_out[i] * branch_out, axis=-1),
                        jnp.sum(grad_mixed * values[i], axis=-1),
                    ]
                    + [jnp.sum(grad_out[j] * values[i], axis=-1) for j in range(number)],
                    axis=-1,
                )
            )
            grads.append(
                sum((coefficients[i, :, 2 + j : 3 + j] * grad_out[j] for j in range(number)))
                + coefficients[i, :, 1:2] * grad_mixed
            )
        coef_grad = jnp.stack(coef_rows)
        pre_grad = coef_grad * (1.0 - dynamic_part * dynamic_part)
        dynamic_grad = jnp.einsum("stk,std->kd", pre_grad, normed, precision=HIGH)
        normed_grad = jnp.einsum("stk,kd->std", pre_grad, dynamic, precision=HIGH)
        grads = jnp.stack(grads) + normalize_back(normed, inverse, normed_grad)
        return (grads, dynamic_grad, jnp.sum(coef_grad, axis=1))

    grad_mixed_two = normalize_back(ffn_normed, ffn_inverse, grad_ffn_normed)
    grad_first, dynamic_grad_two, static_grad_two = connect_back(
        first_out, normed_two, inverse_two, dynamic_two, coef_two, hc_dynamic[1], ffn_branch, grad_final, grad_mixed_two
    )

    grad_attn = low(sum((coef_one[j, :, 0:1] * grad_first[j] for j in range(number))))
    grad_attended = low(mm(grad_attn, w_out, CONTRACT_LAST))
    grad_heads = lax.all_to_all(grad_attended, "ctx", 1, 0, tiled=True)
    grad_attn_rows = gather(grad_attn, "fsdp")
    out_grad = weight_part(attended_cols, grad_attn_rows)
    parts = []
    for h in range(heads):
        parts.append(
            attend_back(
                query[:, h], key[:, h], value[:, h], grad_heads[:, h * size : (h + 1) * size], logs[h], allowed
            )
        )
    query_grad, key_grad, value_grad = (jnp.stack([p[i] for p in parts], axis=1) for i in range(3))
    qkv_grad = low(
        jnp.stack(
            [
                rotate_back(query_grad, cosine_table, sine_table),
                rotate_back(key_grad, cosine_table, sine_table),
                value_grad,
            ],
            axis=1,
        ).reshape(rows, 3 * own)
    )
    grad_attn_normed = scatter(low(mm(qkv_grad, w_qkv, CONTRACT_LAST)), "ctx").astype(jnp.float32)
    inner_grad = scatter(low(mm(attn_all, qkv_grad, CONTRACT_FIRST)), "fsdp").reshape(own_rows, 3, own)
    attn_grad = jnp.concatenate([inner_grad, out_grad[:, None]], axis=1).astype(jnp.float32)

    grad_mixed_one = normalize_back(attn_normed, attn_inverse, grad_attn_normed)
    grad_inputs, dynamic_grad_one, static_grad_one = connect_back(
        inputs, normed_one, inverse_one, dynamic_one, coef_one, hc_dynamic[0], attn_branch, grad_first, grad_mixed_one
    )
    dynamic_total, static_total = lax.psum(
        (
            jnp.stack([dynamic_grad_one, dynamic_grad_two]),
            jnp.stack([static_grad_one, static_grad_two]),
        ),
        both,
    )
    return (streams_out, grad_inputs[None], attn_grad, ffn_grad, dynamic_total, static_total)


def solution(mesh):
    return jax.shard_map(
        functools.partial(local, mesh.shape["ctx"], mesh.shape["fsdp"]),
        mesh=mesh,
        in_specs=(
            P("fsdp", None, "ctx", None),
            P("fsdp", None, None),
            P("fsdp", None, None),
            P(),
            P(),
            P("fsdp", None, "ctx", None),
            P(),
        ),
        out_specs=(
            P("fsdp", None, "ctx", None),
            P("fsdp", None, "ctx", None),
            P("fsdp", None, "ctx"),
            P("fsdp", None, "ctx"),
            P(),
            P(),
        ),
        check_vma=False,
    )
```

```python
import functools

import jax
import jax.numpy as jnp
from jax import lax
from jax.experimental import pallas as pl
from jax.experimental.pallas import tpu as pltpu
from jax.sharding import PartitionSpec as P

HEADS = 16
HEAD_DIM = 128


EPS = 1e-05
THETA = 10000.0
HIGH = lax.Precision.HIGHEST
MASKED = -1e30
CONTRACT_LAST = (((1,), (1,)), ((), ()))
CONTRACT_FIRST = (((0,), (0,)), ((), ()))


def normalize(values):
    centered = values - jnp.mean(values, axis=-1, keepdims=True)
    inverse = lax.rsqrt(jnp.mean(centered * centered, axis=-1, keepdims=True) + EPS)
    return (centered * inverse, inverse)


def normalize_back(normed, inverse, gradient):
    inner = jnp.mean(gradient * normed, axis=-1, keepdims=True)
    return inverse * (gradient - jnp.mean(gradient, axis=-1, keepdims=True) - normed * inner)


def block_positions(pair_order, length):
    half_size = length // 2
    offsets = jnp.arange(half_size, dtype=jnp.int32)
    mirror = 2 * pair_order.shape[0] - 1 - pair_order
    first_half = pair_order[:, None] * half_size + offsets[None, :]
    second_half = mirror[:, None] * half_size + offsets[None, :]
    return jnp.concatenate([first_half, second_half], axis=1).reshape(-1)


def rope_tables(positions, head_size):
    frequency = THETA ** (-(jnp.arange(head_size // 2, dtype=jnp.float32) * 2.0) / head_size)
    angles = positions.astype(jnp.float32)[:, None] * frequency[None, :]
    return (jnp.cos(angles), jnp.sin(angles))


def rotate(values, cosine_table, sine_table):
    half_size = values.shape[-1] // 2
    first_half = values[..., :half_size]
    second_half = values[..., half_size:]
    cosine_part = cosine_table[:, None, :]
    sine_part = sine_table[:, None, :]
    return jnp.concatenate(
        [
            first_half * cosine_part - second_half * sine_part,
            second_half * cosine_part + first_half * sine_part,
        ],
        axis=-1,
    )


def rotate_back(values, cosine_table, sine_table):
    half_size = values.shape[-1] // 2
    first_half = values[..., :half_size]
    second_half = values[..., half_size:]
    cosine_part = cosine_table[:, None, :]
    sine_part = sine_table[:, None, :]
    return jnp.concatenate(
        [
            first_half * cosine_part + second_half * sine_part,
            second_half * cosine_part - first_half * sine_part,
        ],
        axis=-1,
    )


def mixing(streams, dynamic, static):
    normed, inverse = normalize(streams)
    dynamic_part = jnp.tanh(jnp.einsum("std,kd->stk", normed, dynamic, precision=HIGH))
    return (normed, inverse, dynamic_part, dynamic_part + static[:, None, :])


def branch_input(streams, coefficients):
    return sum((coefficients[i, :, 1:2] * streams[i] for i in range(streams.shape[0])))


def mix_output(streams, coefficients, branch_out):
    number = streams.shape[0]
    return jnp.stack(
        [
            sum((coefficients[i, :, 2 + j : 3 + j] * streams[i] for i in range(number)))
            + coefficients[j, :, 0:1] * branch_out
            for j in range(number)
        ]
    )


def low(values):
    return values.astype(jnp.bfloat16)


def mm(a, b, dims=None):
    if dims is None:
        return jnp.dot(a, b, preferred_element_type=jnp.float32)
    return lax.dot_general(a, b, dims, preferred_element_type=jnp.float32)


def gather(values, axis, dim=0):
    return lax.all_gather(values, axis, axis=dim, tiled=True)


def scatter(values, axis, dim=0):
    return lax.psum_scatter(values, axis, scatter_dimension=dim, tiled=True)


def attend(query, key, value, allowed):
    scores = mm(query, key, CONTRACT_LAST) * HEAD_DIM ** (-0.5)
    scores = jnp.where(allowed, scores, MASKED)
    highest = jnp.max(scores, axis=-1, keepdims=True)
    exponent = jnp.exp(scores - highest)
    total = jnp.sum(exponent, axis=-1, keepdims=True)
    return (mm(low(exponent / total), value), highest + jnp.log(total))


def attend_back(query, key, value, grad_out, log_total, allowed):
    scale = HEAD_DIM ** (-0.5)
    scores = jnp.where(allowed, mm(query, key, CONTRACT_LAST) * scale, MASKED)
    probs = jnp.exp(scores - log_total)
    probs_grad = mm(grad_out, value, CONTRACT_LAST)
    centre = jnp.sum(probs * probs_grad, axis=-1, keepdims=True)
    scores_grad = low(probs * (probs_grad - centre))
    return (
        mm(scores_grad, key) * scale,
        mm(scores_grad, query, CONTRACT_FIRST) * scale,
        mm(low(probs), grad_out, CONTRACT_FIRST),
    )


MESH = pl.DeviceIdType.MESH
VMEM_LIMIT = 56 * 1024 * 1024


def place(n_ctx):
    ctx = lax.axis_index("ctx")
    return (ctx // 2, ctx % 2, lax.axis_index("fsdp"), n_ctx // 2)


def greet(peers):
    barrier = pltpu.get_barrier_semaphore()
    for peer in peers:
        pl.semaphore_signal(barrier, inc=1, device_id=peer, device_id_type=MESH)
    pl.semaphore_wait(barrier, len(peers))


def send(source, target, sems, index, peer):
    return pltpu.make_async_remote_copy(
        src_ref=source,
        dst_ref=target,
        send_sem=sems[0].at[index],
        recv_sem=sems[1].at[index],
        device_id=peer,
        device_id_type=MESH,
    )


def fsdp_neighbours(fsdp):
    first = fsdp + 1 - 2 * (fsdp % 2)
    second = (fsdp + 2) % 4
    return (first, second, (first + 2) % 4)


def fsdp_peers(n_fsdp, ctx, fsdp):
    if n_fsdp == 4:
        first, second, _ = fsdp_neighbours(fsdp)
        return [(ctx, first), (ctx, second)]
    return [(ctx, (fsdp + j) % n_fsdp) for j in range(1, n_fsdp)]


def line_peers(chip, core, fsdp, length):
    return [
        (chip * 2 + 1 - core, fsdp),
        ((chip + 1) % length * 2 + core, fsdp),
        ((chip + length - 1) % length * 2 + core, fsdp),
    ]


def line_gather(own_ref, all_ref, sems, where):
    chip, core, fsdp, length = where
    right_sems, left_sems, core_sems = sems
    sibling = (chip * 2 + 1 - core, fsdp)
    right = ((chip + 1) % length * 2 + core, fsdp)
    left = ((chip + length - 1) % length * 2 + core, fsdp)

    def block(index):
        return all_ref.at[(index + length) % length * 2 + core]

    def pass_on(index, source):
        return send(source, block(index), core_sems, (index + length) % length, sibling)

    pass_on(chip, own_ref).start()
    for step in range(length - 1):
        for sign, peer, way in ((-1, right, right_sems), (1, left, left_sems)):
            at = chip + sign * step
            held = (at >= 0) & (at < length)
            if step > 0:

                @pl.when(held)
                def _():
                    send(block(at), block(at), way, step - 1, peer).wait_recv()
                    pass_on(at, block(at)).start()

            more = (chip < length - 1) if sign < 0 else (chip > 0)

            @pl.when(held & more)
            def _():
                send(own_ref if step == 0 else block(at), block(at), way, step, peer).start()

        yield
    last = length - 1
    for sign, peer, way in ((-1, right, right_sems), (1, left, left_sems)):
        at = chip + sign * last

        @pl.when((at >= 0) & (at < length))
        def _():
            send(block(at), block(at), way, last - 1, peer).wait_recv()
            pass_on(at, block(at)).start()

    yield
    for step in range(length - 1):
        for sign, peer, way in ((-1, right, right_sems), (1, left, left_sems)):
            at = chip + sign * step
            more = (chip < length - 1) if sign < 0 else (chip > 0)

            @pl.when((at >= 0) & (at < length) & more)
            def _():
                send(block(at), block(at), way, step, peer).wait_send()

    for index in range(length):
        pass_on(index, block(index)).wait_send()
        other = all_ref.at[index * 2 + 1 - core]
        send(other, other, core_sems, index, sibling).wait_recv()


def square_gather(own_ref, all_ref, sems, ctx, fsdp, n_fsdp, passed=None):
    if n_fsdp != 4:
        copies = [
            send(own_ref, all_ref.at[fsdp], sems, j - 1, (ctx, (fsdp + j) % n_fsdp)) for j in range(1, n_fsdp)
        ]
        for copy in copies:
            copy.start()
        yield
        for j, copy in enumerate(copies):
            copy.wait()
            if passed:
                passed(all_ref.at[(fsdp + n_fsdp - j - 1) % n_fsdp], (fsdp + n_fsdp - j - 1) % n_fsdp, None, j)
        return
    first, second, corner = fsdp_neighbours(fsdp)
    half = own_ref.shape[0] // 2
    top, low_half = pl.ds(0, half), pl.ds(half, half)
    to_first, to_second = (ctx, first), (ctx, second)

    def copy(index, owner, part, peer, source=None):
        source = all_ref.at[owner, part] if source is None else source
        return send(source, all_ref.at[owner, part], sems, index, peer)

    starts = [
        copy(0, fsdp, top, to_first, own_ref.at[top]),
        copy(1, fsdp, low_half, to_second, own_ref.at[low_half]),
        copy(2, fsdp, low_half, to_first, own_ref.at[low_half]),
        copy(3, fsdp, top, to_second, own_ref.at[top]),
        copy(4, first, top, to_second),
        copy(5, second, low_half, to_first),
    ]
    arrivals = [
        (0, first, top),
        (1, second, low_half),
        (2, first, low_half),
        (3, second, top),
        (4, corner, top),
        (5, corner, low_half),
    ]
    for each in starts[:4]:
        each.start()
    yield
    for index, owner, part in arrivals:
        copy(index, owner, part, to_first).wait_recv()
        if index < 2:
            starts[4 + index].start()
        if passed:
            passed(all_ref.at[owner, part], owner, part, index)
        yield
    for each in starts:
        each.wait_send()


def run_all(*parts):
    parts = list(parts)
    while parts:
        for part in list(parts):
            try:
                next(part)
            except StopIteration:
                parts.remove(part)


def dma_pair(count):
    return [pltpu.SemaphoreType.DMA((count,)), pltpu.SemaphoreType.DMA((count,))]


def any_specs(count):
    return [pl.BlockSpec(memory_space=pl.ANY)] * count


def params(collective_id=None, **more):
    if collective_id is not None:
        more.update(collective_id=collective_id, has_side_effects=True)
    return pltpu.CompilerParams(vmem_limit_bytes=VMEM_LIMIT, **more)


def attention_gather(n_ctx, n_fsdp, rows, weights):
    def kernel(
        rows_ref, weights_ref, all_rows, all_weights, right_s, right_r, left_s, left_r, core_s, core_r, sq_s, sq_r, own
    ):
        where = place(n_ctx)
        chip, core, fsdp, length = where
        ctx = chip * 2 + core
        greet(line_peers(*where) + fsdp_peers(n_fsdp, ctx, fsdp))
        mine = [
            pltpu.make_async_copy(weights_ref, all_weights.at[fsdp], own.at[0]),
            pltpu.make_async_copy(rows_ref, all_rows.at[ctx], own.at[1]),
        ]
        for copy in mine:
            copy.start()
        run_all(
            line_gather(rows_ref, all_rows, ((right_s, right_r), (left_s, left_r), (core_s, core_r)), where),
            square_gather(weights_ref, all_weights, (sq_s, sq_r), ctx, fsdp, n_fsdp),
        )
        for copy in mine:
            copy.wait()

    length = n_ctx // 2
    return pl.pallas_call(
        kernel,
        out_shape=(
            jax.ShapeDtypeStruct((n_ctx,) + rows.shape, rows.dtype),
            jax.ShapeDtypeStruct((n_fsdp,) + weights.shape, weights.dtype),
        ),
        in_specs=any_specs(2),
        out_specs=tuple(any_specs(2)),
        scratch_shapes=dma_pair(length)
        + dma_pair(length)
        + dma_pair(length)
        + dma_pair(max(6, n_fsdp))
        + [pltpu.SemaphoreType.DMA((2,))],
        compiler_params=params(0),
        name="attention_gather",
    )(rows, weights)


def square_rows(n_ctx, n_fsdp, rows):
    def kernel(rows_ref, all_ref, sq_s, sq_r, own):
        chip, core, fsdp, _ = place(n_ctx)
        ctx = chip * 2 + core
        greet(fsdp_peers(n_fsdp, ctx, fsdp))
        mine = pltpu.make_async_copy(rows_ref, all_ref.at[fsdp], own)
        mine.start()
        run_all(square_gather(rows_ref, all_ref, (sq_s, sq_r), ctx, fsdp, n_fsdp))
        mine.wait()

    return pl.pallas_call(
        kernel,
        out_shape=jax.ShapeDtypeStruct((n_fsdp,) + rows.shape, rows.dtype),
        in_specs=any_specs(1),
        out_specs=pl.BlockSpec(memory_space=pl.ANY),
        scratch_shapes=dma_pair(max(6, n_fsdp)) + [pltpu.SemaphoreType.DMA],
        compiler_params=params(7),
        name="square_rows",
    )(rows)


def square_core_gather(n_ctx, n_fsdp, rows):
    def kernel(rows_ref, all_ref, sq_s, sq_r, core_s, core_r, own):
        chip, core, fsdp, _ = place(n_ctx)
        ctx = chip * 2 + core
        sibling = (chip * 2 + 1 - core, fsdp)
        greet([sibling] + fsdp_peers(n_fsdp, ctx, fsdp))
        mine = pltpu.make_async_copy(rows_ref, all_ref.at[core, fsdp], own)
        mine.start()
        handed = [send(rows_ref, all_ref.at[core, fsdp], (core_s, core_r), 0, sibling)]
        handed[0].start()
        arriving = [send(rows_ref, all_ref.at[1 - core, fsdp], (core_s, core_r), 0, sibling)]

        def passed(source, owner, part, index):
            target = all_ref.at[core, owner] if part is None else all_ref.at[core, owner, part]
            handed.append(send(source, target, (core_s, core_r), index + 1, sibling))
            handed[-1].start()
            target = all_ref.at[1 - core, owner] if part is None else all_ref.at[1 - core, owner, part]
            arriving.append(send(source, target, (core_s, core_r), index + 1, sibling))

        run_all(square_gather(rows_ref, all_ref.at[core], (sq_s, sq_r), ctx, fsdp, n_fsdp, passed))
        for out, back in zip(handed, arriving):
            out.wait_send()
            back.wait_recv()
        mine.wait()

    return pl.pallas_call(
        kernel,
        out_shape=jax.ShapeDtypeStruct((2, n_fsdp) + rows.shape, rows.dtype),
        in_specs=any_specs(1),
        out_specs=pl.BlockSpec(memory_space=pl.ANY),
        scratch_shapes=dma_pair(max(6, n_fsdp)) + dma_pair(max(7, n_fsdp)) + [pltpu.SemaphoreType.DMA],
        compiler_params=params(1),
        name="square_core_gather",
    )(rows)


def add_into(target, *sources, chunk=64):
    @pl.loop(0, target.shape[0] // chunk)
    def _(step):
        rows = pl.ds(pl.multiple_of(step * chunk, chunk), chunk)
        total = target[rows].astype(jnp.float32)
        for source in sources:
            total = total + source[rows].astype(jnp.float32)
        target[rows] = total.astype(target.dtype)


def square_sum(n_ctx, n_fsdp, partial, with_core, collective_id):
    rows, columns = partial.shape[-2:]
    half = rows // 2

    def kernel(partial_ref, out_ref, held, core_in, square_in, load, core_s, core_r, sq_s, sq_r):
        chip, core, fsdp, _ = place(n_ctx)
        ctx = chip * 2 + core
        sibling = (chip * 2 + 1 - core, fsdp)
        greet(([sibling] if with_core else []) + fsdp_peers(n_fsdp, ctx, fsdp))
        if n_fsdp == 4:
            first, second, corner = fsdp_neighbours(fsdp)
            order = [corner, first, second, fsdp]
        else:
            order = [(fsdp + j) % n_fsdp for j in range(1, n_fsdp + 1)]
        mine, others = [], []
        for j, owner in enumerate(order):
            source = partial_ref.at[core, owner] if with_core else partial_ref.at[owner]
            mine.append(pltpu.make_async_copy(source, held.at[owner], load.at[j]))
            if with_core:
                others.append(
                    send(partial_ref.at[1 - core, owner], core_in.at[owner], (core_s, core_r), j, sibling)
                )
                others[-1].start()
            mine[-1].start()

        def ready(j):
            mine[j].wait()
            if with_core:
                others[j].wait_recv()
                add_into(held.at[order[j]], core_in.at[order[j]])

        if n_fsdp != 4:
            copies = []
            for j in range(n_fsdp - 1):
                ready(j)
                copies.append(
                    send(held.at[order[j]], square_in.at[j], (sq_s, sq_r), j, (ctx, order[j]))
                )
                copies[-1].start()
            ready(n_fsdp - 1)
            total = held.at[fsdp]
            for j, copy in enumerate(copies):
                copy.wait()
            @pl.loop(0, rows // 64)
            def _(step):
                at = pl.ds(pl.multiple_of(step * 64, 64), 64)
                value = total[at].astype(jnp.float32)
                for j in range(n_fsdp - 1):
                    value = value + square_in[j, at].astype(jnp.float32)
                out_ref[at] = value
        else:
            top, low_half = pl.ds(0, half), pl.ds(half, half)
            to_first, to_second = (ctx, first), (ctx, second)

            def copy(index, owner, part, peer):
                return send(
                    held.at[owner, part], square_in.at[index], (sq_s, sq_r), index, peer
                )

            copies = [
                copy(0, corner, top, to_first),
                copy(1, corner, low_half, to_second),
                copy(2, first, top, to_first),
                copy(3, second, low_half, to_second),
                copy(4, second, top, to_second),
                copy(5, first, low_half, to_first),
            ]
            ready(0)
            copies[0].start()
            copies[1].start()
            ready(1)
            copies[2].start()
            ready(2)
            copies[3].start()
            copies[0].wait_recv()
            add_into(held.at[second, top], square_in.at[0])
            copies[4].start()
            copies[1].wait_recv()
            add_into(held.at[first, low_half], square_in.at[1])
            copies[5].start()
            ready(3)
            for j in range(2, 6):
                copies[j].wait_recv()
            for part, sources in ((0, (2, 4)), (half, (3, 5))):

                @pl.loop(0, half // 64)
                def _(step):
                    at = pl.ds(pl.multiple_of(part + step * 64, 64), 64)
                    from_at = pl.ds(pl.multiple_of(step * 64, 64), 64)
                    value = held[fsdp, at].astype(jnp.float32)
                    for j in sources:
                        value = value + square_in[j, from_at].astype(jnp.float32)
                    out_ref[at] = value

            for each in copies:
                each.wait_send()
        for each in others:
            each.wait_send()

    pieces = (6, half, columns) if n_fsdp == 4 else (n_fsdp - 1, rows, columns)
    return pl.pallas_call(
        kernel,
        out_shape=jax.ShapeDtypeStruct((rows, columns), jnp.float32),
        in_specs=any_specs(1),
        out_specs=pl.BlockSpec(memory_space=pltpu.VMEM),
        scratch_shapes=[
            pltpu.VMEM((n_fsdp, rows, columns), partial.dtype),
            pltpu.VMEM((n_fsdp, rows, columns) if with_core else (1, 16, 128), partial.dtype),
            pltpu.VMEM(pieces, partial.dtype),
            pltpu.SemaphoreType.DMA((n_fsdp,)),
        ]
        + dma_pair(n_fsdp)
        + dma_pair(max(6, n_fsdp)),
        compiler_params=params(collective_id),
        name="square_sum",
    )(partial)


def line_sum(n_ctx, partial, collective_id):
    rows, columns = partial.shape[-2:]
    length = n_ctx // 2

    def kernel(partial_ref, out_ref, held, core_in, right_in, left_in, load, core_s, core_r, right_s, right_r, left_s, left_r):
        where = place(n_ctx)
        chip, core, fsdp, _ = where
        sibling, right, left = line_peers(*where)
        greet([sibling, right, left])
        order = [(chip + length - 1 - j) % length for j in range(length)]
        mine, others = [], []
        for j, owner in enumerate(order):
            mine.append(pltpu.make_async_copy(partial_ref.at[owner * 2 + core], held.at[owner], load.at[j]))
            others.append(
                send(partial_ref.at[owner * 2 + 1 - core], core_in.at[owner], (core_s, core_r), j, sibling)
            )
            others[-1].start()
            mine[-1].start()
        for j, owner in enumerate(order):
            mine[j].wait()
            others[j].wait_recv()
            add_into(held.at[owner], core_in.at[owner])
        ways = ((1, right, right_in, (right_s, right_r)), (-1, left, left_in, (left_s, left_r)))
        for step in range(length - 1):
            for sign, peer, arrived, sems in ways:
                block = chip + sign * (length - 1 - step)
                inside = (block >= 0) & (block < length)

                came = (chip >= 1) if sign > 0 else (chip < length - 1)
                if step > 0:

                    @pl.when(inside & came)
                    def _():
                        send(held.at[block], arrived.at[step - 1], sems, step - 1, peer).wait_recv()
                        add_into(held.at[block], arrived.at[step - 1])

                @pl.when(inside)
                def _():
                    send(held.at[block], arrived.at[step], sems, step, peer).start()

        last = length - 2
        for sign, peer, arrived, sems in ways:
            came = (chip >= 1) if sign > 0 else (chip < length - 1)

            @pl.when(came)
            def _():
                send(held.at[chip], arrived.at[last], sems, last, peer).wait_recv()
                add_into(held.at[chip], arrived.at[last])

        @pl.loop(0, rows // 64)
        def _(step):
            at = pl.ds(pl.multiple_of(step * 64, 64), 64)
            out_ref[at] = held[chip, at].astype(jnp.float32)

        for step in range(length - 1):
            for sign, peer, arrived, sems in ways:
                block = chip + sign * (length - 1 - step)

                @pl.when((block >= 0) & (block < length))
                def _():
                    send(held.at[block], arrived.at[step], sems, step, peer).wait_send()

        for each in others:
            each.wait_send()

    return pl.pallas_call(
        kernel,
        out_shape=jax.ShapeDtypeStruct((rows, columns), jnp.float32),
        in_specs=any_specs(1),
        out_specs=pl.BlockSpec(memory_space=pltpu.VMEM),
        scratch_shapes=[
            pltpu.VMEM((length, rows, columns), partial.dtype),
            pltpu.VMEM((length, rows, columns), partial.dtype),
            pltpu.VMEM((length - 1, rows, columns), partial.dtype),
            pltpu.VMEM((length - 1, rows, columns), partial.dtype),
            pltpu.SemaphoreType.DMA((length,)),
        ]
        + dma_pair(length)
        + dma_pair(length)
        + dma_pair(length),
        compiler_params=params(collective_id),
        name="line_sum",
    )(partial)


def sum_everywhere(n_ctx, n_fsdp, values):
    ctx_steps = [1 << i for i in range(n_ctx.bit_length() - 1)]
    fsdp_steps = [1 << i for i in range(n_fsdp.bit_length() - 1)]
    rounds = len(ctx_steps) + len(fsdp_steps)

    def kernel(values_ref, out_ref, out_buf, arrived, sent_s, sent_r):
        ctx = lax.axis_index("ctx")
        fsdp = lax.axis_index("fsdp")
        peers = [(ctx + s - 2 * s * (ctx // s % 2), fsdp) for s in ctx_steps]
        peers += [(ctx, fsdp + s - 2 * s * (fsdp // s % 2)) for s in fsdp_steps]
        greet(peers)
        out_buf[0] = values_ref[...]
        for j, peer in enumerate(peers):
            copy = send(out_buf.at[j], arrived.at[j], (sent_s, sent_r), j, peer)
            copy.start()
            copy.wait()
            out_buf[j + 1] = out_buf[j] + arrived[j]
        out_ref[...] = out_buf[rounds]

    return pl.pallas_call(
        kernel,
        out_shape=jax.ShapeDtypeStruct(values.shape, values.dtype),
        in_specs=[pl.BlockSpec(memory_space=pltpu.VMEM)],
        out_specs=pl.BlockSpec(memory_space=pltpu.VMEM),
        scratch_shapes=[
            pltpu.VMEM((rounds + 1,) + values.shape, values.dtype),
            pltpu.VMEM((rounds,) + values.shape, values.dtype),
        ]
        + dma_pair(rounds),
        compiler_params=params(2),
        name="sum_everywhere",
    )(values)


def ffn_forward(rows, planes, core, length, n_own, chunk=256):
    blocks, _, tokens, features = rows.shape
    total = blocks * tokens
    wide = features // length
    steps = n_own // chunk
    group = max(1, 256 // tokens)

    def kernel(core_ref, rows_ref, gate_ref, up_ref, down_ref, hidden_ref, grad_gate_ref, grad_up_ref, weight_ref):
        for at in range(0, blocks, group):
            here = rows_ref[at : at + group, 0].reshape(group * tokens, features)
            back = rows_ref[at : at + group, 1].reshape(group * tokens, features)
            gate = mm(here, gate_ref[0], CONTRACT_LAST)
            up = mm(here, up_ref[0], CONTRACT_LAST)
            grad_hidden = mm(back, down_ref[0], CONTRACT_LAST)
            sigmoid = jax.nn.sigmoid(gate)
            activated = gate * sigmoid
            span = pl.ds(at * tokens, group * tokens)
            hidden_ref[span] = low(activated * up)
            grad_gate_ref[span] = low(grad_hidden * up * sigmoid * (1.0 + gate * (1.0 - sigmoid)))
            grad_up_ref[span] = low(grad_hidden * activated)
        for plane, (left, which) in enumerate(((grad_gate_ref, 0), (grad_up_ref, 0), (hidden_ref, 1))):
            left = left[...]
            for z in range(length):
                right = rows_ref[:, which, :, z * wide : (z + 1) * wide].reshape(total, wide)
                weight_ref[z, plane] = low(mm(left, right, CONTRACT_FIRST))

    def weight_spec(plane):
        return pl.BlockSpec((1, chunk, features), lambda j, core_ref: (plane, core_ref[0] * steps + j, 0))

    act = jax.ShapeDtypeStruct((total, n_own), jnp.bfloat16)
    act_spec = pl.BlockSpec((total, chunk), lambda j, core_ref: (0, j))
    return pl.pallas_call(
        kernel,
        grid_spec=pltpu.PrefetchScalarGridSpec(
            num_scalar_prefetch=1,
            grid=(steps,),
            in_specs=[
                pl.BlockSpec(rows.shape, lambda j, core_ref: (0, 0, 0, 0), pipeline_mode=pl.Buffered(1)),
                weight_spec(0),
                weight_spec(1),
                weight_spec(2),
            ],
            out_specs=[
                act_spec,
                act_spec,
                act_spec,
                pl.BlockSpec((length, 3, chunk, wide), lambda j, core_ref: (0, 0, j, 0)),
            ],
        ),
        out_shape=[act, act, act, jax.ShapeDtypeStruct((length, 3, n_own, wide), jnp.bfloat16)],
        compiler_params=params(),
        cost_estimate=pl.CostEstimate(
            flops=12 * total * n_own * features, bytes_accessed=40 * 1024 * 1024, transcendentals=total * n_own
        ),
        name="ffn_forward",
    )(core, rows, planes, planes, planes)


def ffn_back(hidden, grad_gate, grad_up, planes, core, blocks, wide=512):
    total, n_own = hidden.shape
    features = planes.shape[2]
    tokens = total // blocks

    def kernel(core_ref, hidden_ref, grad_gate_ref, grad_up_ref, gate_ref, up_ref, down_ref, out_ref):
        out = mm(hidden_ref[...], down_ref[0])
        out_ref[:, 0] = low(out).reshape(blocks, tokens, wide)
        back = mm(grad_gate_ref[...], gate_ref[0]) + mm(grad_up_ref[...], up_ref[0])
        out_ref[:, 1] = low(back).reshape(blocks, tokens, wide)

    def weight_spec(plane):
        return pl.BlockSpec((1, n_own, wide), lambda j, core_ref: (plane, core_ref[0], j))

    act_spec = pl.BlockSpec((total, n_own), lambda j, core_ref: (0, 0), pipeline_mode=pl.Buffered(1))
    return pl.pallas_call(
        kernel,
        grid_spec=pltpu.PrefetchScalarGridSpec(
            num_scalar_prefetch=1,
            grid=(features // wide,),
            in_specs=[act_spec, act_spec, act_spec, weight_spec(0), weight_spec(1), weight_spec(2)],
            out_specs=pl.BlockSpec((blocks, 2, tokens, wide), lambda j, core_ref: (0, 0, 0, j)),
        ),
        out_shape=jax.ShapeDtypeStruct((blocks, 2, tokens, features), jnp.bfloat16),
        compiler_params=params(),
        cost_estimate=pl.CostEstimate(
            flops=6 * total * n_own * features, bytes_accessed=30 * 1024 * 1024, transcendentals=0
        ),
        name="ffn_back",
    )(core, hidden, grad_gate, grad_up, planes, planes, planes)


def local(n_ctx, n_fsdp, streams, w_attn, w_ffn, hc_dynamic, hc_static, cotangent, pair_order):
    number = streams.shape[1]
    length = streams.shape[2]
    features = streams.shape[3]
    size = HEAD_DIM
    own = features // n_ctx
    heads = own // size
    rows = length * n_ctx
    own_rows = w_attn.shape[0]
    ctx = lax.axis_index("ctx")
    fsdp = lax.axis_index("fsdp")
    core = ctx % 2
    chips = n_ctx // 2
    core_index = jnp.reshape(core, (1,)).astype(jnp.int32)

    def in_order(mine, other, axis):
        return jnp.where(
            core == 0, jnp.concatenate([mine, other], axis=axis), jnp.concatenate([other, mine], axis=axis)
        )


    w_planes = jnp.moveaxis(w_attn, 1, 0)
    w_own = lax.dynamic_slice_in_dim(w_planes[0:3], ctx * own, own, 2)
    w_own = jnp.moveaxis(w_own, 0, 1).reshape(own_rows, 3 * own)
    half = features // 2
    w_out_mine = gather(lax.dynamic_slice_in_dim(w_planes[3], core * half, half, 1), "fsdp")
    w_out_other = lax.ppermute(w_out_mine, "ctx", [(i, i ^ 1) for i in range(n_ctx)])

    positions = block_positions(pair_order, length)
    cosine_table, sine_table = rope_tables(positions, size)
    allowed = positions[:, None] >= positions[None, :]

    inputs = streams[0].astype(jnp.float32)
    normed_one, inverse_one, dynamic_one, coef_one = mixing(inputs, hc_dynamic[0], hc_static[0])
    mixed_one = branch_input(inputs, coef_one)
    attn_normed, attn_inverse = normalize(mixed_one)
    attn_low = low(attn_normed)
    attn_all, w_qkv = attention_gather(n_ctx, n_fsdp, attn_low, w_own)
    attn_all = attn_all.reshape(rows, features)
    w_qkv = w_qkv.reshape(features, 3 * own)
    qkv = mm(attn_all, w_qkv).reshape(rows, 3, heads, size)
    query = low(rotate(qkv[:, 0], cosine_table, sine_table))
    key = low(rotate(qkv[:, 1], cosine_table, sine_table))
    value = low(qkv[:, 2])
    outs, logs = [], []
    for h in range(heads):
        out, log_total = attend(query[:, h], key[:, h], value[:, h], allowed)
        outs.append(out)
        logs.append(log_total)
    attended = low(jnp.concatenate(outs, axis=1))
    attended_rows = lax.all_to_all(attended, "ctx", 0, 1, tiled=True)
    attn_branch = in_order(mm(attended_rows, w_out_mine), mm(attended_rows, w_out_other), 1)
    attended_cols = lax.all_to_all(attended_rows, "fsdp", 1, 0, tiled=True)

    first_out = mix_output(inputs, coef_one, attn_branch)
    normed_two, inverse_two, dynamic_two, coef_two = mixing(first_out, hc_dynamic[1], hc_static[1])
    mixed_two = branch_input(first_out, coef_two)
    ffn_normed, ffn_inverse = normalize(mixed_two)
    ffn_low = low(ffn_normed)
    grad_final = cotangent[0].astype(jnp.float32)
    grad_ffn = low(sum((coef_two[j, :, 0:1] * grad_final[j] for j in range(number))))

    planes = jnp.moveaxis(w_ffn, 1, 0)
    n_own = planes.shape[1] // 2
    blocks = 2 * n_fsdp
    ffn_rows = square_core_gather(n_ctx, n_fsdp, jnp.stack([ffn_low, grad_ffn]).reshape(2 * length, features))
    ffn_rows = ffn_rows.reshape(blocks, 2, length, features)
    hidden, grad_gate, grad_up, weight_parts = ffn_forward(ffn_rows, planes, core_index, chips, n_own)
    lines = [[2 * i + j for i in range(chips)] for j in range(2)]
    weight_cols = lax.psum_scatter(weight_parts, "ctx", scatter_dimension=0, axis_index_groups=lines)
    sums = ffn_back(hidden, grad_gate, grad_up, planes, core_index, blocks)
    sums = square_sum(n_ctx, n_fsdp, sums.reshape(2, n_fsdp, 2 * length, features), True, 3)
    ffn_branch = sums[:length]
    grad_ffn_normed = sums[length:]
    mine = lax.dynamic_slice_in_dim(weight_cols, core * own, own, 2)
    other = lax.dynamic_slice_in_dim(weight_cols, (1 - core) * own, own, 2)
    other = lax.ppermute(other, "ctx", [(i, i ^ 1) for i in range(n_ctx)])
    ffn_grad = jnp.moveaxis(in_order(mine, other, 1), 0, 1).astype(jnp.float32)

    second_out = mix_output(first_out, coef_two, ffn_branch)
    streams_out = low(second_out)[None]

    def connect_back(
        values, normed, inverse, dynamic_part, coefficients, dynamic, branch_out, grad_out, grad_mixed
    ):
        coef_rows = []
        grads = []
        for i in range(number):
            coef_rows.append(
                jnp.stack(
                    [
                        jnp.sum(grad_out[i] * branch_out, axis=-1),
                        jnp.sum(grad_mixed * values[i], axis=-1),
                    ]
                    + [jnp.sum(grad_out[j] * values[i], axis=-1) for j in range(number)],
                    axis=-1,
                )
            )
            grads.append(
                sum((coefficients[i, :, 2 + j : 3 + j] * grad_out[j] for j in range(number)))
                + coefficients[i, :, 1:2] * grad_mixed
            )
        coef_grad = jnp.stack(coef_rows)
        pre_grad = coef_grad * (1.0 - dynamic_part * dynamic_part)
        dynamic_grad = jnp.einsum("stk,std->kd", pre_grad, normed, precision=HIGH)
        normed_grad = jnp.einsum("stk,kd->std", pre_grad, dynamic, precision=HIGH)
        grads = jnp.stack(grads) + normalize_back(normed, inverse, normed_grad)
        return (grads, dynamic_grad, jnp.sum(coef_grad, axis=1))

    grad_mixed_two = normalize_back(ffn_normed, ffn_inverse, grad_ffn_normed)
    grad_first, dynamic_grad_two, static_grad_two = connect_back(
        first_out, normed_two, inverse_two, dynamic_two, coef_two, hc_dynamic[1], ffn_branch, grad_final, grad_mixed_two
    )

    grad_attn = low(sum((coef_one[j, :, 0:1] * grad_first[j] for j in range(number))))
    grad_attended = low(
        mm(lax.dynamic_slice_in_dim(grad_attn, core * half, half, 1), w_out_mine, CONTRACT_LAST)
        + mm(lax.dynamic_slice_in_dim(grad_attn, (1 - core) * half, half, 1), w_out_other, CONTRACT_LAST)
    )
    grad_heads = lax.all_to_all(grad_attended, "ctx", 1, 0, tiled=True)
    grad_attn_rows = square_rows(n_ctx, n_fsdp, grad_attn).reshape(n_fsdp * length, n_ctx, own)
    out_part = low(jnp.einsum("tn,tke->kne", attended_cols, grad_attn_rows, preferred_element_type=jnp.float32))
    out_grad = line_sum(n_ctx, out_part, 4)
    parts = []
    for h in range(heads):
        parts.append(
            attend_back(
                query[:, h], key[:, h], value[:, h], grad_heads[:, h * size : (h + 1) * size], logs[h], allowed
            )
        )
    query_grad, key_grad, value_grad = (jnp.stack([p[i] for p in parts], axis=1) for i in range(3))
    qkv_grad = low(
        jnp.stack(
            [
                rotate_back(query_grad, cosine_table, sine_table),
                rotate_back(key_grad, cosine_table, sine_table),
                value_grad,
            ],
            axis=1,
        ).reshape(rows, 3 * own)
    )
    attn_part = low(mm(qkv_grad, w_qkv, CONTRACT_LAST)).reshape(n_ctx, length, features)
    grad_attn_normed = line_sum(n_ctx, attn_part, 5)
    inner_part = low(mm(attn_all, qkv_grad, CONTRACT_FIRST)).reshape(n_fsdp, own_rows, 3 * own)
    inner_grad = square_sum(n_ctx, n_fsdp, inner_part, False, 6).reshape(own_rows, 3, own)
    attn_grad = jnp.concatenate([inner_grad, out_grad[:, None]], axis=1).astype(jnp.float32)

    grad_mixed_one = normalize_back(attn_normed, attn_inverse, grad_attn_normed)
    grad_inputs, dynamic_grad_one, static_grad_one = connect_back(
        inputs, normed_one, inverse_one, dynamic_one, coef_one, hc_dynamic[0], attn_branch, grad_first, grad_mixed_one
    )
    small = jnp.concatenate(
        [
            dynamic_grad_one,
            dynamic_grad_two,
            jnp.pad(
                jnp.concatenate([static_grad_one.reshape(1, -1), static_grad_two.reshape(1, -1)]),
                ((0, 2), (0, features - 6 * number)),
            ),
        ]
    )
    small = sum_everywhere(n_ctx, n_fsdp, small)
    dynamic_total = small[:12].reshape(2, 6, features)
    static_total = small[12:14, : 6 * number].reshape(2, number, 6)
    return (streams_out, grad_inputs[None], attn_grad, ffn_grad, dynamic_total, static_total)


def solution(mesh):
    return jax.shard_map(
        functools.partial(local, mesh.shape["ctx"], mesh.shape["fsdp"]),
        mesh=mesh,
        in_specs=(
            P("fsdp", None, "ctx", None),
            P("fsdp", None, None),
            P("fsdp", None, None),
            P(),
            P(),
            P("fsdp", None, "ctx", None),
            P(),
        ),
        out_specs=(
            P("fsdp", None, "ctx", None),
            P("fsdp", None, "ctx", None),
            P("fsdp", None, "ctx"),
            P("fsdp", None, "ctx"),
            P(),
            P(),
        ),
        check_vma=False,
    )
```

```python
import functools

import jax
import jax.numpy as jnp
from jax import lax
from jax.experimental import pallas as pl
from jax.experimental.pallas import tpu as pltpu
from jax.sharding import PartitionSpec as P

HEADS = 16
HEAD_DIM = 128


EPS = 1e-05
THETA = 10000.0
HIGH = lax.Precision.HIGHEST
MASKED = -1e30
CONTRACT_LAST = (((1,), (1,)), ((), ()))
CONTRACT_FIRST = (((0,), (0,)), ((), ()))


def normalize(values):
    centered = values - jnp.mean(values, axis=-1, keepdims=True)
    inverse = lax.rsqrt(jnp.mean(centered * centered, axis=-1, keepdims=True) + EPS)
    return (centered * inverse, inverse)


def normalize_back(normed, inverse, gradient):
    inner = jnp.mean(gradient * normed, axis=-1, keepdims=True)
    return inverse * (gradient - jnp.mean(gradient, axis=-1, keepdims=True) - normed * inner)


def block_positions(pair_order, length):
    half_size = length // 2
    offsets = jnp.arange(half_size, dtype=jnp.int32)
    mirror = 2 * pair_order.shape[0] - 1 - pair_order
    first_half = pair_order[:, None] * half_size + offsets[None, :]
    second_half = mirror[:, None] * half_size + offsets[None, :]
    return jnp.concatenate([first_half, second_half], axis=1).reshape(-1)


def low(values):
    return values.astype(jnp.bfloat16)


def mm(a, b, dims=None):
    if dims is None:
        return jnp.dot(a, b, preferred_element_type=jnp.float32)
    return lax.dot_general(a, b, dims, preferred_element_type=jnp.float32)


def gather(values, axis, dim=0):
    return lax.all_gather(values, axis, axis=dim, tiled=True)


def scatter(values, axis, dim=0):
    return lax.psum_scatter(values, axis, scatter_dimension=dim, tiled=True)


MESH = pl.DeviceIdType.MESH
VMEM_LIMIT = 60 * 1024 * 1024


def place(n_ctx):
    ctx = lax.axis_index("ctx")
    return (ctx // 2, ctx % 2, lax.axis_index("fsdp"), n_ctx // 2)


def greet(peers):
    barrier = pltpu.get_barrier_semaphore()
    for peer in peers:
        pl.semaphore_signal(barrier, inc=1, device_id=peer, device_id_type=MESH)
    pl.semaphore_wait(barrier, len(peers))


def send(source, target, sems, index, peer):
    return pltpu.make_async_remote_copy(
        src_ref=source,
        dst_ref=target,
        send_sem=sems[0].at[index],
        recv_sem=sems[1].at[index],
        device_id=peer,
        device_id_type=MESH,
    )


def fsdp_neighbours(fsdp):
    first = fsdp + 1 - 2 * (fsdp % 2)
    second = (fsdp + 2) % 4
    return (first, second, (first + 2) % 4)


def fsdp_peers(n_fsdp, ctx, fsdp):
    if n_fsdp == 4:
        first, second, _ = fsdp_neighbours(fsdp)
        return [(ctx, first), (ctx, second)]
    return [(ctx, (fsdp + j) % n_fsdp) for j in range(1, n_fsdp)]


def line_peers(chip, core, fsdp, length):
    return [
        (chip * 2 + 1 - core, fsdp),
        ((chip + 1) % length * 2 + core, fsdp),
        ((chip + length - 1) % length * 2 + core, fsdp),
    ]


def line_gather(own_ref, all_ref, sems, where):
    chip, core, fsdp, length = where
    right_sems, left_sems, core_sems = sems
    sibling = (chip * 2 + 1 - core, fsdp)
    right = ((chip + 1) % length * 2 + core, fsdp)
    left = ((chip + length - 1) % length * 2 + core, fsdp)

    def block(index):
        return all_ref.at[(index + length) % length * 2 + core]

    def pass_on(index, source):
        return send(source, block(index), core_sems, (index + length) % length, sibling)

    pass_on(chip, own_ref).start()
    for step in range(length - 1):
        for sign, peer, way in ((-1, right, right_sems), (1, left, left_sems)):
            at = chip + sign * step
            held = (at >= 0) & (at < length)
            if step > 0:

                @pl.when(held)
                def _():
                    send(block(at), block(at), way, step - 1, peer).wait_recv()
                    pass_on(at, block(at)).start()

            more = (chip < length - 1) if sign < 0 else (chip > 0)

            @pl.when(held & more)
            def _():
                send(own_ref if step == 0 else block(at), block(at), way, step, peer).start()

        yield
    last = length - 1
    for sign, peer, way in ((-1, right, right_sems), (1, left, left_sems)):
        at = chip + sign * last

        @pl.when((at >= 0) & (at < length))
        def _():
            send(block(at), block(at), way, last - 1, peer).wait_recv()
            pass_on(at, block(at)).start()

    yield
    for step in range(length - 1):
        for sign, peer, way in ((-1, right, right_sems), (1, left, left_sems)):
            at = chip + sign * step
            more = (chip < length - 1) if sign < 0 else (chip > 0)

            @pl.when((at >= 0) & (at < length) & more)
            def _():
                send(block(at), block(at), way, step, peer).wait_send()

    for index in range(length):
        pass_on(index, block(index)).wait_send()
        other = all_ref.at[index * 2 + 1 - core]
        send(other, other, core_sems, index, sibling).wait_recv()


def square_gather(own_ref, all_ref, sems, ctx, fsdp, n_fsdp, passed=None):
    if n_fsdp != 4:
        copies = [
            send(own_ref, all_ref.at[fsdp], sems, j - 1, (ctx, (fsdp + j) % n_fsdp)) for j in range(1, n_fsdp)
        ]
        for copy in copies:
            copy.start()
        yield
        for j, copy in enumerate(copies):
            copy.wait()
            if passed:
                passed(all_ref.at[(fsdp + n_fsdp - j - 1) % n_fsdp], (fsdp + n_fsdp - j - 1) % n_fsdp, None, j)
        return
    first, second, corner = fsdp_neighbours(fsdp)
    half = own_ref.shape[0] // 2
    top, low_half = pl.ds(0, half), pl.ds(half, half)
    to_first, to_second = (ctx, first), (ctx, second)

    def copy(index, owner, part, peer, source=None):
        source = all_ref.at[owner, part] if source is None else source
        return send(source, all_ref.at[owner, part], sems, index, peer)

    starts = [
        copy(0, fsdp, top, to_first, own_ref.at[top]),
        copy(1, fsdp, low_half, to_second, own_ref.at[low_half]),
        copy(2, fsdp, low_half, to_first, own_ref.at[low_half]),
        copy(3, fsdp, top, to_second, own_ref.at[top]),
        copy(4, first, top, to_second),
        copy(5, second, low_half, to_first),
    ]
    arrivals = [
        (0, first, top),
        (1, second, low_half),
        (2, first, low_half),
        (3, second, top),
        (4, corner, top),
        (5, corner, low_half),
    ]
    for each in starts[:4]:
        each.start()
    yield
    for index, owner, part in arrivals:
        copy(index, owner, part, to_first).wait_recv()
        if index < 2:
            starts[4 + index].start()
        if passed:
            passed(all_ref.at[owner, part], owner, part, index)
        yield
    for each in starts:
        each.wait_send()


def run_all(*parts):
    parts = list(parts)
    while parts:
        for part in list(parts):
            try:
                next(part)
            except StopIteration:
                parts.remove(part)


def dma_pair(count):
    return [pltpu.SemaphoreType.DMA((count,)), pltpu.SemaphoreType.DMA((count,))]


def any_specs(count):
    return [pl.BlockSpec(memory_space=pl.ANY)] * count


def params(collective_id=None, **more):
    if collective_id is not None:
        more.update(collective_id=collective_id, has_side_effects=True)
    return pltpu.CompilerParams(vmem_limit_bytes=VMEM_LIMIT, **more)


def passing(own_ref, all_ref, sems, core, fsdp, sibling):
    handed = [send(own_ref, all_ref.at[core, fsdp], sems, 0, sibling)]
    handed[0].start()
    arriving = [send(own_ref, all_ref.at[1 - core, fsdp], sems, 0, sibling)]

    def passed(source, owner, part, index):
        for side, copies in ((core, handed), (1 - core, arriving)):
            target = all_ref.at[side, owner] if part is None else all_ref.at[side, owner, part]
            copies.append(send(source, target, sems, index + 1, sibling))
        handed[-1].start()

    def finish():
        for out, back in zip(handed, arriving):
            out.wait_send()
            back.wait_recv()

    return (passed, finish)


def line_rows(n_ctx, rows):
    def kernel(rows_ref, all_rows, right_s, right_r, left_s, left_r, core_s, core_r, own):
        where = place(n_ctx)
        chip, core, fsdp, length = where
        greet(line_peers(*where))
        mine = pltpu.make_async_copy(rows_ref, all_rows.at[chip * 2 + core], own)
        mine.start()
        run_all(line_gather(rows_ref, all_rows, ((right_s, right_r), (left_s, left_r), (core_s, core_r)), where))
        mine.wait()

    length = n_ctx // 2
    return pl.pallas_call(
        kernel,
        out_shape=jax.ShapeDtypeStruct((n_ctx,) + rows.shape, rows.dtype),
        in_specs=any_specs(1),
        out_specs=pl.BlockSpec(memory_space=pl.ANY),
        scratch_shapes=dma_pair(length) + dma_pair(length) + dma_pair(length) + [pltpu.SemaphoreType.DMA],
        compiler_params=params(0),
        name="line_rows",
    )(rows)


def square_core_gather(n_ctx, n_fsdp, rows):
    def kernel(rows_ref, all_ref, sq_s, sq_r, core_s, core_r, own):
        chip, core, fsdp, _ = place(n_ctx)
        ctx = chip * 2 + core
        sibling = (chip * 2 + 1 - core, fsdp)
        greet([sibling] + fsdp_peers(n_fsdp, ctx, fsdp))
        mine = pltpu.make_async_copy(rows_ref, all_ref.at[core, fsdp], own)
        mine.start()
        passed, finish = passing(rows_ref, all_ref, (core_s, core_r), core, fsdp, sibling)
        run_all(square_gather(rows_ref, all_ref.at[core], (sq_s, sq_r), ctx, fsdp, n_fsdp, passed))
        finish()
        mine.wait()

    return pl.pallas_call(
        kernel,
        out_shape=jax.ShapeDtypeStruct((2, n_fsdp) + rows.shape, rows.dtype),
        in_specs=any_specs(1),
        out_specs=pl.BlockSpec(memory_space=pl.ANY),
        scratch_shapes=dma_pair(max(6, n_fsdp)) + dma_pair(max(7, n_fsdp)) + [pltpu.SemaphoreType.DMA],
        compiler_params=params(1),
        name="square_core_gather",
    )(rows)


def add_into(target, *sources, chunk=64):
    @pl.loop(0, target.shape[0] // chunk)
    def _(step):
        rows = pl.ds(pl.multiple_of(step * chunk, chunk), chunk)
        total = target[rows].astype(jnp.float32)
        for source in sources:
            total = total + source[rows].astype(jnp.float32)
        target[rows] = total.astype(target.dtype)


def square_sum_stages(n_ctx, n_fsdp, partial_ref, out_ref, held, core_in, square_in, load, core_sems, sems):
    rows = partial_ref.shape[-2]
    half = rows // 2
    chip, core, fsdp, _ = place(n_ctx)
    ctx = chip * 2 + core
    sibling = (chip * 2 + 1 - core, fsdp)
    if n_fsdp == 4:
        first, second, corner = fsdp_neighbours(fsdp)
        order = [corner, first, second, fsdp]
    else:
        order = [(fsdp + j) % n_fsdp for j in range(1, n_fsdp + 1)]
    mine = [
        pltpu.make_async_copy(partial_ref.at[core, owner], held.at[owner], load.at[j])
        for j, owner in enumerate(order)
    ]
    others = [
        send(partial_ref.at[1 - core, owner], core_in.at[owner], core_sems, j, sibling)
        for j, owner in enumerate(order)
    ]

    def ready(j):
        mine[j].wait()
        others[j].wait_recv()
        add_into(held.at[order[j]], core_in.at[order[j]])

    def total(parts, sources):
        @pl.loop(0, parts[1] // 64)
        def _(step):
            at = pl.ds(pl.multiple_of(parts[0] + step * 64, 64), 64)
            from_at = pl.ds(pl.multiple_of(step * 64, 64), 64)
            value = held[fsdp, at].astype(jnp.float32)
            for j in sources:
                value = value + square_in[j, from_at].astype(jnp.float32)
            out_ref[at] = value

    def begin():
        greet([sibling] + fsdp_peers(n_fsdp, ctx, fsdp))
        for j in range(n_fsdp):
            others[j].start()
            mine[j].start()

    if n_fsdp != 4:
        copies = [
            send(held.at[order[j]], square_in.at[j], sems, j, (ctx, order[j])) for j in range(n_fsdp - 1)
        ]

        def spread():
            for j in range(n_fsdp):
                ready(j)
                if j < n_fsdp - 1:
                    copies[j].start()

        def finish():
            for copy in copies:
                copy.wait()
            total((0, rows), range(n_fsdp - 1))
            for each in others:
                each.wait_send()

        return [begin, spread, finish]

    top, low_half = pl.ds(0, half), pl.ds(half, half)
    to_first, to_second = (ctx, first), (ctx, second)

    def copy(index, owner, part, peer):
        return send(held.at[owner, part], square_in.at[index], sems, index, peer)

    copies = [
        copy(0, corner, top, to_first),
        copy(1, corner, low_half, to_second),
        copy(2, first, top, to_first),
        copy(3, second, low_half, to_second),
        copy(4, second, top, to_second),
        copy(5, first, low_half, to_first),
    ]

    def spread():
        ready(0)
        copies[0].start()
        copies[1].start()
        ready(1)
        copies[2].start()
        ready(2)
        copies[3].start()
        ready(3)

    def pass_on():
        copies[0].wait_recv()
        add_into(held.at[second, top], square_in.at[0])
        copies[4].start()
        copies[1].wait_recv()
        add_into(held.at[first, low_half], square_in.at[1])
        copies[5].start()

    def finish():
        for j in range(2, 6):
            copies[j].wait_recv()
        total((0, half), (2, 4))
        total((half, half), (3, 5))
        for each in copies:
            each.wait_send()
        for each in others:
            each.wait_send()

    return [begin, spread, pass_on, finish]


def square_sum_scratch(n_fsdp, partial):
    rows, columns = partial.shape[-2:]
    pieces = (6, rows // 2, columns) if n_fsdp == 4 else (n_fsdp - 1, rows, columns)
    return (
        [
            pltpu.VMEM((n_fsdp, rows, columns), partial.dtype),
            pltpu.VMEM((n_fsdp, rows, columns), partial.dtype),
            pltpu.VMEM(pieces, partial.dtype),
            pltpu.SemaphoreType.DMA((n_fsdp,)),
        ]
        + dma_pair(n_fsdp)
        + dma_pair(max(6, n_fsdp))
    )


def square_sum(n_ctx, n_fsdp, partial):
    def kernel(partial_ref, out_ref, held, core_in, square_in, load, core_s, core_r, sq_s, sq_r):
        for stage in square_sum_stages(
            n_ctx, n_fsdp, partial_ref, out_ref, held, core_in, square_in, load, (core_s, core_r), (sq_s, sq_r)
        ):
            stage()

    return pl.pallas_call(
        kernel,
        out_shape=jax.ShapeDtypeStruct(partial.shape[-2:], jnp.float32),
        in_specs=any_specs(1),
        out_specs=pl.BlockSpec(memory_space=pltpu.VMEM),
        scratch_shapes=square_sum_scratch(n_fsdp, partial),
        compiler_params=params(1),
        name="square_sum",
    )(partial)


def line_sum(n_ctx, partial, collective_id):
    rows, columns = partial.shape[-2:]
    length = n_ctx // 2

    def kernel(partial_ref, out_ref, held, core_in, right_in, left_in, load, core_s, core_r, right_s, right_r, left_s, left_r):
        where = place(n_ctx)
        chip, core, fsdp, _ = where
        sibling, right, left = line_peers(*where)
        greet([sibling, right, left])
        order = [(chip + length - 1 - j) % length for j in range(length)]
        mine, others = [], []
        for j, owner in enumerate(order):
            mine.append(pltpu.make_async_copy(partial_ref.at[owner * 2 + core], held.at[owner], load.at[j]))
            others.append(
                send(partial_ref.at[owner * 2 + 1 - core], core_in.at[owner], (core_s, core_r), j, sibling)
            )
            others[-1].start()
            mine[-1].start()
        for j, owner in enumerate(order):
            mine[j].wait()
            others[j].wait_recv()
            add_into(held.at[owner], core_in.at[owner])
        ways = ((1, right, right_in, (right_s, right_r)), (-1, left, left_in, (left_s, left_r)))
        for step in range(length - 1):
            for sign, peer, arrived, sems in ways:
                block = chip + sign * (length - 1 - step)
                inside = (block >= 0) & (block < length)

                came = (chip >= 1) if sign > 0 else (chip < length - 1)
                if step > 0:

                    @pl.when(inside & came)
                    def _():
                        send(held.at[block], arrived.at[step - 1], sems, step - 1, peer).wait_recv()
                        add_into(held.at[block], arrived.at[step - 1])

                @pl.when(inside)
                def _():
                    send(held.at[block], arrived.at[step], sems, step, peer).start()

        last = length - 2
        for sign, peer, arrived, sems in ways:
            came = (chip >= 1) if sign > 0 else (chip < length - 1)

            @pl.when(came)
            def _():
                send(held.at[chip], arrived.at[last], sems, last, peer).wait_recv()
                add_into(held.at[chip], arrived.at[last])

        @pl.loop(0, rows // 64)
        def _(step):
            at = pl.ds(pl.multiple_of(step * 64, 64), 64)
            out_ref[at] = held[chip, at].astype(jnp.float32)

        for step in range(length - 1):
            for sign, peer, arrived, sems in ways:
                block = chip + sign * (length - 1 - step)

                @pl.when((block >= 0) & (block < length))
                def _():
                    send(held.at[block], arrived.at[step], sems, step, peer).wait_send()

        for each in others:
            each.wait_send()

    return pl.pallas_call(
        kernel,
        out_shape=jax.ShapeDtypeStruct((rows, columns), jnp.float32),
        in_specs=any_specs(1),
        out_specs=pl.BlockSpec(memory_space=pltpu.VMEM),
        scratch_shapes=[
            pltpu.VMEM((length, rows, columns), partial.dtype),
            pltpu.VMEM((length, rows, columns), partial.dtype),
            pltpu.VMEM((length - 1, rows, columns), partial.dtype),
            pltpu.VMEM((length - 1, rows, columns), partial.dtype),
            pltpu.SemaphoreType.DMA((length,)),
        ]
        + dma_pair(length)
        + dma_pair(length)
        + dma_pair(length),
        compiler_params=params(collective_id),
        name="line_sum",
    )(partial)


def sum_everywhere(n_ctx, n_fsdp, values):
    block = values.shape[1:]

    def kernel(values_ref, out_ref, along_ctx, along_fsdp, result, ctx_s, ctx_r, fsdp_s, fsdp_r, back_s, back_r):
        ctx = lax.axis_index("ctx")
        fsdp = lax.axis_index("fsdp")
        ctx_peers = [((ctx + j) % n_ctx, fsdp) for j in range(1, n_ctx)]
        fsdp_peers = [(ctx, (fsdp + j) % n_fsdp) for j in range(1, n_fsdp)]
        greet(ctx_peers + fsdp_peers)

        def exchange(copies):
            for copy in copies:
                copy.start()
            for copy in copies:
                copy.wait()

        def total(slots, count):
            value = slots[0]
            for j in range(1, count):
                value = value + slots[j]
            return value

        along_ctx[ctx] = values_ref[ctx]
        exchange(
            [
                send(values_ref.at[peer[0]], along_ctx.at[ctx], (ctx_s, ctx_r), j, peer)
                for j, peer in enumerate(ctx_peers)
            ]
        )
        along_fsdp[fsdp] = total(along_ctx, n_ctx)
        exchange(
            [
                send(along_fsdp.at[fsdp], along_fsdp.at[fsdp], (fsdp_s, fsdp_r), j, peer)
                for j, peer in enumerate(fsdp_peers)
            ]
        )
        result[ctx] = total(along_fsdp, n_fsdp)
        exchange(
            [send(result.at[ctx], result.at[ctx], (back_s, back_r), j, peer) for j, peer in enumerate(ctx_peers)]
        )
        out_ref[...] = result[...]

    return pl.pallas_call(
        kernel,
        out_shape=jax.ShapeDtypeStruct(values.shape, values.dtype),
        in_specs=[pl.BlockSpec(memory_space=pltpu.VMEM)],
        out_specs=pl.BlockSpec(memory_space=pltpu.VMEM),
        scratch_shapes=[
            pltpu.VMEM((n_ctx,) + block, values.dtype),
            pltpu.VMEM((n_fsdp,) + block, values.dtype),
            pltpu.VMEM((n_ctx,) + block, values.dtype),
        ]
        + dma_pair(n_ctx)
        + dma_pair(n_fsdp)
        + dma_pair(n_ctx),
        compiler_params=params(2),
        name="sum_everywhere",
    )(values)


def hidden_units(here, back, gate_ref, up_ref, down_ref):
    gate = mm(here, gate_ref[0], CONTRACT_LAST)
    up = mm(here, up_ref[0], CONTRACT_LAST)
    grad_hidden = mm(back, down_ref[0], CONTRACT_LAST)
    sigmoid = jax.nn.sigmoid(gate)
    activated = gate * sigmoid
    return (
        low(activated * up),
        low(grad_hidden * up * sigmoid * (1.0 + gate * (1.0 - sigmoid))),
        low(grad_hidden * activated),
    )


def ffn_forward(rows, planes, core, n_own, chunk=256):
    blocks, _, tokens, features = rows.shape
    total = blocks * tokens
    steps = n_own // chunk
    group = max(1, 256 // tokens)

    def kernel(core_ref, rows_ref, gate_ref, up_ref, down_ref, *outs):
        for at in range(0, blocks, group):
            here = rows_ref[at : at + group, 0].reshape(group * tokens, features)
            back = rows_ref[at : at + group, 1].reshape(group * tokens, features)
            span = pl.ds(at * tokens, group * tokens)
            for out, value in zip(outs, hidden_units(here, back, gate_ref, up_ref, down_ref)):
                out[span] = value

    def weight_spec(plane):
        return pl.BlockSpec((1, chunk, features), lambda j, core_ref: (plane, core_ref[0] * steps + j, 0))

    act = jax.ShapeDtypeStruct((total, n_own), jnp.bfloat16)
    act_spec = pl.BlockSpec((total, chunk), lambda j, core_ref: (0, j))
    return pl.pallas_call(
        kernel,
        grid_spec=pltpu.PrefetchScalarGridSpec(
            num_scalar_prefetch=1,
            grid=(steps,),
            in_specs=[
                pl.BlockSpec(rows.shape, lambda j, core_ref: (0, 0, 0, 0), pipeline_mode=pl.Buffered(1)),
                weight_spec(0),
                weight_spec(1),
                weight_spec(2),
            ],
            out_specs=[act_spec, act_spec, act_spec],
        ),
        out_shape=[act, act, act],
        compiler_params=params(),
        cost_estimate=pl.CostEstimate(
            flops=6 * total * n_own * features, bytes_accessed=30 * 1024 * 1024, transcendentals=total * n_own
        ),
        name="ffn_forward",
    )(core, rows, planes, planes, planes)


def mirror_gather(all_ref, arrivals, sems, pass_sems, ctx, core, fsdp, sibling):
    first, second, corner = fsdp_neighbours(fsdp)
    half = all_ref.shape[2] // 2
    parts = [pl.ds(0, half), pl.ds(half, half)]
    to_first, to_second = (ctx, first), (ctx, second)

    def copy(index, owner, part, peer):
        place_ref = all_ref.at[core, owner, parts[part]]
        return send(place_ref, place_ref, sems, index, peer)

    copies = [
        copy(0, fsdp, 0, to_first),
        copy(1, fsdp, 0, to_second),
        copy(2, fsdp, 1, to_first),
        copy(3, fsdp, 1, to_second),
        copy(4, first, 0, to_second),
        copy(5, second, 1, to_first),
    ]
    passes = [(fsdp, 0), (fsdp, 1), (first, 0), (second, 0), (first, 1), (second, 1), (corner, 0), (corner, 1)]

    def passing_copy(number, side):
        owner, part = passes[number]
        place_ref = all_ref.at[side, owner, parts[part]]
        return send(place_ref, place_ref, pass_sems, number, sibling)

    for part in range(2):
        arrivals[part].wait_recv()
        copies[2 * part].start()
        copies[2 * part + 1].start()
        passing_copy(part, core).start()
        yield
    for index, number, then in ((0, 2, 4), (1, 3, None), (2, 4, None), (3, 5, 5), (4, 6, None), (5, 7, None)):
        owner, part = passes[number]
        copy(index, owner, part, to_first).wait_recv()
        if then is not None:
            copies[then].start()
        passing_copy(number, core).start()
        yield
    for each in copies:
        each.wait_send()
    for number in range(8):
        passing_copy(number, core).wait_send()
        passing_copy(number, 1 - core).wait_recv()


def ffn_rows(n_ctx, own, planes, n_own, chunk=256, wide=512):
    n_fsdp = 4
    size, features = own.shape
    tokens = size // 2
    total = 2 * n_fsdp * tokens

    def kernel(
        own_ref, planes_ref, all_ref, mirror_ref, hidden_a, hidden_b, hidden_c, partial_ref,
        rows, weights, hidden, partial, load, sq_s, sq_r, core_s, core_r, far_s, far_r, mi_s, mi_r, mc_s, mc_r, out_sem,
    ):
        chip, core, fsdp, length = place(n_ctx)
        ctx = chip * 2 + core
        sibling = (chip * 2 + 1 - core, fsdp)
        mirror = ((length - 1 - chip) * 2 + core, fsdp)
        first, second, corner = fsdp_neighbours(fsdp)
        greet([sibling, mirror] + fsdp_peers(n_fsdp, ctx, fsdp))
        mine = pltpu.make_async_copy(own_ref, rows.at[core, fsdp], load.at[3])
        mine.start()
        start = pl.multiple_of(core * n_own, n_own)
        loads = [
            pltpu.make_async_copy(planes_ref.at[p, pl.ds(start, n_own)], weights.at[p], load.at[p]) for p in range(3)
        ]
        handed, arriving = [], []

        def hand(source, owner, part, index):
            for side, copies in ((core, handed), (1 - core, arriving)):
                target = rows.at[side, owner] if part is None else rows.at[side, owner, part]
                copies.append(send(source, target, (core_s, core_r), index + 1, sibling))
            handed[-1].start()

        gathering = square_gather(own_ref, rows.at[core], (sq_s, sq_r), ctx, fsdp, n_fsdp, hand)
        next(gathering)
        hand(own_ref, fsdp, None, -1)
        for each in loads:
            each.start()
        far = [
            send(
                own_ref.at[pl.ds(part * tokens, tokens)],
                mirror_ref.at[core, fsdp, pl.ds(part * tokens, tokens)],
                (far_s, far_r),
                part,
                mirror,
            )
            for part in range(2)
        ]
        for each in far:
            each.start()
        mirroring = mirror_gather(mirror_ref, far, (mi_s, mi_r), (mc_s, mc_r), ctx, core, fsdp, sibling)
        outs = []

        def group(number, owner):
            slot = number % 2
            if number >= 2:
                for each in outs[number - 2]:
                    each.wait()
            here = jnp.concatenate([rows[0, owner, :tokens], rows[1, owner, :tokens]])
            back = jnp.concatenate([rows[0, owner, tokens:], rows[1, owner, tokens:]])

            @pl.loop(0, n_own // chunk)
            def _(step):
                at = pl.ds(pl.multiple_of(step * chunk, chunk), chunk)
                parts = [weights.at[pl.ds(p, 1), at] for p in range(3)]
                for q, value in enumerate(hidden_units(here, back, *parts)):
                    hidden[slot, q, :, at] = value

            @pl.loop(0, features // wide)
            def _(step):
                at = pl.ds(pl.multiple_of(step * wide, wide), wide)
                out = low(mm(hidden[slot, 0], weights[2, :, at]))
                below = low(mm(hidden[slot, 1], weights[0, :, at]) + mm(hidden[slot, 2], weights[1, :, at]))
                for k in range(2):
                    partial[slot, k, :tokens, at] = out[k * tokens : (k + 1) * tokens]
                    partial[slot, k, tokens:, at] = below[k * tokens : (k + 1) * tokens]

            pairs = []
            for k in range(2):
                pairs.append((rows.at[k, owner], all_ref.at[k, owner]))
                pairs.append((partial.at[slot, k], partial_ref.at[k, owner]))
                at = pl.ds(pl.multiple_of((k * n_fsdp + owner) * tokens, tokens), tokens)
                for q, target in enumerate((hidden_a, hidden_b, hidden_c)):
                    pairs.append((hidden.at[slot, q, pl.ds(k * tokens, tokens)], target.at[at]))
            outs.append(
                [pltpu.make_async_copy(a, b, out_sem.at[slot, j]) for j, (a, b) in enumerate(pairs)]
            )
            for each in outs[-1]:
                each.start()

        mine.wait()
        arriving[0].wait_recv()
        for each in loads:
            each.wait()
        group(0, fsdp)
        for _ in range(4):
            next(gathering)
        arriving[1].wait_recv()
        arriving[3].wait_recv()
        group(1, first)
        next(mirroring)
        for _ in range(2):
            next(gathering)
        arriving[2].wait_recv()
        arriving[4].wait_recv()
        group(2, second)
        for _ in range(3):
            next(mirroring)
        arriving[5].wait_recv()
        arriving[6].wait_recv()
        group(3, corner)
        run_all(mirroring, gathering)
        for each in handed:
            each.wait_send()
        for each in far:
            each.wait_send()
        for group_outs in outs[2:]:
            for each in group_outs:
                each.wait()

    act = jax.ShapeDtypeStruct((total, n_own), own.dtype)
    all_rows = jax.ShapeDtypeStruct((2, n_fsdp) + own.shape, own.dtype)
    return pl.pallas_call(
        kernel,
        in_specs=any_specs(2),
        out_specs=any_specs(6),
        out_shape=[all_rows, all_rows, act, act, act, all_rows],
        scratch_shapes=[
            pltpu.VMEM((2, n_fsdp) + own.shape, own.dtype),
            pltpu.VMEM((3, n_own, features), own.dtype),
            pltpu.VMEM((2, 3, 2 * tokens, n_own), own.dtype),
            pltpu.VMEM((2, 2) + own.shape, own.dtype),
            pltpu.SemaphoreType.DMA((4,)),
        ]
        + dma_pair(6)
        + dma_pair(7)
        + dma_pair(2)
        + dma_pair(6)
        + dma_pair(8)
        + [pltpu.SemaphoreType.DMA((2, 10))],
        compiler_params=params(6),
        cost_estimate=pl.CostEstimate(
            flops=12 * total * n_own * features, bytes_accessed=50 * 1024 * 1024, transcendentals=total * n_own
        ),
        name="ffn_rows",
    )(own, planes)


def ffn_weights(n_ctx, n_fsdp, partial, rows, rows_mirror, hidden, planes, n_own, chunk=256):
    blocks, _, tokens, features = rows.shape
    total = blocks * tokens
    steps = n_own // chunk
    group = max(1, 256 // tokens)
    half = features // 2
    sides = n_ctx // 4
    wide = half // sides
    fused = partial is not None

    def kernel(*refs):
        rows_ref, refs = refs[0], refs[1:]
        mirror_refs, refs = refs[: len(rows_mirror)], refs[len(rows_mirror) :]
        mirror_blocks = [ref.at[b] for ref in mirror_refs for b in range(ref.shape[0])]
        hidden_ref, grad_gate_ref, grad_up_ref, planes_ref, *refs = refs
        if fused:
            partial_ref, weight_ref, out_ref, *refs = refs
        else:
            weight_ref, *refs = refs
        mirror, (weights, weight_sems), refs = refs[:3], refs[3:5], refs[5:]
        chip, core, _, length = place(n_ctx)
        side = chip // sides
        step = pl.program_id(0)
        stages = [lambda: None] * 2
        if fused:
            held, core_in, square_in, load, core_s, core_r, sq_s, sq_r = refs
            stages = square_sum_stages(
                n_ctx, n_fsdp, partial_ref, out_ref, held, core_in, square_in, load, (core_s, core_r), (sq_s, sq_r)
            )

        def fetch(at, slot):
            start = pl.multiple_of((core * steps + at) * chunk, chunk)
            return pltpu.make_async_copy(planes_ref.at[:, pl.ds(start, chunk)], weights.at[slot], weight_sems.at[slot])

        @pl.when(step == 0)
        def _():
            fetch(0, 0).start()
            stages[0]()

        @pl.when(step + 1 < steps)
        def _():
            fetch(step + 1, (step + 1) % 2).start()

        slot = step % 2
        fetch(step, slot).wait()
        gate_ref, up_ref, down_ref = (weights.at[slot, pl.ds(plane, 1)] for plane in range(3))
        for at in range(0, blocks, group):
            here = jnp.concatenate([ref[0] for ref in mirror_blocks[at : at + group]])
            back = jnp.concatenate([ref[1] for ref in mirror_blocks[at : at + group]])
            span = pl.ds(at * tokens, group * tokens)
            for out, value in zip(mirror, hidden_units(here, back, gate_ref, up_ref, down_ref)):
                out[span] = value

        @pl.when(step == 0)
        def _():
            stages[1]()

        lefts = ((grad_gate_ref, mirror[1], 0), (grad_up_ref, mirror[2], 0), (hidden_ref, mirror[0], 1))
        for plane, (left, left_mirror, which) in enumerate(lefts):
            left = left[...]
            left_mirror = left_mirror[...]
            for z in range(sides):
                cols = pl.ds(pl.multiple_of(side * half + z * wide, wide), wide)
                right = rows_ref[:, which, :, cols].reshape(total, wide)
                right_mirror = jnp.concatenate([ref[which, :, cols] for ref in mirror_blocks])
                weight_ref[z, plane] = low(
                    mm(left, right, CONTRACT_FIRST) + mm(left_mirror, right_mirror, CONTRACT_FIRST)
                )

        for at, stage in ((1, 2), (steps - 1, 3)):
            if stage < len(stages):

                @pl.when(step == min(at, steps - 1))
                def _():
                    stages[stage]()

    act_spec = pl.BlockSpec((total, chunk), lambda j: (0, j))
    once = dict(pipeline_mode=pl.Buffered(1))
    operands = [rows, *rows_mirror, *hidden, planes]
    in_specs = [whole_block(rows.shape, **once)] + [whole_block(part.shape, **once) for part in rows_mirror]
    in_specs += [act_spec] * 3 + any_specs(1)
    out_specs = [pl.BlockSpec((sides, 3, chunk, wide), lambda j: (0, 0, j, 0))]
    out_shape = [jax.ShapeDtypeStruct((sides, 3, n_own, wide), jnp.bfloat16)]
    scratch = [pltpu.VMEM((total, chunk), jnp.bfloat16)] * 3
    scratch += [pltpu.VMEM((2, 3, chunk, features), jnp.bfloat16), pltpu.SemaphoreType.DMA((2,))]
    if fused:
        operands.append(partial)
        in_specs += any_specs(1)
        out_specs.append(whole_block(partial.shape[-2:], **once))
        out_shape.append(jax.ShapeDtypeStruct(partial.shape[-2:], jnp.float32))
        scratch += square_sum_scratch(n_fsdp, partial)
    return pl.pallas_call(
        kernel,
        grid=(steps,),
        in_specs=in_specs,
        out_specs=out_specs,
        out_shape=out_shape,
        scratch_shapes=scratch,
        compiler_params=params(3) if fused else params(),
        cost_estimate=pl.CostEstimate(
            flops=12 * total * n_own * features, bytes_accessed=50 * 1024 * 1024, transcendentals=total * n_own
        ),
        name="ffn_weights",
    )(*operands)


def ffn_back(hidden, grad_gate, grad_up, planes, core, blocks, wide=512):
    total, n_own = hidden.shape
    features = planes.shape[2]
    tokens = total // blocks

    def kernel(core_ref, hidden_ref, grad_gate_ref, grad_up_ref, gate_ref, up_ref, down_ref, out_ref):
        out = mm(hidden_ref[...], down_ref[0])
        out_ref[:, 0] = low(out).reshape(blocks, tokens, wide)
        back = mm(grad_gate_ref[...], gate_ref[0]) + mm(grad_up_ref[...], up_ref[0])
        out_ref[:, 1] = low(back).reshape(blocks, tokens, wide)

    def weight_spec(plane):
        return pl.BlockSpec((1, n_own, wide), lambda j, core_ref: (plane, core_ref[0], j))

    act_spec = pl.BlockSpec((total, n_own), lambda j, core_ref: (0, 0), pipeline_mode=pl.Buffered(1))
    return pl.pallas_call(
        kernel,
        grid_spec=pltpu.PrefetchScalarGridSpec(
            num_scalar_prefetch=1,
            grid=(features // wide,),
            in_specs=[act_spec, act_spec, act_spec, weight_spec(0), weight_spec(1), weight_spec(2)],
            out_specs=pl.BlockSpec((blocks, 2, tokens, wide), lambda j, core_ref: (0, 0, 0, j)),
        ),
        out_shape=jax.ShapeDtypeStruct((blocks, 2, tokens, features), jnp.bfloat16),
        compiler_params=params(),
        cost_estimate=pl.CostEstimate(
            flops=6 * total * n_own * features, bytes_accessed=30 * 1024 * 1024, transcendentals=0
        ),
        name="ffn_back",
    )(core, hidden, grad_gate, grad_up, planes, planes, planes)


SPAN = 256


def turn(values, cosine, sine):
    return values * cosine + pltpu.roll(values, HEAD_DIM // 2, 1) * sine


def attention_forward(rows, w_qkv, cosine, sine, place_column, place_row, heads):
    total, features = rows.shape
    own = heads * HEAD_DIM
    steps = total // SPAN
    scale = HEAD_DIM ** (-0.5)

    def kernel(
        rows_ref, w_ref, cosine_ref, sine_ref, column_ref, row_ref, query_ref, key_ref, value_ref, out_ref, log_ref
    ):
        step = pl.program_id(0)
        span = pl.ds(pl.multiple_of(step * SPAN, SPAN), SPAN)
        qkv = mm(rows_ref[...], w_ref[...])
        cosine = cosine_ref[span]
        sine = sine_ref[span]
        for h in range(heads):
            at = slice(h * HEAD_DIM, (h + 1) * HEAD_DIM)
            query_ref[span, at] = low(turn(qkv[:, at], cosine, sine))
            key_ref[span, at] = low(turn(qkv[:, own + h * HEAD_DIM : own + (h + 1) * HEAD_DIM], cosine, sine))
        value_ref[span] = low(qkv[:, 2 * own :])

        @pl.when(step == steps - 1)
        def _():
            for h in range(heads):
                at = slice(h * HEAD_DIM, (h + 1) * HEAD_DIM)

                @pl.loop(0, steps)
                def _(block):
                    here = pl.ds(pl.multiple_of(block * SPAN, SPAN), SPAN)
                    scores = mm(query_ref[here, at], key_ref[:, at], CONTRACT_LAST) * scale
                    scores = jnp.where(column_ref[here] >= row_ref[...], scores, MASKED)
                    highest = jnp.max(scores, axis=-1, keepdims=True)
                    exponent = jnp.exp(scores - highest)
                    sums = jnp.sum(exponent, axis=-1, keepdims=True)
                    out_ref[here, at] = low(mm(low(exponent * (1.0 / sums)), value_ref[:, at]))
                    log_ref[h, here] = highest + jnp.log(sums)

    act = jax.ShapeDtypeStruct((total, own), jnp.bfloat16)
    return pl.pallas_call(
        kernel,
        grid=(steps,),
        in_specs=[pl.BlockSpec((SPAN, features), lambda r: (r, 0))]
        + [whole_block(a.shape) for a in (w_qkv, cosine, sine, place_column, place_row)],
        out_specs=[whole_block((total, own))] * 4 + [whole_block((heads, total, 1))],
        out_shape=[act] * 4 + [jax.ShapeDtypeStruct((heads, total, 1), jnp.float32)],
        compiler_params=params(),
        name="attention_forward",
    )(rows, w_qkv, cosine, sine, place_column, place_row)


def attention_backward(query, key, value, grad, logs, w_qkv, cosine, sine, place_column, place_row, heads):
    total, own = query.shape
    features = w_qkv.shape[0]
    steps = total // SPAN
    scale = HEAD_DIM ** (-0.5)

    def kernel(
        query_ref, key_ref, value_ref, grad_ref, log_ref, w_ref, cosine_ref, sine_ref, column_ref, row_ref,
        qkv_ref, out_ref, key_sum, value_sum,
    ):
        step = pl.program_id(0)

        @pl.when(step == 0)
        def _():
            for h in range(heads):
                at = slice(h * HEAD_DIM, (h + 1) * HEAD_DIM)
                key_sum[...] = jnp.zeros_like(key_sum)
                value_sum[...] = jnp.zeros_like(value_sum)

                @pl.loop(0, steps)
                def _(block):
                    here = pl.ds(pl.multiple_of(block * SPAN, SPAN), SPAN)
                    queries = query_ref[here, at]
                    grads = grad_ref[here, at]
                    scores = mm(queries, key_ref[:, at], CONTRACT_LAST) * scale
                    scores = jnp.where(column_ref[here] >= row_ref[...], scores, MASKED)
                    probs = jnp.exp(scores - log_ref[h, here])
                    probs_grad = mm(grads, value_ref[:, at], CONTRACT_LAST)
                    centre = jnp.sum(probs * probs_grad, axis=-1, keepdims=True)
                    scores_grad = low(probs * (probs_grad - centre))
                    query_grad = mm(scores_grad, key_ref[:, at]) * scale
                    qkv_ref[here, at] = low(turn(query_grad, cosine_ref[here], -sine_ref[here]))
                    key_sum[...] += mm(scores_grad, queries, CONTRACT_FIRST)
                    value_sum[...] += mm(low(probs), grads, CONTRACT_FIRST)

                qkv_ref[:, own + h * HEAD_DIM : own + (h + 1) * HEAD_DIM] = low(
                    turn(key_sum[...] * scale, cosine_ref[...], -sine_ref[...])
                )
                qkv_ref[:, 2 * own + h * HEAD_DIM : 2 * own + (h + 1) * HEAD_DIM] = low(value_sum[...])

        span = pl.ds(pl.multiple_of(step * SPAN, SPAN), SPAN)
        out_ref[...] = low(mm(qkv_ref[span], w_ref[...], CONTRACT_LAST))

    return pl.pallas_call(
        kernel,
        grid=(steps,),
        in_specs=[
            whole_block(a.shape)
            for a in (query, key, value, grad, logs, w_qkv, cosine, sine, place_column, place_row)
        ],
        out_specs=[whole_block((total, 3 * own)), pl.BlockSpec((SPAN, features), lambda r: (r, 0))],
        out_shape=[
            jax.ShapeDtypeStruct((total, 3 * own), jnp.bfloat16),
            jax.ShapeDtypeStruct((total, features), jnp.bfloat16),
        ],
        scratch_shapes=[pltpu.VMEM((total, HEAD_DIM), jnp.float32)] * 2,
        compiler_params=params(),
        name="attention_backward",
    )(query, key, value, grad, logs, w_qkv, cosine, sine, place_column, place_row)


ROWS = 32


def row_blocks(count, features):
    return pl.BlockSpec((count, ROWS, features), lambda r, *_: (0, r, 0))


def whole_block(shape, **more):
    zeros = (0,) * len(shape)
    return pl.BlockSpec(shape, lambda r, *_: zeros, **more)


def connect_coefficients(values, dynamic_ref, static_ref, coef_ref, dyn_ref):
    lane = lax.broadcasted_iota(jnp.int32, (values[0].shape[0], 8), 1)
    columns = []
    for i, value in enumerate(values):
        mean = jnp.mean(value, axis=-1, keepdims=True)
        centered = value - mean
        inverse = lax.rsqrt(jnp.mean(centered * centered, axis=-1, keepdims=True) + EPS)
        normed = centered * inverse
        projected = 0.0
        for k in range(6):
            part = jnp.sum(normed * dynamic_ref[k : k + 1], axis=-1, keepdims=True)
            projected = jnp.where(lane == k, part, projected)
        dynamic_part = jnp.tanh(projected)
        coefficient = dynamic_part + static_ref[i : i + 1]
        dyn_ref[i] = dynamic_part
        coef_ref[i] = jnp.where(lane == 6, mean, jnp.where(lane == 7, inverse, coefficient))
        columns.append(coefficient)
    return columns


def connect_first(streams, dynamic, static):
    number, rows, features = streams.shape

    def kernel(streams_ref, dynamic_ref, static_ref, coef_ref, dyn_ref, low_ref):
        values = [streams_ref[i].astype(jnp.float32) for i in range(number)]
        columns = connect_coefficients(values, dynamic_ref, static_ref, coef_ref, dyn_ref)
        mixed = sum((columns[i][:, 1:2] * values[i] for i in range(number)))
        low_ref[...] = low(normalize(mixed)[0])

    small = jax.ShapeDtypeStruct((number, rows, 8), jnp.float32)
    return pl.pallas_call(
        kernel,
        grid=(rows // ROWS,),
        out_shape=(small, small, jax.ShapeDtypeStruct((rows, features), jnp.bfloat16)),
        in_specs=[row_blocks(number, features), whole_block(dynamic.shape), whole_block(static.shape)],
        out_specs=(
            row_blocks(number, 8),
            row_blocks(number, 8),
            pl.BlockSpec((ROWS, features), lambda r: (r, 0)),
        ),
        compiler_params=params(),
        name="connect_first",
    )(streams, dynamic, static)


def connect_middle(streams, coef, attended, w_mine, w_other, cotangent, dynamic, static, core_fsdp, where, depth):
    number, rows, features = streams.shape
    half = features // 2
    count = len(w_mine)

    def kernel(core_ref, streams_ref, coef_ref, attended_ref, *refs):
        weights, refs = refs[: 2 * count], refs[2 * count :]
        cotangent_ref, dynamic_ref, static_ref = refs[:3]
        first_ref, branch_ref, coef_two_ref, dyn_ref, own_ref, projected = refs[3:]
        step = pl.program_id(0)

        @pl.when(step == 0)
        def _():
            for side in range(2):
                total = 0.0
                for j, (d, offset) in enumerate(where):
                    size = w_mine[j].shape[0]
                    columns = pl.ds(pl.multiple_of((core_ref[1] ^ d) * depth + offset, size), size)
                    total = total + mm(attended_ref[:, columns], weights[side * count + j][...])
                projected[core_ref[0] if side == 0 else 1 - core_ref[0]] = total

        span = pl.ds(pl.multiple_of(step * ROWS, ROWS), ROWS)
        branch = jnp.concatenate([projected[0, span], projected[1, span]], axis=1)
        branch_ref[...] = branch
        inputs = [streams_ref[i].astype(jnp.float32) for i in range(number)]
        outs = []
        for j in range(number):
            out = sum((coef_ref[i][:, 2 + j : 3 + j] * inputs[i] for i in range(number)))
            outs.append(out + coef_ref[j][:, 0:1] * branch)
            first_ref[j] = outs[-1]
        columns = connect_coefficients(outs, dynamic_ref, static_ref, coef_two_ref, dyn_ref)
        mixed = sum((columns[i][:, 1:2] * outs[i] for i in range(number)))
        own_ref[0] = low(normalize(mixed)[0])
        own_ref[1] = low(sum((columns[j][:, 0:1] * cotangent_ref[j].astype(jnp.float32) for j in range(number))))

    small = jax.ShapeDtypeStruct((number, rows, 8), jnp.float32)
    once = dict(pipeline_mode=pl.Buffered(1))
    return pl.pallas_call(
        kernel,
        grid_spec=pltpu.PrefetchScalarGridSpec(
            num_scalar_prefetch=1,
            grid=(rows // ROWS,),
            in_specs=[
                row_blocks(number, features),
                row_blocks(number, 8),
                whole_block(attended.shape, **once),
                *[whole_block(w.shape, **once) for w in w_mine + w_other],
                row_blocks(number, features),
                whole_block(dynamic.shape),
                whole_block(static.shape),
            ],
            out_specs=(
                row_blocks(number, features),
                pl.BlockSpec((ROWS, features), lambda r, *_: (r, 0)),
                row_blocks(number, 8),
                row_blocks(number, 8),
                row_blocks(2, features),
            ),
            scratch_shapes=[pltpu.VMEM((2, rows, half), jnp.float32)],
        ),
        out_shape=(
            jax.ShapeDtypeStruct((number, rows, features), jnp.float32),
            jax.ShapeDtypeStruct((rows, features), jnp.float32),
            small,
            small,
            jax.ShapeDtypeStruct((2, rows, features), jnp.bfloat16),
        ),
        compiler_params=params(),
        name="connect_middle",
    )(core_fsdp, streams, coef, attended, *w_mine, *w_other, cotangent, dynamic, static)


def attention_weights(rows, grads, attended, grad_cols):
    total, features = rows.shape
    parts, _, own = attended.shape
    wide = grads.shape[1]

    def kernel(rows_ref, grads_ref, attended_ref, cols_ref, out_ref):
        out_ref[:, :wide] = low(mm(rows_ref[...], grads_ref[...], CONTRACT_FIRST))
        out_ref[:, wide:] = low(mm(attended_ref[0], cols_ref[...], CONTRACT_FIRST))

    return pl.pallas_call(
        kernel,
        grid=(parts,),
        in_specs=[
            pl.BlockSpec((total, own), lambda k: (0, k)),
            whole_block(grads.shape),
            pl.BlockSpec((1, total, own), lambda k: (k, 0, 0)),
            whole_block(grad_cols.shape),
        ],
        out_specs=pl.BlockSpec((own, wide + own), lambda k: (k, 0)),
        out_shape=jax.ShapeDtypeStruct((features, wide + own), jnp.bfloat16),
        compiler_params=params(),
        cost_estimate=pl.CostEstimate(
            flops=2 * total * features * (wide + own), bytes_accessed=16 * 1024 * 1024, transcendentals=0
        ),
        name="attention_weights",
    )(rows, grads, attended, grad_cols)


def project_back(grad, w_mine, w_other, core_fsdp, n_ctx, where, depth):
    rows, features = grad.shape
    half = features // 2
    count = len(w_mine)
    own = features // n_ctx

    def kernel(core_ref, grad_ref, *refs):
        weights, (out_ref, cols_ref) = refs[: 2 * count], refs[2 * count :]
        first = grad_ref[:, pl.ds(pl.multiple_of(core_ref[0] * half, half), half)]
        second = grad_ref[:, pl.ds(pl.multiple_of((1 - core_ref[0]) * half, half), half)]
        for j, (d, offset) in enumerate(where):
            out = low(
                mm(first, weights[j][...], CONTRACT_LAST) + mm(second, weights[count + j][...], CONTRACT_LAST)
            )
            for q in range(w_mine[j].shape[0] // own):
                at = (core_ref[1] ^ d) * (depth // own) + offset // own + q
                out_ref[at] = out[:, q * own : (q + 1) * own]
        for index in range(n_ctx):
            cols_ref[index] = grad_ref[:, index * own : (index + 1) * own]

    return pl.pallas_call(
        kernel,
        grid_spec=pltpu.PrefetchScalarGridSpec(
            num_scalar_prefetch=1,
            grid=(1,),
            in_specs=[whole_block(a.shape) for a in [grad] + w_mine + w_other],
            out_specs=[whole_block((n_ctx, rows, own))] * 2,
        ),
        out_shape=[jax.ShapeDtypeStruct((n_ctx, rows, own), grad.dtype)] * 2,
        compiler_params=params(),
        name="project_back",
    )(core_fsdp, grad, *w_mine, *w_other)


def connect_back(values, coef, dyn, branch, grads, grad_normed, dynamic, coef_before=None):
    number, rows, features = values.shape
    steps = rows // ROWS
    more = coef_before is not None

    def kernel(*refs):
        values_ref, coef_ref, dyn_ref, branch_ref, grads_ref, normed_ref, dynamic_ref = refs[:7]
        refs = refs[7:]
        if more:
            before_ref, refs = refs[0], refs[1:]
        out_ref, dynamic_out, static_out = refs[:3]
        if more:
            forward_ref, grad_low_ref = refs[3:5]
        dynamic_sum = refs[-1]
        step = pl.program_id(0)

        @pl.when(step == 0)
        def _():
            dynamic_sum[...] = jnp.zeros_like(dynamic_sum)
            static_out[...] = jnp.zeros_like(static_out)

        branch = branch_ref[...]
        mixed = sum((coef_ref[i][:, 1:2] * values_ref[i].astype(jnp.float32) for i in range(number)))
        normed, inverse = normalize(mixed)
        grad_mixed = normalize_back(normed, inverse, normed_ref[...])
        lane = lax.broadcasted_iota(jnp.int32, (ROWS, 8), 1)
        totals = [0.0] * 6
        befores = 0.0
        for i in range(number):
            value = values_ref[i].astype(jnp.float32)
            grad_own = grads_ref[i].astype(jnp.float32)
            columns = [
                jnp.sum(grad_own * branch, axis=-1, keepdims=True),
                jnp.sum(grad_mixed * value, axis=-1, keepdims=True),
            ]
            out = coef_ref[i][:, 1:2] * grad_mixed
            for j in range(number):
                grad = grads_ref[j].astype(jnp.float32)
                columns.append(jnp.sum(grad * value, axis=-1, keepdims=True))
                out = out + coef_ref[i][:, 2 + j : 3 + j] * grad
            normed = (value - coef_ref[i][:, 6:7]) * coef_ref[i][:, 7:8]
            normed_grad = 0.0
            coef_grad = jnp.zeros((ROWS, 8), jnp.float32)
            for k in range(6):
                part = dyn_ref[i][:, k : k + 1]
                pre_grad = columns[k] * (1.0 - part * part)
                normed_grad = normed_grad + pre_grad * dynamic_ref[k : k + 1]
                totals[k] = totals[k] + pre_grad * normed
                coef_grad = jnp.where(lane == k, columns[k], coef_grad)
            out = out + normalize_back(normed, coef_ref[i][:, 7:8], normed_grad)
            out_ref[i] = out
            static_out[i : i + 1] += jnp.sum(coef_grad, axis=0, keepdims=True)
            if more:
                befores = befores + before_ref[i][:, 0:1] * out
        for k in range(6):
            dynamic_sum[k] += jnp.sum(totals[k].reshape(ROWS // 8, 8, features), axis=0)
        if more:
            grad_low_ref[...] = low(befores)
            for j in range(number):
                out = coef_ref[j][:, 0:1] * branch
                for i in range(number):
                    out = out + coef_ref[i][:, 2 + j : 3 + j] * values_ref[i].astype(jnp.float32)
                forward_ref[j] = low(out)

        @pl.when(step == steps - 1)
        def _():
            for k in range(6):
                dynamic_out[k : k + 1] = jnp.sum(dynamic_sum[k], axis=0, keepdims=True)
            dynamic_out[6:8] = jnp.zeros((2, features), jnp.float32)

    rows_spec = pl.BlockSpec((ROWS, features), lambda r: (r, 0))
    out_shape = [
        jax.ShapeDtypeStruct((number, rows, features), jnp.float32),
        jax.ShapeDtypeStruct((8, features), jnp.float32),
        jax.ShapeDtypeStruct((8, 8), jnp.float32),
    ]
    out_specs = [row_blocks(number, features), whole_block((8, features)), whole_block((8, 8))]
    operands = [values, coef, dyn, branch, grads, grad_normed, dynamic]
    in_specs = [
        row_blocks(number, features),
        row_blocks(number, 8),
        row_blocks(number, 8),
        rows_spec,
        row_blocks(number, features),
        rows_spec,
        whole_block(dynamic.shape),
    ]
    if more:
        operands.append(coef_before)
        in_specs.append(row_blocks(number, 8))
        out_shape.append(jax.ShapeDtypeStruct((number, rows, features), jnp.bfloat16))
        out_specs.append(row_blocks(number, features))
        out_shape.append(jax.ShapeDtypeStruct((rows, features), jnp.bfloat16))
        out_specs.append(rows_spec)
    return pl.pallas_call(
        kernel,
        grid=(steps,),
        in_specs=in_specs,
        out_specs=out_specs,
        out_shape=out_shape,
        scratch_shapes=[pltpu.VMEM((6, 8, features), jnp.float32)],
        compiler_params=params(),
        name="connect_back",
    )(*operands)


def local(n_ctx, n_fsdp, streams, w_attn, w_ffn, hc_dynamic, hc_static, cotangent, pair_order):
    number = streams.shape[1]
    length = streams.shape[2]
    features = streams.shape[3]
    size = HEAD_DIM
    own = features // n_ctx
    heads = own // size
    rows = length * n_ctx
    own_rows = w_attn.shape[0]
    ctx = lax.axis_index("ctx")
    fsdp = lax.axis_index("fsdp")
    core = ctx % 2
    chips = n_ctx // 2
    core_index = jnp.reshape(core, (1,)).astype(jnp.int32)

    def in_order(mine, other, axis):
        return jnp.where(
            core == 0, jnp.concatenate([mine, other], axis=axis), jnp.concatenate([other, mine], axis=axis)
        )


    w_own = lax.dynamic_slice_in_dim(w_attn, ctx * own, own, 2)[:, 0:3].reshape(own_rows, 3 * own)
    w_qkv = gather(w_own, "fsdp")
    half = features // 2
    w_half = lax.dynamic_slice_in_dim(w_attn, core * half, half, 2)[:, 3]
    siblings = [(i, i ^ 1) for i in range(n_ctx)]
    core_fsdp = jnp.stack([core, fsdp]).astype(jnp.int32)

    def exchange(values, most=0):
        return [values] + [
            lax.ppermute(values, "fsdp", [(i, i ^ d) for i in range(n_fsdp)])
            for d in range(1, most + 1 if most else n_fsdp)
        ]

    def swap(blocks):
        return [lax.ppermute(block, "ctx", siblings) for block in blocks]


    positions = block_positions(pair_order, length)
    frequency = THETA ** (-(jnp.arange(size // 2, dtype=jnp.float32) * 2.0) / size)
    angles = positions.astype(jnp.float32)[:, None] * jnp.concatenate([frequency, frequency])[None, :]
    signs = jnp.where(jnp.arange(size) < size // 2, -1.0, 1.0)
    tables = (jnp.cos(angles), jnp.sin(angles) * signs[None, :], positions[:, None], positions[None, :])

    dynamics = jnp.pad(hc_dynamic, ((0, 0), (0, 2), (0, 0)))
    statics = jnp.pad(hc_static, ((0, 0), (0, 0), (0, 2)))
    coef_one, dyn_one, attn_low = connect_first(streams[0], dynamics[0], statics[0])
    attn_low, w_half = lax.optimization_barrier((attn_low, w_half))
    w_out_mine = exchange(w_half, 2 if n_fsdp == 4 else 0)
    attn_all = line_rows(n_ctx, attn_low).reshape(rows, features)
    w_out_where = [(d, 0) for d in range(len(w_out_mine))]
    if n_fsdp == 4:
        attn_all, *w_out_mine = lax.optimization_barrier((attn_all, *w_out_mine))
        middle = own_rows // 2
        w_out_mine.append(lax.ppermute(w_out_mine[1][:middle], "fsdp", [(i, i ^ 2) for i in range(4)]))
        w_out_mine.append(lax.ppermute(w_out_mine[2][middle:], "fsdp", [(i, i ^ 1) for i in range(4)]))
        w_out_where += [(3, 0), (3, middle)]
    query, key, value, attended, logs = attention_forward(attn_all, w_qkv, *tables, heads)
    attended, w_out_mine = lax.optimization_barrier((attended, w_out_mine))
    w_out_other = swap(w_out_mine)
    attended_rows = lax.all_to_all(attended, "ctx", 0, 1, tiled=True)

    first_out, attn_branch, coef_two, dyn_two, ffn_own = connect_middle(
        streams[0], coef_one, attended_rows, w_out_mine, w_out_other, cotangent[0], dynamics[1], statics[1], core_fsdp,
        w_out_where, own_rows,
    )
    ffn_own = ffn_own.reshape(2 * length, features)

    planes = jnp.moveaxis(w_ffn, 1, 0)
    n_own = planes.shape[1] // 2
    blocks = 2 * n_fsdp
    if n_fsdp == 4:
        ffn_all, mirror_rows, *hidden, sums = ffn_rows(n_ctx, ffn_own, planes, n_own)
        ffn_all, mirror_rows = (part.reshape(blocks, 2, length, features) for part in (ffn_all, mirror_rows))
        mirror_rows = [mirror_rows]
        attended, sums = lax.optimization_barrier((attended, sums))
        attended_all = gather(attended, "ctx").reshape(n_ctx, rows, own)
        *weight_parts, sums = ffn_weights(n_ctx, n_fsdp, sums, ffn_all, mirror_rows, hidden, planes, n_own)
    else:
        ffn_mirror = lax.ppermute(ffn_own, "ctx", [(i, n_ctx - 2 - i + 2 * (i % 2)) for i in range(n_ctx)])
        ffn_all = square_core_gather(n_ctx, n_fsdp, ffn_own).reshape(blocks, 2, length, features)
        attended_all = gather(attended, "ctx").reshape(n_ctx, rows, own)
        mirror_mine = exchange(ffn_mirror)
        hidden = ffn_forward(ffn_all, planes, core_index, n_own)
        sums = ffn_back(*hidden, planes, core_index, blocks)
        mirror_rows = [part.reshape(1, 2, length, features) for part in mirror_mine + swap(mirror_mine)]
        sums = square_sum(n_ctx, n_fsdp, sums.reshape(2, n_fsdp, 2 * length, features))
        weight_parts = ffn_weights(n_ctx, n_fsdp, None, ffn_all, mirror_rows, hidden, planes, n_own)
    sides = chips // 2
    lines = [[2 * (sides * side + i) + j for i in range(sides)] for side in range(2) for j in range(2)]
    weight_cols = lax.psum_scatter(weight_parts[0], "ctx", scatter_dimension=0, axis_index_groups=lines)
    ffn_branch = sums[:length]
    grad_ffn_normed = sums[length:]

    grad_first, dynamic_grad_two, static_grad_two, streams_out, grad_attn = connect_back(
        first_out, coef_two, dyn_two, ffn_branch, cotangent[0], grad_ffn_normed, dynamics[1], coef_one
    )
    grad_heads, grad_cols = project_back(grad_attn, w_out_mine, w_out_other, core_fsdp, n_ctx, w_out_where, own_rows)
    grad_heads = lax.all_to_all(grad_heads, "ctx", 0, 0, tiled=True).reshape(rows, own)
    grad_heads, grad_cols = lax.optimization_barrier((grad_heads, grad_cols))
    grad_cols = lax.all_to_all(grad_cols, "ctx", 0, 0, tiled=True).reshape(rows, own)
    qkv_grad, attn_part = attention_backward(query, key, value, grad_heads, logs, w_qkv, *tables, heads)
    attn_part = attn_part.reshape(n_ctx, length, features)
    grad_attn_normed = line_sum(n_ctx, attn_part, 5)
    grad_attn_normed, weight_cols = lax.optimization_barrier((grad_attn_normed, weight_cols))
    mine = lax.dynamic_slice_in_dim(weight_cols, core * own, own, 2)
    other = lax.dynamic_slice_in_dim(weight_cols, (1 - core) * own, own, 2)
    other = lax.ppermute(other, "ctx", siblings)
    ffn_grad = jnp.moveaxis(in_order(mine, other, 1), 0, 1).astype(jnp.float32)
    weight_part = attention_weights(attn_all, qkv_grad, attended_all, grad_cols)
    attn_grad = scatter(weight_part, "fsdp")

    grad_inputs, dynamic_grad_one, static_grad_one = connect_back(
        streams[0], coef_one, dyn_one, attn_branch, grad_first, grad_attn_normed, dynamics[0]
    )
    static_grads = jnp.concatenate([static_grad_one[:number, :6].reshape(1, -1), static_grad_two[:number, :6].reshape(1, -1)])
    small = jnp.concatenate(
        [
            dynamic_grad_one[:6],
            dynamic_grad_two[:6],
            jnp.pad(static_grads, ((0, 2), (0, features - 6 * number))),
        ]
    )
    small = sum_everywhere(n_ctx, n_fsdp, small.reshape(n_ctx, 8, -1))
    small, attn_grad = lax.optimization_barrier((small, attn_grad))
    small = small.reshape(16, features)
    attn_grad = attn_grad.astype(jnp.float32).reshape(own_rows, 4, own)
    dynamic_total = small[:12].reshape(2, 6, features)
    static_total = small[12:14, : 6 * number].reshape(2, number, 6)
    return (streams_out[None], grad_inputs[None], attn_grad, ffn_grad, dynamic_total, static_total)


def solution(mesh):
    return jax.shard_map(
        functools.partial(local, mesh.shape["ctx"], mesh.shape["fsdp"]),
        mesh=mesh,
        in_specs=(
            P("fsdp", None, "ctx", None),
            P("fsdp", None, None),
            P("fsdp", None, None),
            P(),
            P(),
            P("fsdp", None, "ctx", None),
            P(),
        ),
        out_specs=(
            P("fsdp", None, "ctx", None),
            P("fsdp", None, "ctx", None),
            P("fsdp", None, "ctx"),
            P("fsdp", None, "ctx"),
            P(),
            P(),
        ),
        check_vma=False,
    )
```

```python
import functools

import jax
import jax.numpy as jnp
from jax import lax
from jax.experimental import pallas as pl
from jax.experimental.pallas import tpu as pltpu
from jax.sharding import PartitionSpec as P

HEADS = 16
HEAD_DIM = 128


EPS = 1e-05
THETA = 10000.0
HIGH = lax.Precision.HIGHEST
MASKED = -1e30
CONTRACT_LAST = (((1,), (1,)), ((), ()))
CONTRACT_FIRST = (((0,), (0,)), ((), ()))


def normalize(values):
    centered = values - jnp.mean(values, axis=-1, keepdims=True)
    inverse = lax.rsqrt(jnp.mean(centered * centered, axis=-1, keepdims=True) + EPS)
    return (centered * inverse, inverse)


def normalize_back(normed, inverse, gradient):
    inner = jnp.mean(gradient * normed, axis=-1, keepdims=True)
    return inverse * (gradient - jnp.mean(gradient, axis=-1, keepdims=True) - normed * inner)


def block_positions(pair_order, length):
    half_size = length // 2
    offsets = jnp.arange(half_size, dtype=jnp.int32)
    mirror = 2 * pair_order.shape[0] - 1 - pair_order
    first_half = pair_order[:, None] * half_size + offsets[None, :]
    second_half = mirror[:, None] * half_size + offsets[None, :]
    return jnp.concatenate([first_half, second_half], axis=1).reshape(-1)


def low(values):
    return values.astype(jnp.bfloat16)


def mm(a, b, dims=None):
    if dims is None:
        return jnp.dot(a, b, preferred_element_type=jnp.float32)
    return lax.dot_general(a, b, dims, preferred_element_type=jnp.float32)


def gather(values, axis, dim=0):
    return lax.all_gather(values, axis, axis=dim, tiled=True)


def scatter(values, axis, dim=0):
    return lax.psum_scatter(values, axis, scatter_dimension=dim, tiled=True)


MESH = pl.DeviceIdType.MESH
VMEM_LIMIT = 60 * 1024 * 1024


def place(n_ctx):
    ctx = lax.axis_index("ctx")
    return (ctx // 2, ctx % 2, lax.axis_index("fsdp"), n_ctx // 2)


def greet(peers):
    barrier = pltpu.get_barrier_semaphore()
    for peer in peers:
        pl.semaphore_signal(barrier, inc=1, device_id=peer, device_id_type=MESH)
    pl.semaphore_wait(barrier, len(peers))


def send(source, target, sems, index, peer):
    return pltpu.make_async_remote_copy(
        src_ref=source,
        dst_ref=target,
        send_sem=sems[0].at[index],
        recv_sem=sems[1].at[index],
        device_id=peer,
        device_id_type=MESH,
    )


def fsdp_neighbours(fsdp):
    first = fsdp + 1 - 2 * (fsdp % 2)
    second = (fsdp + 2) % 4
    return (first, second, (first + 2) % 4)


def fsdp_peers(n_fsdp, ctx, fsdp):
    if n_fsdp == 4:
        first, second, _ = fsdp_neighbours(fsdp)
        return [(ctx, first), (ctx, second)]
    return [(ctx, (fsdp + j) % n_fsdp) for j in range(1, n_fsdp)]


def line_peers(chip, core, fsdp, length):
    return [
        (chip * 2 + 1 - core, fsdp),
        ((chip + 1) % length * 2 + core, fsdp),
        ((chip + length - 1) % length * 2 + core, fsdp),
    ]


def line_gather(own_ref, all_ref, sems, where):
    chip, core, fsdp, length = where
    right_sems, left_sems, core_sems = sems
    sibling = (chip * 2 + 1 - core, fsdp)
    right = ((chip + 1) % length * 2 + core, fsdp)
    left = ((chip + length - 1) % length * 2 + core, fsdp)

    def block(index):
        return all_ref.at[(index + length) % length * 2 + core]

    def pass_on(index, source):
        return send(source, block(index), core_sems, (index + length) % length, sibling)

    pass_on(chip, own_ref).start()
    for step in range(length - 1):
        for sign, peer, way in ((-1, right, right_sems), (1, left, left_sems)):
            at = chip + sign * step
            held = (at >= 0) & (at < length)
            if step > 0:

                @pl.when(held)
                def _():
                    send(block(at), block(at), way, step - 1, peer).wait_recv()
                    pass_on(at, block(at)).start()

            more = (chip < length - 1) if sign < 0 else (chip > 0)

            @pl.when(held & more)
            def _():
                send(own_ref if step == 0 else block(at), block(at), way, step, peer).start()

        yield
    last = length - 1
    for sign, peer, way in ((-1, right, right_sems), (1, left, left_sems)):
        at = chip + sign * last

        @pl.when((at >= 0) & (at < length))
        def _():
            send(block(at), block(at), way, last - 1, peer).wait_recv()
            pass_on(at, block(at)).start()

    yield
    for step in range(length - 1):
        for sign, peer, way in ((-1, right, right_sems), (1, left, left_sems)):
            at = chip + sign * step
            more = (chip < length - 1) if sign < 0 else (chip > 0)

            @pl.when((at >= 0) & (at < length) & more)
            def _():
                send(block(at), block(at), way, step, peer).wait_send()

    for index in range(length):
        pass_on(index, block(index)).wait_send()
        other = all_ref.at[index * 2 + 1 - core]
        send(other, other, core_sems, index, sibling).wait_recv()


def square_gather(own_ref, all_ref, sems, ctx, fsdp, n_fsdp, passed=None):
    if n_fsdp != 4:
        copies = [
            send(own_ref, all_ref.at[fsdp], sems, j - 1, (ctx, (fsdp + j) % n_fsdp)) for j in range(1, n_fsdp)
        ]
        for copy in copies:
            copy.start()
        yield
        for j, copy in enumerate(copies):
            copy.wait()
            if passed:
                passed(all_ref.at[(fsdp + n_fsdp - j - 1) % n_fsdp], (fsdp + n_fsdp - j - 1) % n_fsdp, None, j)
        return
    first, second, corner = fsdp_neighbours(fsdp)
    half = own_ref.shape[0] // 2
    top, low_half = pl.ds(0, half), pl.ds(half, half)
    to_first, to_second = (ctx, first), (ctx, second)

    def copy(index, owner, part, peer, source=None):
        source = all_ref.at[owner, part] if source is None else source
        return send(source, all_ref.at[owner, part], sems, index, peer)

    starts = [
        copy(0, fsdp, top, to_first, own_ref.at[top]),
        copy(1, fsdp, low_half, to_second, own_ref.at[low_half]),
        copy(2, fsdp, low_half, to_first, own_ref.at[low_half]),
        copy(3, fsdp, top, to_second, own_ref.at[top]),
        copy(4, first, top, to_second),
        copy(5, second, low_half, to_first),
    ]
    arrivals = [
        (0, first, top),
        (1, second, low_half),
        (2, first, low_half),
        (3, second, top),
        (4, corner, top),
        (5, corner, low_half),
    ]
    for each in starts[:4]:
        each.start()
    yield
    for index, owner, part in arrivals:
        copy(index, owner, part, to_first).wait_recv()
        if index < 2:
            starts[4 + index].start()
        if passed:
            passed(all_ref.at[owner, part], owner, part, index)
        yield
    for each in starts:
        each.wait_send()


def run_all(*parts):
    parts = list(parts)
    while parts:
        for part in list(parts):
            try:
                next(part)
            except StopIteration:
                parts.remove(part)


def dma_pair(count):
    return [pltpu.SemaphoreType.DMA((count,)), pltpu.SemaphoreType.DMA((count,))]


def any_specs(count):
    return [pl.BlockSpec(memory_space=pl.ANY)] * count


def params(collective_id=None, **more):
    if collective_id is not None:
        more.update(collective_id=collective_id, has_side_effects=True)
    return pltpu.CompilerParams(vmem_limit_bytes=VMEM_LIMIT, **more)


def passing(own_ref, all_ref, sems, core, fsdp, sibling):
    handed = [send(own_ref, all_ref.at[core, fsdp], sems, 0, sibling)]
    handed[0].start()
    arriving = [send(own_ref, all_ref.at[1 - core, fsdp], sems, 0, sibling)]

    def passed(source, owner, part, index):
        for side, copies in ((core, handed), (1 - core, arriving)):
            target = all_ref.at[side, owner] if part is None else all_ref.at[side, owner, part]
            copies.append(send(source, target, sems, index + 1, sibling))
        handed[-1].start()

    def finish():
        for out, back in zip(handed, arriving):
            out.wait_send()
            back.wait_recv()

    return (passed, finish)


def line_rows(n_ctx, rows):
    def kernel(rows_ref, all_rows, right_s, right_r, left_s, left_r, core_s, core_r, own):
        where = place(n_ctx)
        chip, core, fsdp, length = where
        greet(line_peers(*where))
        mine = pltpu.make_async_copy(rows_ref, all_rows.at[chip * 2 + core], own)
        mine.start()
        run_all(line_gather(rows_ref, all_rows, ((right_s, right_r), (left_s, left_r), (core_s, core_r)), where))
        mine.wait()

    length = n_ctx // 2
    return pl.pallas_call(
        kernel,
        out_shape=jax.ShapeDtypeStruct((n_ctx,) + rows.shape, rows.dtype),
        in_specs=any_specs(1),
        out_specs=pl.BlockSpec(memory_space=pl.ANY),
        scratch_shapes=dma_pair(length) + dma_pair(length) + dma_pair(length) + [pltpu.SemaphoreType.DMA],
        compiler_params=params(0),
        name="line_rows",
    )(rows)


def square_core_gather(n_ctx, n_fsdp, rows):
    def kernel(rows_ref, all_ref, sq_s, sq_r, core_s, core_r, own):
        chip, core, fsdp, _ = place(n_ctx)
        ctx = chip * 2 + core
        sibling = (chip * 2 + 1 - core, fsdp)
        greet([sibling] + fsdp_peers(n_fsdp, ctx, fsdp))
        mine = pltpu.make_async_copy(rows_ref, all_ref.at[core, fsdp], own)
        mine.start()
        passed, finish = passing(rows_ref, all_ref, (core_s, core_r), core, fsdp, sibling)
        run_all(square_gather(rows_ref, all_ref.at[core], (sq_s, sq_r), ctx, fsdp, n_fsdp, passed))
        finish()
        mine.wait()

    return pl.pallas_call(
        kernel,
        out_shape=jax.ShapeDtypeStruct((2, n_fsdp) + rows.shape, rows.dtype),
        in_specs=any_specs(1),
        out_specs=pl.BlockSpec(memory_space=pl.ANY),
        scratch_shapes=dma_pair(max(6, n_fsdp)) + dma_pair(max(7, n_fsdp)) + [pltpu.SemaphoreType.DMA],
        compiler_params=params(1),
        name="square_core_gather",
    )(rows)


def add_into(target, *sources, chunk=64):
    @pl.loop(0, target.shape[0] // chunk)
    def _(step):
        rows = pl.ds(pl.multiple_of(step * chunk, chunk), chunk)
        total = target[rows].astype(jnp.float32)
        for source in sources:
            total = total + source[rows].astype(jnp.float32)
        target[rows] = total.astype(target.dtype)


def square_sum_stages(n_ctx, n_fsdp, partial_ref, out_ref, held, core_in, square_in, load, core_sems, sems):
    rows = partial_ref.shape[-2]
    half = rows // 2
    chip, core, fsdp, _ = place(n_ctx)
    ctx = chip * 2 + core
    sibling = (chip * 2 + 1 - core, fsdp)
    if n_fsdp == 4:
        first, second, corner = fsdp_neighbours(fsdp)
        order = [corner, first, second, fsdp]
    else:
        order = [(fsdp + j) % n_fsdp for j in range(1, n_fsdp + 1)]
    mine = [
        pltpu.make_async_copy(partial_ref.at[core, owner], held.at[owner], load.at[j])
        for j, owner in enumerate(order)
    ]
    others = [
        send(partial_ref.at[1 - core, owner], core_in.at[owner], core_sems, j, sibling)
        for j, owner in enumerate(order)
    ]

    def ready(j):
        mine[j].wait()
        others[j].wait_recv()
        add_into(held.at[order[j]], core_in.at[order[j]])

    def total(parts, sources):
        @pl.loop(0, parts[1] // 64)
        def _(step):
            at = pl.ds(pl.multiple_of(parts[0] + step * 64, 64), 64)
            from_at = pl.ds(pl.multiple_of(step * 64, 64), 64)
            value = held[fsdp, at].astype(jnp.float32)
            for j in sources:
                value = value + square_in[j, from_at].astype(jnp.float32)
            out_ref[at] = value

    def begin():
        greet([sibling] + fsdp_peers(n_fsdp, ctx, fsdp))
        for j in range(n_fsdp):
            others[j].start()
            mine[j].start()

    if n_fsdp != 4:
        copies = [
            send(held.at[order[j]], square_in.at[j], sems, j, (ctx, order[j])) for j in range(n_fsdp - 1)
        ]

        def spread():
            for j in range(n_fsdp):
                ready(j)
                if j < n_fsdp - 1:
                    copies[j].start()

        def finish():
            for copy in copies:
                copy.wait()
            total((0, rows), range(n_fsdp - 1))
            for each in others:
                each.wait_send()

        return [begin, spread, finish]

    top, low_half = pl.ds(0, half), pl.ds(half, half)
    to_first, to_second = (ctx, first), (ctx, second)

    def copy(index, owner, part, peer):
        return send(held.at[owner, part], square_in.at[index], sems, index, peer)

    copies = [
        copy(0, corner, top, to_first),
        copy(1, corner, low_half, to_second),
        copy(2, first, top, to_first),
        copy(3, second, low_half, to_second),
        copy(4, second, top, to_second),
        copy(5, first, low_half, to_first),
    ]

    def spread():
        ready(0)
        copies[0].start()
        copies[1].start()
        ready(1)
        copies[2].start()
        ready(2)
        copies[3].start()
        ready(3)

    def pass_on():
        copies[0].wait_recv()
        add_into(held.at[second, top], square_in.at[0])
        copies[4].start()
        copies[1].wait_recv()
        add_into(held.at[first, low_half], square_in.at[1])
        copies[5].start()

    def finish():
        for j in range(2, 6):
            copies[j].wait_recv()
        total((0, half), (2, 4))
        total((half, half), (3, 5))
        for each in copies:
            each.wait_send()
        for each in others:
            each.wait_send()

    return [begin, spread, pass_on, finish]


def corner_sum_stages(n_ctx, partial_ref, out_ref, held, square_in, load, sems):
    half = partial_ref.shape[1] // 2
    chip, core, fsdp, _ = place(n_ctx)
    ctx = chip * 2 + core
    first, second, corner = fsdp_neighbours(fsdp)
    top, low_half = pl.ds(0, half), pl.ds(half, half)
    to_first, to_second = (ctx, first), (ctx, second)

    def copy(index, source, peer):
        return send(source, square_in.at[index], sems, index, peer)

    copies = [
        copy(0, partial_ref.at[corner, top], to_first),
        copy(1, partial_ref.at[corner, low_half], to_second),
        copy(2, partial_ref.at[first, top], to_first),
        copy(3, partial_ref.at[second, low_half], to_second),
        copy(4, held.at[0], to_second),
        copy(5, held.at[1], to_first),
    ]
    mine = [
        pltpu.make_async_copy(partial_ref.at[second, top], held.at[0], load.at[0]),
        pltpu.make_async_copy(partial_ref.at[first, low_half], held.at[1], load.at[1]),
        pltpu.make_async_copy(partial_ref.at[fsdp, top], held.at[2], load.at[2]),
        pltpu.make_async_copy(partial_ref.at[fsdp, low_half], held.at[3], load.at[3]),
    ]

    def begin():
        greet(fsdp_peers(4, ctx, fsdp))
        for each in copies[:4]:
            each.start()
        for each in mine:
            each.start()

    def pass_on():
        for index in range(2):
            mine[index].wait()
            copies[index].wait_recv()
            add_into(held.at[index], square_in.at[index])
            copies[4 + index].start()

    def finish():
        for part, sources in ((0, (2, 4)), (1, (3, 5))):
            mine[2 + part].wait()
            for j in sources:
                copies[j].wait_recv()

            @pl.loop(0, half // 64)
            def _(step):
                at = pl.ds(pl.multiple_of(step * 64, 64), 64)
                value = held[2 + part, at].astype(jnp.float32)
                for j in sources:
                    value = value + square_in[j, at].astype(jnp.float32)
                out_ref[pl.ds(pl.multiple_of(part * half + step * 64, 64), 64)] = value

        for each in copies:
            each.wait_send()

    return [begin, pass_on, finish]


def corner_sum_scratch(partial):
    _, rows, columns = partial.shape
    return [
        pltpu.VMEM((4, rows // 2, columns), partial.dtype),
        pltpu.VMEM((6, rows // 2, columns), partial.dtype),
        pltpu.SemaphoreType.DMA((4,)),
    ] + dma_pair(6)


def square_sum_scratch(n_fsdp, partial):
    rows, columns = partial.shape[-2:]
    pieces = (6, rows // 2, columns) if n_fsdp == 4 else (n_fsdp - 1, rows, columns)
    return (
        [
            pltpu.VMEM((n_fsdp, rows, columns), partial.dtype),
            pltpu.VMEM((n_fsdp, rows, columns), partial.dtype),
            pltpu.VMEM(pieces, partial.dtype),
            pltpu.SemaphoreType.DMA((n_fsdp,)),
        ]
        + dma_pair(n_fsdp)
        + dma_pair(max(6, n_fsdp))
    )


def square_sum(n_ctx, n_fsdp, partial):
    def kernel(partial_ref, out_ref, held, core_in, square_in, load, core_s, core_r, sq_s, sq_r):
        for stage in square_sum_stages(
            n_ctx, n_fsdp, partial_ref, out_ref, held, core_in, square_in, load, (core_s, core_r), (sq_s, sq_r)
        ):
            stage()

    return pl.pallas_call(
        kernel,
        out_shape=jax.ShapeDtypeStruct(partial.shape[-2:], jnp.float32),
        in_specs=any_specs(1),
        out_specs=pl.BlockSpec(memory_space=pltpu.VMEM),
        scratch_shapes=square_sum_scratch(n_fsdp, partial),
        compiler_params=params(1),
        name="square_sum",
    )(partial)


def line_sum(n_ctx, partial, collective_id):
    rows, columns = partial.shape[-2:]
    length = n_ctx // 2

    def kernel(partial_ref, out_ref, held, core_in, right_in, left_in, load, core_s, core_r, right_s, right_r, left_s, left_r):
        where = place(n_ctx)
        chip, core, fsdp, _ = where
        sibling, right, left = line_peers(*where)
        greet([sibling, right, left])
        order = [(chip + length - 1 - j) % length for j in range(length)]
        mine, others = [], []
        for j, owner in enumerate(order):
            mine.append(pltpu.make_async_copy(partial_ref.at[owner * 2 + core], held.at[owner], load.at[j]))
            others.append(
                send(partial_ref.at[owner * 2 + 1 - core], core_in.at[owner], (core_s, core_r), j, sibling)
            )
            others[-1].start()
            mine[-1].start()
        for j, owner in enumerate(order):
            mine[j].wait()
            others[j].wait_recv()
            add_into(held.at[owner], core_in.at[owner])
        ways = ((1, right, right_in, (right_s, right_r)), (-1, left, left_in, (left_s, left_r)))
        for step in range(length - 1):
            for sign, peer, arrived, sems in ways:
                block = chip + sign * (length - 1 - step)
                inside = (block >= 0) & (block < length)

                came = (chip >= 1) if sign > 0 else (chip < length - 1)
                if step > 0:

                    @pl.when(inside & came)
                    def _():
                        send(held.at[block], arrived.at[step - 1], sems, step - 1, peer).wait_recv()
                        add_into(held.at[block], arrived.at[step - 1])

                @pl.when(inside)
                def _():
                    send(held.at[block], arrived.at[step], sems, step, peer).start()

        last = length - 2
        for sign, peer, arrived, sems in ways:
            came = (chip >= 1) if sign > 0 else (chip < length - 1)

            @pl.when(came)
            def _():
                send(held.at[chip], arrived.at[last], sems, last, peer).wait_recv()
                add_into(held.at[chip], arrived.at[last])

        @pl.loop(0, rows // 64)
        def _(step):
            at = pl.ds(pl.multiple_of(step * 64, 64), 64)
            out_ref[at] = held[chip, at].astype(jnp.float32)

        for step in range(length - 1):
            for sign, peer, arrived, sems in ways:
                block = chip + sign * (length - 1 - step)

                @pl.when((block >= 0) & (block < length))
                def _():
                    send(held.at[block], arrived.at[step], sems, step, peer).wait_send()

        for each in others:
            each.wait_send()

    return pl.pallas_call(
        kernel,
        out_shape=jax.ShapeDtypeStruct((rows, columns), jnp.float32),
        in_specs=any_specs(1),
        out_specs=pl.BlockSpec(memory_space=pltpu.VMEM),
        scratch_shapes=[
            pltpu.VMEM((length, rows, columns), partial.dtype),
            pltpu.VMEM((length, rows, columns), partial.dtype),
            pltpu.VMEM((length - 1, rows, columns), partial.dtype),
            pltpu.VMEM((length - 1, rows, columns), partial.dtype),
            pltpu.SemaphoreType.DMA((length,)),
        ]
        + dma_pair(length)
        + dma_pair(length)
        + dma_pair(length),
        compiler_params=params(collective_id),
        name="line_sum",
    )(partial)


def sum_everywhere(n_ctx, n_fsdp, values):
    block = values.shape[1:]

    def kernel(values_ref, out_ref, along_ctx, along_fsdp, result, ctx_s, ctx_r, fsdp_s, fsdp_r, back_s, back_r):
        ctx = lax.axis_index("ctx")
        fsdp = lax.axis_index("fsdp")
        ctx_peers = [((ctx + j) % n_ctx, fsdp) for j in range(1, n_ctx)]
        fsdp_peers = [(ctx, (fsdp + j) % n_fsdp) for j in range(1, n_fsdp)]
        greet(ctx_peers + fsdp_peers)

        def exchange(copies):
            for copy in copies:
                copy.start()
            for copy in copies:
                copy.wait()

        def total(slots, count):
            value = slots[0]
            for j in range(1, count):
                value = value + slots[j]
            return value

        along_ctx[ctx] = values_ref[ctx]
        exchange(
            [
                send(values_ref.at[peer[0]], along_ctx.at[ctx], (ctx_s, ctx_r), j, peer)
                for j, peer in enumerate(ctx_peers)
            ]
        )
        along_fsdp[fsdp] = total(along_ctx, n_ctx)
        exchange(
            [
                send(along_fsdp.at[fsdp], along_fsdp.at[fsdp], (fsdp_s, fsdp_r), j, peer)
                for j, peer in enumerate(fsdp_peers)
            ]
        )
        result[ctx] = total(along_fsdp, n_fsdp)
        exchange(
            [send(result.at[ctx], result.at[ctx], (back_s, back_r), j, peer) for j, peer in enumerate(ctx_peers)]
        )
        out_ref[...] = result[...]

    return pl.pallas_call(
        kernel,
        out_shape=jax.ShapeDtypeStruct(values.shape, values.dtype),
        in_specs=[pl.BlockSpec(memory_space=pltpu.VMEM)],
        out_specs=pl.BlockSpec(memory_space=pltpu.VMEM),
        scratch_shapes=[
            pltpu.VMEM((n_ctx,) + block, values.dtype),
            pltpu.VMEM((n_fsdp,) + block, values.dtype),
            pltpu.VMEM((n_ctx,) + block, values.dtype),
        ]
        + dma_pair(n_ctx)
        + dma_pair(n_fsdp)
        + dma_pair(n_ctx),
        compiler_params=params(2),
        name="sum_everywhere",
    )(values)


def hidden_units(here, back, gate_ref, up_ref, down_ref):
    gate = mm(here, gate_ref[0], CONTRACT_LAST)
    up = mm(here, up_ref[0], CONTRACT_LAST)
    grad_hidden = mm(back, down_ref[0], CONTRACT_LAST)
    sigmoid = jax.nn.sigmoid(gate)
    activated = gate * sigmoid
    return (
        low(activated * up),
        low(grad_hidden * up * sigmoid * (1.0 + gate * (1.0 - sigmoid))),
        low(grad_hidden * activated),
    )


def ffn_forward(rows, planes, core, n_own, chunk=256):
    blocks, _, tokens, features = rows.shape
    total = blocks * tokens
    steps = n_own // chunk
    group = max(1, 256 // tokens)

    def kernel(core_ref, rows_ref, gate_ref, up_ref, down_ref, *outs):
        for at in range(0, blocks, group):
            here = rows_ref[at : at + group, 0].reshape(group * tokens, features)
            back = rows_ref[at : at + group, 1].reshape(group * tokens, features)
            span = pl.ds(at * tokens, group * tokens)
            for out, value in zip(outs, hidden_units(here, back, gate_ref, up_ref, down_ref)):
                out[span] = value

    def weight_spec(plane):
        return pl.BlockSpec((1, chunk, features), lambda j, core_ref: (plane, core_ref[0] * steps + j, 0))

    act = jax.ShapeDtypeStruct((total, n_own), jnp.bfloat16)
    act_spec = pl.BlockSpec((total, chunk), lambda j, core_ref: (0, j))
    return pl.pallas_call(
        kernel,
        grid_spec=pltpu.PrefetchScalarGridSpec(
            num_scalar_prefetch=1,
            grid=(steps,),
            in_specs=[
                pl.BlockSpec(rows.shape, lambda j, core_ref: (0, 0, 0, 0), pipeline_mode=pl.Buffered(1)),
                weight_spec(0),
                weight_spec(1),
                weight_spec(2),
            ],
            out_specs=[act_spec, act_spec, act_spec],
        ),
        out_shape=[act, act, act],
        compiler_params=params(),
        cost_estimate=pl.CostEstimate(
            flops=6 * total * n_own * features, bytes_accessed=30 * 1024 * 1024, transcendentals=total * n_own
        ),
        name="ffn_forward",
    )(core, rows, planes, planes, planes)


def mirror_gather(all_ref, arrivals, sems, pass_sems, ctx, core, fsdp, sibling):
    first, second, corner = fsdp_neighbours(fsdp)
    half = all_ref.shape[2] // 2
    parts = [pl.ds(0, half), pl.ds(half, half)]
    to_first, to_second = (ctx, first), (ctx, second)

    def copy(index, owner, part, peer):
        place_ref = all_ref.at[core, owner, parts[part]]
        return send(place_ref, place_ref, sems, index, peer)

    copies = [
        copy(0, fsdp, 0, to_first),
        copy(1, fsdp, 0, to_second),
        copy(2, fsdp, 1, to_first),
        copy(3, fsdp, 1, to_second),
        copy(4, first, 0, to_second),
        copy(5, second, 1, to_first),
    ]
    passes = [(fsdp, 0), (fsdp, 1), (first, 0), (second, 0), (first, 1), (second, 1), (corner, 0), (corner, 1)]

    def passing_copy(number, side):
        owner, part = passes[number]
        place_ref = all_ref.at[side, owner, parts[part]]
        return send(place_ref, place_ref, pass_sems, number, sibling)

    for part in range(2):
        arrivals[part].wait_recv()
        copies[2 * part].start()
        copies[2 * part + 1].start()
        passing_copy(part, core).start()
        yield
    for index, number, then in ((0, 2, 4), (1, 3, None), (2, 4, None), (3, 5, 5), (4, 6, None), (5, 7, None)):
        owner, part = passes[number]
        copy(index, owner, part, to_first).wait_recv()
        if then is not None:
            copies[then].start()
        passing_copy(number, core).start()
        yield
    for each in copies:
        each.wait_send()
    for number in range(8):
        passing_copy(number, core).wait_send()
        passing_copy(number, 1 - core).wait_recv()


def ffn_rows(n_ctx, own, planes, n_own, chunk=256, wide=512):
    n_fsdp = 4
    size, features = own.shape
    tokens = size // 2
    total = 2 * n_fsdp * tokens

    def kernel(
        own_ref, planes_ref, all_ref, mirror_ref, hidden_a, hidden_b, hidden_c, partial_ref,
        rows, weights, hidden, partial, core_in, load, sq_s, sq_r, core_s, core_r, far_s, far_r, mi_s, mi_r, mc_s, mc_r, sum_s, sum_r, out_sem,
    ):
        chip, core, fsdp, length = place(n_ctx)
        ctx = chip * 2 + core
        sibling = (chip * 2 + 1 - core, fsdp)
        mirror = ((length - 1 - chip) * 2 + core, fsdp)
        first, second, corner = fsdp_neighbours(fsdp)
        greet([sibling, mirror] + fsdp_peers(n_fsdp, ctx, fsdp))
        mine = pltpu.make_async_copy(own_ref, rows.at[core, fsdp], load.at[3])
        mine.start()
        start = pl.multiple_of(core * n_own, n_own)
        loads = [
            pltpu.make_async_copy(planes_ref.at[p, pl.ds(start, n_own)], weights.at[p], load.at[p]) for p in range(3)
        ]
        handed, arriving = [], []

        def hand(source, owner, part, index):
            for side, copies in ((core, handed), (1 - core, arriving)):
                target = rows.at[side, owner] if part is None else rows.at[side, owner, part]
                copies.append(send(source, target, (core_s, core_r), index + 1, sibling))
            handed[-1].start()

        gathering = square_gather(own_ref, rows.at[core], (sq_s, sq_r), ctx, fsdp, n_fsdp, hand)
        next(gathering)
        hand(own_ref, fsdp, None, -1)
        for each in loads:
            each.start()
        far = [
            send(
                own_ref.at[pl.ds(part * tokens, tokens)],
                mirror_ref.at[core, fsdp, pl.ds(part * tokens, tokens)],
                (far_s, far_r),
                part,
                mirror,
            )
            for part in range(2)
        ]
        for each in far:
            each.start()
        mirroring = mirror_gather(mirror_ref, far, (mi_s, mi_r), (mc_s, mc_r), ctx, core, fsdp, sibling)
        outs, summing, sums = [], [], []

        def add_up(number, owner):
            summing[number].wait_recv()
            add_into(partial.at[number % 2, core], core_in.at[number])
            sums.append(
                pltpu.make_async_copy(partial.at[number % 2, core], partial_ref.at[owner], out_sem.at[number % 2, 8])
            )
            sums[-1].start()

        def group(number, owner):
            slot = number % 2
            if number >= 2:
                for each in outs[number - 2]:
                    each.wait()
                summing[number - 2].wait_send()
                sums[number - 2].wait()
            here = jnp.concatenate([rows[0, owner, :tokens], rows[1, owner, :tokens]])
            back = jnp.concatenate([rows[0, owner, tokens:], rows[1, owner, tokens:]])

            @pl.loop(0, n_own // chunk)
            def _(step):
                at = pl.ds(pl.multiple_of(step * chunk, chunk), chunk)
                parts = [weights.at[pl.ds(p, 1), at] for p in range(3)]
                for q, value in enumerate(hidden_units(here, back, *parts)):
                    hidden[slot, q, :, at] = value

            @pl.loop(0, features // wide)
            def _(step):
                at = pl.ds(pl.multiple_of(step * wide, wide), wide)
                out = low(mm(hidden[slot, 0], weights[2, :, at]))
                below = low(mm(hidden[slot, 1], weights[0, :, at]) + mm(hidden[slot, 2], weights[1, :, at]))
                for k in range(2):
                    partial[slot, k, :tokens, at] = out[k * tokens : (k + 1) * tokens]
                    partial[slot, k, tokens:, at] = below[k * tokens : (k + 1) * tokens]

            pairs = []
            summing.append(send(partial.at[slot, 1 - core], core_in.at[number], (sum_s, sum_r), number, sibling))
            summing[-1].start()
            for k in range(2):
                pairs.append((rows.at[k, owner], all_ref.at[k, owner]))
                at = pl.ds(pl.multiple_of((k * n_fsdp + owner) * tokens, tokens), tokens)
                for q, target in enumerate((hidden_a, hidden_b, hidden_c)):
                    pairs.append((hidden.at[slot, q, pl.ds(k * tokens, tokens)], target.at[at]))
            outs.append(
                [pltpu.make_async_copy(a, b, out_sem.at[slot, j]) for j, (a, b) in enumerate(pairs)]
            )
            for each in outs[-1]:
                each.start()

        mine.wait()
        arriving[0].wait_recv()
        for each in loads:
            each.wait()
        group(0, fsdp)
        for _ in range(4):
            next(gathering)
        arriving[1].wait_recv()
        arriving[3].wait_recv()
        group(1, first)
        add_up(0, fsdp)
        next(mirroring)
        for _ in range(2):
            next(gathering)
        arriving[2].wait_recv()
        arriving[4].wait_recv()
        group(2, second)
        add_up(1, first)
        for _ in range(3):
            next(mirroring)
        arriving[5].wait_recv()
        arriving[6].wait_recv()
        group(3, corner)
        add_up(2, second)
        next(mirroring)
        add_up(3, corner)
        run_all(mirroring, gathering)
        for each in handed:
            each.wait_send()
        for each in far:
            each.wait_send()
        for each in outs[2] + outs[3] + sums[2:]:
            each.wait()
        for each in summing[2:]:
            each.wait_send()

    act = jax.ShapeDtypeStruct((total, n_own), own.dtype)
    all_rows = jax.ShapeDtypeStruct((2, n_fsdp) + own.shape, own.dtype)
    return pl.pallas_call(
        kernel,
        in_specs=any_specs(2),
        out_specs=any_specs(6),
        out_shape=[all_rows, all_rows, act, act, act, jax.ShapeDtypeStruct((n_fsdp,) + own.shape, own.dtype)],
        scratch_shapes=[
            pltpu.VMEM((2, n_fsdp) + own.shape, own.dtype),
            pltpu.VMEM((3, n_own, features), own.dtype),
            pltpu.VMEM((2, 3, 2 * tokens, n_own), own.dtype),
            pltpu.VMEM((2, 2) + own.shape, own.dtype),
            pltpu.VMEM((n_fsdp,) + own.shape, own.dtype),
            pltpu.SemaphoreType.DMA((4,)),
        ]
        + dma_pair(6)
        + dma_pair(7)
        + dma_pair(2)
        + dma_pair(6)
        + dma_pair(8)
        + dma_pair(4)
        + [pltpu.SemaphoreType.DMA((2, 9))],
        compiler_params=params(6),
        cost_estimate=pl.CostEstimate(
            flops=12 * total * n_own * features, bytes_accessed=50 * 1024 * 1024, transcendentals=total * n_own
        ),
        name="ffn_rows",
    )(own, planes)


def ffn_weights(n_ctx, n_fsdp, partial, rows, rows_mirror, hidden, planes, n_own, chunk=256):
    blocks, _, tokens, features = rows.shape
    total = blocks * tokens
    steps = n_own // chunk
    group = max(1, 256 // tokens)
    half = features // 2
    sides = n_ctx // 4
    wide = half // sides
    fused = partial is not None

    def kernel(*refs):
        rows_ref, refs = refs[0], refs[1:]
        mirror_refs, refs = refs[: len(rows_mirror)], refs[len(rows_mirror) :]
        mirror_blocks = [ref.at[b] for ref in mirror_refs for b in range(ref.shape[0])]
        hidden_ref, grad_gate_ref, grad_up_ref, planes_ref, *refs = refs
        if fused:
            partial_ref, weight_ref, out_ref, *refs = refs
        else:
            weight_ref, *refs = refs
        mirror, (weights, weight_sems), refs = refs[:3], refs[3:5], refs[5:]
        chip, core, _, length = place(n_ctx)
        side = chip // sides
        step = pl.program_id(0)
        stages = [lambda: None]
        if fused:
            held, square_in, load, sq_s, sq_r = refs
            stages = corner_sum_stages(n_ctx, partial_ref, out_ref, held, square_in, load, (sq_s, sq_r))

        def fetch(at, slot):
            start = pl.multiple_of((core * steps + at) * chunk, chunk)
            return pltpu.make_async_copy(planes_ref.at[:, pl.ds(start, chunk)], weights.at[slot], weight_sems.at[slot])

        @pl.when(step == 0)
        def _():
            fetch(0, 0).start()
            stages[0]()

        @pl.when(step + 1 < steps)
        def _():
            fetch(step + 1, (step + 1) % 2).start()

        slot = step % 2
        fetch(step, slot).wait()
        gate_ref, up_ref, down_ref = (weights.at[slot, pl.ds(plane, 1)] for plane in range(3))
        for at in range(0, blocks, group):
            here = jnp.concatenate([ref[0] for ref in mirror_blocks[at : at + group]])
            back = jnp.concatenate([ref[1] for ref in mirror_blocks[at : at + group]])
            span = pl.ds(at * tokens, group * tokens)
            for out, value in zip(mirror, hidden_units(here, back, gate_ref, up_ref, down_ref)):
                out[span] = value

        lefts = ((grad_gate_ref, mirror[1], 0), (grad_up_ref, mirror[2], 0), (hidden_ref, mirror[0], 1))
        for plane, (left, left_mirror, which) in enumerate(lefts):
            left = left[...]
            left_mirror = left_mirror[...]
            for z in range(sides):
                cols = pl.ds(pl.multiple_of(side * half + z * wide, wide), wide)
                right = rows_ref[:, which, :, cols].reshape(total, wide)
                right_mirror = jnp.concatenate([ref[which, :, cols] for ref in mirror_blocks])
                weight_ref[z, plane] = low(
                    mm(left, right, CONTRACT_FIRST) + mm(left_mirror, right_mirror, CONTRACT_FIRST)
                )

        for at, stage in ((1, 1), (steps - 1, 2)):
            if stage < len(stages):

                @pl.when(step == min(at, steps - 1))
                def _():
                    stages[stage]()

    act_spec = pl.BlockSpec((total, chunk), lambda j: (0, j))
    once = dict(pipeline_mode=pl.Buffered(1))
    operands = [rows, *rows_mirror, *hidden, planes]
    in_specs = [whole_block(rows.shape, **once)] + [whole_block(part.shape, **once) for part in rows_mirror]
    in_specs += [act_spec] * 3 + any_specs(1)
    out_specs = [pl.BlockSpec((sides, 3, chunk, wide), lambda j: (0, 0, j, 0))]
    out_shape = [jax.ShapeDtypeStruct((sides, 3, n_own, wide), jnp.bfloat16)]
    scratch = [pltpu.VMEM((total, chunk), jnp.bfloat16)] * 3
    scratch += [pltpu.VMEM((2, 3, chunk, features), jnp.bfloat16), pltpu.SemaphoreType.DMA((2,))]
    if fused:
        operands.append(partial)
        in_specs += any_specs(1)
        out_specs.append(whole_block(partial.shape[-2:], **once))
        out_shape.append(jax.ShapeDtypeStruct(partial.shape[-2:], jnp.float32))
        scratch += corner_sum_scratch(partial)
    return pl.pallas_call(
        kernel,
        grid=(steps,),
        in_specs=in_specs,
        out_specs=out_specs,
        out_shape=out_shape,
        scratch_shapes=scratch,
        compiler_params=params(3) if fused else params(),
        cost_estimate=pl.CostEstimate(
            flops=12 * total * n_own * features, bytes_accessed=50 * 1024 * 1024, transcendentals=total * n_own
        ),
        name="ffn_weights",
    )(*operands)


def ffn_back(hidden, grad_gate, grad_up, planes, core, blocks, wide=512):
    total, n_own = hidden.shape
    features = planes.shape[2]
    tokens = total // blocks

    def kernel(core_ref, hidden_ref, grad_gate_ref, grad_up_ref, gate_ref, up_ref, down_ref, out_ref):
        out = mm(hidden_ref[...], down_ref[0])
        out_ref[:, 0] = low(out).reshape(blocks, tokens, wide)
        back = mm(grad_gate_ref[...], gate_ref[0]) + mm(grad_up_ref[...], up_ref[0])
        out_ref[:, 1] = low(back).reshape(blocks, tokens, wide)

    def weight_spec(plane):
        return pl.BlockSpec((1, n_own, wide), lambda j, core_ref: (plane, core_ref[0], j))

    act_spec = pl.BlockSpec((total, n_own), lambda j, core_ref: (0, 0), pipeline_mode=pl.Buffered(1))
    return pl.pallas_call(
        kernel,
        grid_spec=pltpu.PrefetchScalarGridSpec(
            num_scalar_prefetch=1,
            grid=(features // wide,),
            in_specs=[act_spec, act_spec, act_spec, weight_spec(0), weight_spec(1), weight_spec(2)],
            out_specs=pl.BlockSpec((blocks, 2, tokens, wide), lambda j, core_ref: (0, 0, 0, j)),
        ),
        out_shape=jax.ShapeDtypeStruct((blocks, 2, tokens, features), jnp.bfloat16),
        compiler_params=params(),
        cost_estimate=pl.CostEstimate(
            flops=6 * total * n_own * features, bytes_accessed=30 * 1024 * 1024, transcendentals=0
        ),
        name="ffn_back",
    )(core, hidden, grad_gate, grad_up, planes, planes, planes)


SPAN = 256


def turn(values, cosine, sine):
    return values * cosine + pltpu.roll(values, HEAD_DIM // 2, 1) * sine


def attention_forward(rows, w_qkv, cosine, sine, place_column, place_row, heads):
    total, features = rows.shape
    own = heads * HEAD_DIM
    steps = total // SPAN
    scale = HEAD_DIM ** (-0.5)

    def kernel(
        rows_ref, w_ref, cosine_ref, sine_ref, column_ref, row_ref, query_ref, key_ref, value_ref, out_ref, log_ref
    ):
        step = pl.program_id(0)
        span = pl.ds(pl.multiple_of(step * SPAN, SPAN), SPAN)
        qkv = mm(rows_ref[...], w_ref[...])
        cosine = cosine_ref[span]
        sine = sine_ref[span]
        for h in range(heads):
            at = slice(h * HEAD_DIM, (h + 1) * HEAD_DIM)
            query_ref[span, at] = low(turn(qkv[:, at], cosine, sine))
            key_ref[span, at] = low(turn(qkv[:, own + h * HEAD_DIM : own + (h + 1) * HEAD_DIM], cosine, sine))
        value_ref[span] = low(qkv[:, 2 * own :])

        @pl.when(step == steps - 1)
        def _():
            for h in range(heads):
                at = slice(h * HEAD_DIM, (h + 1) * HEAD_DIM)

                @pl.loop(0, steps)
                def _(block):
                    here = pl.ds(pl.multiple_of(block * SPAN, SPAN), SPAN)
                    scores = mm(query_ref[here, at], key_ref[:, at], CONTRACT_LAST) * scale
                    scores = jnp.where(column_ref[here] >= row_ref[...], scores, MASKED)
                    highest = jnp.max(scores, axis=-1, keepdims=True)
                    exponent = jnp.exp(scores - highest)
                    sums = jnp.sum(exponent, axis=-1, keepdims=True)
                    out_ref[here, at] = low(mm(low(exponent * (1.0 / sums)), value_ref[:, at]))
                    log_ref[h, here] = highest + jnp.log(sums)

    act = jax.ShapeDtypeStruct((total, own), jnp.bfloat16)
    return pl.pallas_call(
        kernel,
        grid=(steps,),
        in_specs=[pl.BlockSpec((SPAN, features), lambda r: (r, 0))]
        + [whole_block(a.shape) for a in (w_qkv, cosine, sine, place_column, place_row)],
        out_specs=[whole_block((total, own))] * 4 + [whole_block((heads, total, 1))],
        out_shape=[act] * 4 + [jax.ShapeDtypeStruct((heads, total, 1), jnp.float32)],
        compiler_params=params(),
        name="attention_forward",
    )(rows, w_qkv, cosine, sine, place_column, place_row)


def attention_backward(query, key, value, grad, logs, w_qkv, cosine, sine, place_column, place_row, heads):
    total, own = query.shape
    features = w_qkv.shape[0]
    steps = total // SPAN
    scale = HEAD_DIM ** (-0.5)

    def kernel(
        query_ref, key_ref, value_ref, grad_ref, log_ref, w_ref, cosine_ref, sine_ref, column_ref, row_ref,
        qkv_ref, out_ref, key_sum, value_sum,
    ):
        step = pl.program_id(0)

        @pl.when(step == 0)
        def _():
            for h in range(heads):
                at = slice(h * HEAD_DIM, (h + 1) * HEAD_DIM)
                key_sum[...] = jnp.zeros_like(key_sum)
                value_sum[...] = jnp.zeros_like(value_sum)

                @pl.loop(0, steps)
                def _(block):
                    here = pl.ds(pl.multiple_of(block * SPAN, SPAN), SPAN)
                    queries = query_ref[here, at]
                    grads = grad_ref[here, at]
                    scores = mm(queries, key_ref[:, at], CONTRACT_LAST) * scale
                    scores = jnp.where(column_ref[here] >= row_ref[...], scores, MASKED)
                    probs = jnp.exp(scores - log_ref[h, here])
                    probs_grad = mm(grads, value_ref[:, at], CONTRACT_LAST)
                    centre = jnp.sum(probs * probs_grad, axis=-1, keepdims=True)
                    scores_grad = low(probs * (probs_grad - centre))
                    query_grad = mm(scores_grad, key_ref[:, at]) * scale
                    qkv_ref[here, at] = low(turn(query_grad, cosine_ref[here], -sine_ref[here]))
                    key_sum[...] += mm(scores_grad, queries, CONTRACT_FIRST)
                    value_sum[...] += mm(low(probs), grads, CONTRACT_FIRST)

                qkv_ref[:, own + h * HEAD_DIM : own + (h + 1) * HEAD_DIM] = low(
                    turn(key_sum[...] * scale, cosine_ref[...], -sine_ref[...])
                )
                qkv_ref[:, 2 * own + h * HEAD_DIM : 2 * own + (h + 1) * HEAD_DIM] = low(value_sum[...])

        span = pl.ds(pl.multiple_of(step * SPAN, SPAN), SPAN)
        out_ref[...] = low(mm(qkv_ref[span], w_ref[...], CONTRACT_LAST))

    return pl.pallas_call(
        kernel,
        grid=(steps,),
        in_specs=[
            whole_block(a.shape)
            for a in (query, key, value, grad, logs, w_qkv, cosine, sine, place_column, place_row)
        ],
        out_specs=[whole_block((total, 3 * own)), pl.BlockSpec((SPAN, features), lambda r: (r, 0))],
        out_shape=[
            jax.ShapeDtypeStruct((total, 3 * own), jnp.bfloat16),
            jax.ShapeDtypeStruct((total, features), jnp.bfloat16),
        ],
        scratch_shapes=[pltpu.VMEM((total, HEAD_DIM), jnp.float32)] * 2,
        compiler_params=params(),
        name="attention_backward",
    )(query, key, value, grad, logs, w_qkv, cosine, sine, place_column, place_row)


ROWS = 32


def row_blocks(count, features):
    return pl.BlockSpec((count, ROWS, features), lambda r, *_: (0, r, 0))


def whole_block(shape, **more):
    zeros = (0,) * len(shape)
    return pl.BlockSpec(shape, lambda r, *_: zeros, **more)


def connect_coefficients(values, dynamic_ref, static_ref, coef_ref, dyn_ref):
    lane = lax.broadcasted_iota(jnp.int32, (values[0].shape[0], 8), 1)
    columns = []
    for i, value in enumerate(values):
        mean = jnp.mean(value, axis=-1, keepdims=True)
        centered = value - mean
        inverse = lax.rsqrt(jnp.mean(centered * centered, axis=-1, keepdims=True) + EPS)
        normed = centered * inverse
        projected = 0.0
        for k in range(6):
            part = jnp.sum(normed * dynamic_ref[k : k + 1], axis=-1, keepdims=True)
            projected = jnp.where(lane == k, part, projected)
        dynamic_part = jnp.tanh(projected)
        coefficient = dynamic_part + static_ref[i : i + 1]
        dyn_ref[i] = dynamic_part
        coef_ref[i] = jnp.where(lane == 6, mean, jnp.where(lane == 7, inverse, coefficient))
        columns.append(coefficient)
    return columns


def connect_first(streams, dynamic, static):
    number, rows, features = streams.shape

    def kernel(streams_ref, dynamic_ref, static_ref, coef_ref, dyn_ref, low_ref):
        values = [streams_ref[i].astype(jnp.float32) for i in range(number)]
        columns = connect_coefficients(values, dynamic_ref, static_ref, coef_ref, dyn_ref)
        mixed = sum((columns[i][:, 1:2] * values[i] for i in range(number)))
        low_ref[...] = low(normalize(mixed)[0])

    small = jax.ShapeDtypeStruct((number, rows, 8), jnp.float32)
    return pl.pallas_call(
        kernel,
        grid=(rows // ROWS,),
        out_shape=(small, small, jax.ShapeDtypeStruct((rows, features), jnp.bfloat16)),
        in_specs=[row_blocks(number, features), whole_block(dynamic.shape), whole_block(static.shape)],
        out_specs=(
            row_blocks(number, 8),
            row_blocks(number, 8),
            pl.BlockSpec((ROWS, features), lambda r: (r, 0)),
        ),
        compiler_params=params(),
        name="connect_first",
    )(streams, dynamic, static)


def connect_middle(streams, coef, attended, w_mine, w_other, cotangent, dynamic, static, core_fsdp, where, depth):
    number, rows, features = streams.shape
    half = features // 2
    count = len(w_mine)

    def kernel(core_ref, streams_ref, coef_ref, attended_ref, *refs):
        weights, refs = refs[: 2 * count], refs[2 * count :]
        cotangent_ref, dynamic_ref, static_ref = refs[:3]
        first_ref, branch_ref, coef_two_ref, dyn_ref, own_ref, projected = refs[3:]
        step = pl.program_id(0)

        @pl.when(step == 0)
        def _():
            for side in range(2):
                total = 0.0
                for j, (d, offset) in enumerate(where):
                    size = w_mine[j].shape[0]
                    columns = pl.ds(pl.multiple_of((core_ref[1] ^ d) * depth + offset, size), size)
                    total = total + mm(attended_ref[:, columns], weights[side * count + j][...])
                projected[core_ref[0] if side == 0 else 1 - core_ref[0]] = total

        span = pl.ds(pl.multiple_of(step * ROWS, ROWS), ROWS)
        branch = jnp.concatenate([projected[0, span], projected[1, span]], axis=1)
        branch_ref[...] = branch
        inputs = [streams_ref[i].astype(jnp.float32) for i in range(number)]
        outs = []
        for j in range(number):
            out = sum((coef_ref[i][:, 2 + j : 3 + j] * inputs[i] for i in range(number)))
            outs.append(out + coef_ref[j][:, 0:1] * branch)
            first_ref[j] = outs[-1]
        columns = connect_coefficients(outs, dynamic_ref, static_ref, coef_two_ref, dyn_ref)
        mixed = sum((columns[i][:, 1:2] * outs[i] for i in range(number)))
        own_ref[0] = low(normalize(mixed)[0])
        own_ref[1] = low(sum((columns[j][:, 0:1] * cotangent_ref[j].astype(jnp.float32) for j in range(number))))

    small = jax.ShapeDtypeStruct((number, rows, 8), jnp.float32)
    once = dict(pipeline_mode=pl.Buffered(1))
    return pl.pallas_call(
        kernel,
        grid_spec=pltpu.PrefetchScalarGridSpec(
            num_scalar_prefetch=1,
            grid=(rows // ROWS,),
            in_specs=[
                row_blocks(number, features),
                row_blocks(number, 8),
                whole_block(attended.shape, **once),
                *[whole_block(w.shape, **once) for w in w_mine + w_other],
                row_blocks(number, features),
                whole_block(dynamic.shape),
                whole_block(static.shape),
            ],
            out_specs=(
                row_blocks(number, features),
                pl.BlockSpec((ROWS, features), lambda r, *_: (r, 0)),
                row_blocks(number, 8),
                row_blocks(number, 8),
                row_blocks(2, features),
            ),
            scratch_shapes=[pltpu.VMEM((2, rows, half), jnp.float32)],
        ),
        out_shape=(
            jax.ShapeDtypeStruct((number, rows, features), jnp.float32),
            jax.ShapeDtypeStruct((rows, features), jnp.float32),
            small,
            small,
            jax.ShapeDtypeStruct((2, rows, features), jnp.bfloat16),
        ),
        compiler_params=params(),
        name="connect_middle",
    )(core_fsdp, streams, coef, attended, *w_mine, *w_other, cotangent, dynamic, static)


def attention_weights(rows, grads, attended, grad_cols):
    total, features = rows.shape
    parts, _, own = attended.shape
    wide = grads.shape[1]

    def kernel(rows_ref, grads_ref, attended_ref, cols_ref, out_ref):
        out_ref[:, :wide] = low(mm(rows_ref[...], grads_ref[...], CONTRACT_FIRST))
        out_ref[:, wide:] = low(mm(attended_ref[0], cols_ref[...], CONTRACT_FIRST))

    return pl.pallas_call(
        kernel,
        grid=(parts,),
        in_specs=[
            pl.BlockSpec((total, own), lambda k: (0, k)),
            whole_block(grads.shape),
            pl.BlockSpec((1, total, own), lambda k: (k, 0, 0)),
            whole_block(grad_cols.shape),
        ],
        out_specs=pl.BlockSpec((own, wide + own), lambda k: (k, 0)),
        out_shape=jax.ShapeDtypeStruct((features, wide + own), jnp.bfloat16),
        compiler_params=params(),
        cost_estimate=pl.CostEstimate(
            flops=2 * total * features * (wide + own), bytes_accessed=16 * 1024 * 1024, transcendentals=0
        ),
        name="attention_weights",
    )(rows, grads, attended, grad_cols)


def project_back(grad, w_mine, w_other, core_fsdp, n_ctx, where, depth):
    rows, features = grad.shape
    half = features // 2
    count = len(w_mine)
    own = features // n_ctx

    def kernel(core_ref, grad_ref, *refs):
        weights, (out_ref, cols_ref) = refs[: 2 * count], refs[2 * count :]
        first = grad_ref[:, pl.ds(pl.multiple_of(core_ref[0] * half, half), half)]
        second = grad_ref[:, pl.ds(pl.multiple_of((1 - core_ref[0]) * half, half), half)]
        for j, (d, offset) in enumerate(where):
            out = low(
                mm(first, weights[j][...], CONTRACT_LAST) + mm(second, weights[count + j][...], CONTRACT_LAST)
            )
            for q in range(w_mine[j].shape[0] // own):
                at = (core_ref[1] ^ d) * (depth // own) + offset // own + q
                out_ref[at] = out[:, q * own : (q + 1) * own]
        for index in range(n_ctx):
            cols_ref[index] = grad_ref[:, index * own : (index + 1) * own]

    return pl.pallas_call(
        kernel,
        grid_spec=pltpu.PrefetchScalarGridSpec(
            num_scalar_prefetch=1,
            grid=(1,),
            in_specs=[whole_block(a.shape) for a in [grad] + w_mine + w_other],
            out_specs=[whole_block((n_ctx, rows, own))] * 2,
        ),
        out_shape=[jax.ShapeDtypeStruct((n_ctx, rows, own), grad.dtype)] * 2,
        compiler_params=params(),
        name="project_back",
    )(core_fsdp, grad, *w_mine, *w_other)


def connect_back(values, coef, dyn, branch, grads, grad_normed, dynamic, coef_before=None, offset=0):
    number, rows, features = values.shape
    steps = rows // ROWS
    more = coef_before is not None

    def kernel(*refs):
        values_ref, coef_ref, dyn_ref, branch_ref, grads_ref, normed_ref, dynamic_ref = refs[:7]
        refs = refs[7:]
        if more:
            before_ref, refs = refs[0], refs[1:]
        out_ref, dynamic_out, static_out = refs[:3]
        if more:
            forward_ref, grad_low_ref = refs[3:5]
        dynamic_sum = refs[-1]
        step = pl.program_id(0)

        @pl.when(step == 0)
        def _():
            dynamic_sum[...] = jnp.zeros_like(dynamic_sum)
            static_out[...] = jnp.zeros_like(static_out)

        branch = branch_ref[...]
        mixed = sum((coef_ref[i][:, 1:2] * values_ref[i].astype(jnp.float32) for i in range(number)))
        normed, inverse = normalize(mixed)
        grad_mixed = normalize_back(normed, inverse, normed_ref[...])
        lane = lax.broadcasted_iota(jnp.int32, (ROWS, 8), 1)
        totals = [0.0] * 6
        befores = 0.0
        for i in range(number):
            value = values_ref[i].astype(jnp.float32)
            grad_own = grads_ref[i].astype(jnp.float32)
            columns = [
                jnp.sum(grad_own * branch, axis=-1, keepdims=True),
                jnp.sum(grad_mixed * value, axis=-1, keepdims=True),
            ]
            out = coef_ref[i][:, 1:2] * grad_mixed
            for j in range(number):
                grad = grads_ref[j].astype(jnp.float32)
                columns.append(jnp.sum(grad * value, axis=-1, keepdims=True))
                out = out + coef_ref[i][:, 2 + j : 3 + j] * grad
            normed = (value - coef_ref[i][:, 6:7]) * coef_ref[i][:, 7:8]
            normed_grad = 0.0
            coef_grad = jnp.zeros((ROWS, 8), jnp.float32)
            for k in range(6):
                part = dyn_ref[i][:, k : k + 1]
                pre_grad = columns[k] * (1.0 - part * part)
                normed_grad = normed_grad + pre_grad * dynamic_ref[k : k + 1]
                totals[k] = totals[k] + pre_grad * normed
                coef_grad = jnp.where(lane == k, columns[k], coef_grad)
            out = out + normalize_back(normed, coef_ref[i][:, 7:8], normed_grad)
            out_ref[i] = out
            static_out[i : i + 1] += jnp.sum(coef_grad, axis=0, keepdims=True)
            if more:
                befores = befores + before_ref[i][:, 0:1] * out
        for k in range(6):
            dynamic_sum[k] += jnp.sum(totals[k].reshape(ROWS // 8, 8, features), axis=0)
        if more:
            grad_low_ref[...] = low(befores)
            for j in range(number):
                out = coef_ref[j][:, 0:1] * branch
                for i in range(number):
                    out = out + coef_ref[i][:, 2 + j : 3 + j] * values_ref[i].astype(jnp.float32)
                forward_ref[j] = low(out)

        @pl.when(step == steps - 1)
        def _():
            for k in range(6):
                dynamic_out[k : k + 1] = jnp.sum(dynamic_sum[k], axis=0, keepdims=True)
            dynamic_out[6:8] = jnp.zeros((2, features), jnp.float32)

    rows_spec = pl.BlockSpec((ROWS, features), lambda r: (r, 0))
    out_shape = [
        jax.ShapeDtypeStruct((number, rows, features), jnp.float32),
        jax.ShapeDtypeStruct((8, features), jnp.float32),
        jax.ShapeDtypeStruct((8, 8), jnp.float32),
    ]
    out_specs = [row_blocks(number, features), whole_block((8, features)), whole_block((8, 8))]
    operands = [values, coef, dyn, branch, grads, grad_normed, dynamic]
    in_specs = [
        row_blocks(number, features),
        row_blocks(number, 8),
        row_blocks(number, 8),
        rows_spec,
        row_blocks(number, features),
        pl.BlockSpec((ROWS, features), lambda r: (offset // ROWS + r, 0)),
        whole_block(dynamic.shape),
    ]
    if more:
        operands.append(coef_before)
        in_specs.append(row_blocks(number, 8))
        out_shape.append(jax.ShapeDtypeStruct((number, rows, features), jnp.bfloat16))
        out_specs.append(row_blocks(number, features))
        out_shape.append(jax.ShapeDtypeStruct((rows, features), jnp.bfloat16))
        out_specs.append(rows_spec)
    return pl.pallas_call(
        kernel,
        grid=(steps,),
        in_specs=in_specs,
        out_specs=out_specs,
        out_shape=out_shape,
        scratch_shapes=[pltpu.VMEM((6, 8, features), jnp.float32)],
        compiler_params=params(),
        name="connect_back",
    )(*operands)


def local(n_ctx, n_fsdp, streams, w_attn, w_ffn, hc_dynamic, hc_static, cotangent, pair_order):
    number = streams.shape[1]
    length = streams.shape[2]
    features = streams.shape[3]
    size = HEAD_DIM
    own = features // n_ctx
    heads = own // size
    rows = length * n_ctx
    own_rows = w_attn.shape[0]
    ctx = lax.axis_index("ctx")
    fsdp = lax.axis_index("fsdp")
    core = ctx % 2
    chips = n_ctx // 2
    core_index = jnp.reshape(core, (1,)).astype(jnp.int32)

    def in_order(mine, other, axis):
        return jnp.where(
            core == 0, jnp.concatenate([mine, other], axis=axis), jnp.concatenate([other, mine], axis=axis)
        )


    w_own = lax.dynamic_slice_in_dim(w_attn, ctx * own, own, 2)[:, 0:3].reshape(own_rows, 3 * own)
    w_qkv = gather(w_own, "fsdp")
    half = features // 2
    w_half = lax.dynamic_slice_in_dim(w_attn, core * half, half, 2)[:, 3]
    siblings = [(i, i ^ 1) for i in range(n_ctx)]
    core_fsdp = jnp.stack([core, fsdp]).astype(jnp.int32)

    def exchange(values, most=0):
        return [values] + [
            lax.ppermute(values, "fsdp", [(i, i ^ d) for i in range(n_fsdp)])
            for d in range(1, most + 1 if most else n_fsdp)
        ]

    def swap(blocks):
        return [lax.ppermute(block, "ctx", siblings) for block in blocks]


    positions = block_positions(pair_order, length)
    frequency = THETA ** (-(jnp.arange(size // 2, dtype=jnp.float32) * 2.0) / size)
    angles = positions.astype(jnp.float32)[:, None] * jnp.concatenate([frequency, frequency])[None, :]
    signs = jnp.where(jnp.arange(size) < size // 2, -1.0, 1.0)
    tables = (jnp.cos(angles), jnp.sin(angles) * signs[None, :], positions[:, None], positions[None, :])

    dynamics = jnp.pad(hc_dynamic, ((0, 0), (0, 2), (0, 0)))
    statics = jnp.pad(hc_static, ((0, 0), (0, 0), (0, 2)))
    coef_one, dyn_one, attn_low = connect_first(streams[0], dynamics[0], statics[0])
    attn_low, w_half = lax.optimization_barrier((attn_low, w_half))
    w_out_mine = exchange(w_half, 2 if n_fsdp == 4 else 0)
    attn_all = line_rows(n_ctx, attn_low).reshape(rows, features)
    w_out_where = [(d, 0) for d in range(len(w_out_mine))]
    if n_fsdp == 4:
        attn_all, *w_out_mine = lax.optimization_barrier((attn_all, *w_out_mine))
        middle = own_rows // 2
        w_out_mine.append(lax.ppermute(w_out_mine[1][:middle], "fsdp", [(i, i ^ 2) for i in range(4)]))
        w_out_mine.append(lax.ppermute(w_out_mine[2][middle:], "fsdp", [(i, i ^ 1) for i in range(4)]))
        w_out_where += [(3, 0), (3, middle)]
    query, key, value, attended, logs = attention_forward(attn_all, w_qkv, *tables, heads)
    attended, w_out_mine = lax.optimization_barrier((attended, w_out_mine))
    w_out_other = swap(w_out_mine)
    attended_rows = lax.all_to_all(attended, "ctx", 0, 1, tiled=True)

    first_out, attn_branch, coef_two, dyn_two, ffn_own = connect_middle(
        streams[0], coef_one, attended_rows, w_out_mine, w_out_other, cotangent[0], dynamics[1], statics[1], core_fsdp,
        w_out_where, own_rows,
    )
    ffn_own = ffn_own.reshape(2 * length, features)

    planes = jnp.moveaxis(w_ffn, 1, 0)
    n_own = planes.shape[1] // 2
    blocks = 2 * n_fsdp
    if n_fsdp == 4:
        ffn_all, mirror_rows, *hidden, sums = ffn_rows(n_ctx, ffn_own, planes, n_own)
        ffn_all, mirror_rows = (part.reshape(blocks, 2, length, features) for part in (ffn_all, mirror_rows))
        mirror_rows = [mirror_rows]
        attended, sums = lax.optimization_barrier((attended, sums))
        attended_all = gather(attended, "ctx").reshape(n_ctx, rows, own)
        *weight_parts, sums = ffn_weights(n_ctx, n_fsdp, sums, ffn_all, mirror_rows, hidden, planes, n_own)
    else:
        ffn_mirror = lax.ppermute(ffn_own, "ctx", [(i, n_ctx - 2 - i + 2 * (i % 2)) for i in range(n_ctx)])
        ffn_all = square_core_gather(n_ctx, n_fsdp, ffn_own).reshape(blocks, 2, length, features)
        attended_all = gather(attended, "ctx").reshape(n_ctx, rows, own)
        mirror_mine = exchange(ffn_mirror)
        hidden = ffn_forward(ffn_all, planes, core_index, n_own)
        sums = ffn_back(*hidden, planes, core_index, blocks)
        mirror_rows = [part.reshape(1, 2, length, features) for part in mirror_mine + swap(mirror_mine)]
        sums = square_sum(n_ctx, n_fsdp, sums.reshape(2, n_fsdp, 2 * length, features))
        weight_parts = ffn_weights(n_ctx, n_fsdp, None, ffn_all, mirror_rows, hidden, planes, n_own)
    sides = chips // 2
    lines = [[2 * (sides * side + i) + j for i in range(sides)] for side in range(2) for j in range(2)]
    weight_cols = lax.psum_scatter(weight_parts[0], "ctx", scatter_dimension=0, axis_index_groups=lines)

    grad_first, dynamic_grad_two, static_grad_two, streams_out, grad_attn = connect_back(
        first_out, coef_two, dyn_two, sums, cotangent[0], sums, dynamics[1], coef_one, length
    )
    grad_heads, grad_cols = project_back(grad_attn, w_out_mine, w_out_other, core_fsdp, n_ctx, w_out_where, own_rows)
    grad_heads = lax.all_to_all(grad_heads, "ctx", 0, 0, tiled=True).reshape(rows, own)
    grad_heads, grad_cols = lax.optimization_barrier((grad_heads, grad_cols))
    grad_cols = lax.all_to_all(grad_cols, "ctx", 0, 0, tiled=True).reshape(rows, own)
    qkv_grad, attn_part = attention_backward(query, key, value, grad_heads, logs, w_qkv, *tables, heads)
    attn_part = attn_part.reshape(n_ctx, length, features)
    grad_attn_normed = line_sum(n_ctx, attn_part, 5)
    grad_attn_normed, weight_cols = lax.optimization_barrier((grad_attn_normed, weight_cols))
    mine = lax.dynamic_slice_in_dim(weight_cols, core * own, own, 2)
    other = lax.dynamic_slice_in_dim(weight_cols, (1 - core) * own, own, 2)
    other = lax.ppermute(other, "ctx", siblings)
    ffn_grad = jnp.moveaxis(in_order(mine, other, 1), 0, 1).astype(jnp.float32)
    weight_part = attention_weights(attn_all, qkv_grad, attended_all, grad_cols)
    attn_grad = scatter(weight_part, "fsdp")

    grad_inputs, dynamic_grad_one, static_grad_one = connect_back(
        streams[0], coef_one, dyn_one, attn_branch, grad_first, grad_attn_normed, dynamics[0]
    )
    static_grads = jnp.concatenate([static_grad_one[:number, :6].reshape(1, -1), static_grad_two[:number, :6].reshape(1, -1)])
    small = jnp.concatenate(
        [
            dynamic_grad_one[:6],
            dynamic_grad_two[:6],
            jnp.pad(static_grads, ((0, 2), (0, features - 6 * number))),
        ]
    )
    small = sum_everywhere(n_ctx, n_fsdp, small.reshape(n_ctx, 8, -1))
    small, attn_grad = lax.optimization_barrier((small, attn_grad))
    small = small.reshape(16, features)
    attn_grad = attn_grad.astype(jnp.float32).reshape(own_rows, 4, own)
    dynamic_total = small[:12].reshape(2, 6, features)
    static_total = small[12:14, : 6 * number].reshape(2, number, 6)
    return (streams_out[None], grad_inputs[None], attn_grad, ffn_grad, dynamic_total, static_total)


def solution(mesh):
    return jax.shard_map(
        functools.partial(local, mesh.shape["ctx"], mesh.shape["fsdp"]),
        mesh=mesh,
        in_specs=(
            P("fsdp", None, "ctx", None),
            P("fsdp", None, None),
            P("fsdp", None, None),
            P(),
            P(),
            P("fsdp", None, "ctx", None),
            P(),
        ),
        out_specs=(
            P("fsdp", None, "ctx", None),
            P("fsdp", None, "ctx", None),
            P("fsdp", None, "ctx"),
            P("fsdp", None, "ctx"),
            P(),
            P(),
        ),
        check_vma=False,
    )
```

```python
import functools

import jax
import jax.numpy as jnp
from jax import lax
from jax.experimental import pallas as pl
from jax.experimental.pallas import tpu as pltpu
from jax.sharding import PartitionSpec as P

HEADS = 16
HEAD_DIM = 128


EPS = 1e-05
THETA = 10000.0
HIGH = lax.Precision.HIGHEST
MASKED = -1e30
CONTRACT_LAST = (((1,), (1,)), ((), ()))
CONTRACT_FIRST = (((0,), (0,)), ((), ()))


def normalize(values):
    centered = values - jnp.mean(values, axis=-1, keepdims=True)
    inverse = lax.rsqrt(jnp.mean(centered * centered, axis=-1, keepdims=True) + EPS)
    return (centered * inverse, inverse)


def normalize_back(normed, inverse, gradient):
    inner = jnp.mean(gradient * normed, axis=-1, keepdims=True)
    return inverse * (gradient - jnp.mean(gradient, axis=-1, keepdims=True) - normed * inner)


def block_positions(pair_order, length):
    half_size = length // 2
    offsets = jnp.arange(half_size, dtype=jnp.int32)
    mirror = 2 * pair_order.shape[0] - 1 - pair_order
    first_half = pair_order[:, None] * half_size + offsets[None, :]
    second_half = mirror[:, None] * half_size + offsets[None, :]
    return jnp.concatenate([first_half, second_half], axis=1).reshape(-1)


def low(values):
    return values.astype(jnp.bfloat16)


def mm(a, b, dims=None):
    if dims is None:
        return jnp.dot(a, b, preferred_element_type=jnp.float32)
    return lax.dot_general(a, b, dims, preferred_element_type=jnp.float32)


def gather(values, axis, dim=0):
    return lax.all_gather(values, axis, axis=dim, tiled=True)


def scatter(values, axis, dim=0):
    return lax.psum_scatter(values, axis, scatter_dimension=dim, tiled=True)


MESH = pl.DeviceIdType.MESH
VMEM_LIMIT = 60 * 1024 * 1024


def place(n_ctx):
    ctx = lax.axis_index("ctx")
    return (ctx // 2, ctx % 2, lax.axis_index("fsdp"), n_ctx // 2)


def greet(peers):
    barrier = pltpu.get_barrier_semaphore()
    for peer in peers:
        pl.semaphore_signal(barrier, inc=1, device_id=peer, device_id_type=MESH)
    pl.semaphore_wait(barrier, len(peers))


def send(source, target, sems, index, peer):
    return pltpu.make_async_remote_copy(
        src_ref=source,
        dst_ref=target,
        send_sem=sems[0].at[index],
        recv_sem=sems[1].at[index],
        device_id=peer,
        device_id_type=MESH,
    )


def fsdp_neighbours(fsdp):
    first = fsdp + 1 - 2 * (fsdp % 2)
    second = (fsdp + 2) % 4
    return (first, second, (first + 2) % 4)


def fsdp_peers(n_fsdp, ctx, fsdp):
    if n_fsdp == 4:
        first, second, _ = fsdp_neighbours(fsdp)
        return [(ctx, first), (ctx, second)]
    return [(ctx, (fsdp + j) % n_fsdp) for j in range(1, n_fsdp)]


def line_peers(chip, core, fsdp, length):
    return [
        (chip * 2 + 1 - core, fsdp),
        ((chip + 1) % length * 2 + core, fsdp),
        ((chip + length - 1) % length * 2 + core, fsdp),
    ]


def line_gather(own_ref, all_ref, sems, where):
    chip, core, fsdp, length = where
    right_sems, left_sems, core_sems = sems
    sibling = (chip * 2 + 1 - core, fsdp)
    right = ((chip + 1) % length * 2 + core, fsdp)
    left = ((chip + length - 1) % length * 2 + core, fsdp)

    def block(index):
        return all_ref.at[(index + length) % length * 2 + core]

    def pass_on(index, source):
        return send(source, block(index), core_sems, (index + length) % length, sibling)

    pass_on(chip, own_ref).start()
    for step in range(length - 1):
        for sign, peer, way in ((-1, right, right_sems), (1, left, left_sems)):
            at = chip + sign * step
            held = (at >= 0) & (at < length)
            if step > 0:

                @pl.when(held)
                def _():
                    send(block(at), block(at), way, step - 1, peer).wait_recv()
                    pass_on(at, block(at)).start()

            more = (chip < length - 1) if sign < 0 else (chip > 0)

            @pl.when(held & more)
            def _():
                send(own_ref if step == 0 else block(at), block(at), way, step, peer).start()

        yield
    last = length - 1
    for sign, peer, way in ((-1, right, right_sems), (1, left, left_sems)):
        at = chip + sign * last

        @pl.when((at >= 0) & (at < length))
        def _():
            send(block(at), block(at), way, last - 1, peer).wait_recv()
            pass_on(at, block(at)).start()

    yield
    for step in range(length - 1):
        for sign, peer, way in ((-1, right, right_sems), (1, left, left_sems)):
            at = chip + sign * step
            more = (chip < length - 1) if sign < 0 else (chip > 0)

            @pl.when((at >= 0) & (at < length) & more)
            def _():
                send(block(at), block(at), way, step, peer).wait_send()

    for index in range(length):
        pass_on(index, block(index)).wait_send()
        other = all_ref.at[index * 2 + 1 - core]
        send(other, other, core_sems, index, sibling).wait_recv()


def square_gather(own_ref, all_ref, sems, ctx, fsdp, n_fsdp, passed=None):
    if n_fsdp != 4:
        copies = [
            send(own_ref, all_ref.at[fsdp], sems, j - 1, (ctx, (fsdp + j) % n_fsdp)) for j in range(1, n_fsdp)
        ]
        for copy in copies:
            copy.start()
        yield
        for j, copy in enumerate(copies):
            copy.wait()
            if passed:
                passed(all_ref.at[(fsdp + n_fsdp - j - 1) % n_fsdp], (fsdp + n_fsdp - j - 1) % n_fsdp, None, j)
        return
    first, second, corner = fsdp_neighbours(fsdp)
    half = own_ref.shape[0] // 2
    top, low_half = pl.ds(0, half), pl.ds(half, half)
    to_first, to_second = (ctx, first), (ctx, second)

    def copy(index, owner, part, peer, source=None):
        source = all_ref.at[owner, part] if source is None else source
        return send(source, all_ref.at[owner, part], sems, index, peer)

    starts = [
        copy(0, fsdp, top, to_first, own_ref.at[top]),
        copy(1, fsdp, low_half, to_second, own_ref.at[low_half]),
        copy(2, fsdp, low_half, to_first, own_ref.at[low_half]),
        copy(3, fsdp, top, to_second, own_ref.at[top]),
        copy(4, first, top, to_second),
        copy(5, second, low_half, to_first),
    ]
    arrivals = [
        (0, first, top),
        (1, second, low_half),
        (2, first, low_half),
        (3, second, top),
        (4, corner, top),
        (5, corner, low_half),
    ]
    for each in starts[:4]:
        each.start()
    yield
    for index, owner, part in arrivals:
        copy(index, owner, part, to_first).wait_recv()
        if index < 2:
            starts[4 + index].start()
        if passed:
            passed(all_ref.at[owner, part], owner, part, index)
        yield
    for each in starts:
        each.wait_send()


def run_all(*parts):
    parts = list(parts)
    while parts:
        for part in list(parts):
            try:
                next(part)
            except StopIteration:
                parts.remove(part)


def dma_pair(count):
    return [pltpu.SemaphoreType.DMA((count,)), pltpu.SemaphoreType.DMA((count,))]


def any_specs(count):
    return [pl.BlockSpec(memory_space=pl.ANY)] * count


def params(collective_id=None, **more):
    if collective_id is not None:
        more.update(collective_id=collective_id, has_side_effects=True)
    return pltpu.CompilerParams(vmem_limit_bytes=VMEM_LIMIT, **more)


def passing(own_ref, all_ref, sems, core, fsdp, sibling):
    handed = [send(own_ref, all_ref.at[core, fsdp], sems, 0, sibling)]
    handed[0].start()
    arriving = [send(own_ref, all_ref.at[1 - core, fsdp], sems, 0, sibling)]

    def passed(source, owner, part, index):
        for side, copies in ((core, handed), (1 - core, arriving)):
            target = all_ref.at[side, owner] if part is None else all_ref.at[side, owner, part]
            copies.append(send(source, target, sems, index + 1, sibling))
        handed[-1].start()

    def finish():
        for out, back in zip(handed, arriving):
            out.wait_send()
            back.wait_recv()

    return (passed, finish)


def line_rows(n_ctx, rows):
    def kernel(rows_ref, all_rows, right_s, right_r, left_s, left_r, core_s, core_r, own):
        where = place(n_ctx)
        chip, core, fsdp, length = where
        greet(line_peers(*where))
        mine = pltpu.make_async_copy(rows_ref, all_rows.at[chip * 2 + core], own)
        mine.start()
        run_all(line_gather(rows_ref, all_rows, ((right_s, right_r), (left_s, left_r), (core_s, core_r)), where))
        mine.wait()

    length = n_ctx // 2
    return pl.pallas_call(
        kernel,
        out_shape=jax.ShapeDtypeStruct((n_ctx,) + rows.shape, rows.dtype),
        in_specs=any_specs(1),
        out_specs=pl.BlockSpec(memory_space=pl.ANY),
        scratch_shapes=dma_pair(length) + dma_pair(length) + dma_pair(length) + [pltpu.SemaphoreType.DMA],
        compiler_params=params(0),
        name="line_rows",
    )(rows)


def square_core_gather(n_ctx, n_fsdp, rows):
    def kernel(rows_ref, all_ref, sq_s, sq_r, core_s, core_r, own):
        chip, core, fsdp, _ = place(n_ctx)
        ctx = chip * 2 + core
        sibling = (chip * 2 + 1 - core, fsdp)
        greet([sibling] + fsdp_peers(n_fsdp, ctx, fsdp))
        mine = pltpu.make_async_copy(rows_ref, all_ref.at[core, fsdp], own)
        mine.start()
        passed, finish = passing(rows_ref, all_ref, (core_s, core_r), core, fsdp, sibling)
        run_all(square_gather(rows_ref, all_ref.at[core], (sq_s, sq_r), ctx, fsdp, n_fsdp, passed))
        finish()
        mine.wait()

    return pl.pallas_call(
        kernel,
        out_shape=jax.ShapeDtypeStruct((2, n_fsdp) + rows.shape, rows.dtype),
        in_specs=any_specs(1),
        out_specs=pl.BlockSpec(memory_space=pl.ANY),
        scratch_shapes=dma_pair(max(6, n_fsdp)) + dma_pair(max(7, n_fsdp)) + [pltpu.SemaphoreType.DMA],
        compiler_params=params(1),
        name="square_core_gather",
    )(rows)


def add_into(target, *sources, chunk=64):
    @pl.loop(0, target.shape[0] // chunk)
    def _(step):
        rows = pl.ds(pl.multiple_of(step * chunk, chunk), chunk)
        total = target[rows].astype(jnp.float32)
        for source in sources:
            total = total + source[rows].astype(jnp.float32)
        target[rows] = total.astype(target.dtype)


def square_sum_stages(n_ctx, n_fsdp, partial_ref, out_ref, held, core_in, square_in, load, core_sems, sems):
    rows = partial_ref.shape[-2]
    half = rows // 2
    chip, core, fsdp, _ = place(n_ctx)
    ctx = chip * 2 + core
    sibling = (chip * 2 + 1 - core, fsdp)
    if n_fsdp == 4:
        first, second, corner = fsdp_neighbours(fsdp)
        order = [corner, first, second, fsdp]
    else:
        order = [(fsdp + j) % n_fsdp for j in range(1, n_fsdp + 1)]
    mine = [
        pltpu.make_async_copy(partial_ref.at[core, owner], held.at[owner], load.at[j])
        for j, owner in enumerate(order)
    ]
    others = [
        send(partial_ref.at[1 - core, owner], core_in.at[owner], core_sems, j, sibling)
        for j, owner in enumerate(order)
    ]

    def ready(j):
        mine[j].wait()
        others[j].wait_recv()
        add_into(held.at[order[j]], core_in.at[order[j]])

    def total(parts, sources):
        @pl.loop(0, parts[1] // 64)
        def _(step):
            at = pl.ds(pl.multiple_of(parts[0] + step * 64, 64), 64)
            from_at = pl.ds(pl.multiple_of(step * 64, 64), 64)
            value = held[fsdp, at].astype(jnp.float32)
            for j in sources:
                value = value + square_in[j, from_at].astype(jnp.float32)
            out_ref[at] = value

    def begin():
        greet([sibling] + fsdp_peers(n_fsdp, ctx, fsdp))
        for j in range(n_fsdp):
            others[j].start()
            mine[j].start()

    if n_fsdp != 4:
        copies = [
            send(held.at[order[j]], square_in.at[j], sems, j, (ctx, order[j])) for j in range(n_fsdp - 1)
        ]

        def spread():
            for j in range(n_fsdp):
                ready(j)
                if j < n_fsdp - 1:
                    copies[j].start()

        def finish():
            for copy in copies:
                copy.wait()
            total((0, rows), range(n_fsdp - 1))
            for each in others:
                each.wait_send()

        return [begin, spread, finish]

    top, low_half = pl.ds(0, half), pl.ds(half, half)
    to_first, to_second = (ctx, first), (ctx, second)

    def copy(index, owner, part, peer):
        return send(held.at[owner, part], square_in.at[index], sems, index, peer)

    copies = [
        copy(0, corner, top, to_first),
        copy(1, corner, low_half, to_second),
        copy(2, first, top, to_first),
        copy(3, second, low_half, to_second),
        copy(4, second, top, to_second),
        copy(5, first, low_half, to_first),
    ]

    def spread():
        ready(0)
        copies[0].start()
        copies[1].start()
        ready(1)
        copies[2].start()
        ready(2)
        copies[3].start()
        ready(3)

    def pass_on():
        copies[0].wait_recv()
        add_into(held.at[second, top], square_in.at[0])
        copies[4].start()
        copies[1].wait_recv()
        add_into(held.at[first, low_half], square_in.at[1])
        copies[5].start()

    def finish():
        for j in range(2, 6):
            copies[j].wait_recv()
        total((0, half), (2, 4))
        total((half, half), (3, 5))
        for each in copies:
            each.wait_send()
        for each in others:
            each.wait_send()

    return [begin, spread, pass_on, finish]


def corner_sum_stages(n_ctx, partial_ref, out_ref, held, square_in, load, sems):
    half = partial_ref.shape[1] // 2
    chip, core, fsdp, _ = place(n_ctx)
    ctx = chip * 2 + core
    first, second, corner = fsdp_neighbours(fsdp)
    top, low_half = pl.ds(0, half), pl.ds(half, half)
    to_first, to_second = (ctx, first), (ctx, second)

    def copy(index, source, peer):
        return send(source, square_in.at[index], sems, index, peer)

    copies = [
        copy(0, partial_ref.at[corner, top], to_first),
        copy(1, partial_ref.at[corner, low_half], to_second),
        copy(2, partial_ref.at[first, top], to_first),
        copy(3, partial_ref.at[second, low_half], to_second),
        copy(4, held.at[0], to_second),
        copy(5, held.at[1], to_first),
    ]
    mine = [
        pltpu.make_async_copy(partial_ref.at[second, top], held.at[0], load.at[0]),
        pltpu.make_async_copy(partial_ref.at[first, low_half], held.at[1], load.at[1]),
        pltpu.make_async_copy(partial_ref.at[fsdp, top], held.at[2], load.at[2]),
        pltpu.make_async_copy(partial_ref.at[fsdp, low_half], held.at[3], load.at[3]),
    ]

    def begin():
        greet(fsdp_peers(4, ctx, fsdp))
        for each in copies[:4]:
            each.start()
        for each in mine:
            each.start()

    def pass_on():
        for index in range(2):
            mine[index].wait()
            copies[index].wait_recv()
            add_into(held.at[index], square_in.at[index])
            copies[4 + index].start()

    def finish():
        for part, sources in ((0, (2, 4)), (1, (3, 5))):
            mine[2 + part].wait()
            for j in sources:
                copies[j].wait_recv()

            @pl.loop(0, half // 64)
            def _(step):
                at = pl.ds(pl.multiple_of(step * 64, 64), 64)
                value = held[2 + part, at].astype(jnp.float32)
                for j in sources:
                    value = value + square_in[j, at].astype(jnp.float32)
                out_ref[pl.ds(pl.multiple_of(part * half + step * 64, 64), 64)] = value

        for each in copies:
            each.wait_send()

    return [begin, pass_on, finish]


def corner_sum_scratch(partial):
    _, rows, columns = partial.shape
    return [
        pltpu.VMEM((4, rows // 2, columns), partial.dtype),
        pltpu.VMEM((6, rows // 2, columns), partial.dtype),
        pltpu.SemaphoreType.DMA((4,)),
    ] + dma_pair(6)


def square_sum_scratch(n_fsdp, partial):
    rows, columns = partial.shape[-2:]
    pieces = (6, rows // 2, columns) if n_fsdp == 4 else (n_fsdp - 1, rows, columns)
    return (
        [
            pltpu.VMEM((n_fsdp, rows, columns), partial.dtype),
            pltpu.VMEM((n_fsdp, rows, columns), partial.dtype),
            pltpu.VMEM(pieces, partial.dtype),
            pltpu.SemaphoreType.DMA((n_fsdp,)),
        ]
        + dma_pair(n_fsdp)
        + dma_pair(max(6, n_fsdp))
    )


def square_sum(n_ctx, n_fsdp, partial):
    def kernel(partial_ref, out_ref, held, core_in, square_in, load, core_s, core_r, sq_s, sq_r):
        for stage in square_sum_stages(
            n_ctx, n_fsdp, partial_ref, out_ref, held, core_in, square_in, load, (core_s, core_r), (sq_s, sq_r)
        ):
            stage()

    return pl.pallas_call(
        kernel,
        out_shape=jax.ShapeDtypeStruct(partial.shape[-2:], jnp.float32),
        in_specs=any_specs(1),
        out_specs=pl.BlockSpec(memory_space=pltpu.VMEM),
        scratch_shapes=square_sum_scratch(n_fsdp, partial),
        compiler_params=params(1),
        name="square_sum",
    )(partial)


def line_sum(n_ctx, partial, collective_id):
    rows, columns = partial.shape[-2:]
    length = n_ctx // 2

    def kernel(partial_ref, out_ref, held, core_in, right_in, left_in, load, core_s, core_r, right_s, right_r, left_s, left_r):
        where = place(n_ctx)
        chip, core, fsdp, _ = where
        sibling, right, left = line_peers(*where)
        greet([sibling, right, left])
        order = [(chip + length - 1 - j) % length for j in range(length)]
        mine, others = [], []
        for j, owner in enumerate(order):
            mine.append(pltpu.make_async_copy(partial_ref.at[owner * 2 + core], held.at[owner], load.at[j]))
            others.append(
                send(partial_ref.at[owner * 2 + 1 - core], core_in.at[owner], (core_s, core_r), j, sibling)
            )
            others[-1].start()
            mine[-1].start()
        for j, owner in enumerate(order):
            mine[j].wait()
            others[j].wait_recv()
            add_into(held.at[owner], core_in.at[owner])
        ways = ((1, right, right_in, (right_s, right_r)), (-1, left, left_in, (left_s, left_r)))
        for step in range(length - 1):
            for sign, peer, arrived, sems in ways:
                block = chip + sign * (length - 1 - step)
                inside = (block >= 0) & (block < length)

                came = (chip >= 1) if sign > 0 else (chip < length - 1)
                if step > 0:

                    @pl.when(inside & came)
                    def _():
                        send(held.at[block], arrived.at[step - 1], sems, step - 1, peer).wait_recv()
                        add_into(held.at[block], arrived.at[step - 1])

                @pl.when(inside)
                def _():
                    send(held.at[block], arrived.at[step], sems, step, peer).start()

        last = length - 2
        for sign, peer, arrived, sems in ways:
            came = (chip >= 1) if sign > 0 else (chip < length - 1)

            @pl.when(came)
            def _():
                send(held.at[chip], arrived.at[last], sems, last, peer).wait_recv()
                add_into(held.at[chip], arrived.at[last])

        @pl.loop(0, rows // 64)
        def _(step):
            at = pl.ds(pl.multiple_of(step * 64, 64), 64)
            out_ref[at] = held[chip, at].astype(jnp.float32)

        for step in range(length - 1):
            for sign, peer, arrived, sems in ways:
                block = chip + sign * (length - 1 - step)

                @pl.when((block >= 0) & (block < length))
                def _():
                    send(held.at[block], arrived.at[step], sems, step, peer).wait_send()

        for each in others:
            each.wait_send()

    return pl.pallas_call(
        kernel,
        out_shape=jax.ShapeDtypeStruct((rows, columns), jnp.float32),
        in_specs=any_specs(1),
        out_specs=pl.BlockSpec(memory_space=pltpu.VMEM),
        scratch_shapes=[
            pltpu.VMEM((length, rows, columns), partial.dtype),
            pltpu.VMEM((length, rows, columns), partial.dtype),
            pltpu.VMEM((length - 1, rows, columns), partial.dtype),
            pltpu.VMEM((length - 1, rows, columns), partial.dtype),
            pltpu.SemaphoreType.DMA((length,)),
        ]
        + dma_pair(length)
        + dma_pair(length)
        + dma_pair(length),
        compiler_params=params(collective_id),
        name="line_sum",
    )(partial)


def sum_everywhere(n_ctx, n_fsdp, values):
    block = values.shape[1:]

    def kernel(values_ref, out_ref, along_ctx, along_fsdp, result, ctx_s, ctx_r, fsdp_s, fsdp_r, back_s, back_r):
        ctx = lax.axis_index("ctx")
        fsdp = lax.axis_index("fsdp")
        ctx_peers = [((ctx + j) % n_ctx, fsdp) for j in range(1, n_ctx)]
        fsdp_peers = [(ctx, (fsdp + j) % n_fsdp) for j in range(1, n_fsdp)]
        greet(ctx_peers + fsdp_peers)

        def exchange(copies):
            for copy in copies:
                copy.start()
            for copy in copies:
                copy.wait()

        def total(slots, count):
            value = slots[0]
            for j in range(1, count):
                value = value + slots[j]
            return value

        along_ctx[ctx] = values_ref[ctx]
        exchange(
            [
                send(values_ref.at[peer[0]], along_ctx.at[ctx], (ctx_s, ctx_r), j, peer)
                for j, peer in enumerate(ctx_peers)
            ]
        )
        along_fsdp[fsdp] = total(along_ctx, n_ctx)
        exchange(
            [
                send(along_fsdp.at[fsdp], along_fsdp.at[fsdp], (fsdp_s, fsdp_r), j, peer)
                for j, peer in enumerate(fsdp_peers)
            ]
        )
        result[ctx] = total(along_fsdp, n_fsdp)
        exchange(
            [send(result.at[ctx], result.at[ctx], (back_s, back_r), j, peer) for j, peer in enumerate(ctx_peers)]
        )
        out_ref[...] = result[...]

    return pl.pallas_call(
        kernel,
        out_shape=jax.ShapeDtypeStruct(values.shape, values.dtype),
        in_specs=[pl.BlockSpec(memory_space=pltpu.VMEM)],
        out_specs=pl.BlockSpec(memory_space=pltpu.VMEM),
        scratch_shapes=[
            pltpu.VMEM((n_ctx,) + block, values.dtype),
            pltpu.VMEM((n_fsdp,) + block, values.dtype),
            pltpu.VMEM((n_ctx,) + block, values.dtype),
        ]
        + dma_pair(n_ctx)
        + dma_pair(n_fsdp)
        + dma_pair(n_ctx),
        compiler_params=params(2),
        name="sum_everywhere",
    )(values)


def hidden_units(here, back, gate_ref, up_ref, down_ref):
    gate = mm(here, gate_ref[0], CONTRACT_LAST)
    up = mm(here, up_ref[0], CONTRACT_LAST)
    grad_hidden = mm(back, down_ref[0], CONTRACT_LAST)
    sigmoid = jax.nn.sigmoid(gate)
    activated = gate * sigmoid
    return (
        low(activated * up),
        low(grad_hidden * up * sigmoid * (1.0 + gate * (1.0 - sigmoid))),
        low(grad_hidden * activated),
    )


def ffn_forward(rows, planes, core, n_own, chunk=256):
    blocks, _, tokens, features = rows.shape
    total = blocks * tokens
    steps = n_own // chunk
    group = max(1, 256 // tokens)

    def kernel(core_ref, rows_ref, gate_ref, up_ref, down_ref, *outs):
        for at in range(0, blocks, group):
            here = rows_ref[at : at + group, 0].reshape(group * tokens, features)
            back = rows_ref[at : at + group, 1].reshape(group * tokens, features)
            span = pl.ds(at * tokens, group * tokens)
            for out, value in zip(outs, hidden_units(here, back, gate_ref, up_ref, down_ref)):
                out[span] = value

    def weight_spec(plane):
        return pl.BlockSpec((1, chunk, features), lambda j, core_ref: (plane, core_ref[0] * steps + j, 0))

    act = jax.ShapeDtypeStruct((total, n_own), jnp.bfloat16)
    act_spec = pl.BlockSpec((total, chunk), lambda j, core_ref: (0, j))
    return pl.pallas_call(
        kernel,
        grid_spec=pltpu.PrefetchScalarGridSpec(
            num_scalar_prefetch=1,
            grid=(steps,),
            in_specs=[
                pl.BlockSpec(rows.shape, lambda j, core_ref: (0, 0, 0, 0), pipeline_mode=pl.Buffered(1)),
                weight_spec(0),
                weight_spec(1),
                weight_spec(2),
            ],
            out_specs=[act_spec, act_spec, act_spec],
        ),
        out_shape=[act, act, act],
        compiler_params=params(),
        cost_estimate=pl.CostEstimate(
            flops=6 * total * n_own * features, bytes_accessed=30 * 1024 * 1024, transcendentals=total * n_own
        ),
        name="ffn_forward",
    )(core, rows, planes, planes, planes)


def mirror_gather(all_ref, arrivals, sems, pass_sems, ctx, core, fsdp, sibling):
    first, second, corner = fsdp_neighbours(fsdp)
    half = all_ref.shape[2] // 2
    parts = [pl.ds(0, half), pl.ds(half, half)]
    to_first, to_second = (ctx, first), (ctx, second)

    def copy(index, owner, part, peer):
        place_ref = all_ref.at[core, owner, parts[part]]
        return send(place_ref, place_ref, sems, index, peer)

    copies = [
        copy(0, fsdp, 0, to_first),
        copy(1, fsdp, 0, to_second),
        copy(2, fsdp, 1, to_first),
        copy(3, fsdp, 1, to_second),
        copy(4, first, 0, to_second),
        copy(5, second, 1, to_first),
    ]
    passes = [(fsdp, 0), (fsdp, 1), (first, 0), (second, 0), (first, 1), (second, 1), (corner, 0), (corner, 1)]

    def passing_copy(number, side):
        owner, part = passes[number]
        place_ref = all_ref.at[side, owner, parts[part]]
        return send(place_ref, place_ref, pass_sems, number, sibling)

    for part in range(2):
        arrivals[part].wait_recv()
        copies[2 * part].start()
        copies[2 * part + 1].start()
        passing_copy(part, core).start()
        yield
    for index, number, then in ((0, 2, 4), (1, 3, None), (2, 4, None), (3, 5, 5), (4, 6, None), (5, 7, None)):
        owner, part = passes[number]
        copy(index, owner, part, to_first).wait_recv()
        if then is not None:
            copies[then].start()
        passing_copy(number, core).start()
        yield
    for each in copies:
        each.wait_send()
    for number in range(8):
        passing_copy(number, core).wait_send()
        passing_copy(number, 1 - core).wait_recv()


def ffn_rows(n_ctx, own, planes, n_own, chunk=256, wide=512):
    n_fsdp = 4
    size, features = own.shape
    tokens = size // 2
    total = 2 * n_fsdp * tokens

    def kernel(
        own_ref, planes_ref, all_ref, mirror_ref, hidden_a, hidden_b, hidden_c, partial_ref,
        rows, weights, hidden, partial, core_in, load, sq_s, sq_r, core_s, core_r, far_s, far_r, mi_s, mi_r, mc_s, mc_r, sum_s, sum_r, out_sem,
    ):
        chip, core, fsdp, length = place(n_ctx)
        ctx = chip * 2 + core
        sibling = (chip * 2 + 1 - core, fsdp)
        mirror = ((length - 1 - chip) * 2 + core, fsdp)
        first, second, corner = fsdp_neighbours(fsdp)
        greet([sibling, mirror] + fsdp_peers(n_fsdp, ctx, fsdp))
        mine = pltpu.make_async_copy(own_ref, rows.at[core, fsdp], load.at[3])
        mine.start()
        start = pl.multiple_of(core * n_own, n_own)
        loads = [
            pltpu.make_async_copy(planes_ref.at[p, pl.ds(start, n_own)], weights.at[p], load.at[p]) for p in range(3)
        ]
        handed, arriving = [], []

        def hand(source, owner, part, index):
            for side, copies in ((core, handed), (1 - core, arriving)):
                target = rows.at[side, owner] if part is None else rows.at[side, owner, part]
                copies.append(send(source, target, (core_s, core_r), index + 1, sibling))
            handed[-1].start()

        gathering = square_gather(own_ref, rows.at[core], (sq_s, sq_r), ctx, fsdp, n_fsdp, hand)
        next(gathering)
        hand(own_ref, fsdp, None, -1)
        for each in loads:
            each.start()
        far = [
            send(
                own_ref.at[pl.ds(part * tokens, tokens)],
                mirror_ref.at[core, fsdp, pl.ds(part * tokens, tokens)],
                (far_s, far_r),
                part,
                mirror,
            )
            for part in range(2)
        ]
        for each in far:
            each.start()
        mirroring = mirror_gather(mirror_ref, far, (mi_s, mi_r), (mc_s, mc_r), ctx, core, fsdp, sibling)
        outs, summing, sums = [], [], []

        def add_up(number, owner):
            summing[number].wait_recv()
            add_into(partial.at[number % 2, core], core_in.at[number])
            sums.append(
                pltpu.make_async_copy(partial.at[number % 2, core], partial_ref.at[owner], out_sem.at[number % 2, 8])
            )
            sums[-1].start()

        def group(number, owner):
            slot = number % 2
            if number >= 2:
                for each in outs[number - 2]:
                    each.wait()
                summing[number - 2].wait_send()
                sums[number - 2].wait()
            here = jnp.concatenate([rows[0, owner, :tokens], rows[1, owner, :tokens]])
            back = jnp.concatenate([rows[0, owner, tokens:], rows[1, owner, tokens:]])

            @pl.loop(0, n_own // chunk)
            def _(step):
                at = pl.ds(pl.multiple_of(step * chunk, chunk), chunk)
                parts = [weights.at[pl.ds(p, 1), at] for p in range(3)]
                for q, value in enumerate(hidden_units(here, back, *parts)):
                    hidden[slot, q, :, at] = value

            @pl.loop(0, features // wide)
            def _(step):
                at = pl.ds(pl.multiple_of(step * wide, wide), wide)
                out = low(mm(hidden[slot, 0], weights[2, :, at]))
                below = low(mm(hidden[slot, 1], weights[0, :, at]) + mm(hidden[slot, 2], weights[1, :, at]))
                for k in range(2):
                    partial[slot, k, :tokens, at] = out[k * tokens : (k + 1) * tokens]
                    partial[slot, k, tokens:, at] = below[k * tokens : (k + 1) * tokens]

            pairs = []
            summing.append(send(partial.at[slot, 1 - core], core_in.at[number], (sum_s, sum_r), number, sibling))
            summing[-1].start()
            for k in range(2):
                pairs.append((rows.at[k, owner], all_ref.at[k, owner]))
                at = pl.ds(pl.multiple_of((k * n_fsdp + owner) * tokens, tokens), tokens)
                for q, target in enumerate((hidden_a, hidden_b, hidden_c)):
                    pairs.append((hidden.at[slot, q, pl.ds(k * tokens, tokens)], target.at[at]))
            outs.append(
                [pltpu.make_async_copy(a, b, out_sem.at[slot, j]) for j, (a, b) in enumerate(pairs)]
            )
            for each in outs[-1]:
                each.start()

        mine.wait()
        arriving[0].wait_recv()
        for each in loads:
            each.wait()
        group(0, fsdp)
        for _ in range(4):
            next(gathering)
        arriving[1].wait_recv()
        arriving[3].wait_recv()
        group(1, first)
        add_up(0, fsdp)
        next(mirroring)
        for _ in range(2):
            next(gathering)
        arriving[2].wait_recv()
        arriving[4].wait_recv()
        group(2, second)
        add_up(1, first)
        for _ in range(3):
            next(mirroring)
        arriving[5].wait_recv()
        arriving[6].wait_recv()
        group(3, corner)
        add_up(2, second)
        next(mirroring)
        add_up(3, corner)
        run_all(mirroring, gathering)
        for each in handed:
            each.wait_send()
        for each in far:
            each.wait_send()
        for each in outs[2] + outs[3] + sums[2:]:
            each.wait()
        for each in summing[2:]:
            each.wait_send()

    act = jax.ShapeDtypeStruct((total, n_own), own.dtype)
    all_rows = jax.ShapeDtypeStruct((2, n_fsdp) + own.shape, own.dtype)
    return pl.pallas_call(
        kernel,
        in_specs=any_specs(2),
        out_specs=any_specs(6),
        out_shape=[all_rows, all_rows, act, act, act, jax.ShapeDtypeStruct((n_fsdp,) + own.shape, own.dtype)],
        scratch_shapes=[
            pltpu.VMEM((2, n_fsdp) + own.shape, own.dtype),
            pltpu.VMEM((3, n_own, features), own.dtype),
            pltpu.VMEM((2, 3, 2 * tokens, n_own), own.dtype),
            pltpu.VMEM((2, 2) + own.shape, own.dtype),
            pltpu.VMEM((n_fsdp,) + own.shape, own.dtype),
            pltpu.SemaphoreType.DMA((4,)),
        ]
        + dma_pair(6)
        + dma_pair(7)
        + dma_pair(2)
        + dma_pair(6)
        + dma_pair(8)
        + dma_pair(4)
        + [pltpu.SemaphoreType.DMA((2, 9))],
        compiler_params=params(6),
        cost_estimate=pl.CostEstimate(
            flops=12 * total * n_own * features, bytes_accessed=50 * 1024 * 1024, transcendentals=total * n_own
        ),
        name="ffn_rows",
    )(own, planes)


def ffn_weights(n_ctx, n_fsdp, partial, rows, rows_mirror, hidden, planes, n_own, chunk=256):
    blocks, _, tokens, features = rows.shape
    total = blocks * tokens
    steps = n_own // chunk
    group = max(1, 256 // tokens)
    half = features // 2
    sides = n_ctx // 4
    wide = half // sides
    fused = partial is not None

    def kernel(*refs):
        rows_ref, refs = refs[0], refs[1:]
        mirror_refs, refs = refs[: len(rows_mirror)], refs[len(rows_mirror) :]
        mirror_blocks = [ref.at[b] for ref in mirror_refs for b in range(ref.shape[0])]
        hidden_ref, grad_gate_ref, grad_up_ref, planes_ref, *refs = refs
        if fused:
            partial_ref, weight_ref, out_ref, *refs = refs
        else:
            weight_ref, *refs = refs
        mirror, (weights, weight_sems), refs = refs[:3], refs[3:5], refs[5:]
        chip, core, _, length = place(n_ctx)
        side = chip // sides
        step = pl.program_id(0)
        stages = [lambda: None]
        if fused:
            held, square_in, load, sq_s, sq_r = refs
            stages = corner_sum_stages(n_ctx, partial_ref, out_ref, held, square_in, load, (sq_s, sq_r))

        def fetch(at, slot):
            start = pl.multiple_of((core * steps + at) * chunk, chunk)
            return pltpu.make_async_copy(planes_ref.at[:, pl.ds(start, chunk)], weights.at[slot], weight_sems.at[slot])

        @pl.when(step == 0)
        def _():
            fetch(0, 0).start()
            stages[0]()

        @pl.when(step + 1 < steps)
        def _():
            fetch(step + 1, (step + 1) % 2).start()

        slot = step % 2
        fetch(step, slot).wait()
        gate_ref, up_ref, down_ref = (weights.at[slot, pl.ds(plane, 1)] for plane in range(3))
        for at in range(0, blocks, group):
            here = jnp.concatenate([ref[0] for ref in mirror_blocks[at : at + group]])
            back = jnp.concatenate([ref[1] for ref in mirror_blocks[at : at + group]])
            span = pl.ds(at * tokens, group * tokens)
            for out, value in zip(mirror, hidden_units(here, back, gate_ref, up_ref, down_ref)):
                out[span] = value

        lefts = ((grad_gate_ref, mirror[1], 0), (grad_up_ref, mirror[2], 0), (hidden_ref, mirror[0], 1))
        for plane, (left, left_mirror, which) in enumerate(lefts):
            left = left[...]
            left_mirror = left_mirror[...]
            for z in range(sides):
                cols = pl.ds(pl.multiple_of(side * half + z * wide, wide), wide)
                right = rows_ref[:, which, :, cols].reshape(total, wide)
                right_mirror = jnp.concatenate([ref[which, :, cols] for ref in mirror_blocks])
                weight_ref[z, plane] = low(
                    mm(left, right, CONTRACT_FIRST) + mm(left_mirror, right_mirror, CONTRACT_FIRST)
                )

        for at, stage in ((1, 1), (steps - 1, 2)):
            if stage < len(stages):

                @pl.when(step == min(at, steps - 1))
                def _():
                    stages[stage]()

    act_spec = pl.BlockSpec((total, chunk), lambda j: (0, j))
    once = dict(pipeline_mode=pl.Buffered(1))
    operands = [rows, *rows_mirror, *hidden, planes]
    in_specs = [whole_block(rows.shape, **once)] + [whole_block(part.shape, **once) for part in rows_mirror]
    in_specs += [act_spec] * 3 + any_specs(1)
    out_specs = [pl.BlockSpec((sides, 3, chunk, wide), lambda j: (0, 0, j, 0))]
    out_shape = [jax.ShapeDtypeStruct((sides, 3, n_own, wide), jnp.bfloat16)]
    scratch = [pltpu.VMEM((total, chunk), jnp.bfloat16)] * 3
    scratch += [pltpu.VMEM((2, 3, chunk, features), jnp.bfloat16), pltpu.SemaphoreType.DMA((2,))]
    if fused:
        operands.append(partial)
        in_specs += any_specs(1)
        out_specs.append(whole_block(partial.shape[-2:], **once))
        out_shape.append(jax.ShapeDtypeStruct(partial.shape[-2:], jnp.float32))
        scratch += corner_sum_scratch(partial)
    return pl.pallas_call(
        kernel,
        grid=(steps,),
        in_specs=in_specs,
        out_specs=out_specs,
        out_shape=out_shape,
        scratch_shapes=scratch,
        compiler_params=params(3) if fused else params(),
        cost_estimate=pl.CostEstimate(
            flops=12 * total * n_own * features, bytes_accessed=50 * 1024 * 1024, transcendentals=total * n_own
        ),
        name="ffn_weights",
    )(*operands)


def ffn_back(hidden, grad_gate, grad_up, planes, core, blocks, wide=512):
    total, n_own = hidden.shape
    features = planes.shape[2]
    tokens = total // blocks

    def kernel(core_ref, hidden_ref, grad_gate_ref, grad_up_ref, gate_ref, up_ref, down_ref, out_ref):
        out = mm(hidden_ref[...], down_ref[0])
        out_ref[:, 0] = low(out).reshape(blocks, tokens, wide)
        back = mm(grad_gate_ref[...], gate_ref[0]) + mm(grad_up_ref[...], up_ref[0])
        out_ref[:, 1] = low(back).reshape(blocks, tokens, wide)

    def weight_spec(plane):
        return pl.BlockSpec((1, n_own, wide), lambda j, core_ref: (plane, core_ref[0], j))

    act_spec = pl.BlockSpec((total, n_own), lambda j, core_ref: (0, 0), pipeline_mode=pl.Buffered(1))
    return pl.pallas_call(
        kernel,
        grid_spec=pltpu.PrefetchScalarGridSpec(
            num_scalar_prefetch=1,
            grid=(features // wide,),
            in_specs=[act_spec, act_spec, act_spec, weight_spec(0), weight_spec(1), weight_spec(2)],
            out_specs=pl.BlockSpec((blocks, 2, tokens, wide), lambda j, core_ref: (0, 0, 0, j)),
        ),
        out_shape=jax.ShapeDtypeStruct((blocks, 2, tokens, features), jnp.bfloat16),
        compiler_params=params(),
        cost_estimate=pl.CostEstimate(
            flops=6 * total * n_own * features, bytes_accessed=30 * 1024 * 1024, transcendentals=0
        ),
        name="ffn_back",
    )(core, hidden, grad_gate, grad_up, planes, planes, planes)


SPAN = 256


def ctx_peers(n_ctx):
    ctx = lax.axis_index("ctx")
    fsdp = lax.axis_index("fsdp")
    return [((ctx + j) % n_ctx, fsdp) for j in range(1, n_ctx)]


def deal(n_ctx, block, target, landed, sems, own_sem):
    ctx = lax.axis_index("ctx")
    fsdp = lax.axis_index("fsdp")

    @pl.when(target != ctx)
    def _():
        send(block, landed.at[ctx], sems, (target - ctx + n_ctx) % n_ctx, (target, fsdp)).start()

    @pl.when(target == ctx)
    def _():
        pltpu.make_async_copy(block, landed.at[ctx], own_sem).start()


def dealt(n_ctx, block, landed, sems, own_sem):
    ctx = lax.axis_index("ctx")
    pltpu.make_async_copy(block, landed.at[ctx], own_sem).wait()
    for j, peer in enumerate(ctx_peers(n_ctx)):
        copy = send(block, landed.at[(ctx + n_ctx - j - 1) % n_ctx], sems, j + 1, peer)
        copy.wait_send()
        copy.wait_recv()


def turn(values, cosine, sine):
    return values * cosine + pltpu.roll(values, HEAD_DIM // 2, 1) * sine


def attention_forward(n_ctx, rows, w_qkv, cosine, sine, place_column, place_row, heads):
    total, features = rows.shape
    own = heads * HEAD_DIM
    steps = total // SPAN
    length = total // n_ctx
    scale = HEAD_DIM ** (-0.5)

    def kernel(
        rows_ref, w_ref, cosine_ref, sine_ref, column_ref, row_ref,
        query_ref, key_ref, value_ref, out_ref, log_ref, landed, deal_s, deal_r, own_sem,
    ):
        step = pl.program_id(0)

        @pl.when(step == 0)
        def _():
            greet(ctx_peers(n_ctx))

        span = pl.ds(pl.multiple_of(step * SPAN, SPAN), SPAN)
        qkv = mm(rows_ref[...], w_ref[...])
        cosine = cosine_ref[span]
        sine = sine_ref[span]
        for h in range(heads):
            at = slice(h * HEAD_DIM, (h + 1) * HEAD_DIM)
            query_ref[span, at] = low(turn(qkv[:, at], cosine, sine))
            key_ref[span, at] = low(turn(qkv[:, own + h * HEAD_DIM : own + (h + 1) * HEAD_DIM], cosine, sine))
        value_ref[span] = low(qkv[:, 2 * own :])

        @pl.when(step == steps - 1)
        def _():
            @pl.loop(0, steps)
            def _(block):
                here = pl.ds(pl.multiple_of(block * SPAN, SPAN), SPAN)
                for h in range(heads):
                    at = slice(h * HEAD_DIM, (h + 1) * HEAD_DIM)
                    scores = mm(query_ref[here, at], key_ref[:, at], CONTRACT_LAST) * scale
                    scores = jnp.where(column_ref[here] >= row_ref[...], scores, MASKED)
                    highest = jnp.max(scores, axis=-1, keepdims=True)
                    exponent = jnp.exp(scores - highest)
                    sums = jnp.sum(exponent, axis=-1, keepdims=True)
                    out_ref[here, at] = low(mm(low(exponent * (1.0 / sums)), value_ref[:, at]))
                    log_ref[h, here] = highest + jnp.log(sums)
                for r in range(SPAN // length):
                    mine = out_ref.at[pl.ds(pl.multiple_of(block * SPAN + r * length, length), length)]
                    deal(n_ctx, mine, block * (SPAN // length) + r, landed, (deal_s, deal_r), own_sem)

            dealt(n_ctx, out_ref.at[pl.ds(0, length)], landed, (deal_s, deal_r), own_sem)

    act = jax.ShapeDtypeStruct((total, own), jnp.bfloat16)
    return pl.pallas_call(
        kernel,
        grid=(steps,),
        in_specs=[pl.BlockSpec((SPAN, features), lambda r: (r, 0))]
        + [whole_block(a.shape) for a in (w_qkv, cosine, sine, place_column, place_row)],
        out_specs=[whole_block((total, own))] * 4 + [whole_block((heads, total, 1))] + any_specs(1),
        out_shape=[act] * 4
        + [
            jax.ShapeDtypeStruct((heads, total, 1), jnp.float32),
            jax.ShapeDtypeStruct((n_ctx, length, own), jnp.bfloat16),
        ],
        scratch_shapes=dma_pair(n_ctx) + [pltpu.SemaphoreType.DMA],
        compiler_params=params(8),
        name="attention_forward",
    )(rows, w_qkv, cosine, sine, place_column, place_row)


def attention_backward(query, key, value, grad, logs, w_qkv, cosine, sine, place_column, place_row, heads):
    total, own = query.shape
    features = w_qkv.shape[0]
    steps = total // SPAN
    scale = HEAD_DIM ** (-0.5)

    def kernel(
        query_ref, key_ref, value_ref, grad_ref, log_ref, w_ref, cosine_ref, sine_ref, column_ref, row_ref,
        qkv_ref, out_ref, key_sum, value_sum,
    ):
        step = pl.program_id(0)

        @pl.when(step == 0)
        def _():
            for h in range(heads):
                at = slice(h * HEAD_DIM, (h + 1) * HEAD_DIM)
                key_sum[...] = jnp.zeros_like(key_sum)
                value_sum[...] = jnp.zeros_like(value_sum)

                @pl.loop(0, steps)
                def _(block):
                    here = pl.ds(pl.multiple_of(block * SPAN, SPAN), SPAN)
                    queries = query_ref[here, at]
                    grads = grad_ref[here, at]
                    scores = mm(queries, key_ref[:, at], CONTRACT_LAST) * scale
                    scores = jnp.where(column_ref[here] >= row_ref[...], scores, MASKED)
                    probs = jnp.exp(scores - log_ref[h, here])
                    probs_grad = mm(grads, value_ref[:, at], CONTRACT_LAST)
                    centre = jnp.sum(probs * probs_grad, axis=-1, keepdims=True)
                    scores_grad = low(probs * (probs_grad - centre))
                    query_grad = mm(scores_grad, key_ref[:, at]) * scale
                    qkv_ref[here, at] = low(turn(query_grad, cosine_ref[here], -sine_ref[here]))
                    key_sum[...] += mm(scores_grad, queries, CONTRACT_FIRST)
                    value_sum[...] += mm(low(probs), grads, CONTRACT_FIRST)

                qkv_ref[:, own + h * HEAD_DIM : own + (h + 1) * HEAD_DIM] = low(
                    turn(key_sum[...] * scale, cosine_ref[...], -sine_ref[...])
                )
                qkv_ref[:, 2 * own + h * HEAD_DIM : 2 * own + (h + 1) * HEAD_DIM] = low(value_sum[...])

        span = pl.ds(pl.multiple_of(step * SPAN, SPAN), SPAN)
        out_ref[...] = low(mm(qkv_ref[span], w_ref[...], CONTRACT_LAST))

    return pl.pallas_call(
        kernel,
        grid=(steps,),
        in_specs=[
            whole_block(a.shape)
            for a in (query, key, value, grad, logs, w_qkv, cosine, sine, place_column, place_row)
        ],
        out_specs=[whole_block((total, 3 * own)), pl.BlockSpec((SPAN, features), lambda r: (r, 0))],
        out_shape=[
            jax.ShapeDtypeStruct((total, 3 * own), jnp.bfloat16),
            jax.ShapeDtypeStruct((total, features), jnp.bfloat16),
        ],
        scratch_shapes=[pltpu.VMEM((total, HEAD_DIM), jnp.float32)] * 2,
        compiler_params=params(),
        name="attention_backward",
    )(query, key, value, grad, logs, w_qkv, cosine, sine, place_column, place_row)


ROWS = 32


def row_blocks(count, features):
    return pl.BlockSpec((count, ROWS, features), lambda r, *_: (0, r, 0))


def whole_block(shape, **more):
    zeros = (0,) * len(shape)
    return pl.BlockSpec(shape, lambda r, *_: zeros, **more)


def connect_coefficients(values, dynamic_ref, static_ref, coef_ref, dyn_ref):
    lane = lax.broadcasted_iota(jnp.int32, (values[0].shape[0], 8), 1)
    columns = []
    for i, value in enumerate(values):
        mean = jnp.mean(value, axis=-1, keepdims=True)
        centered = value - mean
        inverse = lax.rsqrt(jnp.mean(centered * centered, axis=-1, keepdims=True) + EPS)
        normed = centered * inverse
        projected = 0.0
        for k in range(6):
            part = jnp.sum(normed * dynamic_ref[k : k + 1], axis=-1, keepdims=True)
            projected = jnp.where(lane == k, part, projected)
        dynamic_part = jnp.tanh(projected)
        coefficient = dynamic_part + static_ref[i : i + 1]
        dyn_ref[i] = dynamic_part
        coef_ref[i] = jnp.where(lane == 6, mean, jnp.where(lane == 7, inverse, coefficient))
        columns.append(coefficient)
    return columns


def connect_first(streams, dynamic, static):
    number, rows, features = streams.shape

    def kernel(streams_ref, dynamic_ref, static_ref, coef_ref, dyn_ref, low_ref):
        values = [streams_ref[i].astype(jnp.float32) for i in range(number)]
        columns = connect_coefficients(values, dynamic_ref, static_ref, coef_ref, dyn_ref)
        mixed = sum((columns[i][:, 1:2] * values[i] for i in range(number)))
        low_ref[...] = low(normalize(mixed)[0])

    small = jax.ShapeDtypeStruct((number, rows, 8), jnp.float32)
    return pl.pallas_call(
        kernel,
        grid=(rows // ROWS,),
        out_shape=(small, small, jax.ShapeDtypeStruct((rows, features), jnp.bfloat16)),
        in_specs=[row_blocks(number, features), whole_block(dynamic.shape), whole_block(static.shape)],
        out_specs=(
            row_blocks(number, 8),
            row_blocks(number, 8),
            pl.BlockSpec((ROWS, features), lambda r: (r, 0)),
        ),
        compiler_params=params(),
        name="connect_first",
    )(streams, dynamic, static)


def connect_middle(streams, coef, attended, w_mine, w_other, cotangent, dynamic, static, core_fsdp, where, depth):
    number, rows, features = streams.shape
    half = features // 2
    own = attended.shape[2]
    count = len(w_mine)

    def kernel(core_ref, streams_ref, coef_ref, attended_ref, *refs):
        weights, refs = refs[: 2 * count], refs[2 * count :]
        cotangent_ref, dynamic_ref, static_ref = refs[:3]
        first_ref, branch_ref, coef_two_ref, dyn_ref, own_ref, projected = refs[3:]
        step = pl.program_id(0)

        @pl.when(step == 0)
        def _():
            for side in range(2):
                total = 0.0
                for j, (d, offset) in enumerate(where):
                    for q in range(w_mine[j].shape[0] // own):
                        part = attended_ref[(core_ref[1] ^ d) * (depth // own) + offset // own + q]
                        total = total + mm(part, weights[side * count + j][q * own : (q + 1) * own])
                projected[core_ref[0] if side == 0 else 1 - core_ref[0]] = total

        span = pl.ds(pl.multiple_of(step * ROWS, ROWS), ROWS)
        branch = jnp.concatenate([projected[0, span], projected[1, span]], axis=1)
        branch_ref[...] = branch
        inputs = [streams_ref[i].astype(jnp.float32) for i in range(number)]
        outs = []
        for j in range(number):
            out = sum((coef_ref[i][:, 2 + j : 3 + j] * inputs[i] for i in range(number)))
            outs.append(out + coef_ref[j][:, 0:1] * branch)
            first_ref[j] = outs[-1]
        columns = connect_coefficients(outs, dynamic_ref, static_ref, coef_two_ref, dyn_ref)
        mixed = sum((columns[i][:, 1:2] * outs[i] for i in range(number)))
        own_ref[0] = low(normalize(mixed)[0])
        own_ref[1] = low(sum((columns[j][:, 0:1] * cotangent_ref[j].astype(jnp.float32) for j in range(number))))

    small = jax.ShapeDtypeStruct((number, rows, 8), jnp.float32)
    once = dict(pipeline_mode=pl.Buffered(1))
    return pl.pallas_call(
        kernel,
        grid_spec=pltpu.PrefetchScalarGridSpec(
            num_scalar_prefetch=1,
            grid=(rows // ROWS,),
            in_specs=[
                row_blocks(number, features),
                row_blocks(number, 8),
                whole_block(attended.shape, **once),
                *[whole_block(w.shape, **once) for w in w_mine + w_other],
                row_blocks(number, features),
                whole_block(dynamic.shape),
                whole_block(static.shape),
            ],
            out_specs=(
                row_blocks(number, features),
                pl.BlockSpec((ROWS, features), lambda r, *_: (r, 0)),
                row_blocks(number, 8),
                row_blocks(number, 8),
                row_blocks(2, features),
            ),
            scratch_shapes=[pltpu.VMEM((2, rows, half), jnp.float32)],
        ),
        out_shape=(
            jax.ShapeDtypeStruct((number, rows, features), jnp.float32),
            jax.ShapeDtypeStruct((rows, features), jnp.float32),
            small,
            small,
            jax.ShapeDtypeStruct((2, rows, features), jnp.bfloat16),
        ),
        compiler_params=params(),
        name="connect_middle",
    )(core_fsdp, streams, coef, attended, *w_mine, *w_other, cotangent, dynamic, static)


def attention_weights(rows, grads, attended, grad_cols):
    total, features = rows.shape
    parts, _, own = attended.shape
    wide = grads.shape[1]

    def kernel(rows_ref, grads_ref, attended_ref, cols_ref, out_ref):
        out_ref[:, :wide] = low(mm(rows_ref[...], grads_ref[...], CONTRACT_FIRST))
        out_ref[:, wide:] = low(mm(attended_ref[0], cols_ref[...], CONTRACT_FIRST))

    return pl.pallas_call(
        kernel,
        grid=(parts,),
        in_specs=[
            pl.BlockSpec((total, own), lambda k: (0, k)),
            whole_block(grads.shape),
            pl.BlockSpec((1, total, own), lambda k: (k, 0, 0)),
            whole_block(grad_cols.shape),
        ],
        out_specs=pl.BlockSpec((own, wide + own), lambda k: (k, 0)),
        out_shape=jax.ShapeDtypeStruct((features, wide + own), jnp.bfloat16),
        compiler_params=params(),
        cost_estimate=pl.CostEstimate(
            flops=2 * total * features * (wide + own), bytes_accessed=16 * 1024 * 1024, transcendentals=0
        ),
        name="attention_weights",
    )(rows, grads, attended, grad_cols)


def flip(index, bits, count):
    result = index
    bit = 1
    while bit < count:
        if bits & bit:
            result = result + bit - 2 * bit * (index // bit % 2)
        bit *= 2
    return result


def project_back(n_ctx, n_fsdp, grad, w_mine, w_other, where, depth):
    rows, features = grad.shape
    half = features // 2
    count = len(w_mine)
    own = features // n_ctx

    def kernel(grad_ref, *refs):
        weights, refs = refs[: 2 * count], refs[2 * count :]
        landed, cols_ref, outs, deal_s, deal_r, own_sem = refs
        _, core, fsdp, _ = place(n_ctx)
        greet(ctx_peers(n_ctx))
        first = grad_ref[:, pl.ds(pl.multiple_of(core * half, half), half)]
        second = grad_ref[:, pl.ds(pl.multiple_of((1 - core) * half, half), half)]
        for j, (d, offset) in enumerate(where):
            out = low(
                mm(first, weights[j][...], CONTRACT_LAST) + mm(second, weights[count + j][...], CONTRACT_LAST)
            )
            for q in range(w_mine[j].shape[0] // own):
                at = flip(fsdp, d, n_fsdp) * (depth // own) + offset // own + q
                outs[at] = out[:, q * own : (q + 1) * own]
                deal(n_ctx, outs.at[at], at, landed, (deal_s, deal_r), own_sem)
        for index in range(n_ctx):
            cols_ref[index] = grad_ref[:, index * own : (index + 1) * own]
        dealt(n_ctx, outs.at[0], landed, (deal_s, deal_r), own_sem)

    shape = (n_ctx, rows, own)
    return pl.pallas_call(
        kernel,
        in_specs=[pl.BlockSpec(memory_space=pltpu.VMEM)] * (1 + 2 * count),
        out_specs=any_specs(1) + [pl.BlockSpec(memory_space=pltpu.VMEM)],
        out_shape=[jax.ShapeDtypeStruct(shape, grad.dtype)] * 2,
        scratch_shapes=[pltpu.VMEM(shape, grad.dtype)] + dma_pair(n_ctx) + [pltpu.SemaphoreType.DMA],
        compiler_params=params(9),
        name="project_back",
    )(grad, *w_mine, *w_other)


def connect_back(values, coef, dyn, branch, grads, grad_normed, dynamic, coef_before=None, offset=0):
    number, rows, features = values.shape
    steps = rows // ROWS
    more = coef_before is not None

    def kernel(*refs):
        values_ref, coef_ref, dyn_ref, branch_ref, grads_ref, normed_ref, dynamic_ref = refs[:7]
        refs = refs[7:]
        if more:
            before_ref, refs = refs[0], refs[1:]
        out_ref, dynamic_out, static_out = refs[:3]
        if more:
            forward_ref, grad_low_ref = refs[3:5]
        dynamic_sum = refs[-1]
        step = pl.program_id(0)

        @pl.when(step == 0)
        def _():
            dynamic_sum[...] = jnp.zeros_like(dynamic_sum)
            static_out[...] = jnp.zeros_like(static_out)

        branch = branch_ref[...]
        mixed = sum((coef_ref[i][:, 1:2] * values_ref[i].astype(jnp.float32) for i in range(number)))
        normed, inverse = normalize(mixed)
        grad_mixed = normalize_back(normed, inverse, normed_ref[...])
        lane = lax.broadcasted_iota(jnp.int32, (ROWS, 8), 1)
        totals = [0.0] * 6
        befores = 0.0
        for i in range(number):
            value = values_ref[i].astype(jnp.float32)
            grad_own = grads_ref[i].astype(jnp.float32)
            columns = [
                jnp.sum(grad_own * branch, axis=-1, keepdims=True),
                jnp.sum(grad_mixed * value, axis=-1, keepdims=True),
            ]
            out = coef_ref[i][:, 1:2] * grad_mixed
            for j in range(number):
                grad = grads_ref[j].astype(jnp.float32)
                columns.append(jnp.sum(grad * value, axis=-1, keepdims=True))
                out = out + coef_ref[i][:, 2 + j : 3 + j] * grad
            normed = (value - coef_ref[i][:, 6:7]) * coef_ref[i][:, 7:8]
            normed_grad = 0.0
            coef_grad = jnp.zeros((ROWS, 8), jnp.float32)
            for k in range(6):
                part = dyn_ref[i][:, k : k + 1]
                pre_grad = columns[k] * (1.0 - part * part)
                normed_grad = normed_grad + pre_grad * dynamic_ref[k : k + 1]
                totals[k] = totals[k] + pre_grad * normed
                coef_grad = jnp.where(lane == k, columns[k], coef_grad)
            out = out + normalize_back(normed, coef_ref[i][:, 7:8], normed_grad)
            out_ref[i] = out
            static_out[i : i + 1] += jnp.sum(coef_grad, axis=0, keepdims=True)
            if more:
                befores = befores + before_ref[i][:, 0:1] * out
        for k in range(6):
            dynamic_sum[k] += jnp.sum(totals[k].reshape(ROWS // 8, 8, features), axis=0)
        if more:
            grad_low_ref[...] = low(befores)
            for j in range(number):
                out = coef_ref[j][:, 0:1] * branch
                for i in range(number):
                    out = out + coef_ref[i][:, 2 + j : 3 + j] * values_ref[i].astype(jnp.float32)
                forward_ref[j] = low(out)

        @pl.when(step == steps - 1)
        def _():
            for k in range(6):
                dynamic_out[k : k + 1] = jnp.sum(dynamic_sum[k], axis=0, keepdims=True)
            dynamic_out[6:8] = jnp.zeros((2, features), jnp.float32)

    rows_spec = pl.BlockSpec((ROWS, features), lambda r: (r, 0))
    out_shape = [
        jax.ShapeDtypeStruct((number, rows, features), jnp.float32),
        jax.ShapeDtypeStruct((8, features), jnp.float32),
        jax.ShapeDtypeStruct((8, 8), jnp.float32),
    ]
    out_specs = [row_blocks(number, features), whole_block((8, features)), whole_block((8, 8))]
    operands = [values, coef, dyn, branch, grads, grad_normed, dynamic]
    in_specs = [
        row_blocks(number, features),
        row_blocks(number, 8),
        row_blocks(number, 8),
        rows_spec,
        row_blocks(number, features),
        pl.BlockSpec((ROWS, features), lambda r: (offset // ROWS + r, 0)),
        whole_block(dynamic.shape),
    ]
    if more:
        operands.append(coef_before)
        in_specs.append(row_blocks(number, 8))
        out_shape.append(jax.ShapeDtypeStruct((number, rows, features), jnp.bfloat16))
        out_specs.append(row_blocks(number, features))
        out_shape.append(jax.ShapeDtypeStruct((rows, features), jnp.bfloat16))
        out_specs.append(rows_spec)
    return pl.pallas_call(
        kernel,
        grid=(steps,),
        in_specs=in_specs,
        out_specs=out_specs,
        out_shape=out_shape,
        scratch_shapes=[pltpu.VMEM((6, 8, features), jnp.float32)],
        compiler_params=params(),
        name="connect_back",
    )(*operands)


def local(n_ctx, n_fsdp, streams, w_attn, w_ffn, hc_dynamic, hc_static, cotangent, pair_order):
    number = streams.shape[1]
    length = streams.shape[2]
    features = streams.shape[3]
    size = HEAD_DIM
    own = features // n_ctx
    heads = own // size
    rows = length * n_ctx
    own_rows = w_attn.shape[0]
    ctx = lax.axis_index("ctx")
    fsdp = lax.axis_index("fsdp")
    core = ctx % 2
    chips = n_ctx // 2
    core_index = jnp.reshape(core, (1,)).astype(jnp.int32)

    def in_order(mine, other, axis):
        return jnp.where(
            core == 0, jnp.concatenate([mine, other], axis=axis), jnp.concatenate([other, mine], axis=axis)
        )


    w_own = lax.dynamic_slice_in_dim(w_attn, ctx * own, own, 2)[:, 0:3].reshape(own_rows, 3 * own)
    w_qkv = gather(w_own, "fsdp")
    half = features // 2
    w_half = lax.dynamic_slice_in_dim(w_attn, core * half, half, 2)[:, 3]
    siblings = [(i, i ^ 1) for i in range(n_ctx)]
    core_fsdp = jnp.stack([core, fsdp]).astype(jnp.int32)

    def exchange(values, most=0):
        return [values] + [
            lax.ppermute(values, "fsdp", [(i, i ^ d) for i in range(n_fsdp)])
            for d in range(1, most + 1 if most else n_fsdp)
        ]

    def swap(blocks):
        return [lax.ppermute(block, "ctx", siblings) for block in blocks]


    positions = block_positions(pair_order, length)
    frequency = THETA ** (-(jnp.arange(size // 2, dtype=jnp.float32) * 2.0) / size)
    angles = positions.astype(jnp.float32)[:, None] * jnp.concatenate([frequency, frequency])[None, :]
    signs = jnp.where(jnp.arange(size) < size // 2, -1.0, 1.0)
    tables = (jnp.cos(angles), jnp.sin(angles) * signs[None, :], positions[:, None], positions[None, :])

    dynamics = jnp.pad(hc_dynamic, ((0, 0), (0, 2), (0, 0)))
    statics = jnp.pad(hc_static, ((0, 0), (0, 0), (0, 2)))
    coef_one, dyn_one, attn_low = connect_first(streams[0], dynamics[0], statics[0])
    attn_low, w_half = lax.optimization_barrier((attn_low, w_half))
    w_out_mine = exchange(w_half, 2 if n_fsdp == 4 else 0)
    attn_all = line_rows(n_ctx, attn_low).reshape(rows, features)
    w_out_where = [(d, 0) for d in range(len(w_out_mine))]
    attn_all, *w_out_mine = lax.optimization_barrier((attn_all, *w_out_mine))
    w_out_other = swap(w_out_mine)
    if n_fsdp == 4:
        middle = own_rows // 2
        corners = [
            lax.ppermute(w_out_mine[1][:middle], "fsdp", [(i, i ^ 2) for i in range(4)]),
            lax.ppermute(w_out_mine[2][middle:], "fsdp", [(i, i ^ 1) for i in range(4)]),
        ]
        w_out_where += [(3, 0), (3, middle)]
    query, key, value, attended, logs, attended_rows = attention_forward(n_ctx, attn_all, w_qkv, *tables, heads)
    if n_fsdp == 4:
        attended, *corners = lax.optimization_barrier((attended, *corners))
        w_out_mine += corners
        w_out_other += swap(corners)

    first_out, attn_branch, coef_two, dyn_two, ffn_own = connect_middle(
        streams[0], coef_one, attended_rows, w_out_mine, w_out_other, cotangent[0], dynamics[1], statics[1], core_fsdp,
        w_out_where, own_rows,
    )
    ffn_own = ffn_own.reshape(2 * length, features)

    planes = jnp.moveaxis(w_ffn, 1, 0)
    n_own = planes.shape[1] // 2
    blocks = 2 * n_fsdp
    if n_fsdp == 4:
        ffn_all, mirror_rows, *hidden, sums = ffn_rows(n_ctx, ffn_own, planes, n_own)
        ffn_all, mirror_rows = (part.reshape(blocks, 2, length, features) for part in (ffn_all, mirror_rows))
        mirror_rows = [mirror_rows]
        attended, sums = lax.optimization_barrier((attended, sums))
        attended_all = gather(attended, "ctx").reshape(n_ctx, rows, own)
        *weight_parts, sums = ffn_weights(n_ctx, n_fsdp, sums, ffn_all, mirror_rows, hidden, planes, n_own)
    else:
        ffn_mirror = lax.ppermute(ffn_own, "ctx", [(i, n_ctx - 2 - i + 2 * (i % 2)) for i in range(n_ctx)])
        ffn_all = square_core_gather(n_ctx, n_fsdp, ffn_own).reshape(blocks, 2, length, features)
        attended_all = gather(attended, "ctx").reshape(n_ctx, rows, own)
        mirror_mine = exchange(ffn_mirror)
        hidden = ffn_forward(ffn_all, planes, core_index, n_own)
        sums = ffn_back(*hidden, planes, core_index, blocks)
        mirror_rows = [part.reshape(1, 2, length, features) for part in mirror_mine + swap(mirror_mine)]
        sums = square_sum(n_ctx, n_fsdp, sums.reshape(2, n_fsdp, 2 * length, features))
        weight_parts = ffn_weights(n_ctx, n_fsdp, None, ffn_all, mirror_rows, hidden, planes, n_own)
    sides = chips // 2
    lines = [[2 * (sides * side + i) + j for i in range(sides)] for side in range(2) for j in range(2)]
    weight_cols = lax.psum_scatter(weight_parts[0], "ctx", scatter_dimension=0, axis_index_groups=lines)

    grad_first, dynamic_grad_two, static_grad_two, streams_out, grad_attn = connect_back(
        first_out, coef_two, dyn_two, sums, cotangent[0], sums, dynamics[1], coef_one, length
    )
    grad_heads, grad_cols = project_back(n_ctx, n_fsdp, grad_attn, w_out_mine, w_out_other, w_out_where, own_rows)
    grad_heads = grad_heads.reshape(rows, own)
    grad_heads, grad_cols = lax.optimization_barrier((grad_heads, grad_cols))
    grad_cols = lax.all_to_all(grad_cols, "ctx", 0, 0, tiled=True).reshape(rows, own)
    qkv_grad, attn_part = attention_backward(query, key, value, grad_heads, logs, w_qkv, *tables, heads)
    attn_part = attn_part.reshape(n_ctx, length, features)
    grad_attn_normed = line_sum(n_ctx, attn_part, 5)
    grad_attn_normed, weight_cols = lax.optimization_barrier((grad_attn_normed, weight_cols))
    mine = lax.dynamic_slice_in_dim(weight_cols, core * own, own, 2)
    other = lax.dynamic_slice_in_dim(weight_cols, (1 - core) * own, own, 2)
    other = lax.ppermute(other, "ctx", siblings)
    ffn_grad = jnp.moveaxis(in_order(mine, other, 1), 0, 1).astype(jnp.float32)
    weight_part = attention_weights(attn_all, qkv_grad, attended_all, grad_cols)
    attn_grad = scatter(weight_part, "fsdp")

    grad_inputs, dynamic_grad_one, static_grad_one = connect_back(
        streams[0], coef_one, dyn_one, attn_branch, grad_first, grad_attn_normed, dynamics[0]
    )
    static_grads = jnp.concatenate([static_grad_one[:number, :6].reshape(1, -1), static_grad_two[:number, :6].reshape(1, -1)])
    small = jnp.concatenate(
        [
            dynamic_grad_one[:6],
            dynamic_grad_two[:6],
            jnp.pad(static_grads, ((0, 2), (0, features - 6 * number))),
        ]
    )
    small = sum_everywhere(n_ctx, n_fsdp, small.reshape(n_ctx, 8, -1))
    small, attn_grad = lax.optimization_barrier((small, attn_grad))
    small = small.reshape(16, features)
    attn_grad = attn_grad.astype(jnp.float32).reshape(own_rows, 4, own)
    dynamic_total = small[:12].reshape(2, 6, features)
    static_total = small[12:14, : 6 * number].reshape(2, number, 6)
    return (streams_out[None], grad_inputs[None], attn_grad, ffn_grad, dynamic_total, static_total)


def solution(mesh):
    return jax.shard_map(
        functools.partial(local, mesh.shape["ctx"], mesh.shape["fsdp"]),
        mesh=mesh,
        in_specs=(
            P("fsdp", None, "ctx", None),
            P("fsdp", None, None),
            P("fsdp", None, None),
            P(),
            P(),
            P("fsdp", None, "ctx", None),
            P(),
        ),
        out_specs=(
            P("fsdp", None, "ctx", None),
            P("fsdp", None, "ctx", None),
            P("fsdp", None, "ctx"),
            P("fsdp", None, "ctx"),
            P(),
            P(),
        ),
        check_vma=False,
    )
```

```python
import functools

import jax
import jax.numpy as jnp
from jax import lax
from jax.experimental import pallas as pl
from jax.experimental.pallas import tpu as pltpu
from jax.sharding import PartitionSpec as P

HEADS = 16
HEAD_DIM = 128


EPS = 1e-05
THETA = 10000.0
HIGH = lax.Precision.HIGHEST
MASKED = -1e30
CONTRACT_LAST = (((1,), (1,)), ((), ()))
CONTRACT_FIRST = (((0,), (0,)), ((), ()))


def normalize(values):
    centered = values - jnp.mean(values, axis=-1, keepdims=True)
    inverse = lax.rsqrt(jnp.mean(centered * centered, axis=-1, keepdims=True) + EPS)
    return (centered * inverse, inverse)


def normalize_back(normed, inverse, gradient):
    inner = jnp.mean(gradient * normed, axis=-1, keepdims=True)
    return inverse * (gradient - jnp.mean(gradient, axis=-1, keepdims=True) - normed * inner)


def block_positions(pair_order, length):
    half_size = length // 2
    offsets = jnp.arange(half_size, dtype=jnp.int32)
    mirror = 2 * pair_order.shape[0] - 1 - pair_order
    first_half = pair_order[:, None] * half_size + offsets[None, :]
    second_half = mirror[:, None] * half_size + offsets[None, :]
    return jnp.concatenate([first_half, second_half], axis=1).reshape(-1)


def low(values):
    return values.astype(jnp.bfloat16)


def mm(a, b, dims=None):
    if dims is None:
        return jnp.dot(a, b, preferred_element_type=jnp.float32)
    return lax.dot_general(a, b, dims, preferred_element_type=jnp.float32)


def gather(values, axis, dim=0):
    return lax.all_gather(values, axis, axis=dim, tiled=True)


def scatter(values, axis, dim=0):
    return lax.psum_scatter(values, axis, scatter_dimension=dim, tiled=True)


MESH = pl.DeviceIdType.MESH
VMEM_LIMIT = 60 * 1024 * 1024


def place(n_ctx):
    ctx = lax.axis_index("ctx")
    return (ctx // 2, ctx % 2, lax.axis_index("fsdp"), n_ctx // 2)


def greet(peers):
    barrier = pltpu.get_barrier_semaphore()
    for peer in peers:
        pl.semaphore_signal(barrier, inc=1, device_id=peer, device_id_type=MESH)
    pl.semaphore_wait(barrier, len(peers))


def send(source, target, sems, index, peer):
    return pltpu.make_async_remote_copy(
        src_ref=source,
        dst_ref=target,
        send_sem=sems[0].at[index],
        recv_sem=sems[1].at[index],
        device_id=peer,
        device_id_type=MESH,
    )


def fsdp_neighbours(fsdp):
    first = fsdp + 1 - 2 * (fsdp % 2)
    second = (fsdp + 2) % 4
    return (first, second, (first + 2) % 4)


def fsdp_peers(n_fsdp, ctx, fsdp):
    if n_fsdp == 4:
        first, second, _ = fsdp_neighbours(fsdp)
        return [(ctx, first), (ctx, second)]
    return [(ctx, (fsdp + j) % n_fsdp) for j in range(1, n_fsdp)]


def line_peers(chip, core, fsdp, length):
    return [
        (chip * 2 + 1 - core, fsdp),
        ((chip + 1) % length * 2 + core, fsdp),
        ((chip + length - 1) % length * 2 + core, fsdp),
    ]


def line_gather(own_ref, all_ref, sems, where):
    chip, core, fsdp, length = where
    right_sems, left_sems, core_sems = sems
    sibling = (chip * 2 + 1 - core, fsdp)
    right = ((chip + 1) % length * 2 + core, fsdp)
    left = ((chip + length - 1) % length * 2 + core, fsdp)

    def block(index):
        return all_ref.at[(index + length) % length * 2 + core]

    def pass_on(index, source):
        return send(source, block(index), core_sems, (index + length) % length, sibling)

    pass_on(chip, own_ref).start()
    for step in range(length - 1):
        for sign, peer, way in ((-1, right, right_sems), (1, left, left_sems)):
            at = chip + sign * step
            held = (at >= 0) & (at < length)
            if step > 0:

                @pl.when(held)
                def _():
                    send(block(at), block(at), way, step - 1, peer).wait_recv()
                    pass_on(at, block(at)).start()

            more = (chip < length - 1) if sign < 0 else (chip > 0)

            @pl.when(held & more)
            def _():
                send(own_ref if step == 0 else block(at), block(at), way, step, peer).start()

        yield
    last = length - 1
    for sign, peer, way in ((-1, right, right_sems), (1, left, left_sems)):
        at = chip + sign * last

        @pl.when((at >= 0) & (at < length))
        def _():
            send(block(at), block(at), way, last - 1, peer).wait_recv()
            pass_on(at, block(at)).start()

    yield
    for step in range(length - 1):
        for sign, peer, way in ((-1, right, right_sems), (1, left, left_sems)):
            at = chip + sign * step
            more = (chip < length - 1) if sign < 0 else (chip > 0)

            @pl.when((at >= 0) & (at < length) & more)
            def _():
                send(block(at), block(at), way, step, peer).wait_send()

    for index in range(length):
        pass_on(index, block(index)).wait_send()
        other = all_ref.at[index * 2 + 1 - core]
        send(other, other, core_sems, index, sibling).wait_recv()


def square_gather(own_ref, all_ref, sems, ctx, fsdp, n_fsdp, passed=None):
    if n_fsdp != 4:
        copies = [
            send(own_ref, all_ref.at[fsdp], sems, j - 1, (ctx, (fsdp + j) % n_fsdp)) for j in range(1, n_fsdp)
        ]
        for copy in copies:
            copy.start()
        yield
        for j, copy in enumerate(copies):
            copy.wait()
            if passed:
                passed(all_ref.at[(fsdp + n_fsdp - j - 1) % n_fsdp], (fsdp + n_fsdp - j - 1) % n_fsdp, None, j)
        return
    first, second, corner = fsdp_neighbours(fsdp)
    half = own_ref.shape[0] // 2
    top, low_half = pl.ds(0, half), pl.ds(half, half)
    to_first, to_second = (ctx, first), (ctx, second)

    def copy(index, owner, part, peer, source=None):
        source = all_ref.at[owner, part] if source is None else source
        return send(source, all_ref.at[owner, part], sems, index, peer)

    starts = [
        copy(0, fsdp, top, to_first, own_ref.at[top]),
        copy(1, fsdp, low_half, to_second, own_ref.at[low_half]),
        copy(2, fsdp, low_half, to_first, own_ref.at[low_half]),
        copy(3, fsdp, top, to_second, own_ref.at[top]),
        copy(4, first, top, to_second),
        copy(5, second, low_half, to_first),
    ]
    arrivals = [
        (0, first, top),
        (1, second, low_half),
        (2, first, low_half),
        (3, second, top),
        (4, corner, top),
        (5, corner, low_half),
    ]
    for each in starts[:4]:
        each.start()
    yield
    for index, owner, part in arrivals:
        copy(index, owner, part, to_first).wait_recv()
        if index < 2:
            starts[4 + index].start()
        if passed:
            passed(all_ref.at[owner, part], owner, part, index)
        yield
    for each in starts:
        each.wait_send()


def run_all(*parts):
    parts = list(parts)
    while parts:
        for part in list(parts):
            try:
                next(part)
            except StopIteration:
                parts.remove(part)


def dma_pair(count):
    return [pltpu.SemaphoreType.DMA((count,)), pltpu.SemaphoreType.DMA((count,))]


def any_specs(count):
    return [pl.BlockSpec(memory_space=pl.ANY)] * count


def params(collective_id=None, **more):
    if collective_id is not None:
        more.update(collective_id=collective_id, has_side_effects=True)
    return pltpu.CompilerParams(vmem_limit_bytes=VMEM_LIMIT, **more)


def passing(own_ref, all_ref, sems, core, fsdp, sibling):
    handed = [send(own_ref, all_ref.at[core, fsdp], sems, 0, sibling)]
    handed[0].start()
    arriving = [send(own_ref, all_ref.at[1 - core, fsdp], sems, 0, sibling)]

    def passed(source, owner, part, index):
        for side, copies in ((core, handed), (1 - core, arriving)):
            target = all_ref.at[side, owner] if part is None else all_ref.at[side, owner, part]
            copies.append(send(source, target, sems, index + 1, sibling))
        handed[-1].start()

    def finish():
        for out, back in zip(handed, arriving):
            out.wait_send()
            back.wait_recv()

    return (passed, finish)


def line_rows(n_ctx, rows):
    def kernel(rows_ref, all_rows, right_s, right_r, left_s, left_r, core_s, core_r, own):
        where = place(n_ctx)
        chip, core, fsdp, length = where
        greet(line_peers(*where))
        mine = pltpu.make_async_copy(rows_ref, all_rows.at[chip * 2 + core], own)
        mine.start()
        run_all(line_gather(rows_ref, all_rows, ((right_s, right_r), (left_s, left_r), (core_s, core_r)), where))
        mine.wait()

    length = n_ctx // 2
    return pl.pallas_call(
        kernel,
        out_shape=jax.ShapeDtypeStruct((n_ctx,) + rows.shape, rows.dtype),
        in_specs=any_specs(1),
        out_specs=pl.BlockSpec(memory_space=pl.ANY),
        scratch_shapes=dma_pair(length) + dma_pair(length) + dma_pair(length) + [pltpu.SemaphoreType.DMA],
        compiler_params=params(0),
        name="line_rows",
    )(rows)


def square_core_gather(n_ctx, n_fsdp, rows):
    def kernel(rows_ref, all_ref, sq_s, sq_r, core_s, core_r, own):
        chip, core, fsdp, _ = place(n_ctx)
        ctx = chip * 2 + core
        sibling = (chip * 2 + 1 - core, fsdp)
        greet([sibling] + fsdp_peers(n_fsdp, ctx, fsdp))
        mine = pltpu.make_async_copy(rows_ref, all_ref.at[core, fsdp], own)
        mine.start()
        passed, finish = passing(rows_ref, all_ref, (core_s, core_r), core, fsdp, sibling)
        run_all(square_gather(rows_ref, all_ref.at[core], (sq_s, sq_r), ctx, fsdp, n_fsdp, passed))
        finish()
        mine.wait()

    return pl.pallas_call(
        kernel,
        out_shape=jax.ShapeDtypeStruct((2, n_fsdp) + rows.shape, rows.dtype),
        in_specs=any_specs(1),
        out_specs=pl.BlockSpec(memory_space=pl.ANY),
        scratch_shapes=dma_pair(max(6, n_fsdp)) + dma_pair(max(7, n_fsdp)) + [pltpu.SemaphoreType.DMA],
        compiler_params=params(1),
        name="square_core_gather",
    )(rows)


def add_into(target, *sources, chunk=64):
    @pl.loop(0, target.shape[0] // chunk)
    def _(step):
        rows = pl.ds(pl.multiple_of(step * chunk, chunk), chunk)
        total = target[rows].astype(jnp.float32)
        for source in sources:
            total = total + source[rows].astype(jnp.float32)
        target[rows] = total.astype(target.dtype)


def square_sum_stages(n_ctx, n_fsdp, partial_ref, out_ref, held, core_in, square_in, load, core_sems, sems):
    rows = partial_ref.shape[-2]
    half = rows // 2
    chip, core, fsdp, _ = place(n_ctx)
    ctx = chip * 2 + core
    sibling = (chip * 2 + 1 - core, fsdp)
    if n_fsdp == 4:
        first, second, corner = fsdp_neighbours(fsdp)
        order = [corner, first, second, fsdp]
    else:
        order = [(fsdp + j) % n_fsdp for j in range(1, n_fsdp + 1)]
    mine = [
        pltpu.make_async_copy(partial_ref.at[core, owner], held.at[owner], load.at[j])
        for j, owner in enumerate(order)
    ]
    others = [
        send(partial_ref.at[1 - core, owner], core_in.at[owner], core_sems, j, sibling)
        for j, owner in enumerate(order)
    ]

    def ready(j):
        mine[j].wait()
        others[j].wait_recv()
        add_into(held.at[order[j]], core_in.at[order[j]])

    def total(parts, sources):
        @pl.loop(0, parts[1] // 64)
        def _(step):
            at = pl.ds(pl.multiple_of(parts[0] + step * 64, 64), 64)
            from_at = pl.ds(pl.multiple_of(step * 64, 64), 64)
            value = held[fsdp, at].astype(jnp.float32)
            for j in sources:
                value = value + square_in[j, from_at].astype(jnp.float32)
            out_ref[at] = value

    def begin():
        greet([sibling] + fsdp_peers(n_fsdp, ctx, fsdp))
        for j in range(n_fsdp):
            others[j].start()
            mine[j].start()

    if n_fsdp != 4:
        copies = [
            send(held.at[order[j]], square_in.at[j], sems, j, (ctx, order[j])) for j in range(n_fsdp - 1)
        ]

        def spread():
            for j in range(n_fsdp):
                ready(j)
                if j < n_fsdp - 1:
                    copies[j].start()

        def finish():
            for copy in copies:
                copy.wait()
            total((0, rows), range(n_fsdp - 1))
            for each in others:
                each.wait_send()

        return [begin, spread, finish]

    top, low_half = pl.ds(0, half), pl.ds(half, half)
    to_first, to_second = (ctx, first), (ctx, second)

    def copy(index, owner, part, peer):
        return send(held.at[owner, part], square_in.at[index], sems, index, peer)

    copies = [
        copy(0, corner, top, to_first),
        copy(1, corner, low_half, to_second),
        copy(2, first, top, to_first),
        copy(3, second, low_half, to_second),
        copy(4, second, top, to_second),
        copy(5, first, low_half, to_first),
    ]

    def spread():
        ready(0)
        copies[0].start()
        copies[1].start()
        ready(1)
        copies[2].start()
        ready(2)
        copies[3].start()
        ready(3)

    def pass_on():
        copies[0].wait_recv()
        add_into(held.at[second, top], square_in.at[0])
        copies[4].start()
        copies[1].wait_recv()
        add_into(held.at[first, low_half], square_in.at[1])
        copies[5].start()

    def finish():
        for j in range(2, 6):
            copies[j].wait_recv()
        total((0, half), (2, 4))
        total((half, half), (3, 5))
        for each in copies:
            each.wait_send()
        for each in others:
            each.wait_send()

    return [begin, spread, pass_on, finish]


def corner_sum_stages(n_ctx, partial_ref, out_ref, held, square_in, load, sems):
    half = partial_ref.shape[1] // 2
    chip, core, fsdp, _ = place(n_ctx)
    ctx = chip * 2 + core
    first, second, corner = fsdp_neighbours(fsdp)
    top, low_half = pl.ds(0, half), pl.ds(half, half)
    to_first, to_second = (ctx, first), (ctx, second)

    def copy(index, source, peer):
        return send(source, square_in.at[index], sems, index, peer)

    copies = [
        copy(0, partial_ref.at[corner, top], to_first),
        copy(1, partial_ref.at[corner, low_half], to_second),
        copy(2, partial_ref.at[first, top], to_first),
        copy(3, partial_ref.at[second, low_half], to_second),
        copy(4, held.at[0], to_second),
        copy(5, held.at[1], to_first),
    ]
    mine = [
        pltpu.make_async_copy(partial_ref.at[second, top], held.at[0], load.at[0]),
        pltpu.make_async_copy(partial_ref.at[first, low_half], held.at[1], load.at[1]),
        pltpu.make_async_copy(partial_ref.at[fsdp, top], held.at[2], load.at[2]),
        pltpu.make_async_copy(partial_ref.at[fsdp, low_half], held.at[3], load.at[3]),
    ]

    starts = [
        [copies[0].start, copies[1].start],
        [copies[2].start, mine[1].start],
        [copies[3].start, mine[0].start],
        [mine[2].start, mine[3].start],
    ]

    def pass_on():
        for index in range(2):
            mine[index].wait()
            copies[index].wait_recv()
            add_into(held.at[index], square_in.at[index])
            copies[4 + index].start()

    def finish():
        for part, sources in ((0, (2, 4)), (1, (3, 5))):
            mine[2 + part].wait()
            for j in sources:
                copies[j].wait_recv()

            @pl.loop(0, half // 64)
            def _(step):
                at = pl.ds(pl.multiple_of(step * 64, 64), 64)
                value = held[2 + part, at].astype(jnp.float32)
                for j in sources:
                    value = value + square_in[j, at].astype(jnp.float32)
                out_ref[pl.ds(pl.multiple_of(part * half + step * 64, 64), 64)] = value

        for each in copies:
            each.wait_send()

    return [starts, pass_on, finish]


def corner_sum_scratch(partial):
    _, rows, columns = partial.shape
    return [
        pltpu.VMEM((4, rows // 2, columns), partial.dtype),
        pltpu.VMEM((6, rows // 2, columns), partial.dtype),
        pltpu.SemaphoreType.DMA((4,)),
    ] + dma_pair(6)


def square_sum_scratch(n_fsdp, partial):
    rows, columns = partial.shape[-2:]
    pieces = (6, rows // 2, columns) if n_fsdp == 4 else (n_fsdp - 1, rows, columns)
    return (
        [
            pltpu.VMEM((n_fsdp, rows, columns), partial.dtype),
            pltpu.VMEM((n_fsdp, rows, columns), partial.dtype),
            pltpu.VMEM(pieces, partial.dtype),
            pltpu.SemaphoreType.DMA((n_fsdp,)),
        ]
        + dma_pair(n_fsdp)
        + dma_pair(max(6, n_fsdp))
    )


def square_sum(n_ctx, n_fsdp, partial):
    def kernel(partial_ref, out_ref, held, core_in, square_in, load, core_s, core_r, sq_s, sq_r):
        for stage in square_sum_stages(
            n_ctx, n_fsdp, partial_ref, out_ref, held, core_in, square_in, load, (core_s, core_r), (sq_s, sq_r)
        ):
            stage()

    return pl.pallas_call(
        kernel,
        out_shape=jax.ShapeDtypeStruct(partial.shape[-2:], jnp.float32),
        in_specs=any_specs(1),
        out_specs=pl.BlockSpec(memory_space=pltpu.VMEM),
        scratch_shapes=square_sum_scratch(n_fsdp, partial),
        compiler_params=params(1),
        name="square_sum",
    )(partial)


def line_sum_steps(n_ctx, partial_ref, out_ref, held, core_in, right_in, left_in, load, core_sems, right_sems, left_sems):
    rows = partial_ref.shape[1]
    where = place(n_ctx)
    chip, core, fsdp, length = where
    sibling, right, left = line_peers(*where)
    order = [(chip + length - 1 - j) % length for j in range(length)]
    mine, others = [], []
    for j, owner in enumerate(order):
        mine.append(pltpu.make_async_copy(partial_ref.at[owner * 2 + core], held.at[owner], load.at[j]))
        others.append(send(partial_ref.at[owner * 2 + 1 - core], core_in.at[owner], core_sems, j, sibling))
        others[-1].start()
        mine[-1].start()
    yield
    for j, owner in enumerate(order):
        mine[j].wait()
        others[j].wait_recv()
        add_into(held.at[owner], core_in.at[owner])
    ways = ((1, right, right_in, right_sems), (-1, left, left_in, left_sems))
    for step in range(length - 1):
        for sign, peer, arrived, sems in ways:
            block = chip + sign * (length - 1 - step)
            inside = (block >= 0) & (block < length)
            came = (chip >= 1) if sign > 0 else (chip < length - 1)
            if step > 0:

                @pl.when(inside & came)
                def _():
                    send(held.at[block], arrived.at[step - 1], sems, step - 1, peer).wait_recv()
                    add_into(held.at[block], arrived.at[step - 1])

            @pl.when(inside)
            def _():
                send(held.at[block], arrived.at[step], sems, step, peer).start()

        yield
    last = length - 2
    for sign, peer, arrived, sems in ways:
        came = (chip >= 1) if sign > 0 else (chip < length - 1)

        @pl.when(came)
        def _():
            send(held.at[chip], arrived.at[last], sems, last, peer).wait_recv()
            add_into(held.at[chip], arrived.at[last])

    @pl.loop(0, rows // 64)
    def _(step):
        at = pl.ds(pl.multiple_of(step * 64, 64), 64)
        out_ref[at] = held[chip, at].astype(jnp.float32)

    for step in range(length - 1):
        for sign, peer, arrived, sems in ways:
            block = chip + sign * (length - 1 - step)

            @pl.when((block >= 0) & (block < length))
            def _():
                send(held.at[block], arrived.at[step], sems, step, peer).wait_send()

    for each in others:
        each.wait_send()


def line_sum_scratch(n_ctx, partial):
    rows, columns = partial.shape[-2:]
    length = n_ctx // 2
    return [
        pltpu.VMEM((length, rows, columns), partial.dtype),
        pltpu.VMEM((length, rows, columns), partial.dtype),
        pltpu.VMEM((length - 1, rows, columns), partial.dtype),
        pltpu.VMEM((length - 1, rows, columns), partial.dtype),
        pltpu.SemaphoreType.DMA((length,)),
    ] + dma_pair(length) * 3


def line_sum(n_ctx, partial):
    def kernel(partial_ref, out_ref, held, core_in, right_in, left_in, load, core_s, core_r, right_s, right_r, left_s, left_r):
        greet(line_peers(*place(n_ctx)))
        run_all(
            line_sum_steps(
                n_ctx, partial_ref, out_ref, held, core_in, right_in, left_in, load,
                (core_s, core_r), (right_s, right_r), (left_s, left_r),
            )
        )

    return pl.pallas_call(
        kernel,
        out_shape=jax.ShapeDtypeStruct(partial.shape[-2:], jnp.float32),
        in_specs=any_specs(1),
        out_specs=pl.BlockSpec(memory_space=pltpu.VMEM),
        scratch_shapes=line_sum_scratch(n_ctx, partial),
        compiler_params=params(5),
        name="line_sum",
    )(partial)


def attention_sums(n_ctx, partial, rows, grads, attended, grad_cols):
    total, features = rows.shape
    parts, _, own = attended.shape
    wide = grads.shape[1]
    depth = features // 4
    weight_shape = jax.ShapeDtypeStruct((4, depth, wide + own), jnp.bfloat16)
    inputs = (rows, grads, attended, grad_cols)

    def kernel(partial_ref, *refs):
        inputs_refs, refs = refs[:4], refs[4:]
        out_ref, weight_ref, rows_v, grads_v, attended_v, cols_v, weights, in_sem, *refs = refs
        line_refs, refs = refs[:5], refs[5:]
        core_s, core_r, right_s, right_r, left_s, left_r, *refs = refs
        held, square_in, load, sq_s, sq_r = refs
        where = place(n_ctx)
        chip, core, fsdp, _ = where
        loads = [
            pltpu.make_async_copy(a, b, in_sem.at[j])
            for j, (a, b) in enumerate(zip(inputs_refs, (rows_v, grads_v, attended_v, cols_v)))
        ]
        for each in loads:
            each.start()
        greet(line_peers(*where) + fsdp_peers(4, chip * 2 + core, fsdp))
        line = line_sum_steps(
            n_ctx, partial_ref, out_ref, *line_refs, (core_s, core_r), (right_s, right_r), (left_s, left_r)
        )
        next(line)
        starts, pass_on, finish = corner_sum_stages(n_ctx, weights, weight_ref, held, square_in, load, (sq_s, sq_r))
        for each in loads:
            each.wait()
        first, second, corner = fsdp_neighbours(fsdp)
        for number, owner in enumerate((corner, first, second, fsdp)):
            at = pl.ds(pl.multiple_of(owner * depth, depth), depth)
            weights[owner, :, :wide] = low(mm(rows_v[:, at], grads_v[...], CONTRACT_FIRST))
            for q in range(depth // own):
                weights[owner, q * own : (q + 1) * own, wide:] = low(
                    mm(attended_v[owner * (depth // own) + q], cols_v[...], CONTRACT_FIRST)
                )
            for start in starts[number]:
                start()
            if number < 2:
                next(line)
        pass_on()
        run_all(line)
        finish()

    return pl.pallas_call(
        kernel,
        out_shape=[
            jax.ShapeDtypeStruct(partial.shape[-2:], jnp.float32),
            jax.ShapeDtypeStruct(weight_shape.shape[1:], jnp.float32),
        ],
        in_specs=any_specs(5),
        out_specs=[pl.BlockSpec(memory_space=pltpu.VMEM)] * 2,
        scratch_shapes=[pltpu.VMEM(a.shape, a.dtype) for a in inputs]
        + [pltpu.VMEM(weight_shape.shape, weight_shape.dtype), pltpu.SemaphoreType.DMA((4,))]
        + line_sum_scratch(n_ctx, partial)
        + corner_sum_scratch(weight_shape),
        compiler_params=params(4),
        cost_estimate=pl.CostEstimate(
            flops=2 * total * features * (wide + own), bytes_accessed=16 * 1024 * 1024, transcendentals=0
        ),
        name="attention_sums",
    )(partial, *inputs)


def sum_everywhere(n_ctx, n_fsdp, values):
    block = values.shape[1:]

    def kernel(values_ref, out_ref, along_ctx, along_fsdp, result, ctx_s, ctx_r, fsdp_s, fsdp_r, back_s, back_r):
        ctx = lax.axis_index("ctx")
        fsdp = lax.axis_index("fsdp")
        ctx_peers = [((ctx + j) % n_ctx, fsdp) for j in range(1, n_ctx)]
        fsdp_peers = [(ctx, (fsdp + j) % n_fsdp) for j in range(1, n_fsdp)]
        greet(ctx_peers + fsdp_peers)

        def exchange(copies):
            for copy in copies:
                copy.start()
            for copy in copies:
                copy.wait()

        def total(slots, count):
            value = slots[0]
            for j in range(1, count):
                value = value + slots[j]
            return value

        along_ctx[ctx] = values_ref[ctx]
        exchange(
            [
                send(values_ref.at[peer[0]], along_ctx.at[ctx], (ctx_s, ctx_r), j, peer)
                for j, peer in enumerate(ctx_peers)
            ]
        )
        along_fsdp[fsdp] = total(along_ctx, n_ctx)
        exchange(
            [
                send(along_fsdp.at[fsdp], along_fsdp.at[fsdp], (fsdp_s, fsdp_r), j, peer)
                for j, peer in enumerate(fsdp_peers)
            ]
        )
        result[ctx] = total(along_fsdp, n_fsdp)
        exchange(
            [send(result.at[ctx], result.at[ctx], (back_s, back_r), j, peer) for j, peer in enumerate(ctx_peers)]
        )
        out_ref[...] = result[...]

    return pl.pallas_call(
        kernel,
        out_shape=jax.ShapeDtypeStruct(values.shape, values.dtype),
        in_specs=[pl.BlockSpec(memory_space=pltpu.VMEM)],
        out_specs=pl.BlockSpec(memory_space=pltpu.VMEM),
        scratch_shapes=[
            pltpu.VMEM((n_ctx,) + block, values.dtype),
            pltpu.VMEM((n_fsdp,) + block, values.dtype),
            pltpu.VMEM((n_ctx,) + block, values.dtype),
        ]
        + dma_pair(n_ctx)
        + dma_pair(n_fsdp)
        + dma_pair(n_ctx),
        compiler_params=params(2),
        name="sum_everywhere",
    )(values)


def hidden_units(here, back, gate_ref, up_ref, down_ref):
    gate = mm(here, gate_ref[0], CONTRACT_LAST)
    up = mm(here, up_ref[0], CONTRACT_LAST)
    grad_hidden = mm(back, down_ref[0], CONTRACT_LAST)
    sigmoid = jax.nn.sigmoid(gate)
    activated = gate * sigmoid
    return (
        low(activated * up),
        low(grad_hidden * up * sigmoid * (1.0 + gate * (1.0 - sigmoid))),
        low(grad_hidden * activated),
    )


def ffn_forward(rows, planes, core, n_own, chunk=256):
    blocks, _, tokens, features = rows.shape
    total = blocks * tokens
    steps = n_own // chunk
    group = max(1, 256 // tokens)

    def kernel(core_ref, rows_ref, gate_ref, up_ref, down_ref, *outs):
        for at in range(0, blocks, group):
            here = rows_ref[at : at + group, 0].reshape(group * tokens, features)
            back = rows_ref[at : at + group, 1].reshape(group * tokens, features)
            span = pl.ds(at * tokens, group * tokens)
            for out, value in zip(outs, hidden_units(here, back, gate_ref, up_ref, down_ref)):
                out[span] = value

    def weight_spec(plane):
        return pl.BlockSpec((1, chunk, features), lambda j, core_ref: (plane, core_ref[0] * steps + j, 0))

    act = jax.ShapeDtypeStruct((total, n_own), jnp.bfloat16)
    act_spec = pl.BlockSpec((total, chunk), lambda j, core_ref: (0, j))
    return pl.pallas_call(
        kernel,
        grid_spec=pltpu.PrefetchScalarGridSpec(
            num_scalar_prefetch=1,
            grid=(steps,),
            in_specs=[
                pl.BlockSpec(rows.shape, lambda j, core_ref: (0, 0, 0, 0), pipeline_mode=pl.Buffered(1)),
                weight_spec(0),
                weight_spec(1),
                weight_spec(2),
            ],
            out_specs=[act_spec, act_spec, act_spec],
        ),
        out_shape=[act, act, act],
        compiler_params=params(),
        cost_estimate=pl.CostEstimate(
            flops=6 * total * n_own * features, bytes_accessed=30 * 1024 * 1024, transcendentals=total * n_own
        ),
        name="ffn_forward",
    )(core, rows, planes, planes, planes)


def mirror_gather(all_ref, arrivals, sems, pass_sems, ctx, core, fsdp, sibling):
    first, second, corner = fsdp_neighbours(fsdp)
    half = all_ref.shape[2] // 2
    parts = [pl.ds(0, half), pl.ds(half, half)]
    to_first, to_second = (ctx, first), (ctx, second)

    def copy(index, owner, part, peer):
        place_ref = all_ref.at[core, owner, parts[part]]
        return send(place_ref, place_ref, sems, index, peer)

    copies = [
        copy(0, fsdp, 0, to_first),
        copy(1, fsdp, 0, to_second),
        copy(2, fsdp, 1, to_first),
        copy(3, fsdp, 1, to_second),
        copy(4, first, 0, to_second),
        copy(5, second, 1, to_first),
    ]
    passes = [(fsdp, 0), (fsdp, 1), (first, 0), (second, 0), (first, 1), (second, 1), (corner, 0), (corner, 1)]

    def passing_copy(number, side):
        owner, part = passes[number]
        place_ref = all_ref.at[side, owner, parts[part]]
        return send(place_ref, place_ref, pass_sems, number, sibling)

    for part in range(2):
        arrivals[part].wait_recv()
        copies[2 * part].start()
        copies[2 * part + 1].start()
        passing_copy(part, core).start()
        yield
    for index, number, then in ((0, 2, 4), (1, 3, None), (2, 4, None), (3, 5, 5), (4, 6, None), (5, 7, None)):
        owner, part = passes[number]
        copy(index, owner, part, to_first).wait_recv()
        if then is not None:
            copies[then].start()
        passing_copy(number, core).start()
        yield
    for each in copies:
        each.wait_send()
    for number in range(8):
        passing_copy(number, core).wait_send()
        passing_copy(number, 1 - core).wait_recv()


def ffn_rows(n_ctx, own, planes, n_own, chunk=256, wide=512):
    n_fsdp = 4
    size, features = own.shape
    tokens = size // 2
    total = 2 * n_fsdp * tokens

    def kernel(
        own_ref, planes_ref, all_ref, mirror_ref, hidden_a, hidden_b, hidden_c, partial_ref,
        rows, weights, hidden, partial, core_in, load, sq_s, sq_r, core_s, core_r, far_s, far_r, mi_s, mi_r, mc_s, mc_r, sum_s, sum_r, out_sem,
    ):
        chip, core, fsdp, length = place(n_ctx)
        ctx = chip * 2 + core
        sibling = (chip * 2 + 1 - core, fsdp)
        mirror = ((length - 1 - chip) * 2 + core, fsdp)
        first, second, corner = fsdp_neighbours(fsdp)
        greet([sibling, mirror] + fsdp_peers(n_fsdp, ctx, fsdp))
        mine = pltpu.make_async_copy(own_ref, rows.at[core, fsdp], load.at[3])
        mine.start()
        start = pl.multiple_of(core * n_own, n_own)
        loads = [
            pltpu.make_async_copy(planes_ref.at[p, pl.ds(start, n_own)], weights.at[p], load.at[p]) for p in range(3)
        ]
        handed, arriving = [], []

        def hand(source, owner, part, index):
            for side, copies in ((core, handed), (1 - core, arriving)):
                target = rows.at[side, owner] if part is None else rows.at[side, owner, part]
                copies.append(send(source, target, (core_s, core_r), index + 1, sibling))
            handed[-1].start()

        gathering = square_gather(own_ref, rows.at[core], (sq_s, sq_r), ctx, fsdp, n_fsdp, hand)
        next(gathering)
        hand(own_ref, fsdp, None, -1)
        for each in loads:
            each.start()
        far = [
            send(
                own_ref.at[pl.ds(part * tokens, tokens)],
                mirror_ref.at[core, fsdp, pl.ds(part * tokens, tokens)],
                (far_s, far_r),
                part,
                mirror,
            )
            for part in range(2)
        ]
        for each in far:
            each.start()
        mirroring = mirror_gather(mirror_ref, far, (mi_s, mi_r), (mc_s, mc_r), ctx, core, fsdp, sibling)
        outs, summing, sums = [], [], []

        def add_up(number, owner):
            summing[number].wait_recv()
            add_into(partial.at[number % 2, core], core_in.at[number])
            sums.append(
                pltpu.make_async_copy(partial.at[number % 2, core], partial_ref.at[owner], out_sem.at[number % 2, 8])
            )
            sums[-1].start()

        def group(number, owner):
            slot = number % 2
            if number >= 2:
                for each in outs[number - 2]:
                    each.wait()
                summing[number - 2].wait_send()
                sums[number - 2].wait()
            here = jnp.concatenate([rows[0, owner, :tokens], rows[1, owner, :tokens]])
            back = jnp.concatenate([rows[0, owner, tokens:], rows[1, owner, tokens:]])

            @pl.loop(0, n_own // chunk)
            def _(step):
                at = pl.ds(pl.multiple_of(step * chunk, chunk), chunk)
                parts = [weights.at[pl.ds(p, 1), at] for p in range(3)]
                for q, value in enumerate(hidden_units(here, back, *parts)):
                    hidden[slot, q, :, at] = value

            @pl.loop(0, features // wide)
            def _(step):
                at = pl.ds(pl.multiple_of(step * wide, wide), wide)
                out = low(mm(hidden[slot, 0], weights[2, :, at]))
                below = low(mm(hidden[slot, 1], weights[0, :, at]) + mm(hidden[slot, 2], weights[1, :, at]))
                for k in range(2):
                    partial[slot, k, :tokens, at] = out[k * tokens : (k + 1) * tokens]
                    partial[slot, k, tokens:, at] = below[k * tokens : (k + 1) * tokens]

            pairs = []
            summing.append(send(partial.at[slot, 1 - core], core_in.at[number], (sum_s, sum_r), number, sibling))
            summing[-1].start()
            for k in range(2):
                pairs.append((rows.at[k, owner], all_ref.at[k, owner]))
                at = pl.ds(pl.multiple_of((k * n_fsdp + owner) * tokens, tokens), tokens)
                for q, target in enumerate((hidden_a, hidden_b, hidden_c)):
                    pairs.append((hidden.at[slot, q, pl.ds(k * tokens, tokens)], target.at[at]))
            outs.append(
                [pltpu.make_async_copy(a, b, out_sem.at[slot, j]) for j, (a, b) in enumerate(pairs)]
            )
            for each in outs[-1]:
                each.start()

        mine.wait()
        arriving[0].wait_recv()
        for each in loads:
            each.wait()
        group(0, fsdp)
        for _ in range(4):
            next(gathering)
        arriving[1].wait_recv()
        arriving[3].wait_recv()
        group(1, first)
        add_up(0, fsdp)
        next(mirroring)
        for _ in range(2):
            next(gathering)
        arriving[2].wait_recv()
        arriving[4].wait_recv()
        group(2, second)
        add_up(1, first)
        for _ in range(3):
            next(mirroring)
        arriving[5].wait_recv()
        arriving[6].wait_recv()
        group(3, corner)
        add_up(2, second)
        next(mirroring)
        add_up(3, corner)
        run_all(mirroring, gathering)
        for each in handed:
            each.wait_send()
        for each in far:
            each.wait_send()
        for each in outs[2] + outs[3] + sums[2:]:
            each.wait()
        for each in summing[2:]:
            each.wait_send()

    act = jax.ShapeDtypeStruct((total, n_own), own.dtype)
    all_rows = jax.ShapeDtypeStruct((2, n_fsdp) + own.shape, own.dtype)
    return pl.pallas_call(
        kernel,
        in_specs=any_specs(2),
        out_specs=any_specs(6),
        out_shape=[all_rows, all_rows, act, act, act, jax.ShapeDtypeStruct((n_fsdp,) + own.shape, own.dtype)],
        scratch_shapes=[
            pltpu.VMEM((2, n_fsdp) + own.shape, own.dtype),
            pltpu.VMEM((3, n_own, features), own.dtype),
            pltpu.VMEM((2, 3, 2 * tokens, n_own), own.dtype),
            pltpu.VMEM((2, 2) + own.shape, own.dtype),
            pltpu.VMEM((n_fsdp,) + own.shape, own.dtype),
            pltpu.SemaphoreType.DMA((4,)),
        ]
        + dma_pair(6)
        + dma_pair(7)
        + dma_pair(2)
        + dma_pair(6)
        + dma_pair(8)
        + dma_pair(4)
        + [pltpu.SemaphoreType.DMA((2, 9))],
        compiler_params=params(6),
        cost_estimate=pl.CostEstimate(
            flops=12 * total * n_own * features, bytes_accessed=50 * 1024 * 1024, transcendentals=total * n_own
        ),
        name="ffn_rows",
    )(own, planes)


def ffn_weights(n_ctx, n_fsdp, partial, rows, rows_mirror, hidden, planes, n_own, chunk=256):
    blocks, _, tokens, features = rows.shape
    total = blocks * tokens
    steps = n_own // chunk
    group = max(1, 256 // tokens)
    half = features // 2
    sides = n_ctx // 4
    wide = half // sides
    fused = partial is not None

    def kernel(*refs):
        rows_ref, refs = refs[0], refs[1:]
        mirror_refs, refs = refs[: len(rows_mirror)], refs[len(rows_mirror) :]
        mirror_blocks = [ref.at[b] for ref in mirror_refs for b in range(ref.shape[0])]
        hidden_ref, grad_gate_ref, grad_up_ref, planes_ref, *refs = refs
        if fused:
            partial_ref, weight_ref, out_ref, *refs = refs
        else:
            weight_ref, *refs = refs
        mirror, (weights, weight_sems), refs = refs[:3], refs[3:5], refs[5:]
        chip, core, _, length = place(n_ctx)
        side = chip // sides
        step = pl.program_id(0)
        stages = []
        if fused:
            held, square_in, load, sq_s, sq_r = refs
            starts, *stages = corner_sum_stages(n_ctx, partial_ref, out_ref, held, square_in, load, (sq_s, sq_r))

        def fetch(at, slot):
            start = pl.multiple_of((core * steps + at) * chunk, chunk)
            return pltpu.make_async_copy(planes_ref.at[:, pl.ds(start, chunk)], weights.at[slot], weight_sems.at[slot])

        @pl.when(step == 0)
        def _():
            fetch(0, 0).start()
            if fused:
                greet(fsdp_peers(4, chip * 2 + core, lax.axis_index("fsdp")))
                for start in sum(starts, []):
                    start()

        @pl.when(step + 1 < steps)
        def _():
            fetch(step + 1, (step + 1) % 2).start()

        slot = step % 2
        fetch(step, slot).wait()
        gate_ref, up_ref, down_ref = (weights.at[slot, pl.ds(plane, 1)] for plane in range(3))
        for at in range(0, blocks, group):
            here = jnp.concatenate([ref[0] for ref in mirror_blocks[at : at + group]])
            back = jnp.concatenate([ref[1] for ref in mirror_blocks[at : at + group]])
            span = pl.ds(at * tokens, group * tokens)
            for out, value in zip(mirror, hidden_units(here, back, gate_ref, up_ref, down_ref)):
                out[span] = value

        lefts = ((grad_gate_ref, mirror[1], 0), (grad_up_ref, mirror[2], 0), (hidden_ref, mirror[0], 1))
        for plane, (left, left_mirror, which) in enumerate(lefts):
            left = left[...]
            left_mirror = left_mirror[...]
            for z in range(sides):
                cols = pl.ds(pl.multiple_of(side * half + z * wide, wide), wide)
                right = rows_ref[:, which, :, cols].reshape(total, wide)
                right_mirror = jnp.concatenate([ref[which, :, cols] for ref in mirror_blocks])
                weight_ref[z, plane] = low(
                    mm(left, right, CONTRACT_FIRST) + mm(left_mirror, right_mirror, CONTRACT_FIRST)
                )

        for at, stage in ((1, 0), (steps - 1, 1)):
            if stage < len(stages):

                @pl.when(step == min(at, steps - 1))
                def _():
                    stages[stage]()

    act_spec = pl.BlockSpec((total, chunk), lambda j: (0, j))
    once = dict(pipeline_mode=pl.Buffered(1))
    operands = [rows, *rows_mirror, *hidden, planes]
    in_specs = [whole_block(rows.shape, **once)] + [whole_block(part.shape, **once) for part in rows_mirror]
    in_specs += [act_spec] * 3 + any_specs(1)
    out_specs = [pl.BlockSpec((sides, 3, chunk, wide), lambda j: (0, 0, j, 0))]
    out_shape = [jax.ShapeDtypeStruct((sides, 3, n_own, wide), jnp.bfloat16)]
    scratch = [pltpu.VMEM((total, chunk), jnp.bfloat16)] * 3
    scratch += [pltpu.VMEM((2, 3, chunk, features), jnp.bfloat16), pltpu.SemaphoreType.DMA((2,))]
    if fused:
        operands.append(partial)
        in_specs += any_specs(1)
        out_specs.append(whole_block(partial.shape[-2:], **once))
        out_shape.append(jax.ShapeDtypeStruct(partial.shape[-2:], jnp.float32))
        scratch += corner_sum_scratch(partial)
    return pl.pallas_call(
        kernel,
        grid=(steps,),
        in_specs=in_specs,
        out_specs=out_specs,
        out_shape=out_shape,
        scratch_shapes=scratch,
        compiler_params=params(3) if fused else params(),
        cost_estimate=pl.CostEstimate(
            flops=12 * total * n_own * features, bytes_accessed=50 * 1024 * 1024, transcendentals=total * n_own
        ),
        name="ffn_weights",
    )(*operands)


def ffn_back(hidden, grad_gate, grad_up, planes, core, blocks, wide=512):
    total, n_own = hidden.shape
    features = planes.shape[2]
    tokens = total // blocks

    def kernel(core_ref, hidden_ref, grad_gate_ref, grad_up_ref, gate_ref, up_ref, down_ref, out_ref):
        out = mm(hidden_ref[...], down_ref[0])
        out_ref[:, 0] = low(out).reshape(blocks, tokens, wide)
        back = mm(grad_gate_ref[...], gate_ref[0]) + mm(grad_up_ref[...], up_ref[0])
        out_ref[:, 1] = low(back).reshape(blocks, tokens, wide)

    def weight_spec(plane):
        return pl.BlockSpec((1, n_own, wide), lambda j, core_ref: (plane, core_ref[0], j))

    act_spec = pl.BlockSpec((total, n_own), lambda j, core_ref: (0, 0), pipeline_mode=pl.Buffered(1))
    return pl.pallas_call(
        kernel,
        grid_spec=pltpu.PrefetchScalarGridSpec(
            num_scalar_prefetch=1,
            grid=(features // wide,),
            in_specs=[act_spec, act_spec, act_spec, weight_spec(0), weight_spec(1), weight_spec(2)],
            out_specs=pl.BlockSpec((blocks, 2, tokens, wide), lambda j, core_ref: (0, 0, 0, j)),
        ),
        out_shape=jax.ShapeDtypeStruct((blocks, 2, tokens, features), jnp.bfloat16),
        compiler_params=params(),
        cost_estimate=pl.CostEstimate(
            flops=6 * total * n_own * features, bytes_accessed=30 * 1024 * 1024, transcendentals=0
        ),
        name="ffn_back",
    )(core, hidden, grad_gate, grad_up, planes, planes, planes)


SPAN = 256


def ctx_peers(n_ctx):
    ctx = lax.axis_index("ctx")
    fsdp = lax.axis_index("fsdp")
    return [((ctx + j) % n_ctx, fsdp) for j in range(1, n_ctx)]


def deal(n_ctx, block, target, landed, sems, own_sem):
    ctx = lax.axis_index("ctx")
    fsdp = lax.axis_index("fsdp")

    @pl.when(target != ctx)
    def _():
        send(block, landed.at[ctx], sems, (target - ctx + n_ctx) % n_ctx, (target, fsdp)).start()

    @pl.when(target == ctx)
    def _():
        pltpu.make_async_copy(block, landed.at[ctx], own_sem).start()


def dealt(n_ctx, block, landed, sems, own_sem):
    ctx = lax.axis_index("ctx")
    pltpu.make_async_copy(block, landed.at[ctx], own_sem).wait()
    for j, peer in enumerate(ctx_peers(n_ctx)):
        copy = send(block, landed.at[(ctx + n_ctx - j - 1) % n_ctx], sems, j + 1, peer)
        copy.wait_send()
        copy.wait_recv()


def turn(values, cosine, sine):
    return values * cosine + pltpu.roll(values, HEAD_DIM // 2, 1) * sine


def attention_forward(n_ctx, rows, w_qkv, cosine, sine, place_column, place_row, heads):
    total, features = rows.shape
    own = heads * HEAD_DIM
    steps = total // SPAN
    length = total // n_ctx
    scale = HEAD_DIM ** (-0.5)

    def kernel(
        rows_ref, w_ref, cosine_ref, sine_ref, column_ref, row_ref,
        query_ref, key_ref, value_ref, out_ref, log_ref, landed, deal_s, deal_r, own_sem,
    ):
        step = pl.program_id(0)

        @pl.when(step == 0)
        def _():
            greet(ctx_peers(n_ctx))

        span = pl.ds(pl.multiple_of(step * SPAN, SPAN), SPAN)
        qkv = mm(rows_ref[...], w_ref[...])
        cosine = cosine_ref[span]
        sine = sine_ref[span]
        for h in range(heads):
            at = slice(h * HEAD_DIM, (h + 1) * HEAD_DIM)
            query_ref[span, at] = low(turn(qkv[:, at], cosine, sine))
            key_ref[span, at] = low(turn(qkv[:, own + h * HEAD_DIM : own + (h + 1) * HEAD_DIM], cosine, sine))
        value_ref[span] = low(qkv[:, 2 * own :])

        @pl.when(step == steps - 1)
        def _():
            @pl.loop(0, steps)
            def _(block):
                here = pl.ds(pl.multiple_of(block * SPAN, SPAN), SPAN)
                for h in range(heads):
                    at = slice(h * HEAD_DIM, (h + 1) * HEAD_DIM)
                    scores = mm(query_ref[here, at], key_ref[:, at], CONTRACT_LAST) * scale
                    scores = jnp.where(column_ref[here] >= row_ref[...], scores, MASKED)
                    highest = jnp.max(scores, axis=-1, keepdims=True)
                    exponent = jnp.exp(scores - highest)
                    sums = jnp.sum(exponent, axis=-1, keepdims=True)
                    out_ref[here, at] = low(mm(low(exponent * (1.0 / sums)), value_ref[:, at]))
                    log_ref[h, here] = highest + jnp.log(sums)
                for r in range(SPAN // length):
                    mine = out_ref.at[pl.ds(pl.multiple_of(block * SPAN + r * length, length), length)]
                    deal(n_ctx, mine, block * (SPAN // length) + r, landed, (deal_s, deal_r), own_sem)

            dealt(n_ctx, out_ref.at[pl.ds(0, length)], landed, (deal_s, deal_r), own_sem)

    act = jax.ShapeDtypeStruct((total, own), jnp.bfloat16)
    return pl.pallas_call(
        kernel,
        grid=(steps,),
        in_specs=[pl.BlockSpec((SPAN, features), lambda r: (r, 0))]
        + [whole_block(a.shape) for a in (w_qkv, cosine, sine, place_column, place_row)],
        out_specs=[whole_block((total, own))] * 4 + [whole_block((heads, total, 1))] + any_specs(1),
        out_shape=[act] * 4
        + [
            jax.ShapeDtypeStruct((heads, total, 1), jnp.float32),
            jax.ShapeDtypeStruct((n_ctx, length, own), jnp.bfloat16),
        ],
        scratch_shapes=dma_pair(n_ctx) + [pltpu.SemaphoreType.DMA],
        compiler_params=params(8),
        name="attention_forward",
    )(rows, w_qkv, cosine, sine, place_column, place_row)


def attention_backward(query, key, value, grad, logs, w_qkv, cosine, sine, place_column, place_row, heads):
    total, own = query.shape
    features = w_qkv.shape[0]
    steps = total // SPAN
    scale = HEAD_DIM ** (-0.5)

    def kernel(
        query_ref, key_ref, value_ref, grad_ref, log_ref, w_ref, cosine_ref, sine_ref, column_ref, row_ref,
        qkv_ref, out_ref, key_sum, value_sum,
    ):
        step = pl.program_id(0)

        @pl.when(step == 0)
        def _():
            for h in range(heads):
                at = slice(h * HEAD_DIM, (h + 1) * HEAD_DIM)
                key_sum[...] = jnp.zeros_like(key_sum)
                value_sum[...] = jnp.zeros_like(value_sum)

                @pl.loop(0, steps)
                def _(block):
                    here = pl.ds(pl.multiple_of(block * SPAN, SPAN), SPAN)
                    queries = query_ref[here, at]
                    grads = grad_ref[here, at]
                    scores = mm(queries, key_ref[:, at], CONTRACT_LAST) * scale
                    scores = jnp.where(column_ref[here] >= row_ref[...], scores, MASKED)
                    probs = jnp.exp(scores - log_ref[h, here])
                    probs_grad = mm(grads, value_ref[:, at], CONTRACT_LAST)
                    centre = jnp.sum(probs * probs_grad, axis=-1, keepdims=True)
                    scores_grad = low(probs * (probs_grad - centre))
                    query_grad = mm(scores_grad, key_ref[:, at]) * scale
                    qkv_ref[here, at] = low(turn(query_grad, cosine_ref[here], -sine_ref[here]))
                    key_sum[...] += mm(scores_grad, queries, CONTRACT_FIRST)
                    value_sum[...] += mm(low(probs), grads, CONTRACT_FIRST)

                qkv_ref[:, own + h * HEAD_DIM : own + (h + 1) * HEAD_DIM] = low(
                    turn(key_sum[...] * scale, cosine_ref[...], -sine_ref[...])
                )
                qkv_ref[:, 2 * own + h * HEAD_DIM : 2 * own + (h + 1) * HEAD_DIM] = low(value_sum[...])

        span = pl.ds(pl.multiple_of(step * SPAN, SPAN), SPAN)
        out_ref[...] = low(mm(qkv_ref[span], w_ref[...], CONTRACT_LAST))

    return pl.pallas_call(
        kernel,
        grid=(steps,),
        in_specs=[
            whole_block(a.shape)
            for a in (query, key, value, grad, logs, w_qkv, cosine, sine, place_column, place_row)
        ],
        out_specs=[whole_block((total, 3 * own)), pl.BlockSpec((SPAN, features), lambda r: (r, 0))],
        out_shape=[
            jax.ShapeDtypeStruct((total, 3 * own), jnp.bfloat16),
            jax.ShapeDtypeStruct((total, features), jnp.bfloat16),
        ],
        scratch_shapes=[pltpu.VMEM((total, HEAD_DIM), jnp.float32)] * 2,
        compiler_params=params(),
        name="attention_backward",
    )(query, key, value, grad, logs, w_qkv, cosine, sine, place_column, place_row)


ROWS = 32


def row_blocks(count, features):
    return pl.BlockSpec((count, ROWS, features), lambda r, *_: (0, r, 0))


def whole_block(shape, **more):
    zeros = (0,) * len(shape)
    return pl.BlockSpec(shape, lambda r, *_: zeros, **more)


def split(values):
    high = low(values)
    return (high, low(values - high.astype(jnp.float32)))


def connect_coefficients(values, dynamic_ref, static_ref, coef_ref, dyn_ref):
    rows = values[0].shape[0]
    lane = lax.broadcasted_iota(jnp.int32, (rows, 8), 1)
    stats, highs, lows = [], [], []
    for value in values:
        mean = jnp.mean(value, axis=-1, keepdims=True)
        centered = value - mean
        inverse = lax.rsqrt(jnp.mean(centered * centered, axis=-1, keepdims=True) + EPS)
        stats.append((mean, inverse))
        high, rest = split(centered * inverse)
        highs.append(high)
        lows.append(rest)
    dynamic, dynamic_rest = split(dynamic_ref[...])
    highs = jnp.concatenate(highs)
    projected = (
        mm(highs, dynamic, CONTRACT_LAST)
        + mm(highs, dynamic_rest, CONTRACT_LAST)
        + mm(jnp.concatenate(lows), dynamic, CONTRACT_LAST)
    )
    columns = []
    for i, (mean, inverse) in enumerate(stats):
        part = projected[i * rows : (i + 1) * rows]
        coefficient = jnp.tanh(part) + static_ref[i : i + 1]
        dyn_ref[i] = part
        coef_ref[i] = jnp.where(lane == 6, mean, jnp.where(lane == 7, inverse, coefficient))
        columns.append(coefficient)
    return columns


def connect_first(streams, dynamic, static):
    number, rows, features = streams.shape

    def kernel(streams_ref, dynamic_ref, static_ref, coef_ref, dyn_ref, low_ref):
        values = [streams_ref[i].astype(jnp.float32) for i in range(number)]
        columns = connect_coefficients(values, dynamic_ref, static_ref, coef_ref, dyn_ref)
        mixed = sum((columns[i][:, 1:2] * values[i] for i in range(number)))
        low_ref[...] = low(normalize(mixed)[0])

    small = jax.ShapeDtypeStruct((number, rows, 8), jnp.float32)
    return pl.pallas_call(
        kernel,
        grid=(rows // ROWS,),
        out_shape=(small, small, jax.ShapeDtypeStruct((rows, features), jnp.bfloat16)),
        in_specs=[row_blocks(number, features), whole_block(dynamic.shape), whole_block(static.shape)],
        out_specs=(
            row_blocks(number, 8),
            row_blocks(number, 8),
            pl.BlockSpec((ROWS, features), lambda r: (r, 0)),
        ),
        compiler_params=params(),
        name="connect_first",
    )(streams, dynamic, static)


def connect_middle(streams, coef, attended, w_mine, w_other, cotangent, dynamic, static, core_fsdp, where, depth):
    number, rows, features = streams.shape
    half = features // 2
    own = attended.shape[2]
    count = len(w_mine)

    def kernel(core_ref, streams_ref, coef_ref, attended_ref, *refs):
        weights, refs = refs[: 2 * count], refs[2 * count :]
        cotangent_ref, dynamic_ref, static_ref = refs[:3]
        first_ref, branch_ref, coef_two_ref, dyn_ref, own_ref, projected = refs[3:]
        step = pl.program_id(0)

        @pl.when(step == 0)
        def _():
            for side in range(2):
                total = 0.0
                for j, (d, offset) in enumerate(where):
                    for q in range(w_mine[j].shape[0] // own):
                        part = attended_ref[(core_ref[1] ^ d) * (depth // own) + offset // own + q]
                        total = total + mm(part, weights[side * count + j][q * own : (q + 1) * own])
                projected[core_ref[0] if side == 0 else 1 - core_ref[0]] = total

        span = pl.ds(pl.multiple_of(step * ROWS, ROWS), ROWS)
        branch = jnp.concatenate([projected[0, span], projected[1, span]], axis=1)
        branch_ref[...] = branch
        inputs = [streams_ref[i].astype(jnp.float32) for i in range(number)]
        outs = []
        for j in range(number):
            out = sum((coef_ref[i][:, 2 + j : 3 + j] * inputs[i] for i in range(number)))
            outs.append(out + coef_ref[j][:, 0:1] * branch)
            first_ref[j] = outs[-1]
        columns = connect_coefficients(outs, dynamic_ref, static_ref, coef_two_ref, dyn_ref)
        mixed = sum((columns[i][:, 1:2] * outs[i] for i in range(number)))
        own_ref[0] = low(normalize(mixed)[0])
        own_ref[1] = low(sum((columns[j][:, 0:1] * cotangent_ref[j].astype(jnp.float32) for j in range(number))))

    small = jax.ShapeDtypeStruct((number, rows, 8), jnp.float32)
    once = dict(pipeline_mode=pl.Buffered(1))
    return pl.pallas_call(
        kernel,
        grid_spec=pltpu.PrefetchScalarGridSpec(
            num_scalar_prefetch=1,
            grid=(rows // ROWS,),
            in_specs=[
                row_blocks(number, features),
                row_blocks(number, 8),
                whole_block(attended.shape, **once),
                *[whole_block(w.shape, **once) for w in w_mine + w_other],
                row_blocks(number, features),
                whole_block(dynamic.shape),
                whole_block(static.shape),
            ],
            out_specs=(
                row_blocks(number, features),
                pl.BlockSpec((ROWS, features), lambda r, *_: (r, 0)),
                row_blocks(number, 8),
                row_blocks(number, 8),
                row_blocks(2, features),
            ),
            scratch_shapes=[pltpu.VMEM((2, rows, half), jnp.float32)],
        ),
        out_shape=(
            jax.ShapeDtypeStruct((number, rows, features), jnp.float32),
            jax.ShapeDtypeStruct((rows, features), jnp.float32),
            small,
            small,
            jax.ShapeDtypeStruct((2, rows, features), jnp.bfloat16),
        ),
        compiler_params=params(),
        name="connect_middle",
    )(core_fsdp, streams, coef, attended, *w_mine, *w_other, cotangent, dynamic, static)


def attention_weights(rows, grads, attended, grad_cols):
    total, features = rows.shape
    parts, _, own = attended.shape
    wide = grads.shape[1]

    def kernel(rows_ref, grads_ref, attended_ref, cols_ref, out_ref):
        out_ref[:, :wide] = low(mm(rows_ref[...], grads_ref[...], CONTRACT_FIRST))
        out_ref[:, wide:] = low(mm(attended_ref[0], cols_ref[...], CONTRACT_FIRST))

    return pl.pallas_call(
        kernel,
        grid=(parts,),
        in_specs=[
            pl.BlockSpec((total, own), lambda k: (0, k)),
            whole_block(grads.shape),
            pl.BlockSpec((1, total, own), lambda k: (k, 0, 0)),
            whole_block(grad_cols.shape),
        ],
        out_specs=pl.BlockSpec((own, wide + own), lambda k: (k, 0)),
        out_shape=jax.ShapeDtypeStruct((features, wide + own), jnp.bfloat16),
        compiler_params=params(),
        cost_estimate=pl.CostEstimate(
            flops=2 * total * features * (wide + own), bytes_accessed=16 * 1024 * 1024, transcendentals=0
        ),
        name="attention_weights",
    )(rows, grads, attended, grad_cols)


def flip(index, bits, count):
    result = index
    bit = 1
    while bit < count:
        if bits & bit:
            result = result + bit - 2 * bit * (index // bit % 2)
        bit *= 2
    return result


def project_back(n_ctx, n_fsdp, grad, w_mine, w_other, where, depth):
    rows, features = grad.shape
    half = features // 2
    count = len(w_mine)
    own = features // n_ctx

    def kernel(grad_ref, *refs):
        weights, refs = refs[: 2 * count], refs[2 * count :]
        landed, cols_ref, outs, deal_s, deal_r, own_sem = refs
        _, core, fsdp, _ = place(n_ctx)
        greet(ctx_peers(n_ctx))
        first = grad_ref[:, pl.ds(pl.multiple_of(core * half, half), half)]
        second = grad_ref[:, pl.ds(pl.multiple_of((1 - core) * half, half), half)]
        for j, (d, offset) in enumerate(where):
            out = low(
                mm(first, weights[j][...], CONTRACT_LAST) + mm(second, weights[count + j][...], CONTRACT_LAST)
            )
            for q in range(w_mine[j].shape[0] // own):
                at = flip(fsdp, d, n_fsdp) * (depth // own) + offset // own + q
                outs[at] = out[:, q * own : (q + 1) * own]
                deal(n_ctx, outs.at[at], at, landed, (deal_s, deal_r), own_sem)
        for index in range(n_ctx):
            cols_ref[index] = grad_ref[:, index * own : (index + 1) * own]
        dealt(n_ctx, outs.at[0], landed, (deal_s, deal_r), own_sem)

    shape = (n_ctx, rows, own)
    return pl.pallas_call(
        kernel,
        in_specs=[pl.BlockSpec(memory_space=pltpu.VMEM)] * (1 + 2 * count),
        out_specs=any_specs(1) + [pl.BlockSpec(memory_space=pltpu.VMEM)],
        out_shape=[jax.ShapeDtypeStruct(shape, grad.dtype)] * 2,
        scratch_shapes=[pltpu.VMEM(shape, grad.dtype)] + dma_pair(n_ctx) + [pltpu.SemaphoreType.DMA],
        compiler_params=params(9),
        name="project_back",
    )(grad, *w_mine, *w_other)


def connect_back(values, coef, dyn, branch, grads, grad_normed, dynamic, means, coef_before=None, offset=0):
    number, rows, features = values.shape
    steps = rows // ROWS
    more = coef_before is not None

    def kernel(*refs):
        values_ref, coef_ref, dyn_ref, branch_ref, grads_ref, normed_ref, dynamic_ref, means_ref = refs[:8]
        refs = refs[8:]
        if more:
            before_ref, refs = refs[0], refs[1:]
        out_ref, dynamic_out, static_out = refs[:3]
        if more:
            forward_ref, grad_low_ref = refs[3:5]
        step = pl.program_id(0)

        @pl.when(step == 0)
        def _():
            dynamic_out[...] = jnp.zeros_like(dynamic_out)
            static_out[...] = jnp.zeros_like(static_out)

        branch = branch_ref[...]
        grads = [grads_ref[j].astype(jnp.float32) for j in range(number)]
        mixed = sum((coef_ref[i][:, 1:2] * values_ref[i].astype(jnp.float32) for i in range(number)))
        normed, inverse = normalize(mixed)
        grad_mixed = normalize_back(normed, inverse, normed_ref[...])
        lane = lax.broadcasted_iota(jnp.int32, (ROWS, 8), 1)
        pre_grads, highs, lows = [], [], []
        for i in range(number):
            value = values_ref[i].astype(jnp.float32)
            columns = [grads[i] * branch, grad_mixed * value] + [grads[j] * value for j in range(number)]
            coef_grad = jnp.zeros((ROWS, 8), jnp.float32)
            for k, column in enumerate(columns):
                coef_grad = jnp.where(lane == k, jnp.sum(column, axis=-1, keepdims=True), coef_grad)
            static_out[i : i + 1] += jnp.sum(coef_grad, axis=0, keepdims=True)
            part = jnp.tanh(dyn_ref[i])
            pre_grads.append(coef_grad * (1.0 - part * part))
            high, rest = split((value - coef_ref[i][:, 6:7]) * coef_ref[i][:, 7:8])
            highs.append(high)
            lows.append(rest)
        pre, pre_rest = split(jnp.concatenate(pre_grads))
        dynamic, dynamic_rest = split(dynamic_ref[...])
        normed_grads = mm(
            jnp.concatenate([pre, pre_rest, pre], axis=1), jnp.concatenate([dynamic, dynamic, dynamic_rest], axis=0)
        )
        highs = jnp.concatenate(highs)
        dynamic_out[...] += (
            mm(pre, highs, CONTRACT_FIRST)
            + mm(pre_rest, highs, CONTRACT_FIRST)
            + mm(pre, jnp.concatenate(lows), CONTRACT_FIRST)
        )
        befores = 0.0
        for i in range(number):
            coef = coef_ref[i]
            mean_grad = jnp.sum(pre_grads[i] * means_ref[...], axis=-1, keepdims=True)
            inner = jnp.sum(pre_grads[i] * dyn_ref[i], axis=-1, keepdims=True) / features
            normed = (values_ref[i].astype(jnp.float32) - coef[:, 6:7]) * coef[:, 7:8]
            out = coef[:, 7:8] * (normed_grads[i * ROWS : (i + 1) * ROWS] - mean_grad - normed * inner)
            out = out + coef[:, 1:2] * grad_mixed
            for j in range(number):
                out = out + coef[:, 2 + j : 3 + j] * grads[j]
            out_ref[i] = out
            if more:
                befores = befores + before_ref[i][:, 0:1] * out
        if more:
            grad_low_ref[...] = low(befores)
            for j in range(number):
                out = coef_ref[j][:, 0:1] * branch
                for i in range(number):
                    out = out + coef_ref[i][:, 2 + j : 3 + j] * values_ref[i].astype(jnp.float32)
                forward_ref[j] = low(out)

    rows_spec = pl.BlockSpec((ROWS, features), lambda r: (r, 0))
    out_shape = [
        jax.ShapeDtypeStruct((number, rows, features), jnp.float32),
        jax.ShapeDtypeStruct((8, features), jnp.float32),
        jax.ShapeDtypeStruct((8, 8), jnp.float32),
    ]
    out_specs = [row_blocks(number, features), whole_block((8, features)), whole_block((8, 8))]
    operands = [values, coef, dyn, branch, grads, grad_normed, dynamic, means]
    in_specs = [
        row_blocks(number, features),
        row_blocks(number, 8),
        row_blocks(number, 8),
        rows_spec,
        row_blocks(number, features),
        pl.BlockSpec((ROWS, features), lambda r: (offset // ROWS + r, 0)),
        whole_block(dynamic.shape),
        whole_block(means.shape),
    ]
    if more:
        operands.append(coef_before)
        in_specs.append(row_blocks(number, 8))
        out_shape.append(jax.ShapeDtypeStruct((number, rows, features), jnp.bfloat16))
        out_specs.append(row_blocks(number, features))
        out_shape.append(jax.ShapeDtypeStruct((rows, features), jnp.bfloat16))
        out_specs.append(rows_spec)
    return pl.pallas_call(
        kernel,
        grid=(steps,),
        in_specs=in_specs,
        out_specs=out_specs,
        out_shape=out_shape,
        compiler_params=params(),
        name="connect_back",
    )(*operands)


def local(n_ctx, n_fsdp, streams, w_attn, w_ffn, hc_dynamic, hc_static, cotangent, pair_order):
    number = streams.shape[1]
    length = streams.shape[2]
    features = streams.shape[3]
    size = HEAD_DIM
    own = features // n_ctx
    heads = own // size
    rows = length * n_ctx
    own_rows = w_attn.shape[0]
    ctx = lax.axis_index("ctx")
    fsdp = lax.axis_index("fsdp")
    core = ctx % 2
    chips = n_ctx // 2
    core_index = jnp.reshape(core, (1,)).astype(jnp.int32)

    def in_order(mine, other, axis):
        return jnp.where(
            core == 0, jnp.concatenate([mine, other], axis=axis), jnp.concatenate([other, mine], axis=axis)
        )


    w_own = lax.dynamic_slice_in_dim(w_attn, ctx * own, own, 2)[:, 0:3].reshape(own_rows, 3 * own)
    w_qkv = gather(w_own, "fsdp")
    half = features // 2
    w_half = lax.dynamic_slice_in_dim(w_attn, core * half, half, 2)[:, 3]
    siblings = [(i, i ^ 1) for i in range(n_ctx)]
    core_fsdp = jnp.stack([core, fsdp]).astype(jnp.int32)

    def exchange(values, most=0):
        return [values] + [
            lax.ppermute(values, "fsdp", [(i, i ^ d) for i in range(n_fsdp)])
            for d in range(1, most + 1 if most else n_fsdp)
        ]

    def swap(blocks):
        return [lax.ppermute(block, "ctx", siblings) for block in blocks]


    positions = block_positions(pair_order, length)
    frequency = THETA ** (-(jnp.arange(size // 2, dtype=jnp.float32) * 2.0) / size)
    angles = positions.astype(jnp.float32)[:, None] * jnp.concatenate([frequency, frequency])[None, :]
    signs = jnp.where(jnp.arange(size) < size // 2, -1.0, 1.0)
    tables = (jnp.cos(angles), jnp.sin(angles) * signs[None, :], positions[:, None], positions[None, :])

    dynamics = jnp.pad(hc_dynamic, ((0, 0), (0, 2), (0, 0)))
    means = jnp.mean(dynamics, axis=-1)
    statics = jnp.pad(hc_static, ((0, 0), (0, 0), (0, 2)))
    coef_one, dyn_one, attn_low = connect_first(streams[0], dynamics[0], statics[0])
    attn_low, w_half = lax.optimization_barrier((attn_low, w_half))
    w_out_mine = exchange(w_half, 2 if n_fsdp == 4 else 0)
    attn_all = line_rows(n_ctx, attn_low).reshape(rows, features)
    w_out_where = [(d, 0) for d in range(len(w_out_mine))]
    attn_all, *w_out_mine = lax.optimization_barrier((attn_all, *w_out_mine))
    w_out_other = swap(w_out_mine)
    if n_fsdp == 4:
        middle = own_rows // 2
        corners = [
            lax.ppermute(w_out_mine[1][:middle], "fsdp", [(i, i ^ 2) for i in range(4)]),
            lax.ppermute(w_out_mine[2][middle:], "fsdp", [(i, i ^ 1) for i in range(4)]),
        ]
        w_out_where += [(3, 0), (3, middle)]
    query, key, value, attended, logs, attended_rows = attention_forward(n_ctx, attn_all, w_qkv, *tables, heads)
    if n_fsdp == 4:
        attended, *corners = lax.optimization_barrier((attended, *corners))
        w_out_mine += corners
        w_out_other += swap(corners)

    first_out, attn_branch, coef_two, dyn_two, ffn_own = connect_middle(
        streams[0], coef_one, attended_rows, w_out_mine, w_out_other, cotangent[0], dynamics[1], statics[1], core_fsdp,
        w_out_where, own_rows,
    )
    ffn_own = ffn_own.reshape(2 * length, features)

    planes = jnp.moveaxis(w_ffn, 1, 0)
    n_own = planes.shape[1] // 2
    blocks = 2 * n_fsdp
    if n_fsdp == 4:
        ffn_all, mirror_rows, *hidden, sums = ffn_rows(n_ctx, ffn_own, planes, n_own)
        ffn_all, mirror_rows = (part.reshape(blocks, 2, length, features) for part in (ffn_all, mirror_rows))
        mirror_rows = [mirror_rows]
        attended, sums = lax.optimization_barrier((attended, sums))
        attended_all = gather(attended, "ctx").reshape(n_ctx, rows, own)
        *weight_parts, sums = ffn_weights(n_ctx, n_fsdp, sums, ffn_all, mirror_rows, hidden, planes, n_own)
    else:
        ffn_mirror = lax.ppermute(ffn_own, "ctx", [(i, n_ctx - 2 - i + 2 * (i % 2)) for i in range(n_ctx)])
        ffn_all = square_core_gather(n_ctx, n_fsdp, ffn_own).reshape(blocks, 2, length, features)
        attended_all = gather(attended, "ctx").reshape(n_ctx, rows, own)
        mirror_mine = exchange(ffn_mirror)
        hidden = ffn_forward(ffn_all, planes, core_index, n_own)
        sums = ffn_back(*hidden, planes, core_index, blocks)
        mirror_rows = [part.reshape(1, 2, length, features) for part in mirror_mine + swap(mirror_mine)]
        sums = square_sum(n_ctx, n_fsdp, sums.reshape(2, n_fsdp, 2 * length, features))
        weight_parts = ffn_weights(n_ctx, n_fsdp, None, ffn_all, mirror_rows, hidden, planes, n_own)
    sides = chips // 2
    lines = [[2 * (sides * side + i) + j for i in range(sides)] for side in range(2) for j in range(2)]
    weight_cols = lax.psum_scatter(weight_parts[0], "ctx", scatter_dimension=0, axis_index_groups=lines)

    grad_first, dynamic_grad_two, static_grad_two, streams_out, grad_attn = connect_back(
        first_out, coef_two, dyn_two, sums, cotangent[0], sums, dynamics[1], means[1:], coef_one, length
    )
    grad_heads, grad_cols = project_back(n_ctx, n_fsdp, grad_attn, w_out_mine, w_out_other, w_out_where, own_rows)
    grad_heads = grad_heads.reshape(rows, own)
    grad_heads, grad_cols = lax.optimization_barrier((grad_heads, grad_cols))
    grad_cols = lax.all_to_all(grad_cols, "ctx", 0, 0, tiled=True).reshape(rows, own)
    qkv_grad, attn_part = attention_backward(query, key, value, grad_heads, logs, w_qkv, *tables, heads)
    attn_part = attn_part.reshape(n_ctx, length, features)
    if n_fsdp == 4:
        grad_attn_normed, attn_grad = attention_sums(n_ctx, attn_part, attn_all, qkv_grad, attended_all, grad_cols)
    else:
        grad_attn_normed = line_sum(n_ctx, attn_part)
        attn_grad = scatter(attention_weights(attn_all, qkv_grad, attended_all, grad_cols), "fsdp").astype(jnp.float32)
    grad_attn_normed, weight_cols = lax.optimization_barrier((grad_attn_normed, weight_cols))
    mine = lax.dynamic_slice_in_dim(weight_cols, core * own, own, 2)
    other = lax.dynamic_slice_in_dim(weight_cols, (1 - core) * own, own, 2)
    other = lax.ppermute(other, "ctx", siblings)
    ffn_grad = jnp.moveaxis(in_order(mine, other, 1), 0, 1).astype(jnp.float32)
    grad_inputs, dynamic_grad_one, static_grad_one = connect_back(
        streams[0], coef_one, dyn_one, attn_branch, grad_first, grad_attn_normed, dynamics[0], means[:1]
    )
    static_grads = jnp.concatenate([static_grad_one[:number, :6].reshape(1, -1), static_grad_two[:number, :6].reshape(1, -1)])
    small = jnp.concatenate(
        [
            dynamic_grad_one[:6],
            dynamic_grad_two[:6],
            jnp.pad(static_grads, ((0, 2), (0, features - 6 * number))),
        ]
    )
    small = sum_everywhere(n_ctx, n_fsdp, small.reshape(n_ctx, 8, -1))
    small = small.reshape(16, features)
    attn_grad = attn_grad.reshape(own_rows, 4, own)
    dynamic_total = small[:12].reshape(2, 6, features)
    static_total = small[12:14, : 6 * number].reshape(2, number, 6)
    return (streams_out[None], grad_inputs[None], attn_grad, ffn_grad, dynamic_total, static_total)


def solution(mesh):
    return jax.shard_map(
        functools.partial(local, mesh.shape["ctx"], mesh.shape["fsdp"]),
        mesh=mesh,
        in_specs=(
            P("fsdp", None, "ctx", None),
            P("fsdp", None, None),
            P("fsdp", None, None),
            P(),
            P(),
            P("fsdp", None, "ctx", None),
            P(),
        ),
        out_specs=(
            P("fsdp", None, "ctx", None),
            P("fsdp", None, "ctx", None),
            P("fsdp", None, "ctx"),
            P("fsdp", None, "ctx"),
            P(),
            P(),
        ),
        check_vma=False,
    )
```

```python
import functools

import jax
import jax.numpy as jnp
from jax import lax
from jax.experimental import pallas as pl
from jax.experimental.pallas import tpu as pltpu
from jax.sharding import PartitionSpec as P

HEADS = 16
HEAD_DIM = 128


EPS = 1e-05
THETA = 10000.0
HIGH = lax.Precision.HIGHEST
MASKED = -1e30
CONTRACT_LAST = (((1,), (1,)), ((), ()))
CONTRACT_FIRST = (((0,), (0,)), ((), ()))


def normalize(values):
    centered = values - jnp.mean(values, axis=-1, keepdims=True)
    inverse = lax.rsqrt(jnp.mean(centered * centered, axis=-1, keepdims=True) + EPS)
    return (centered * inverse, inverse)


def normalize_back(normed, inverse, gradient):
    inner = jnp.mean(gradient * normed, axis=-1, keepdims=True)
    return inverse * (gradient - jnp.mean(gradient, axis=-1, keepdims=True) - normed * inner)


def block_positions(pair_order, length):
    half_size = length // 2
    offsets = jnp.arange(half_size, dtype=jnp.int32)
    mirror = 2 * pair_order.shape[0] - 1 - pair_order
    first_half = pair_order[:, None] * half_size + offsets[None, :]
    second_half = mirror[:, None] * half_size + offsets[None, :]
    return jnp.concatenate([first_half, second_half], axis=1).reshape(-1)


def low(values):
    return values.astype(jnp.bfloat16)


def mm(a, b, dims=None):
    if dims is None:
        return jnp.dot(a, b, preferred_element_type=jnp.float32)
    return lax.dot_general(a, b, dims, preferred_element_type=jnp.float32)


def gather(values, axis, dim=0):
    return lax.all_gather(values, axis, axis=dim, tiled=True)


def scatter(values, axis, dim=0):
    return lax.psum_scatter(values, axis, scatter_dimension=dim, tiled=True)


MESH = pl.DeviceIdType.MESH
VMEM_LIMIT = 60 * 1024 * 1024


def place(n_ctx):
    ctx = lax.axis_index("ctx")
    return (ctx // 2, ctx % 2, lax.axis_index("fsdp"), n_ctx // 2)


def greet(peers):
    barrier = pltpu.get_barrier_semaphore()
    for peer in peers:
        pl.semaphore_signal(barrier, inc=1, device_id=peer, device_id_type=MESH)
    pl.semaphore_wait(barrier, len(peers))


def send(source, target, sems, index, peer):
    return pltpu.make_async_remote_copy(
        src_ref=source,
        dst_ref=target,
        send_sem=sems[0].at[index],
        recv_sem=sems[1].at[index],
        device_id=peer,
        device_id_type=MESH,
    )


def fsdp_neighbours(fsdp):
    first = fsdp + 1 - 2 * (fsdp % 2)
    second = (fsdp + 2) % 4
    return (first, second, (first + 2) % 4)


def fsdp_peers(n_fsdp, ctx, fsdp):
    if n_fsdp == 4:
        first, second, _ = fsdp_neighbours(fsdp)
        return [(ctx, first), (ctx, second)]
    return [(ctx, (fsdp + j) % n_fsdp) for j in range(1, n_fsdp)]


def line_peers(chip, core, fsdp, length):
    return [
        (chip * 2 + 1 - core, fsdp),
        ((chip + 1) % length * 2 + core, fsdp),
        ((chip + length - 1) % length * 2 + core, fsdp),
    ]


def line_gather(own_ref, all_ref, sems, where):
    chip, core, fsdp, length = where
    right_sems, left_sems, core_sems = sems
    sibling = (chip * 2 + 1 - core, fsdp)
    right = ((chip + 1) % length * 2 + core, fsdp)
    left = ((chip + length - 1) % length * 2 + core, fsdp)

    def block(index):
        return all_ref.at[(index + length) % length * 2 + core]

    def pass_on(index, source):
        return send(source, block(index), core_sems, (index + length) % length, sibling)

    pass_on(chip, own_ref).start()
    for step in range(length - 1):
        for sign, peer, way in ((-1, right, right_sems), (1, left, left_sems)):
            at = chip + sign * step
            held = (at >= 0) & (at < length)
            if step > 0:

                @pl.when(held)
                def _():
                    send(block(at), block(at), way, step - 1, peer).wait_recv()
                    pass_on(at, block(at)).start()

            more = (chip < length - 1) if sign < 0 else (chip > 0)

            @pl.when(held & more)
            def _():
                send(own_ref if step == 0 else block(at), block(at), way, step, peer).start()

        yield
    last = length - 1
    for sign, peer, way in ((-1, right, right_sems), (1, left, left_sems)):
        at = chip + sign * last

        @pl.when((at >= 0) & (at < length))
        def _():
            send(block(at), block(at), way, last - 1, peer).wait_recv()
            pass_on(at, block(at)).start()

    yield
    for step in range(length - 1):
        for sign, peer, way in ((-1, right, right_sems), (1, left, left_sems)):
            at = chip + sign * step
            more = (chip < length - 1) if sign < 0 else (chip > 0)

            @pl.when((at >= 0) & (at < length) & more)
            def _():
                send(block(at), block(at), way, step, peer).wait_send()

    for index in range(length):
        pass_on(index, block(index)).wait_send()
        other = all_ref.at[index * 2 + 1 - core]
        send(other, other, core_sems, index, sibling).wait_recv()


def square_gather(own_ref, all_ref, sems, ctx, fsdp, n_fsdp, passed=None):
    if n_fsdp != 4:
        copies = [
            send(own_ref, all_ref.at[fsdp], sems, j - 1, (ctx, (fsdp + j) % n_fsdp)) for j in range(1, n_fsdp)
        ]
        for copy in copies:
            copy.start()
        yield
        for j, copy in enumerate(copies):
            copy.wait()
            if passed:
                passed(all_ref.at[(fsdp + n_fsdp - j - 1) % n_fsdp], (fsdp + n_fsdp - j - 1) % n_fsdp, None, j)
        return
    first, second, corner = fsdp_neighbours(fsdp)
    half = own_ref.shape[0] // 2
    top, low_half = pl.ds(0, half), pl.ds(half, half)
    to_first, to_second = (ctx, first), (ctx, second)

    def copy(index, owner, part, peer, source=None):
        source = all_ref.at[owner, part] if source is None else source
        return send(source, all_ref.at[owner, part], sems, index, peer)

    starts = [
        copy(0, fsdp, top, to_first, own_ref.at[top]),
        copy(1, fsdp, low_half, to_second, own_ref.at[low_half]),
        copy(2, fsdp, low_half, to_first, own_ref.at[low_half]),
        copy(3, fsdp, top, to_second, own_ref.at[top]),
        copy(4, first, top, to_second),
        copy(5, second, low_half, to_first),
    ]
    arrivals = [
        (0, first, top),
        (1, second, low_half),
        (2, first, low_half),
        (3, second, top),
        (4, corner, top),
        (5, corner, low_half),
    ]
    for each in starts[:4]:
        each.start()
    yield
    for index, owner, part in arrivals:
        copy(index, owner, part, to_first).wait_recv()
        if index < 2:
            starts[4 + index].start()
        if passed:
            passed(all_ref.at[owner, part], owner, part, index)
        yield
    for each in starts:
        each.wait_send()


def run_all(*parts):
    parts = list(parts)
    while parts:
        for part in list(parts):
            try:
                next(part)
            except StopIteration:
                parts.remove(part)


def dma_pair(count):
    return [pltpu.SemaphoreType.DMA((count,)), pltpu.SemaphoreType.DMA((count,))]


def any_specs(count):
    return [pl.BlockSpec(memory_space=pl.ANY)] * count


def params(collective_id=None, **more):
    if collective_id is not None:
        more.update(collective_id=collective_id, has_side_effects=True)
    return pltpu.CompilerParams(vmem_limit_bytes=VMEM_LIMIT, **more)


def passing(own_ref, all_ref, sems, core, fsdp, sibling):
    handed = [send(own_ref, all_ref.at[core, fsdp], sems, 0, sibling)]
    handed[0].start()
    arriving = [send(own_ref, all_ref.at[1 - core, fsdp], sems, 0, sibling)]

    def passed(source, owner, part, index):
        for side, copies in ((core, handed), (1 - core, arriving)):
            target = all_ref.at[side, owner] if part is None else all_ref.at[side, owner, part]
            copies.append(send(source, target, sems, index + 1, sibling))
        handed[-1].start()

    def finish():
        for out, back in zip(handed, arriving):
            out.wait_send()
            back.wait_recv()

    return (passed, finish)


def line_rows(n_ctx, rows):
    def kernel(rows_ref, all_rows, right_s, right_r, left_s, left_r, core_s, core_r, own):
        where = place(n_ctx)
        chip, core, fsdp, length = where
        greet(line_peers(*where))
        mine = pltpu.make_async_copy(rows_ref, all_rows.at[chip * 2 + core], own)
        mine.start()
        run_all(line_gather(rows_ref, all_rows, ((right_s, right_r), (left_s, left_r), (core_s, core_r)), where))
        mine.wait()

    length = n_ctx // 2
    return pl.pallas_call(
        kernel,
        out_shape=jax.ShapeDtypeStruct((n_ctx,) + rows.shape, rows.dtype),
        in_specs=any_specs(1),
        out_specs=pl.BlockSpec(memory_space=pl.ANY),
        scratch_shapes=dma_pair(length) + dma_pair(length) + dma_pair(length) + [pltpu.SemaphoreType.DMA],
        compiler_params=params(0),
        name="line_rows",
    )(rows)


def square_core_gather(n_ctx, n_fsdp, rows):
    def kernel(rows_ref, all_ref, sq_s, sq_r, core_s, core_r, own):
        chip, core, fsdp, _ = place(n_ctx)
        ctx = chip * 2 + core
        sibling = (chip * 2 + 1 - core, fsdp)
        greet([sibling] + fsdp_peers(n_fsdp, ctx, fsdp))
        mine = pltpu.make_async_copy(rows_ref, all_ref.at[core, fsdp], own)
        mine.start()
        passed, finish = passing(rows_ref, all_ref, (core_s, core_r), core, fsdp, sibling)
        run_all(square_gather(rows_ref, all_ref.at[core], (sq_s, sq_r), ctx, fsdp, n_fsdp, passed))
        finish()
        mine.wait()

    return pl.pallas_call(
        kernel,
        out_shape=jax.ShapeDtypeStruct((2, n_fsdp) + rows.shape, rows.dtype),
        in_specs=any_specs(1),
        out_specs=pl.BlockSpec(memory_space=pl.ANY),
        scratch_shapes=dma_pair(max(6, n_fsdp)) + dma_pair(max(7, n_fsdp)) + [pltpu.SemaphoreType.DMA],
        compiler_params=params(1),
        name="square_core_gather",
    )(rows)


def add_into(target, *sources, chunk=64):
    @pl.loop(0, target.shape[0] // chunk)
    def _(step):
        rows = pl.ds(pl.multiple_of(step * chunk, chunk), chunk)
        total = target[rows].astype(jnp.float32)
        for source in sources:
            total = total + source[rows].astype(jnp.float32)
        target[rows] = total.astype(target.dtype)


def square_sum_stages(n_ctx, n_fsdp, partial_ref, out_ref, held, core_in, square_in, load, core_sems, sems):
    rows = partial_ref.shape[-2]
    half = rows // 2
    chip, core, fsdp, _ = place(n_ctx)
    ctx = chip * 2 + core
    sibling = (chip * 2 + 1 - core, fsdp)
    if n_fsdp == 4:
        first, second, corner = fsdp_neighbours(fsdp)
        order = [corner, first, second, fsdp]
    else:
        order = [(fsdp + j) % n_fsdp for j in range(1, n_fsdp + 1)]
    mine = [
        pltpu.make_async_copy(partial_ref.at[core, owner], held.at[owner], load.at[j])
        for j, owner in enumerate(order)
    ]
    others = [
        send(partial_ref.at[1 - core, owner], core_in.at[owner], core_sems, j, sibling)
        for j, owner in enumerate(order)
    ]

    def ready(j):
        mine[j].wait()
        others[j].wait_recv()
        add_into(held.at[order[j]], core_in.at[order[j]])

    def total(parts, sources):
        @pl.loop(0, parts[1] // 64)
        def _(step):
            at = pl.ds(pl.multiple_of(parts[0] + step * 64, 64), 64)
            from_at = pl.ds(pl.multiple_of(step * 64, 64), 64)
            value = held[fsdp, at].astype(jnp.float32)
            for j in sources:
                value = value + square_in[j, from_at].astype(jnp.float32)
            out_ref[at] = value

    def begin():
        greet([sibling] + fsdp_peers(n_fsdp, ctx, fsdp))
        for j in range(n_fsdp):
            others[j].start()
            mine[j].start()

    if n_fsdp != 4:
        copies = [
            send(held.at[order[j]], square_in.at[j], sems, j, (ctx, order[j])) for j in range(n_fsdp - 1)
        ]

        def spread():
            for j in range(n_fsdp):
                ready(j)
                if j < n_fsdp - 1:
                    copies[j].start()

        def finish():
            for copy in copies:
                copy.wait()
            total((0, rows), range(n_fsdp - 1))
            for each in others:
                each.wait_send()

        return [begin, spread, finish]

    top, low_half = pl.ds(0, half), pl.ds(half, half)
    to_first, to_second = (ctx, first), (ctx, second)

    def copy(index, owner, part, peer):
        return send(held.at[owner, part], square_in.at[index], sems, index, peer)

    copies = [
        copy(0, corner, top, to_first),
        copy(1, corner, low_half, to_second),
        copy(2, first, top, to_first),
        copy(3, second, low_half, to_second),
        copy(4, second, top, to_second),
        copy(5, first, low_half, to_first),
    ]

    def spread():
        ready(0)
        copies[0].start()
        copies[1].start()
        ready(1)
        copies[2].start()
        ready(2)
        copies[3].start()
        ready(3)

    def pass_on():
        copies[0].wait_recv()
        add_into(held.at[second, top], square_in.at[0])
        copies[4].start()
        copies[1].wait_recv()
        add_into(held.at[first, low_half], square_in.at[1])
        copies[5].start()

    def finish():
        for j in range(2, 6):
            copies[j].wait_recv()
        total((0, half), (2, 4))
        total((half, half), (3, 5))
        for each in copies:
            each.wait_send()
        for each in others:
            each.wait_send()

    return [begin, spread, pass_on, finish]


def corner_sum_stages(n_ctx, partial_ref, out_ref, held, square_in, load, sems):
    half = partial_ref.shape[1] // 2
    chip, core, fsdp, _ = place(n_ctx)
    ctx = chip * 2 + core
    first, second, corner = fsdp_neighbours(fsdp)
    top, low_half = pl.ds(0, half), pl.ds(half, half)
    to_first, to_second = (ctx, first), (ctx, second)

    def copy(index, source, peer):
        return send(source, square_in.at[index], sems, index, peer)

    copies = [
        copy(0, partial_ref.at[corner, top], to_first),
        copy(1, partial_ref.at[corner, low_half], to_second),
        copy(2, partial_ref.at[first, top], to_first),
        copy(3, partial_ref.at[second, low_half], to_second),
        copy(4, held.at[0], to_second),
        copy(5, held.at[1], to_first),
    ]
    mine = [
        pltpu.make_async_copy(partial_ref.at[second, top], held.at[0], load.at[0]),
        pltpu.make_async_copy(partial_ref.at[first, low_half], held.at[1], load.at[1]),
        pltpu.make_async_copy(partial_ref.at[fsdp, top], held.at[2], load.at[2]),
        pltpu.make_async_copy(partial_ref.at[fsdp, low_half], held.at[3], load.at[3]),
    ]

    starts = [
        [copies[0].start, copies[1].start],
        [copies[2].start, mine[1].start],
        [copies[3].start, mine[0].start],
        [mine[2].start, mine[3].start],
    ]

    def pass_on():
        for index in range(2):
            mine[index].wait()
            copies[index].wait_recv()
            add_into(held.at[index], square_in.at[index])
            copies[4 + index].start()

    def finish():
        for part, sources in ((0, (2, 4)), (1, (3, 5))):
            mine[2 + part].wait()
            for j in sources:
                copies[j].wait_recv()

            @pl.loop(0, half // 64)
            def _(step):
                at = pl.ds(pl.multiple_of(step * 64, 64), 64)
                value = held[2 + part, at].astype(jnp.float32)
                for j in sources:
                    value = value + square_in[j, at].astype(jnp.float32)
                out_ref[pl.ds(pl.multiple_of(part * half + step * 64, 64), 64)] = value

        for each in copies:
            each.wait_send()

    return [starts, pass_on, finish]


def corner_sum_scratch(partial):
    _, rows, columns = partial.shape
    return [
        pltpu.VMEM((4, rows // 2, columns), partial.dtype),
        pltpu.VMEM((6, rows // 2, columns), partial.dtype),
        pltpu.SemaphoreType.DMA((4,)),
    ] + dma_pair(6)


def square_sum_scratch(n_fsdp, partial):
    rows, columns = partial.shape[-2:]
    pieces = (6, rows // 2, columns) if n_fsdp == 4 else (n_fsdp - 1, rows, columns)
    return (
        [
            pltpu.VMEM((n_fsdp, rows, columns), partial.dtype),
            pltpu.VMEM((n_fsdp, rows, columns), partial.dtype),
            pltpu.VMEM(pieces, partial.dtype),
            pltpu.SemaphoreType.DMA((n_fsdp,)),
        ]
        + dma_pair(n_fsdp)
        + dma_pair(max(6, n_fsdp))
    )


def square_sum(n_ctx, n_fsdp, partial):
    def kernel(partial_ref, out_ref, held, core_in, square_in, load, core_s, core_r, sq_s, sq_r):
        for stage in square_sum_stages(
            n_ctx, n_fsdp, partial_ref, out_ref, held, core_in, square_in, load, (core_s, core_r), (sq_s, sq_r)
        ):
            stage()

    return pl.pallas_call(
        kernel,
        out_shape=jax.ShapeDtypeStruct(partial.shape[-2:], jnp.float32),
        in_specs=any_specs(1),
        out_specs=pl.BlockSpec(memory_space=pltpu.VMEM),
        scratch_shapes=square_sum_scratch(n_fsdp, partial),
        compiler_params=params(1),
        name="square_sum",
    )(partial)


def line_sum_steps(n_ctx, partial_ref, out_ref, held, core_in, right_in, left_in, load, core_sems, right_sems, left_sems):
    rows = partial_ref.shape[1]
    where = place(n_ctx)
    chip, core, fsdp, length = where
    sibling, right, left = line_peers(*where)
    order = [(chip + length - 1 - j) % length for j in range(length)]
    mine, others = [], []
    for j, owner in enumerate(order):
        mine.append(pltpu.make_async_copy(partial_ref.at[owner * 2 + core], held.at[owner], load.at[j]))
        others.append(send(partial_ref.at[owner * 2 + 1 - core], core_in.at[owner], core_sems, j, sibling))
        others[-1].start()
        mine[-1].start()
    yield
    for j, owner in enumerate(order):
        mine[j].wait()
        others[j].wait_recv()
        add_into(held.at[owner], core_in.at[owner])
    ways = ((1, right, right_in, right_sems), (-1, left, left_in, left_sems))
    for step in range(length - 1):
        for sign, peer, arrived, sems in ways:
            block = chip + sign * (length - 1 - step)
            inside = (block >= 0) & (block < length)
            came = (chip >= 1) if sign > 0 else (chip < length - 1)
            if step > 0:

                @pl.when(inside & came)
                def _():
                    send(held.at[block], arrived.at[step - 1], sems, step - 1, peer).wait_recv()
                    add_into(held.at[block], arrived.at[step - 1])

            @pl.when(inside)
            def _():
                send(held.at[block], arrived.at[step], sems, step, peer).start()

        yield
    last = length - 2
    for sign, peer, arrived, sems in ways:
        came = (chip >= 1) if sign > 0 else (chip < length - 1)

        @pl.when(came)
        def _():
            send(held.at[chip], arrived.at[last], sems, last, peer).wait_recv()
            add_into(held.at[chip], arrived.at[last])

    @pl.loop(0, rows // 64)
    def _(step):
        at = pl.ds(pl.multiple_of(step * 64, 64), 64)
        out_ref[at] = held[chip, at].astype(jnp.float32)

    for step in range(length - 1):
        for sign, peer, arrived, sems in ways:
            block = chip + sign * (length - 1 - step)

            @pl.when((block >= 0) & (block < length))
            def _():
                send(held.at[block], arrived.at[step], sems, step, peer).wait_send()

    for each in others:
        each.wait_send()


def line_sum_scratch(n_ctx, partial):
    rows, columns = partial.shape[-2:]
    length = n_ctx // 2
    return [
        pltpu.VMEM((length, rows, columns), partial.dtype),
        pltpu.VMEM((length, rows, columns), partial.dtype),
        pltpu.VMEM((length - 1, rows, columns), partial.dtype),
        pltpu.VMEM((length - 1, rows, columns), partial.dtype),
        pltpu.SemaphoreType.DMA((length,)),
    ] + dma_pair(length) * 3


def line_sum(n_ctx, partial):
    def kernel(partial_ref, out_ref, held, core_in, right_in, left_in, load, core_s, core_r, right_s, right_r, left_s, left_r):
        greet(line_peers(*place(n_ctx)))
        run_all(
            line_sum_steps(
                n_ctx, partial_ref, out_ref, held, core_in, right_in, left_in, load,
                (core_s, core_r), (right_s, right_r), (left_s, left_r),
            )
        )

    return pl.pallas_call(
        kernel,
        out_shape=jax.ShapeDtypeStruct(partial.shape[-2:], jnp.float32),
        in_specs=any_specs(1),
        out_specs=pl.BlockSpec(memory_space=pltpu.VMEM),
        scratch_shapes=line_sum_scratch(n_ctx, partial),
        compiler_params=params(5),
        name="line_sum",
    )(partial)


def attention_sums(n_ctx, partial, rows, grads, attended, grad_cols):
    total, features = rows.shape
    parts, _, own = attended.shape
    wide = grads.shape[1]
    depth = features // 4
    weight_shape = jax.ShapeDtypeStruct((4, depth, wide + own), jnp.bfloat16)
    inputs = (rows, grads, attended, grad_cols)

    def kernel(partial_ref, *refs):
        inputs_refs, refs = refs[:4], refs[4:]
        out_ref, weight_ref, rows_v, grads_v, attended_v, cols_v, weights, in_sem, *refs = refs
        line_refs, refs = refs[:5], refs[5:]
        core_s, core_r, right_s, right_r, left_s, left_r, *refs = refs
        held, square_in, load, sq_s, sq_r = refs
        where = place(n_ctx)
        chip, core, fsdp, _ = where
        loads = [
            pltpu.make_async_copy(a, b, in_sem.at[j])
            for j, (a, b) in enumerate(zip(inputs_refs, (rows_v, grads_v, attended_v, cols_v)))
        ]
        for each in loads:
            each.start()
        greet(line_peers(*where) + fsdp_peers(4, chip * 2 + core, fsdp))
        line = line_sum_steps(
            n_ctx, partial_ref, out_ref, *line_refs, (core_s, core_r), (right_s, right_r), (left_s, left_r)
        )
        next(line)
        starts, pass_on, finish = corner_sum_stages(n_ctx, weights, weight_ref, held, square_in, load, (sq_s, sq_r))
        for each in loads:
            each.wait()
        first, second, corner = fsdp_neighbours(fsdp)
        for number, owner in enumerate((corner, first, second, fsdp)):
            at = pl.ds(pl.multiple_of(owner * depth, depth), depth)
            weights[owner, :, :wide] = low(mm(rows_v[:, at], grads_v[...], CONTRACT_FIRST))
            for q in range(depth // own):
                weights[owner, q * own : (q + 1) * own, wide:] = low(
                    mm(attended_v[owner * (depth // own) + q], cols_v[...], CONTRACT_FIRST)
                )
            for start in starts[number]:
                start()
            if number < 2:
                next(line)
        pass_on()
        run_all(line)
        finish()

    return pl.pallas_call(
        kernel,
        out_shape=[
            jax.ShapeDtypeStruct(partial.shape[-2:], jnp.float32),
            jax.ShapeDtypeStruct(weight_shape.shape[1:], jnp.float32),
        ],
        in_specs=any_specs(5),
        out_specs=[pl.BlockSpec(memory_space=pltpu.VMEM)] * 2,
        scratch_shapes=[pltpu.VMEM(a.shape, a.dtype) for a in inputs]
        + [pltpu.VMEM(weight_shape.shape, weight_shape.dtype), pltpu.SemaphoreType.DMA((4,))]
        + line_sum_scratch(n_ctx, partial)
        + corner_sum_scratch(weight_shape),
        compiler_params=params(4),
        cost_estimate=pl.CostEstimate(
            flops=2 * total * features * (wide + own), bytes_accessed=16 * 1024 * 1024, transcendentals=0
        ),
        name="attention_sums",
    )(partial, *inputs)


def sum_everywhere(n_ctx, n_fsdp, values):
    block = values.shape[1:]

    def kernel(values_ref, out_ref, along_ctx, along_fsdp, result, ctx_s, ctx_r, fsdp_s, fsdp_r, back_s, back_r):
        ctx = lax.axis_index("ctx")
        fsdp = lax.axis_index("fsdp")
        ctx_peers = [((ctx + j) % n_ctx, fsdp) for j in range(1, n_ctx)]
        fsdp_peers = [(ctx, (fsdp + j) % n_fsdp) for j in range(1, n_fsdp)]
        greet(ctx_peers + fsdp_peers)

        def exchange(copies):
            for copy in copies:
                copy.start()
            for copy in copies:
                copy.wait()

        def total(slots, count):
            value = slots[0]
            for j in range(1, count):
                value = value + slots[j]
            return value

        along_ctx[ctx] = values_ref[ctx]
        exchange(
            [
                send(values_ref.at[peer[0]], along_ctx.at[ctx], (ctx_s, ctx_r), j, peer)
                for j, peer in enumerate(ctx_peers)
            ]
        )
        along_fsdp[fsdp] = total(along_ctx, n_ctx)
        exchange(
            [
                send(along_fsdp.at[fsdp], along_fsdp.at[fsdp], (fsdp_s, fsdp_r), j, peer)
                for j, peer in enumerate(fsdp_peers)
            ]
        )
        result[ctx] = total(along_fsdp, n_fsdp)
        exchange(
            [send(result.at[ctx], result.at[ctx], (back_s, back_r), j, peer) for j, peer in enumerate(ctx_peers)]
        )
        out_ref[...] = result[...]

    return pl.pallas_call(
        kernel,
        out_shape=jax.ShapeDtypeStruct(values.shape, values.dtype),
        in_specs=[pl.BlockSpec(memory_space=pltpu.VMEM)],
        out_specs=pl.BlockSpec(memory_space=pltpu.VMEM),
        scratch_shapes=[
            pltpu.VMEM((n_ctx,) + block, values.dtype),
            pltpu.VMEM((n_fsdp,) + block, values.dtype),
            pltpu.VMEM((n_ctx,) + block, values.dtype),
        ]
        + dma_pair(n_ctx)
        + dma_pair(n_fsdp)
        + dma_pair(n_ctx),
        compiler_params=params(2),
        name="sum_everywhere",
    )(values)


def hidden_units(here, back, gate_ref, up_ref, down_ref):
    gate = mm(here, gate_ref[0], CONTRACT_LAST)
    up = mm(here, up_ref[0], CONTRACT_LAST)
    grad_hidden = mm(back, down_ref[0], CONTRACT_LAST)
    sigmoid = jax.nn.sigmoid(gate)
    activated = gate * sigmoid
    return (
        low(activated * up),
        low(grad_hidden * up * sigmoid * (1.0 + gate * (1.0 - sigmoid))),
        low(grad_hidden * activated),
    )


def ffn_forward(rows, planes, core, n_own, chunk=256):
    blocks, _, tokens, features = rows.shape
    total = blocks * tokens
    steps = n_own // chunk
    group = max(1, 256 // tokens)

    def kernel(core_ref, rows_ref, gate_ref, up_ref, down_ref, *outs):
        for at in range(0, blocks, group):
            here = rows_ref[at : at + group, 0].reshape(group * tokens, features)
            back = rows_ref[at : at + group, 1].reshape(group * tokens, features)
            span = pl.ds(at * tokens, group * tokens)
            for out, value in zip(outs, hidden_units(here, back, gate_ref, up_ref, down_ref)):
                out[span] = value

    def weight_spec(plane):
        return pl.BlockSpec((1, chunk, features), lambda j, core_ref: (plane, core_ref[0] * steps + j, 0))

    act = jax.ShapeDtypeStruct((total, n_own), jnp.bfloat16)
    act_spec = pl.BlockSpec((total, chunk), lambda j, core_ref: (0, j))
    return pl.pallas_call(
        kernel,
        grid_spec=pltpu.PrefetchScalarGridSpec(
            num_scalar_prefetch=1,
            grid=(steps,),
            in_specs=[
                pl.BlockSpec(rows.shape, lambda j, core_ref: (0, 0, 0, 0), pipeline_mode=pl.Buffered(1)),
                weight_spec(0),
                weight_spec(1),
                weight_spec(2),
            ],
            out_specs=[act_spec, act_spec, act_spec],
        ),
        out_shape=[act, act, act],
        compiler_params=params(),
        cost_estimate=pl.CostEstimate(
            flops=6 * total * n_own * features, bytes_accessed=30 * 1024 * 1024, transcendentals=total * n_own
        ),
        name="ffn_forward",
    )(core, rows, planes, planes, planes)


def mirror_gather(all_ref, arrivals, sems, pass_sems, ctx, core, fsdp, sibling):
    first, second, corner = fsdp_neighbours(fsdp)
    half = all_ref.shape[2] // 2
    parts = [pl.ds(0, half), pl.ds(half, half)]
    to_first, to_second = (ctx, first), (ctx, second)

    def copy(index, owner, part, peer):
        place_ref = all_ref.at[core, owner, parts[part]]
        return send(place_ref, place_ref, sems, index, peer)

    copies = [
        copy(0, fsdp, 0, to_first),
        copy(1, fsdp, 0, to_second),
        copy(2, fsdp, 1, to_first),
        copy(3, fsdp, 1, to_second),
        copy(4, first, 0, to_second),
        copy(5, second, 1, to_first),
    ]
    passes = [(fsdp, 0), (fsdp, 1), (first, 0), (second, 0), (first, 1), (second, 1), (corner, 0), (corner, 1)]

    def passing_copy(number, side):
        owner, part = passes[number]
        place_ref = all_ref.at[side, owner, parts[part]]
        return send(place_ref, place_ref, pass_sems, number, sibling)

    for part in range(2):
        arrivals[part].wait_recv()
        copies[2 * part].start()
        copies[2 * part + 1].start()
        passing_copy(part, core).start()
        yield
    for index, number, then in ((0, 2, 4), (1, 3, None), (2, 4, None), (3, 5, 5), (4, 6, None), (5, 7, None)):
        owner, part = passes[number]
        copy(index, owner, part, to_first).wait_recv()
        if then is not None:
            copies[then].start()
        passing_copy(number, core).start()
        yield
    for each in copies:
        each.wait_send()
    for number in range(8):
        passing_copy(number, core).wait_send()
        passing_copy(number, 1 - core).wait_recv()


def ffn_rows(n_ctx, own, planes, n_own, chunk=256, wide=512):
    n_fsdp = 4
    size, features = own.shape
    tokens = size // 2
    total = 2 * n_fsdp * tokens

    def kernel(
        own_ref, planes_ref, all_ref, mirror_ref, hidden_a, hidden_b, hidden_c, partial_ref,
        rows, weights, hidden, partial, core_in, load, sq_s, sq_r, core_s, core_r, far_s, far_r, mi_s, mi_r, mc_s, mc_r, sum_s, sum_r, out_sem,
    ):
        chip, core, fsdp, length = place(n_ctx)
        ctx = chip * 2 + core
        sibling = (chip * 2 + 1 - core, fsdp)
        mirror = ((length - 1 - chip) * 2 + core, fsdp)
        first, second, corner = fsdp_neighbours(fsdp)
        greet([sibling, mirror] + fsdp_peers(n_fsdp, ctx, fsdp))
        mine = pltpu.make_async_copy(own_ref, rows.at[core, fsdp], load.at[3])
        mine.start()
        start = pl.multiple_of(core * n_own, n_own)
        loads = [
            pltpu.make_async_copy(planes_ref.at[p, pl.ds(start, n_own)], weights.at[p], load.at[p]) for p in range(3)
        ]
        handed, arriving = [], []

        def hand(source, owner, part, index):
            for side, copies in ((core, handed), (1 - core, arriving)):
                target = rows.at[side, owner] if part is None else rows.at[side, owner, part]
                copies.append(send(source, target, (core_s, core_r), index + 1, sibling))
            handed[-1].start()

        gathering = square_gather(own_ref, rows.at[core], (sq_s, sq_r), ctx, fsdp, n_fsdp, hand)
        next(gathering)
        hand(own_ref, fsdp, None, -1)
        for each in loads:
            each.start()
        far = [
            send(
                own_ref.at[pl.ds(part * tokens, tokens)],
                mirror_ref.at[core, fsdp, pl.ds(part * tokens, tokens)],
                (far_s, far_r),
                part,
                mirror,
            )
            for part in range(2)
        ]
        for each in far:
            each.start()
        mirroring = mirror_gather(mirror_ref, far, (mi_s, mi_r), (mc_s, mc_r), ctx, core, fsdp, sibling)
        outs, summing, sums = [], [], []

        def add_up(number, owner):
            summing[number].wait_recv()
            add_into(partial.at[number % 2, core], core_in.at[number])
            sums.append(
                pltpu.make_async_copy(partial.at[number % 2, core], partial_ref.at[owner], out_sem.at[number % 2, 8])
            )
            sums[-1].start()

        def group(number, owner):
            slot = number % 2
            if number >= 2:
                for each in outs[number - 2]:
                    each.wait()
                summing[number - 2].wait_send()
                sums[number - 2].wait()
            here = jnp.concatenate([rows[0, owner, :tokens], rows[1, owner, :tokens]])
            back = jnp.concatenate([rows[0, owner, tokens:], rows[1, owner, tokens:]])

            @pl.loop(0, n_own // chunk)
            def _(step):
                at = pl.ds(pl.multiple_of(step * chunk, chunk), chunk)
                parts = [weights.at[pl.ds(p, 1), at] for p in range(3)]
                for q, value in enumerate(hidden_units(here, back, *parts)):
                    hidden[slot, q, :, at] = value

            @pl.loop(0, features // wide)
            def _(step):
                at = pl.ds(pl.multiple_of(step * wide, wide), wide)
                out = low(mm(hidden[slot, 0], weights[2, :, at]))
                below = low(mm(hidden[slot, 1], weights[0, :, at]) + mm(hidden[slot, 2], weights[1, :, at]))
                for k in range(2):
                    partial[slot, k, :tokens, at] = out[k * tokens : (k + 1) * tokens]
                    partial[slot, k, tokens:, at] = below[k * tokens : (k + 1) * tokens]

            pairs = []
            summing.append(send(partial.at[slot, 1 - core], core_in.at[number], (sum_s, sum_r), number, sibling))
            summing[-1].start()
            for k in range(2):
                pairs.append((rows.at[k, owner], all_ref.at[k, owner]))
                at = pl.ds(pl.multiple_of((k * n_fsdp + owner) * tokens, tokens), tokens)
                for q, target in enumerate((hidden_a, hidden_b, hidden_c)):
                    pairs.append((hidden.at[slot, q, pl.ds(k * tokens, tokens)], target.at[at]))
            outs.append(
                [pltpu.make_async_copy(a, b, out_sem.at[slot, j]) for j, (a, b) in enumerate(pairs)]
            )
            for each in outs[-1]:
                each.start()

        mine.wait()
        arriving[0].wait_recv()
        for each in loads:
            each.wait()
        group(0, fsdp)
        for _ in range(4):
            next(gathering)
        arriving[1].wait_recv()
        arriving[3].wait_recv()
        group(1, first)
        add_up(0, fsdp)
        next(mirroring)
        for _ in range(2):
            next(gathering)
        arriving[2].wait_recv()
        arriving[4].wait_recv()
        group(2, second)
        add_up(1, first)
        for _ in range(3):
            next(mirroring)
        arriving[5].wait_recv()
        arriving[6].wait_recv()
        group(3, corner)
        add_up(2, second)
        next(mirroring)
        add_up(3, corner)
        run_all(mirroring, gathering)
        for each in handed:
            each.wait_send()
        for each in far:
            each.wait_send()
        for each in outs[2] + outs[3] + sums[2:]:
            each.wait()
        for each in summing[2:]:
            each.wait_send()

    act = jax.ShapeDtypeStruct((total, n_own), own.dtype)
    all_rows = jax.ShapeDtypeStruct((2, n_fsdp) + own.shape, own.dtype)
    return pl.pallas_call(
        kernel,
        in_specs=any_specs(2),
        out_specs=any_specs(6),
        out_shape=[all_rows, all_rows, act, act, act, jax.ShapeDtypeStruct((n_fsdp,) + own.shape, own.dtype)],
        scratch_shapes=[
            pltpu.VMEM((2, n_fsdp) + own.shape, own.dtype),
            pltpu.VMEM((3, n_own, features), own.dtype),
            pltpu.VMEM((2, 3, 2 * tokens, n_own), own.dtype),
            pltpu.VMEM((2, 2) + own.shape, own.dtype),
            pltpu.VMEM((n_fsdp,) + own.shape, own.dtype),
            pltpu.SemaphoreType.DMA((4,)),
        ]
        + dma_pair(6)
        + dma_pair(7)
        + dma_pair(2)
        + dma_pair(6)
        + dma_pair(8)
        + dma_pair(4)
        + [pltpu.SemaphoreType.DMA((2, 9))],
        compiler_params=params(6),
        cost_estimate=pl.CostEstimate(
            flops=12 * total * n_own * features, bytes_accessed=50 * 1024 * 1024, transcendentals=total * n_own
        ),
        name="ffn_rows",
    )(own, planes)


def ffn_weights(n_ctx, n_fsdp, partial, rows, rows_mirror, hidden, planes, n_own, chunk=256):
    blocks, _, tokens, features = rows.shape
    total = blocks * tokens
    steps = n_own // chunk
    group = max(1, 256 // tokens)
    half = features // 2
    sides = n_ctx // 4
    wide = half // sides
    fused = partial is not None
    early = steps // 2 if fused else 0
    assert not fused or sides == 2

    def kernel(*refs):
        rows_ref, refs = refs[0], refs[1:]
        mirror_refs, refs = refs[: len(rows_mirror)], refs[len(rows_mirror) :]
        mirror_blocks = [ref.at[b] for ref in mirror_refs for b in range(ref.shape[0])]
        hidden_ref, grad_gate_ref, grad_up_ref, planes_ref, *refs = refs
        if fused:
            partial_ref, weight_ref, out_ref, early_ref, *refs = refs
        else:
            weight_ref, *refs = refs
        mirror, (weights, weight_sems), refs = refs[:3], refs[3:5], refs[5:]
        chip, core, _, length = place(n_ctx)
        side = chip // sides
        step = pl.program_id(0)
        stages = []
        if fused:
            keep, give, take, side_s, side_r, held, square_in, load, sq_s, sq_r = refs
            member = chip % 2
            other = (chip + 1 - 2 * member) * 2 + core
            crossing = [
                send(give.at[j], take.at[j], (side_s, side_r), j, (other, lax.axis_index("fsdp"))) for j in range(early)
            ]
            starts, *stages = corner_sum_stages(n_ctx, partial_ref, out_ref, held, square_in, load, (sq_s, sq_r))

        def fetch(at, slot):
            start = pl.multiple_of((core * steps + at) * chunk, chunk)
            return pltpu.make_async_copy(planes_ref.at[:, pl.ds(start, chunk)], weights.at[slot], weight_sems.at[slot])

        @pl.when(step == 0)
        def _():
            fetch(0, 0).start()
            if fused:
                fsdp = lax.axis_index("fsdp")
                greet(fsdp_peers(4, chip * 2 + core, fsdp) + [(other, fsdp)])
                for start in sum(starts, []):
                    start()

        @pl.when(step + 1 < steps)
        def _():
            fetch(step + 1, (step + 1) % 2).start()

        slot = step % 2
        fetch(step, slot).wait()
        gate_ref, up_ref, down_ref = (weights.at[slot, pl.ds(plane, 1)] for plane in range(3))
        for at in range(0, blocks, group):
            here = jnp.concatenate([ref[0] for ref in mirror_blocks[at : at + group]])
            back = jnp.concatenate([ref[1] for ref in mirror_blocks[at : at + group]])
            span = pl.ds(at * tokens, group * tokens)
            for out, value in zip(mirror, hidden_units(here, back, gate_ref, up_ref, down_ref)):
                out[span] = value

        lefts = ((grad_gate_ref, mirror[1], 0), (grad_up_ref, mirror[2], 0), (hidden_ref, mirror[0], 1))
        for plane, (left, left_mirror, which) in enumerate(lefts):
            left = left[...]
            left_mirror = left_mirror[...]
            for z in range(sides):
                cols = pl.ds(pl.multiple_of(side * half + z * wide, wide), wide)
                right = rows_ref[:, which, :, cols].reshape(total, wide)
                right_mirror = jnp.concatenate([ref[which, :, cols] for ref in mirror_blocks])
                value = mm(left, right, CONTRACT_FIRST) + mm(left_mirror, right_mirror, CONTRACT_FIRST)
                if not fused:
                    weight_ref[z, plane] = low(value)
                    continue

                @pl.when((step < early) & (z == member))
                def _():
                    keep[step % early, plane] = value

                @pl.when((step < early) & (z != member))
                def _():
                    give[step % early, plane] = low(value)

                @pl.when(step >= early)
                def _():
                    weight_ref[z, plane] = low(value)

        for j in range(early):

            @pl.when(step == j)
            def _():
                crossing[j].start()

        for at, stage in ((1, 0), (steps - 1, 1)):
            if stage < len(stages):

                @pl.when(step == min(at, steps - 1))
                def _():
                    stages[stage]()

        if fused:

            @pl.when(step == steps - 1)
            def _():
                for j in range(early):
                    crossing[j].wait()
                    for plane in range(3):
                        early_ref[plane, j * chunk : (j + 1) * chunk] = low(
                            keep[j, plane] + take[j, plane].astype(jnp.float32)
                        )

    act_spec = pl.BlockSpec((total, chunk), lambda j: (0, j))
    once = dict(pipeline_mode=pl.Buffered(1))
    operands = [rows, *rows_mirror, *hidden, planes]
    in_specs = [whole_block(rows.shape, **once)] + [whole_block(part.shape, **once) for part in rows_mirror]
    in_specs += [act_spec] * 3 + any_specs(1)
    out_specs = [pl.BlockSpec((sides, 3, chunk, wide), lambda j: (0, 0, jnp.maximum(j - early, 0), 0))]
    out_shape = [jax.ShapeDtypeStruct((sides, 3, n_own - early * chunk, wide), jnp.bfloat16)]
    scratch = [pltpu.VMEM((total, chunk), jnp.bfloat16)] * 3
    scratch += [pltpu.VMEM((2, 3, chunk, features), jnp.bfloat16), pltpu.SemaphoreType.DMA((2,))]
    if fused:
        operands.append(partial)
        in_specs += any_specs(1)
        out_specs.append(whole_block(partial.shape[-2:], **once))
        out_shape.append(jax.ShapeDtypeStruct(partial.shape[-2:], jnp.float32))
        out_specs.append(whole_block((3, early * chunk, wide), **once))
        out_shape.append(jax.ShapeDtypeStruct((3, early * chunk, wide), jnp.bfloat16))
        scratch.append(pltpu.VMEM((early, 3, chunk, wide), jnp.float32))
        scratch += [pltpu.VMEM((early, 3, chunk, wide), jnp.bfloat16)] * 2 + dma_pair(early)
        scratch += corner_sum_scratch(partial)
    return pl.pallas_call(
        kernel,
        grid=(steps,),
        in_specs=in_specs,
        out_specs=out_specs,
        out_shape=out_shape,
        scratch_shapes=scratch,
        compiler_params=params(3) if fused else params(),
        cost_estimate=pl.CostEstimate(
            flops=12 * total * n_own * features, bytes_accessed=50 * 1024 * 1024, transcendentals=total * n_own
        ),
        name="ffn_weights",
    )(*operands)


def ffn_back(hidden, grad_gate, grad_up, planes, core, blocks, wide=512):
    total, n_own = hidden.shape
    features = planes.shape[2]
    tokens = total // blocks

    def kernel(core_ref, hidden_ref, grad_gate_ref, grad_up_ref, gate_ref, up_ref, down_ref, out_ref):
        out = mm(hidden_ref[...], down_ref[0])
        out_ref[:, 0] = low(out).reshape(blocks, tokens, wide)
        back = mm(grad_gate_ref[...], gate_ref[0]) + mm(grad_up_ref[...], up_ref[0])
        out_ref[:, 1] = low(back).reshape(blocks, tokens, wide)

    def weight_spec(plane):
        return pl.BlockSpec((1, n_own, wide), lambda j, core_ref: (plane, core_ref[0], j))

    act_spec = pl.BlockSpec((total, n_own), lambda j, core_ref: (0, 0), pipeline_mode=pl.Buffered(1))
    return pl.pallas_call(
        kernel,
        grid_spec=pltpu.PrefetchScalarGridSpec(
            num_scalar_prefetch=1,
            grid=(features // wide,),
            in_specs=[act_spec, act_spec, act_spec, weight_spec(0), weight_spec(1), weight_spec(2)],
            out_specs=pl.BlockSpec((blocks, 2, tokens, wide), lambda j, core_ref: (0, 0, 0, j)),
        ),
        out_shape=jax.ShapeDtypeStruct((blocks, 2, tokens, features), jnp.bfloat16),
        compiler_params=params(),
        cost_estimate=pl.CostEstimate(
            flops=6 * total * n_own * features, bytes_accessed=30 * 1024 * 1024, transcendentals=0
        ),
        name="ffn_back",
    )(core, hidden, grad_gate, grad_up, planes, planes, planes)


SPAN = 256


def ctx_peers(n_ctx):
    ctx = lax.axis_index("ctx")
    fsdp = lax.axis_index("fsdp")
    return [((ctx + j) % n_ctx, fsdp) for j in range(1, n_ctx)]


def deal(n_ctx, block, target, landed, sems, own_sem):
    ctx = lax.axis_index("ctx")
    fsdp = lax.axis_index("fsdp")

    @pl.when(target != ctx)
    def _():
        send(block, landed.at[ctx], sems, (target - ctx + n_ctx) % n_ctx, (target, fsdp)).start()

    @pl.when(target == ctx)
    def _():
        pltpu.make_async_copy(block, landed.at[ctx], own_sem).start()


def dealt(n_ctx, block, landed, sems, own_sem):
    ctx = lax.axis_index("ctx")
    pltpu.make_async_copy(block, landed.at[ctx], own_sem).wait()
    for j, peer in enumerate(ctx_peers(n_ctx)):
        copy = send(block, landed.at[(ctx + n_ctx - j - 1) % n_ctx], sems, j + 1, peer)
        copy.wait_send()
        copy.wait_recv()


def turn(values, cosine, sine):
    return values * cosine + pltpu.roll(values, HEAD_DIM // 2, 1) * sine


def attention_forward(n_ctx, rows, w_qkv, cosine, sine, place_column, place_row, heads):
    total, features = rows.shape
    own = heads * HEAD_DIM
    steps = total // SPAN
    length = total // n_ctx
    scale = HEAD_DIM ** (-0.5)

    def kernel(
        rows_ref, w_ref, cosine_ref, sine_ref, column_ref, row_ref,
        query_ref, key_ref, value_ref, out_ref, log_ref, landed, deal_s, deal_r, own_sem,
    ):
        step = pl.program_id(0)

        @pl.when(step == 0)
        def _():
            greet(ctx_peers(n_ctx))

        span = pl.ds(pl.multiple_of(step * SPAN, SPAN), SPAN)
        qkv = mm(rows_ref[...], w_ref[...])
        cosine = cosine_ref[span]
        sine = sine_ref[span]
        for h in range(heads):
            at = slice(h * HEAD_DIM, (h + 1) * HEAD_DIM)
            query_ref[span, at] = low(turn(qkv[:, at], cosine, sine))
            key_ref[span, at] = low(turn(qkv[:, own + h * HEAD_DIM : own + (h + 1) * HEAD_DIM], cosine, sine))
        value_ref[span] = low(qkv[:, 2 * own :])

        @pl.when(step == steps - 1)
        def _():
            @pl.loop(0, steps)
            def _(block):
                here = pl.ds(pl.multiple_of(block * SPAN, SPAN), SPAN)
                for h in range(heads):
                    at = slice(h * HEAD_DIM, (h + 1) * HEAD_DIM)
                    scores = mm(query_ref[here, at], key_ref[:, at], CONTRACT_LAST) * scale
                    scores = jnp.where(column_ref[here] >= row_ref[...], scores, MASKED)
                    highest = jnp.max(scores, axis=-1, keepdims=True)
                    exponent = jnp.exp(scores - highest)
                    sums = jnp.sum(exponent, axis=-1, keepdims=True)
                    out_ref[here, at] = low(mm(low(exponent * (1.0 / sums)), value_ref[:, at]))
                    log_ref[h, here] = highest + jnp.log(sums)
                for r in range(SPAN // length):
                    mine = out_ref.at[pl.ds(pl.multiple_of(block * SPAN + r * length, length), length)]
                    deal(n_ctx, mine, block * (SPAN // length) + r, landed, (deal_s, deal_r), own_sem)

            dealt(n_ctx, out_ref.at[pl.ds(0, length)], landed, (deal_s, deal_r), own_sem)

    act = jax.ShapeDtypeStruct((total, own), jnp.bfloat16)
    return pl.pallas_call(
        kernel,
        grid=(steps,),
        in_specs=[pl.BlockSpec((SPAN, features), lambda r: (r, 0))]
        + [whole_block(a.shape) for a in (w_qkv, cosine, sine, place_column, place_row)],
        out_specs=[whole_block((total, own))] * 4 + [whole_block((heads, total, 1))] + any_specs(1),
        out_shape=[act] * 4
        + [
            jax.ShapeDtypeStruct((heads, total, 1), jnp.float32),
            jax.ShapeDtypeStruct((n_ctx, length, own), jnp.bfloat16),
        ],
        scratch_shapes=dma_pair(n_ctx) + [pltpu.SemaphoreType.DMA],
        compiler_params=params(8),
        name="attention_forward",
    )(rows, w_qkv, cosine, sine, place_column, place_row)


def attention_backward(query, key, value, grad, logs, w_qkv, cosine, sine, place_column, place_row, heads):
    total, own = query.shape
    features = w_qkv.shape[0]
    steps = total // SPAN
    scale = HEAD_DIM ** (-0.5)

    def kernel(
        query_ref, key_ref, value_ref, grad_ref, log_ref, w_ref, cosine_ref, sine_ref, column_ref, row_ref,
        qkv_ref, out_ref, key_sum, value_sum,
    ):
        step = pl.program_id(0)

        @pl.when(step == 0)
        def _():
            for h in range(heads):
                at = slice(h * HEAD_DIM, (h + 1) * HEAD_DIM)
                key_sum[...] = jnp.zeros_like(key_sum)
                value_sum[...] = jnp.zeros_like(value_sum)

                @pl.loop(0, steps)
                def _(block):
                    here = pl.ds(pl.multiple_of(block * SPAN, SPAN), SPAN)
                    queries = query_ref[here, at]
                    grads = grad_ref[here, at]
                    scores = mm(queries, key_ref[:, at], CONTRACT_LAST) * scale
                    scores = jnp.where(column_ref[here] >= row_ref[...], scores, MASKED)
                    probs = jnp.exp(scores - log_ref[h, here])
                    probs_grad = mm(grads, value_ref[:, at], CONTRACT_LAST)
                    centre = jnp.sum(probs * probs_grad, axis=-1, keepdims=True)
                    scores_grad = low(probs * (probs_grad - centre))
                    query_grad = mm(scores_grad, key_ref[:, at]) * scale
                    qkv_ref[here, at] = low(turn(query_grad, cosine_ref[here], -sine_ref[here]))
                    key_sum[...] += mm(scores_grad, queries, CONTRACT_FIRST)
                    value_sum[...] += mm(low(probs), grads, CONTRACT_FIRST)

                qkv_ref[:, own + h * HEAD_DIM : own + (h + 1) * HEAD_DIM] = low(
                    turn(key_sum[...] * scale, cosine_ref[...], -sine_ref[...])
                )
                qkv_ref[:, 2 * own + h * HEAD_DIM : 2 * own + (h + 1) * HEAD_DIM] = low(value_sum[...])

        span = pl.ds(pl.multiple_of(step * SPAN, SPAN), SPAN)
        out_ref[...] = low(mm(qkv_ref[span], w_ref[...], CONTRACT_LAST))

    return pl.pallas_call(
        kernel,
        grid=(steps,),
        in_specs=[
            whole_block(a.shape)
            for a in (query, key, value, grad, logs, w_qkv, cosine, sine, place_column, place_row)
        ],
        out_specs=[whole_block((total, 3 * own)), pl.BlockSpec((SPAN, features), lambda r: (r, 0))],
        out_shape=[
            jax.ShapeDtypeStruct((total, 3 * own), jnp.bfloat16),
            jax.ShapeDtypeStruct((total, features), jnp.bfloat16),
        ],
        scratch_shapes=[pltpu.VMEM((total, HEAD_DIM), jnp.float32)] * 2,
        compiler_params=params(),
        name="attention_backward",
    )(query, key, value, grad, logs, w_qkv, cosine, sine, place_column, place_row)


ROWS = 32


def row_blocks(count, features):
    return pl.BlockSpec((count, ROWS, features), lambda r, *_: (0, r, 0))


def whole_block(shape, **more):
    zeros = (0,) * len(shape)
    return pl.BlockSpec(shape, lambda r, *_: zeros, **more)


def split(values):
    high = low(values)
    return (high, low(values - high.astype(jnp.float32)))


def connect_coefficients(values, dynamic_ref, static_ref, coef_ref, dyn_ref):
    lane = lax.broadcasted_iota(jnp.int32, (values[0].shape[0], 8), 1)
    columns = []
    for i, value in enumerate(values):
        mean = jnp.mean(value, axis=-1, keepdims=True)
        centered = value - mean
        inverse = lax.rsqrt(jnp.mean(centered * centered, axis=-1, keepdims=True) + EPS)
        normed = centered * inverse
        projected = jnp.zeros(lane.shape, jnp.float32)
        for k in range(6):
            part = jnp.sum(normed * dynamic_ref[k : k + 1], axis=-1, keepdims=True)
            projected = jnp.where(lane == k, part, projected)
        coefficient = jnp.tanh(projected) + static_ref[i : i + 1]
        dyn_ref[i] = projected
        coef_ref[i] = jnp.where(lane == 6, mean, jnp.where(lane == 7, inverse, coefficient))
        columns.append(coefficient)
    return columns


def connect_first(streams, dynamic, static):
    number, rows, features = streams.shape

    def kernel(streams_ref, dynamic_ref, static_ref, coef_ref, dyn_ref, low_ref):
        values = [streams_ref[i].astype(jnp.float32) for i in range(number)]
        columns = connect_coefficients(values, dynamic_ref, static_ref, coef_ref, dyn_ref)
        mixed = sum((columns[i][:, 1:2] * values[i] for i in range(number)))
        low_ref[...] = low(normalize(mixed)[0])

    small = jax.ShapeDtypeStruct((number, rows, 8), jnp.float32)
    return pl.pallas_call(
        kernel,
        grid=(rows // ROWS,),
        out_shape=(small, small, jax.ShapeDtypeStruct((rows, features), jnp.bfloat16)),
        in_specs=[row_blocks(number, features), whole_block(dynamic.shape), whole_block(static.shape)],
        out_specs=(
            row_blocks(number, 8),
            row_blocks(number, 8),
            pl.BlockSpec((ROWS, features), lambda r: (r, 0)),
        ),
        compiler_params=params(),
        name="connect_first",
    )(streams, dynamic, static)


def connect_middle(streams, coef, attended, w_mine, w_other, cotangent, dynamic, static, core_fsdp, where, depth):
    number, rows, features = streams.shape
    half = features // 2
    own = attended.shape[2]
    count = len(w_mine)

    def kernel(core_ref, streams_ref, coef_ref, attended_ref, *refs):
        weights, refs = refs[: 2 * count], refs[2 * count :]
        cotangent_ref, dynamic_ref, static_ref = refs[:3]
        first_ref, branch_ref, coef_two_ref, dyn_ref, own_ref, projected = refs[3:]
        step = pl.program_id(0)

        @pl.when(step == 0)
        def _():
            for side in range(2):
                total = 0.0
                for j, (d, offset) in enumerate(where):
                    for q in range(w_mine[j].shape[0] // own):
                        part = attended_ref[(core_ref[1] ^ d) * (depth // own) + offset // own + q]
                        total = total + mm(part, weights[side * count + j][q * own : (q + 1) * own])
                projected[core_ref[0] if side == 0 else 1 - core_ref[0]] = total

        span = pl.ds(pl.multiple_of(step * ROWS, ROWS), ROWS)
        branch = jnp.concatenate([projected[0, span], projected[1, span]], axis=1)
        branch_ref[...] = branch
        inputs = [streams_ref[i].astype(jnp.float32) for i in range(number)]
        outs = []
        for j in range(number):
            out = sum((coef_ref[i][:, 2 + j : 3 + j] * inputs[i] for i in range(number)))
            outs.append(out + coef_ref[j][:, 0:1] * branch)
            first_ref[j] = outs[-1]
        columns = connect_coefficients(outs, dynamic_ref, static_ref, coef_two_ref, dyn_ref)
        mixed = sum((columns[i][:, 1:2] * outs[i] for i in range(number)))
        own_ref[0] = low(normalize(mixed)[0])
        own_ref[1] = low(sum((columns[j][:, 0:1] * cotangent_ref[j].astype(jnp.float32) for j in range(number))))

    small = jax.ShapeDtypeStruct((number, rows, 8), jnp.float32)
    once = dict(pipeline_mode=pl.Buffered(1))
    return pl.pallas_call(
        kernel,
        grid_spec=pltpu.PrefetchScalarGridSpec(
            num_scalar_prefetch=1,
            grid=(rows // ROWS,),
            in_specs=[
                row_blocks(number, features),
                row_blocks(number, 8),
                whole_block(attended.shape, **once),
                *[whole_block(w.shape, **once) for w in w_mine + w_other],
                row_blocks(number, features),
                whole_block(dynamic.shape),
                whole_block(static.shape),
            ],
            out_specs=(
                row_blocks(number, features),
                pl.BlockSpec((ROWS, features), lambda r, *_: (r, 0)),
                row_blocks(number, 8),
                row_blocks(number, 8),
                row_blocks(2, features),
            ),
            scratch_shapes=[pltpu.VMEM((2, rows, half), jnp.float32)],
        ),
        out_shape=(
            jax.ShapeDtypeStruct((number, rows, features), jnp.float32),
            jax.ShapeDtypeStruct((rows, features), jnp.float32),
            small,
            small,
            jax.ShapeDtypeStruct((2, rows, features), jnp.bfloat16),
        ),
        compiler_params=params(),
        name="connect_middle",
    )(core_fsdp, streams, coef, attended, *w_mine, *w_other, cotangent, dynamic, static)


def attention_weights(rows, grads, attended, grad_cols):
    total, features = rows.shape
    parts, _, own = attended.shape
    wide = grads.shape[1]

    def kernel(rows_ref, grads_ref, attended_ref, cols_ref, out_ref):
        out_ref[:, :wide] = low(mm(rows_ref[...], grads_ref[...], CONTRACT_FIRST))
        out_ref[:, wide:] = low(mm(attended_ref[0], cols_ref[...], CONTRACT_FIRST))

    return pl.pallas_call(
        kernel,
        grid=(parts,),
        in_specs=[
            pl.BlockSpec((total, own), lambda k: (0, k)),
            whole_block(grads.shape),
            pl.BlockSpec((1, total, own), lambda k: (k, 0, 0)),
            whole_block(grad_cols.shape),
        ],
        out_specs=pl.BlockSpec((own, wide + own), lambda k: (k, 0)),
        out_shape=jax.ShapeDtypeStruct((features, wide + own), jnp.bfloat16),
        compiler_params=params(),
        cost_estimate=pl.CostEstimate(
            flops=2 * total * features * (wide + own), bytes_accessed=16 * 1024 * 1024, transcendentals=0
        ),
        name="attention_weights",
    )(rows, grads, attended, grad_cols)


def flip(index, bits, count):
    result = index
    bit = 1
    while bit < count:
        if bits & bit:
            result = result + bit - 2 * bit * (index // bit % 2)
        bit *= 2
    return result


def project_back(n_ctx, n_fsdp, grad, w_mine, w_other, where, depth):
    rows, features = grad.shape
    half = features // 2
    count = len(w_mine)
    own = features // n_ctx

    def kernel(grad_ref, *refs):
        weights, refs = refs[: 2 * count], refs[2 * count :]
        landed, cols_ref, outs, deal_s, deal_r, own_sem = refs
        _, core, fsdp, _ = place(n_ctx)
        greet(ctx_peers(n_ctx))
        first = grad_ref[:, pl.ds(pl.multiple_of(core * half, half), half)]
        second = grad_ref[:, pl.ds(pl.multiple_of((1 - core) * half, half), half)]
        for j, (d, offset) in enumerate(where):
            out = low(
                mm(first, weights[j][...], CONTRACT_LAST) + mm(second, weights[count + j][...], CONTRACT_LAST)
            )
            for q in range(w_mine[j].shape[0] // own):
                at = flip(fsdp, d, n_fsdp) * (depth // own) + offset // own + q
                outs[at] = out[:, q * own : (q + 1) * own]
                deal(n_ctx, outs.at[at], at, landed, (deal_s, deal_r), own_sem)
        for index in range(n_ctx):
            cols_ref[index] = grad_ref[:, index * own : (index + 1) * own]
        dealt(n_ctx, outs.at[0], landed, (deal_s, deal_r), own_sem)

    shape = (n_ctx, rows, own)
    return pl.pallas_call(
        kernel,
        in_specs=[pl.BlockSpec(memory_space=pltpu.VMEM)] * (1 + 2 * count),
        out_specs=any_specs(1) + [pl.BlockSpec(memory_space=pltpu.VMEM)],
        out_shape=[jax.ShapeDtypeStruct(shape, grad.dtype)] * 2,
        scratch_shapes=[pltpu.VMEM(shape, grad.dtype)] + dma_pair(n_ctx) + [pltpu.SemaphoreType.DMA],
        compiler_params=params(9),
        name="project_back",
    )(grad, *w_mine, *w_other)


def connect_back(values, coef, dyn, branch, grads, grad_normed, dynamic, means, coef_before=None, offset=0):
    number, rows, features = values.shape
    steps = rows // ROWS
    more = coef_before is not None

    def kernel(*refs):
        values_ref, coef_ref, dyn_ref, branch_ref, grads_ref, normed_ref, dynamic_ref, means_ref = refs[:8]
        refs = refs[8:]
        if more:
            before_ref, refs = refs[0], refs[1:]
        out_ref, dynamic_out, static_out = refs[:3]
        if more:
            forward_ref, grad_low_ref = refs[3:5]
        step = pl.program_id(0)

        @pl.when(step == 0)
        def _():
            dynamic_out[...] = jnp.zeros_like(dynamic_out)
            static_out[...] = jnp.zeros_like(static_out)

        branch = branch_ref[...]
        grads = [grads_ref[j].astype(jnp.float32) for j in range(number)]
        mixed = sum((coef_ref[i][:, 1:2] * values_ref[i].astype(jnp.float32) for i in range(number)))
        normed, inverse = normalize(mixed)
        grad_mixed = normalize_back(normed, inverse, normed_ref[...])
        lane = lax.broadcasted_iota(jnp.int32, (ROWS, 8), 1)
        pre_grads, highs, lows = [], [], []
        for i in range(number):
            value = values_ref[i].astype(jnp.float32)
            columns = [grads[i] * branch, grad_mixed * value] + [grads[j] * value for j in range(number)]
            coef_grad = jnp.zeros((ROWS, 8), jnp.float32)
            for k, column in enumerate(columns):
                coef_grad = jnp.where(lane == k, jnp.sum(column, axis=-1, keepdims=True), coef_grad)
            static_out[i : i + 1] += jnp.sum(coef_grad, axis=0, keepdims=True)
            part = jnp.tanh(dyn_ref[i])
            pre_grads.append(coef_grad * (1.0 - part * part))
            high, rest = split((value - coef_ref[i][:, 6:7]) * coef_ref[i][:, 7:8])
            highs.append(high)
            lows.append(rest)
        pre, pre_rest = split(jnp.concatenate(pre_grads))
        dynamic, dynamic_rest = split(dynamic_ref[...])
        normed_grads = mm(
            jnp.concatenate([pre, pre_rest, pre], axis=1), jnp.concatenate([dynamic, dynamic, dynamic_rest], axis=0)
        )
        highs = jnp.concatenate(highs)
        dynamic_out[...] += (
            mm(pre, highs, CONTRACT_FIRST)
            + mm(pre_rest, highs, CONTRACT_FIRST)
            + mm(pre, jnp.concatenate(lows), CONTRACT_FIRST)
        )
        befores = 0.0
        for i in range(number):
            coef = coef_ref[i]
            mean_grad = jnp.sum(pre_grads[i] * means_ref[...], axis=-1, keepdims=True)
            inner = jnp.sum(pre_grads[i] * dyn_ref[i], axis=-1, keepdims=True) / features
            normed = (values_ref[i].astype(jnp.float32) - coef[:, 6:7]) * coef[:, 7:8]
            out = coef[:, 7:8] * (normed_grads[i * ROWS : (i + 1) * ROWS] - mean_grad - normed * inner)
            out = out + coef[:, 1:2] * grad_mixed
            for j in range(number):
                out = out + coef[:, 2 + j : 3 + j] * grads[j]
            out_ref[i] = out
            if more:
                befores = befores + before_ref[i][:, 0:1] * out
        if more:
            grad_low_ref[...] = low(befores)
            for j in range(number):
                out = coef_ref[j][:, 0:1] * branch
                for i in range(number):
                    out = out + coef_ref[i][:, 2 + j : 3 + j] * values_ref[i].astype(jnp.float32)
                forward_ref[j] = low(out)

    rows_spec = pl.BlockSpec((ROWS, features), lambda r: (r, 0))
    out_shape = [
        jax.ShapeDtypeStruct((number, rows, features), jnp.float32),
        jax.ShapeDtypeStruct((8, features), jnp.float32),
        jax.ShapeDtypeStruct((8, 8), jnp.float32),
    ]
    out_specs = [row_blocks(number, features), whole_block((8, features)), whole_block((8, 8))]
    operands = [values, coef, dyn, branch, grads, grad_normed, dynamic, means]
    in_specs = [
        row_blocks(number, features),
        row_blocks(number, 8),
        row_blocks(number, 8),
        rows_spec,
        row_blocks(number, features),
        pl.BlockSpec((ROWS, features), lambda r: (offset // ROWS + r, 0)),
        whole_block(dynamic.shape),
        whole_block(means.shape),
    ]
    if more:
        operands.append(coef_before)
        in_specs.append(row_blocks(number, 8))
        out_shape.append(jax.ShapeDtypeStruct((number, rows, features), jnp.bfloat16))
        out_specs.append(row_blocks(number, features))
        out_shape.append(jax.ShapeDtypeStruct((rows, features), jnp.bfloat16))
        out_specs.append(rows_spec)
    return pl.pallas_call(
        kernel,
        grid=(steps,),
        in_specs=in_specs,
        out_specs=out_specs,
        out_shape=out_shape,
        compiler_params=params(),
        name="connect_back",
    )(*operands)


def local(n_ctx, n_fsdp, streams, w_attn, w_ffn, hc_dynamic, hc_static, cotangent, pair_order):
    number = streams.shape[1]
    length = streams.shape[2]
    features = streams.shape[3]
    size = HEAD_DIM
    own = features // n_ctx
    heads = own // size
    rows = length * n_ctx
    own_rows = w_attn.shape[0]
    ctx = lax.axis_index("ctx")
    fsdp = lax.axis_index("fsdp")
    core = ctx % 2
    chips = n_ctx // 2
    core_index = jnp.reshape(core, (1,)).astype(jnp.int32)

    def in_order(mine, other, axis):
        return jnp.where(
            core == 0, jnp.concatenate([mine, other], axis=axis), jnp.concatenate([other, mine], axis=axis)
        )


    w_own = lax.dynamic_slice_in_dim(w_attn, ctx * own, own, 2)[:, 0:3].reshape(own_rows, 3 * own)
    w_qkv = gather(w_own, "fsdp")
    half = features // 2
    w_half = lax.dynamic_slice_in_dim(w_attn, core * half, half, 2)[:, 3]
    siblings = [(i, i ^ 1) for i in range(n_ctx)]
    core_fsdp = jnp.stack([core, fsdp]).astype(jnp.int32)

    def exchange(values, most=0):
        return [values] + [
            lax.ppermute(values, "fsdp", [(i, i ^ d) for i in range(n_fsdp)])
            for d in range(1, most + 1 if most else n_fsdp)
        ]

    def swap(blocks):
        return [lax.ppermute(block, "ctx", siblings) for block in blocks]


    positions = block_positions(pair_order, length)
    frequency = THETA ** (-(jnp.arange(size // 2, dtype=jnp.float32) * 2.0) / size)
    angles = positions.astype(jnp.float32)[:, None] * jnp.concatenate([frequency, frequency])[None, :]
    signs = jnp.where(jnp.arange(size) < size // 2, -1.0, 1.0)
    tables = (jnp.cos(angles), jnp.sin(angles) * signs[None, :], positions[:, None], positions[None, :])

    dynamics = jnp.pad(hc_dynamic, ((0, 0), (0, 2), (0, 0)))
    means = jnp.mean(dynamics, axis=-1)
    statics = jnp.pad(hc_static, ((0, 0), (0, 0), (0, 2)))
    coef_one, dyn_one, attn_low = connect_first(streams[0], dynamics[0], statics[0])
    attn_low, w_half = lax.optimization_barrier((attn_low, w_half))
    w_out_mine = exchange(w_half, 2 if n_fsdp == 4 else 0)
    attn_all = line_rows(n_ctx, attn_low).reshape(rows, features)
    w_out_where = [(d, 0) for d in range(len(w_out_mine))]
    attn_all, *w_out_mine = lax.optimization_barrier((attn_all, *w_out_mine))
    w_out_other = swap(w_out_mine)
    if n_fsdp == 4:
        middle = own_rows // 2
        corners = [
            lax.ppermute(w_out_mine[1][:middle], "fsdp", [(i, i ^ 2) for i in range(4)]),
            lax.ppermute(w_out_mine[2][middle:], "fsdp", [(i, i ^ 1) for i in range(4)]),
        ]
        w_out_where += [(3, 0), (3, middle)]
    query, key, value, attended, logs, attended_rows = attention_forward(n_ctx, attn_all, w_qkv, *tables, heads)
    if n_fsdp == 4:
        attended, *corners = lax.optimization_barrier((attended, *corners))
        w_out_mine += corners
        w_out_other += swap(corners)

    first_out, attn_branch, coef_two, dyn_two, ffn_own = connect_middle(
        streams[0], coef_one, attended_rows, w_out_mine, w_out_other, cotangent[0], dynamics[1], statics[1], core_fsdp,
        w_out_where, own_rows,
    )
    ffn_own = ffn_own.reshape(2 * length, features)

    planes = jnp.moveaxis(w_ffn, 1, 0)
    n_own = planes.shape[1] // 2
    blocks = 2 * n_fsdp
    if n_fsdp == 4:
        ffn_all, mirror_rows, *hidden, sums = ffn_rows(n_ctx, ffn_own, planes, n_own)
        ffn_all, mirror_rows = (part.reshape(blocks, 2, length, features) for part in (ffn_all, mirror_rows))
        mirror_rows = [mirror_rows]
        attended_all = gather(attended, "ctx").reshape(n_ctx, rows, own)
        weight_parts, sums, weight_early = ffn_weights(
            n_ctx, n_fsdp, sums, ffn_all, mirror_rows, hidden, planes, n_own
        )
    else:
        ffn_mirror = lax.ppermute(ffn_own, "ctx", [(i, n_ctx - 2 - i + 2 * (i % 2)) for i in range(n_ctx)])
        ffn_all = square_core_gather(n_ctx, n_fsdp, ffn_own).reshape(blocks, 2, length, features)
        attended_all = gather(attended, "ctx").reshape(n_ctx, rows, own)
        mirror_mine = exchange(ffn_mirror)
        hidden = ffn_forward(ffn_all, planes, core_index, n_own)
        sums = ffn_back(*hidden, planes, core_index, blocks)
        mirror_rows = [part.reshape(1, 2, length, features) for part in mirror_mine + swap(mirror_mine)]
        sums = square_sum(n_ctx, n_fsdp, sums.reshape(2, n_fsdp, 2 * length, features))
        (weight_parts,) = ffn_weights(n_ctx, n_fsdp, None, ffn_all, mirror_rows, hidden, planes, n_own)
    sides = chips // 2
    lines = [[2 * (sides * side + i) + j for i in range(sides)] for side in range(2) for j in range(2)]
    weight_cols = lax.psum_scatter(weight_parts, "ctx", scatter_dimension=0, axis_index_groups=lines)

    grad_first, dynamic_grad_two, static_grad_two, streams_out, grad_attn = connect_back(
        first_out, coef_two, dyn_two, sums, cotangent[0], sums, dynamics[1], means[1:], coef_one, length
    )
    grad_heads, grad_cols = project_back(n_ctx, n_fsdp, grad_attn, w_out_mine, w_out_other, w_out_where, own_rows)
    grad_heads = grad_heads.reshape(rows, own)
    grad_heads, grad_cols = lax.optimization_barrier((grad_heads, grad_cols))
    grad_cols = lax.all_to_all(grad_cols, "ctx", 0, 0, tiled=True).reshape(rows, own)
    qkv_grad, attn_part = attention_backward(query, key, value, grad_heads, logs, w_qkv, *tables, heads)
    attn_part = attn_part.reshape(n_ctx, length, features)
    if n_fsdp == 4:
        grad_attn_normed, attn_grad = attention_sums(n_ctx, attn_part, attn_all, qkv_grad, attended_all, grad_cols)
    else:
        grad_attn_normed = line_sum(n_ctx, attn_part)
        attn_grad = scatter(attention_weights(attn_all, qkv_grad, attended_all, grad_cols), "fsdp").astype(jnp.float32)
    grad_attn_normed, weight_cols = lax.optimization_barrier((grad_attn_normed, weight_cols))
    if n_fsdp == 4:
        weight_cols = jnp.concatenate([weight_early, weight_cols], axis=1)
    mine = lax.dynamic_slice_in_dim(weight_cols, core * own, own, 2)
    other = lax.dynamic_slice_in_dim(weight_cols, (1 - core) * own, own, 2)
    other = lax.ppermute(other, "ctx", siblings)
    ffn_grad = jnp.moveaxis(in_order(mine, other, 1), 0, 1).astype(jnp.float32)
    grad_inputs, dynamic_grad_one, static_grad_one = connect_back(
        streams[0], coef_one, dyn_one, attn_branch, grad_first, grad_attn_normed, dynamics[0], means[:1]
    )
    static_grads = jnp.concatenate([static_grad_one[:number, :6].reshape(1, -1), static_grad_two[:number, :6].reshape(1, -1)])
    small = jnp.concatenate(
        [
            dynamic_grad_one[:6],
            dynamic_grad_two[:6],
            jnp.pad(static_grads, ((0, 2), (0, features - 6 * number))),
        ]
    )
    small = sum_everywhere(n_ctx, n_fsdp, small.reshape(n_ctx, 8, -1))
    small = small.reshape(16, features)
    attn_grad = attn_grad.reshape(own_rows, 4, own)
    dynamic_total = small[:12].reshape(2, 6, features)
    static_total = small[12:14, : 6 * number].reshape(2, number, 6)
    return (streams_out[None], grad_inputs[None], attn_grad, ffn_grad, dynamic_total, static_total)


def solution(mesh):
    return jax.shard_map(
        functools.partial(local, mesh.shape["ctx"], mesh.shape["fsdp"]),
        mesh=mesh,
        in_specs=(
            P("fsdp", None, "ctx", None),
            P("fsdp", None, None),
            P("fsdp", None, None),
            P(),
            P(),
            P("fsdp", None, "ctx", None),
            P(),
        ),
        out_specs=(
            P("fsdp", None, "ctx", None),
            P("fsdp", None, "ctx", None),
            P("fsdp", None, "ctx"),
            P("fsdp", None, "ctx"),
            P(),
            P(),
        ),
        check_vma=False,
    )
```

```python
import functools

import jax
import jax.numpy as jnp
from jax import lax
from jax.experimental import pallas as pl
from jax.experimental.pallas import tpu as pltpu
from jax.sharding import PartitionSpec as P

HEADS = 16
HEAD_DIM = 128


EPS = 1e-05
THETA = 10000.0
HIGH = lax.Precision.HIGHEST
MASKED = -1e30
CONTRACT_LAST = (((1,), (1,)), ((), ()))
CONTRACT_FIRST = (((0,), (0,)), ((), ()))


def normalize(values):
    centered = values - jnp.mean(values, axis=-1, keepdims=True)
    inverse = lax.rsqrt(jnp.mean(centered * centered, axis=-1, keepdims=True) + EPS)
    return (centered * inverse, inverse)


def normalize_back(normed, inverse, gradient):
    inner = jnp.mean(gradient * normed, axis=-1, keepdims=True)
    return inverse * (gradient - jnp.mean(gradient, axis=-1, keepdims=True) - normed * inner)


def block_positions(pair_order, length):
    half_size = length // 2
    offsets = jnp.arange(half_size, dtype=jnp.int32)
    mirror = 2 * pair_order.shape[0] - 1 - pair_order
    first_half = pair_order[:, None] * half_size + offsets[None, :]
    second_half = mirror[:, None] * half_size + offsets[None, :]
    return jnp.concatenate([first_half, second_half], axis=1).reshape(-1)


def low(values):
    return values.astype(jnp.bfloat16)


def mm(a, b, dims=None):
    if dims is None:
        return jnp.dot(a, b, preferred_element_type=jnp.float32)
    return lax.dot_general(a, b, dims, preferred_element_type=jnp.float32)


def gather(values, axis, dim=0):
    return lax.all_gather(values, axis, axis=dim, tiled=True)


def scatter(values, axis, dim=0):
    return lax.psum_scatter(values, axis, scatter_dimension=dim, tiled=True)


MESH = pl.DeviceIdType.MESH
VMEM_LIMIT = 60 * 1024 * 1024


def place(n_ctx):
    ctx = lax.axis_index("ctx")
    return (ctx // 2, ctx % 2, lax.axis_index("fsdp"), n_ctx // 2)


def greet(peers):
    barrier = pltpu.get_barrier_semaphore()
    for peer in peers:
        pl.semaphore_signal(barrier, inc=1, device_id=peer, device_id_type=MESH)
    pl.semaphore_wait(barrier, len(peers))


def send(source, target, sems, index, peer):
    return pltpu.make_async_remote_copy(
        src_ref=source,
        dst_ref=target,
        send_sem=sems[0].at[index],
        recv_sem=sems[1].at[index],
        device_id=peer,
        device_id_type=MESH,
    )


def fsdp_neighbours(fsdp):
    first = fsdp + 1 - 2 * (fsdp % 2)
    second = (fsdp + 2) % 4
    return (first, second, (first + 2) % 4)


def fsdp_peers(n_fsdp, ctx, fsdp):
    if n_fsdp == 4:
        first, second, _ = fsdp_neighbours(fsdp)
        return [(ctx, first), (ctx, second)]
    return [(ctx, (fsdp + j) % n_fsdp) for j in range(1, n_fsdp)]


def line_peers(chip, core, fsdp, length):
    return [
        (chip * 2 + 1 - core, fsdp),
        ((chip + 1) % length * 2 + core, fsdp),
        ((chip + length - 1) % length * 2 + core, fsdp),
    ]


def line_gather(own_ref, all_ref, sems, where):
    chip, core, fsdp, length = where
    right_sems, left_sems, core_sems = sems
    sibling = (chip * 2 + 1 - core, fsdp)
    right = ((chip + 1) % length * 2 + core, fsdp)
    left = ((chip + length - 1) % length * 2 + core, fsdp)

    def block(index):
        return all_ref.at[(index + length) % length * 2 + core]

    def pass_on(index, source):
        return send(source, block(index), core_sems, (index + length) % length, sibling)

    pass_on(chip, own_ref).start()
    for step in range(length - 1):
        for sign, peer, way in ((-1, right, right_sems), (1, left, left_sems)):
            at = chip + sign * step
            held = (at >= 0) & (at < length)
            if step > 0:

                @pl.when(held)
                def _():
                    send(block(at), block(at), way, step - 1, peer).wait_recv()
                    pass_on(at, block(at)).start()

            more = (chip < length - 1) if sign < 0 else (chip > 0)

            @pl.when(held & more)
            def _():
                send(own_ref if step == 0 else block(at), block(at), way, step, peer).start()

        yield
    last = length - 1
    for sign, peer, way in ((-1, right, right_sems), (1, left, left_sems)):
        at = chip + sign * last

        @pl.when((at >= 0) & (at < length))
        def _():
            send(block(at), block(at), way, last - 1, peer).wait_recv()
            pass_on(at, block(at)).start()

    yield
    for step in range(length - 1):
        for sign, peer, way in ((-1, right, right_sems), (1, left, left_sems)):
            at = chip + sign * step
            more = (chip < length - 1) if sign < 0 else (chip > 0)

            @pl.when((at >= 0) & (at < length) & more)
            def _():
                send(block(at), block(at), way, step, peer).wait_send()

    for index in range(length):
        pass_on(index, block(index)).wait_send()
        other = all_ref.at[index * 2 + 1 - core]
        send(other, other, core_sems, index, sibling).wait_recv()


def square_gather(own_ref, all_ref, sems, ctx, fsdp, n_fsdp, passed=None):
    if n_fsdp != 4:
        copies = [
            send(own_ref, all_ref.at[fsdp], sems, j - 1, (ctx, (fsdp + j) % n_fsdp)) for j in range(1, n_fsdp)
        ]
        for copy in copies:
            copy.start()
        yield
        for j, copy in enumerate(copies):
            copy.wait()
            if passed:
                passed(all_ref.at[(fsdp + n_fsdp - j - 1) % n_fsdp], (fsdp + n_fsdp - j - 1) % n_fsdp, None, j)
        return
    first, second, corner = fsdp_neighbours(fsdp)
    half = own_ref.shape[0] // 2
    top, low_half = pl.ds(0, half), pl.ds(half, half)
    to_first, to_second = (ctx, first), (ctx, second)

    def copy(index, owner, part, peer, source=None):
        source = all_ref.at[owner, part] if source is None else source
        return send(source, all_ref.at[owner, part], sems, index, peer)

    starts = [
        copy(0, fsdp, top, to_first, own_ref.at[top]),
        copy(1, fsdp, low_half, to_second, own_ref.at[low_half]),
        copy(2, fsdp, low_half, to_first, own_ref.at[low_half]),
        copy(3, fsdp, top, to_second, own_ref.at[top]),
        copy(4, first, top, to_second),
        copy(5, second, low_half, to_first),
    ]
    arrivals = [
        (0, first, top),
        (1, second, low_half),
        (2, first, low_half),
        (3, second, top),
        (4, corner, top),
        (5, corner, low_half),
    ]
    for each in starts[:4]:
        each.start()
    yield
    for index, owner, part in arrivals:
        copy(index, owner, part, to_first).wait_recv()
        if index < 2:
            starts[4 + index].start()
        if passed:
            passed(all_ref.at[owner, part], owner, part, index)
        yield
    for each in starts:
        each.wait_send()


def run_all(*parts):
    parts = list(parts)
    while parts:
        for part in list(parts):
            try:
                next(part)
            except StopIteration:
                parts.remove(part)


def dma_pair(count):
    return [pltpu.SemaphoreType.DMA((count,)), pltpu.SemaphoreType.DMA((count,))]


def any_specs(count):
    return [pl.BlockSpec(memory_space=pl.ANY)] * count


def params(collective_id=None, **more):
    if collective_id is not None:
        more.update(collective_id=collective_id, has_side_effects=True)
    return pltpu.CompilerParams(vmem_limit_bytes=VMEM_LIMIT, **more)


def passing(own_ref, all_ref, sems, core, fsdp, sibling):
    handed = [send(own_ref, all_ref.at[core, fsdp], sems, 0, sibling)]
    handed[0].start()
    arriving = [send(own_ref, all_ref.at[1 - core, fsdp], sems, 0, sibling)]

    def passed(source, owner, part, index):
        for side, copies in ((core, handed), (1 - core, arriving)):
            target = all_ref.at[side, owner] if part is None else all_ref.at[side, owner, part]
            copies.append(send(source, target, sems, index + 1, sibling))
        handed[-1].start()

    def finish():
        for out, back in zip(handed, arriving):
            out.wait_send()
            back.wait_recv()

    return (passed, finish)


def line_rows(n_ctx, rows):
    def kernel(rows_ref, all_rows, right_s, right_r, left_s, left_r, core_s, core_r, own):
        where = place(n_ctx)
        chip, core, fsdp, length = where
        greet(line_peers(*where))
        mine = pltpu.make_async_copy(rows_ref, all_rows.at[chip * 2 + core], own)
        mine.start()
        run_all(line_gather(rows_ref, all_rows, ((right_s, right_r), (left_s, left_r), (core_s, core_r)), where))
        mine.wait()

    length = n_ctx // 2
    return pl.pallas_call(
        kernel,
        out_shape=jax.ShapeDtypeStruct((n_ctx,) + rows.shape, rows.dtype),
        in_specs=any_specs(1),
        out_specs=pl.BlockSpec(memory_space=pl.ANY),
        scratch_shapes=dma_pair(length) + dma_pair(length) + dma_pair(length) + [pltpu.SemaphoreType.DMA],
        compiler_params=params(0),
        name="line_rows",
    )(rows)


def square_core_gather(n_ctx, n_fsdp, rows):
    def kernel(rows_ref, all_ref, sq_s, sq_r, core_s, core_r, own):
        chip, core, fsdp, _ = place(n_ctx)
        ctx = chip * 2 + core
        sibling = (chip * 2 + 1 - core, fsdp)
        greet([sibling] + fsdp_peers(n_fsdp, ctx, fsdp))
        mine = pltpu.make_async_copy(rows_ref, all_ref.at[core, fsdp], own)
        mine.start()
        passed, finish = passing(rows_ref, all_ref, (core_s, core_r), core, fsdp, sibling)
        run_all(square_gather(rows_ref, all_ref.at[core], (sq_s, sq_r), ctx, fsdp, n_fsdp, passed))
        finish()
        mine.wait()

    return pl.pallas_call(
        kernel,
        out_shape=jax.ShapeDtypeStruct((2, n_fsdp) + rows.shape, rows.dtype),
        in_specs=any_specs(1),
        out_specs=pl.BlockSpec(memory_space=pl.ANY),
        scratch_shapes=dma_pair(max(6, n_fsdp)) + dma_pair(max(7, n_fsdp)) + [pltpu.SemaphoreType.DMA],
        compiler_params=params(1),
        name="square_core_gather",
    )(rows)


def add_into(target, *sources, chunk=64):
    @pl.loop(0, target.shape[0] // chunk)
    def _(step):
        rows = pl.ds(pl.multiple_of(step * chunk, chunk), chunk)
        total = target[rows].astype(jnp.float32)
        for source in sources:
            total = total + source[rows].astype(jnp.float32)
        target[rows] = total.astype(target.dtype)


def square_sum_stages(n_ctx, n_fsdp, partial_ref, out_ref, held, core_in, square_in, load, core_sems, sems):
    rows = partial_ref.shape[-2]
    half = rows // 2
    chip, core, fsdp, _ = place(n_ctx)
    ctx = chip * 2 + core
    sibling = (chip * 2 + 1 - core, fsdp)
    if n_fsdp == 4:
        first, second, corner = fsdp_neighbours(fsdp)
        order = [corner, first, second, fsdp]
    else:
        order = [(fsdp + j) % n_fsdp for j in range(1, n_fsdp + 1)]
    mine = [
        pltpu.make_async_copy(partial_ref.at[core, owner], held.at[owner], load.at[j])
        for j, owner in enumerate(order)
    ]
    others = [
        send(partial_ref.at[1 - core, owner], core_in.at[owner], core_sems, j, sibling)
        for j, owner in enumerate(order)
    ]

    def ready(j):
        mine[j].wait()
        others[j].wait_recv()
        add_into(held.at[order[j]], core_in.at[order[j]])

    def total(parts, sources):
        @pl.loop(0, parts[1] // 64)
        def _(step):
            at = pl.ds(pl.multiple_of(parts[0] + step * 64, 64), 64)
            from_at = pl.ds(pl.multiple_of(step * 64, 64), 64)
            value = held[fsdp, at].astype(jnp.float32)
            for j in sources:
                value = value + square_in[j, from_at].astype(jnp.float32)
            out_ref[at] = value

    def begin():
        greet([sibling] + fsdp_peers(n_fsdp, ctx, fsdp))
        for j in range(n_fsdp):
            others[j].start()
            mine[j].start()

    if n_fsdp != 4:
        copies = [
            send(held.at[order[j]], square_in.at[j], sems, j, (ctx, order[j])) for j in range(n_fsdp - 1)
        ]

        def spread():
            for j in range(n_fsdp):
                ready(j)
                if j < n_fsdp - 1:
                    copies[j].start()

        def finish():
            for copy in copies:
                copy.wait()
            total((0, rows), range(n_fsdp - 1))
            for each in others:
                each.wait_send()

        return [begin, spread, finish]

    top, low_half = pl.ds(0, half), pl.ds(half, half)
    to_first, to_second = (ctx, first), (ctx, second)

    def copy(index, owner, part, peer):
        return send(held.at[owner, part], square_in.at[index], sems, index, peer)

    copies = [
        copy(0, corner, top, to_first),
        copy(1, corner, low_half, to_second),
        copy(2, first, top, to_first),
        copy(3, second, low_half, to_second),
        copy(4, second, top, to_second),
        copy(5, first, low_half, to_first),
    ]

    def spread():
        ready(0)
        copies[0].start()
        copies[1].start()
        ready(1)
        copies[2].start()
        ready(2)
        copies[3].start()
        ready(3)

    def pass_on():
        copies[0].wait_recv()
        add_into(held.at[second, top], square_in.at[0])
        copies[4].start()
        copies[1].wait_recv()
        add_into(held.at[first, low_half], square_in.at[1])
        copies[5].start()

    def finish():
        for j in range(2, 6):
            copies[j].wait_recv()
        total((0, half), (2, 4))
        total((half, half), (3, 5))
        for each in copies:
            each.wait_send()
        for each in others:
            each.wait_send()

    return [begin, spread, pass_on, finish]


def corner_sum_stages(n_ctx, partial_ref, out_ref, held, square_in, load, sems):
    half = partial_ref.shape[1] // 2
    chip, core, fsdp, _ = place(n_ctx)
    ctx = chip * 2 + core
    first, second, corner = fsdp_neighbours(fsdp)
    top, low_half = pl.ds(0, half), pl.ds(half, half)
    to_first, to_second = (ctx, first), (ctx, second)

    def copy(index, source, peer):
        return send(source, square_in.at[index], sems, index, peer)

    copies = [
        copy(0, partial_ref.at[corner, top], to_first),
        copy(1, partial_ref.at[corner, low_half], to_second),
        copy(2, partial_ref.at[first, top], to_first),
        copy(3, partial_ref.at[second, low_half], to_second),
        copy(4, held.at[0], to_second),
        copy(5, held.at[1], to_first),
    ]
    mine = [
        pltpu.make_async_copy(partial_ref.at[second, top], held.at[0], load.at[0]),
        pltpu.make_async_copy(partial_ref.at[first, low_half], held.at[1], load.at[1]),
        pltpu.make_async_copy(partial_ref.at[fsdp, top], held.at[2], load.at[2]),
        pltpu.make_async_copy(partial_ref.at[fsdp, low_half], held.at[3], load.at[3]),
    ]

    starts = [
        [copies[0].start, copies[1].start],
        [copies[2].start, mine[1].start],
        [copies[3].start, mine[0].start],
        [mine[2].start, mine[3].start],
    ]

    def pass_on():
        for index in range(2):
            mine[index].wait()
            copies[index].wait_recv()
            add_into(held.at[index], square_in.at[index])
            copies[4 + index].start()

    def finish():
        for part, sources in ((0, (2, 4)), (1, (3, 5))):
            mine[2 + part].wait()
            for j in sources:
                copies[j].wait_recv()

            @pl.loop(0, half // 64)
            def _(step):
                at = pl.ds(pl.multiple_of(step * 64, 64), 64)
                value = held[2 + part, at].astype(jnp.float32)
                for j in sources:
                    value = value + square_in[j, at].astype(jnp.float32)
                out_ref[pl.ds(pl.multiple_of(part * half + step * 64, 64), 64)] = value

        for each in copies:
            each.wait_send()

    return [starts, pass_on, finish]


def corner_sum_scratch(partial):
    _, rows, columns = partial.shape
    return [
        pltpu.VMEM((4, rows // 2, columns), partial.dtype),
        pltpu.VMEM((6, rows // 2, columns), partial.dtype),
        pltpu.SemaphoreType.DMA((4,)),
    ] + dma_pair(6)


def square_sum_scratch(n_fsdp, partial):
    rows, columns = partial.shape[-2:]
    pieces = (6, rows // 2, columns) if n_fsdp == 4 else (n_fsdp - 1, rows, columns)
    return (
        [
            pltpu.VMEM((n_fsdp, rows, columns), partial.dtype),
            pltpu.VMEM((n_fsdp, rows, columns), partial.dtype),
            pltpu.VMEM(pieces, partial.dtype),
            pltpu.SemaphoreType.DMA((n_fsdp,)),
        ]
        + dma_pair(n_fsdp)
        + dma_pair(max(6, n_fsdp))
    )


def square_sum(n_ctx, n_fsdp, partial):
    def kernel(partial_ref, out_ref, held, core_in, square_in, load, core_s, core_r, sq_s, sq_r):
        for stage in square_sum_stages(
            n_ctx, n_fsdp, partial_ref, out_ref, held, core_in, square_in, load, (core_s, core_r), (sq_s, sq_r)
        ):
            stage()

    return pl.pallas_call(
        kernel,
        out_shape=jax.ShapeDtypeStruct(partial.shape[-2:], jnp.float32),
        in_specs=any_specs(1),
        out_specs=pl.BlockSpec(memory_space=pltpu.VMEM),
        scratch_shapes=square_sum_scratch(n_fsdp, partial),
        compiler_params=params(1),
        name="square_sum",
    )(partial)


def line_sum_steps(n_ctx, partial_ref, out_ref, held, core_in, right_in, left_in, load, core_sems, right_sems, left_sems):
    rows = partial_ref.shape[1]
    where = place(n_ctx)
    chip, core, fsdp, length = where
    sibling, right, left = line_peers(*where)
    order = [(chip + length - 1 - j) % length for j in range(length)]
    mine, others = [], []
    for j, owner in enumerate(order):
        mine.append(pltpu.make_async_copy(partial_ref.at[owner * 2 + core], held.at[owner], load.at[j]))
        others.append(send(partial_ref.at[owner * 2 + 1 - core], core_in.at[owner], core_sems, j, sibling))
        others[-1].start()
        mine[-1].start()
    yield
    for j, owner in enumerate(order):
        mine[j].wait()
        others[j].wait_recv()
        add_into(held.at[owner], core_in.at[owner])
    ways = ((1, right, right_in, right_sems), (-1, left, left_in, left_sems))
    for step in range(length - 1):
        for sign, peer, arrived, sems in ways:
            block = chip + sign * (length - 1 - step)
            inside = (block >= 0) & (block < length)
            came = (chip >= 1) if sign > 0 else (chip < length - 1)
            if step > 0:

                @pl.when(inside & came)
                def _():
                    send(held.at[block], arrived.at[step - 1], sems, step - 1, peer).wait_recv()
                    add_into(held.at[block], arrived.at[step - 1])

            @pl.when(inside)
            def _():
                send(held.at[block], arrived.at[step], sems, step, peer).start()

        yield
    last = length - 2
    for sign, peer, arrived, sems in ways:
        came = (chip >= 1) if sign > 0 else (chip < length - 1)

        @pl.when(came)
        def _():
            send(held.at[chip], arrived.at[last], sems, last, peer).wait_recv()
            add_into(held.at[chip], arrived.at[last])

    @pl.loop(0, rows // 64)
    def _(step):
        at = pl.ds(pl.multiple_of(step * 64, 64), 64)
        out_ref[at] = held[chip, at].astype(jnp.float32)

    for step in range(length - 1):
        for sign, peer, arrived, sems in ways:
            block = chip + sign * (length - 1 - step)

            @pl.when((block >= 0) & (block < length))
            def _():
                send(held.at[block], arrived.at[step], sems, step, peer).wait_send()

    for each in others:
        each.wait_send()


def line_sum_scratch(n_ctx, partial):
    rows, columns = partial.shape[-2:]
    length = n_ctx // 2
    return [
        pltpu.VMEM((length, rows, columns), partial.dtype),
        pltpu.VMEM((length, rows, columns), partial.dtype),
        pltpu.VMEM((length - 1, rows, columns), partial.dtype),
        pltpu.VMEM((length - 1, rows, columns), partial.dtype),
        pltpu.SemaphoreType.DMA((length,)),
    ] + dma_pair(length) * 3


def line_sum(n_ctx, partial):
    def kernel(partial_ref, out_ref, held, core_in, right_in, left_in, load, core_s, core_r, right_s, right_r, left_s, left_r):
        greet(line_peers(*place(n_ctx)))
        run_all(
            line_sum_steps(
                n_ctx, partial_ref, out_ref, held, core_in, right_in, left_in, load,
                (core_s, core_r), (right_s, right_r), (left_s, left_r),
            )
        )

    return pl.pallas_call(
        kernel,
        out_shape=jax.ShapeDtypeStruct(partial.shape[-2:], jnp.float32),
        in_specs=any_specs(1),
        out_specs=pl.BlockSpec(memory_space=pltpu.VMEM),
        scratch_shapes=line_sum_scratch(n_ctx, partial),
        compiler_params=params(5),
        name="line_sum",
    )(partial)


def attention_sums(n_ctx, partial, rows, grads, attended, grad_cols):
    total, features = rows.shape
    parts, _, own = attended.shape
    wide = grads.shape[1]
    depth = features // 4
    weight_shape = jax.ShapeDtypeStruct((4, depth, wide + own), jnp.bfloat16)
    inputs = (rows, grads, attended, grad_cols)

    def kernel(partial_ref, *refs):
        inputs_refs, refs = refs[:4], refs[4:]
        out_ref, weight_ref, rows_v, grads_v, attended_v, cols_v, weights, in_sem, *refs = refs
        line_refs, refs = refs[:5], refs[5:]
        core_s, core_r, right_s, right_r, left_s, left_r, *refs = refs
        held, square_in, load, sq_s, sq_r = refs
        where = place(n_ctx)
        chip, core, fsdp, _ = where
        loads = [
            pltpu.make_async_copy(a, b, in_sem.at[j])
            for j, (a, b) in enumerate(zip(inputs_refs, (rows_v, grads_v, attended_v, cols_v)))
        ]
        for each in loads:
            each.start()
        greet(line_peers(*where) + fsdp_peers(4, chip * 2 + core, fsdp))
        line = line_sum_steps(
            n_ctx, partial_ref, out_ref, *line_refs, (core_s, core_r), (right_s, right_r), (left_s, left_r)
        )
        next(line)
        starts, pass_on, finish = corner_sum_stages(n_ctx, weights, weight_ref, held, square_in, load, (sq_s, sq_r))
        for each in loads:
            each.wait()
        first, second, corner = fsdp_neighbours(fsdp)
        for number, owner in enumerate((corner, first, second, fsdp)):
            at = pl.ds(pl.multiple_of(owner * depth, depth), depth)
            weights[owner, :, :wide] = low(mm(rows_v[:, at], grads_v[...], CONTRACT_FIRST))
            for q in range(depth // own):
                weights[owner, q * own : (q + 1) * own, wide:] = low(
                    mm(attended_v[owner * (depth // own) + q], cols_v[...], CONTRACT_FIRST)
                )
            for start in starts[number]:
                start()
            if number < 2:
                next(line)
        pass_on()
        run_all(line)
        finish()

    return pl.pallas_call(
        kernel,
        out_shape=[
            jax.ShapeDtypeStruct(partial.shape[-2:], jnp.float32),
            jax.ShapeDtypeStruct(weight_shape.shape[1:], jnp.float32),
        ],
        in_specs=any_specs(5),
        out_specs=[pl.BlockSpec(memory_space=pltpu.VMEM)] * 2,
        scratch_shapes=[pltpu.VMEM(a.shape, a.dtype) for a in inputs]
        + [pltpu.VMEM(weight_shape.shape, weight_shape.dtype), pltpu.SemaphoreType.DMA((4,))]
        + line_sum_scratch(n_ctx, partial)
        + corner_sum_scratch(weight_shape),
        compiler_params=params(4),
        cost_estimate=pl.CostEstimate(
            flops=2 * total * features * (wide + own), bytes_accessed=16 * 1024 * 1024, transcendentals=0
        ),
        name="attention_sums",
    )(partial, *inputs)


def sum_everywhere(n_ctx, n_fsdp, values):
    block = values.shape[1:]

    def kernel(values_ref, out_ref, along_ctx, along_fsdp, result, ctx_s, ctx_r, fsdp_s, fsdp_r, back_s, back_r):
        ctx = lax.axis_index("ctx")
        fsdp = lax.axis_index("fsdp")
        ctx_peers = [((ctx + j) % n_ctx, fsdp) for j in range(1, n_ctx)]
        fsdp_peers = [(ctx, (fsdp + j) % n_fsdp) for j in range(1, n_fsdp)]
        greet(ctx_peers + fsdp_peers)

        def exchange(copies):
            for copy in copies:
                copy.start()
            for copy in copies:
                copy.wait()

        def total(slots, count):
            value = slots[0]
            for j in range(1, count):
                value = value + slots[j]
            return value

        along_ctx[ctx] = values_ref[ctx]
        exchange(
            [
                send(values_ref.at[peer[0]], along_ctx.at[ctx], (ctx_s, ctx_r), j, peer)
                for j, peer in enumerate(ctx_peers)
            ]
        )
        along_fsdp[fsdp] = total(along_ctx, n_ctx)
        exchange(
            [
                send(along_fsdp.at[fsdp], along_fsdp.at[fsdp], (fsdp_s, fsdp_r), j, peer)
                for j, peer in enumerate(fsdp_peers)
            ]
        )
        result[ctx] = total(along_fsdp, n_fsdp)
        exchange(
            [send(result.at[ctx], result.at[ctx], (back_s, back_r), j, peer) for j, peer in enumerate(ctx_peers)]
        )
        out_ref[...] = result[...]

    return pl.pallas_call(
        kernel,
        out_shape=jax.ShapeDtypeStruct(values.shape, values.dtype),
        in_specs=[pl.BlockSpec(memory_space=pltpu.VMEM)],
        out_specs=pl.BlockSpec(memory_space=pltpu.VMEM),
        scratch_shapes=[
            pltpu.VMEM((n_ctx,) + block, values.dtype),
            pltpu.VMEM((n_fsdp,) + block, values.dtype),
            pltpu.VMEM((n_ctx,) + block, values.dtype),
        ]
        + dma_pair(n_ctx)
        + dma_pair(n_fsdp)
        + dma_pair(n_ctx),
        compiler_params=params(2),
        name="sum_everywhere",
    )(values)


def hidden_units(here, back, gate_ref, up_ref, down_ref):
    gate = mm(here, gate_ref[0], CONTRACT_LAST)
    up = mm(here, up_ref[0], CONTRACT_LAST)
    grad_hidden = mm(back, down_ref[0], CONTRACT_LAST)
    sigmoid = jax.nn.sigmoid(gate)
    activated = gate * sigmoid
    return (
        low(activated * up),
        low(grad_hidden * up * sigmoid * (1.0 + gate * (1.0 - sigmoid))),
        low(grad_hidden * activated),
    )


def ffn_forward(rows, planes, core, n_own, chunk=256):
    blocks, _, tokens, features = rows.shape
    total = blocks * tokens
    steps = n_own // chunk
    group = max(1, 256 // tokens)

    def kernel(core_ref, rows_ref, gate_ref, up_ref, down_ref, *outs):
        for at in range(0, blocks, group):
            here = rows_ref[at : at + group, 0].reshape(group * tokens, features)
            back = rows_ref[at : at + group, 1].reshape(group * tokens, features)
            span = pl.ds(at * tokens, group * tokens)
            for out, value in zip(outs, hidden_units(here, back, gate_ref, up_ref, down_ref)):
                out[span] = value

    def weight_spec(plane):
        return pl.BlockSpec((1, chunk, features), lambda j, core_ref: (plane, core_ref[0] * steps + j, 0))

    act = jax.ShapeDtypeStruct((total, n_own), jnp.bfloat16)
    act_spec = pl.BlockSpec((total, chunk), lambda j, core_ref: (0, j))
    return pl.pallas_call(
        kernel,
        grid_spec=pltpu.PrefetchScalarGridSpec(
            num_scalar_prefetch=1,
            grid=(steps,),
            in_specs=[
                pl.BlockSpec(rows.shape, lambda j, core_ref: (0, 0, 0, 0), pipeline_mode=pl.Buffered(1)),
                weight_spec(0),
                weight_spec(1),
                weight_spec(2),
            ],
            out_specs=[act_spec, act_spec, act_spec],
        ),
        out_shape=[act, act, act],
        compiler_params=params(),
        cost_estimate=pl.CostEstimate(
            flops=6 * total * n_own * features, bytes_accessed=30 * 1024 * 1024, transcendentals=total * n_own
        ),
        name="ffn_forward",
    )(core, rows, planes, planes, planes)


def mirror_gather(all_ref, arrivals, sems, pass_sems, ctx, core, fsdp, sibling):
    first, second, corner = fsdp_neighbours(fsdp)
    half = all_ref.shape[2] // 2
    parts = [pl.ds(0, half), pl.ds(half, half)]
    to_first, to_second = (ctx, first), (ctx, second)

    def copy(index, owner, part, peer):
        place_ref = all_ref.at[core, owner, parts[part]]
        return send(place_ref, place_ref, sems, index, peer)

    copies = [
        copy(0, fsdp, 0, to_first),
        copy(1, fsdp, 0, to_second),
        copy(2, fsdp, 1, to_first),
        copy(3, fsdp, 1, to_second),
        copy(4, first, 0, to_second),
        copy(5, second, 1, to_first),
    ]
    passes = [(fsdp, 0), (fsdp, 1), (first, 0), (second, 0), (first, 1), (second, 1), (corner, 0), (corner, 1)]

    def passing_copy(number, side):
        owner, part = passes[number]
        place_ref = all_ref.at[side, owner, parts[part]]
        return send(place_ref, place_ref, pass_sems, number, sibling)

    for part in range(2):
        arrivals[part].wait_recv()
        copies[2 * part].start()
        copies[2 * part + 1].start()
        passing_copy(part, core).start()
        yield
    for index, number, then in ((0, 2, 4), (1, 3, None), (2, 4, None), (3, 5, 5), (4, 6, None), (5, 7, None)):
        owner, part = passes[number]
        copy(index, owner, part, to_first).wait_recv()
        if then is not None:
            copies[then].start()
        passing_copy(number, core).start()
        yield
    for each in copies:
        each.wait_send()
    for number in range(8):
        passing_copy(number, core).wait_send()
        passing_copy(number, 1 - core).wait_recv()


def ffn_rows(n_ctx, own, planes, n_own, chunk=256, wide=512):
    n_fsdp = 4
    size, features = own.shape
    tokens = size // 2
    total = 2 * n_fsdp * tokens

    def kernel(
        own_ref, planes_ref, all_ref, mirror_ref, hidden_a, hidden_b, hidden_c, partial_ref,
        rows, weights, hidden, partial, core_in, load, sq_s, sq_r, core_s, core_r, far_s, far_r, mi_s, mi_r, mc_s, mc_r, sum_s, sum_r, out_sem,
    ):
        chip, core, fsdp, length = place(n_ctx)
        ctx = chip * 2 + core
        sibling = (chip * 2 + 1 - core, fsdp)
        mirror = ((length - 1 - chip) * 2 + core, fsdp)
        first, second, corner = fsdp_neighbours(fsdp)
        greet([sibling, mirror] + fsdp_peers(n_fsdp, ctx, fsdp))
        mine = pltpu.make_async_copy(own_ref, rows.at[core, fsdp], load.at[3])
        mine.start()
        start = pl.multiple_of(core * n_own, n_own)
        loads = [
            pltpu.make_async_copy(planes_ref.at[p, pl.ds(start, n_own)], weights.at[p], load.at[p]) for p in range(3)
        ]
        handed, arriving = [], []

        def hand(source, owner, part, index):
            for side, copies in ((core, handed), (1 - core, arriving)):
                target = rows.at[side, owner] if part is None else rows.at[side, owner, part]
                copies.append(send(source, target, (core_s, core_r), index + 1, sibling))
            handed[-1].start()

        gathering = square_gather(own_ref, rows.at[core], (sq_s, sq_r), ctx, fsdp, n_fsdp, hand)
        next(gathering)
        hand(own_ref, fsdp, None, -1)
        for each in loads:
            each.start()
        far = [
            send(
                own_ref.at[pl.ds(part * tokens, tokens)],
                mirror_ref.at[core, fsdp, pl.ds(part * tokens, tokens)],
                (far_s, far_r),
                part,
                mirror,
            )
            for part in range(2)
        ]
        for each in far:
            each.start()
        mirroring = mirror_gather(mirror_ref, far, (mi_s, mi_r), (mc_s, mc_r), ctx, core, fsdp, sibling)
        outs, summing, sums = [], [], []

        def add_up(number, owner):
            summing[number].wait_recv()
            add_into(partial.at[number % 2, core], core_in.at[number])
            sums.append(
                pltpu.make_async_copy(partial.at[number % 2, core], partial_ref.at[owner], out_sem.at[number % 2, 8])
            )
            sums[-1].start()

        def group(number, owner):
            slot = number % 2
            if number >= 2:
                for each in outs[number - 2]:
                    each.wait()
                summing[number - 2].wait_send()
                sums[number - 2].wait()
            here = jnp.concatenate([rows[0, owner, :tokens], rows[1, owner, :tokens]])
            back = jnp.concatenate([rows[0, owner, tokens:], rows[1, owner, tokens:]])

            @pl.loop(0, n_own // chunk)
            def _(step):
                at = pl.ds(pl.multiple_of(step * chunk, chunk), chunk)
                parts = [weights.at[pl.ds(p, 1), at] for p in range(3)]
                for q, value in enumerate(hidden_units(here, back, *parts)):
                    hidden[slot, q, :, at] = value

            @pl.loop(0, features // wide)
            def _(step):
                at = pl.ds(pl.multiple_of(step * wide, wide), wide)
                out = low(mm(hidden[slot, 0], weights[2, :, at]))
                below = low(mm(hidden[slot, 1], weights[0, :, at]) + mm(hidden[slot, 2], weights[1, :, at]))
                for k in range(2):
                    partial[slot, k, :tokens, at] = out[k * tokens : (k + 1) * tokens]
                    partial[slot, k, tokens:, at] = below[k * tokens : (k + 1) * tokens]

            pairs = []
            summing.append(send(partial.at[slot, 1 - core], core_in.at[number], (sum_s, sum_r), number, sibling))
            summing[-1].start()
            for k in range(2):
                pairs.append((rows.at[k, owner], all_ref.at[k, owner]))
                at = pl.ds(pl.multiple_of((k * n_fsdp + owner) * tokens, tokens), tokens)
                for q, target in enumerate((hidden_a, hidden_b, hidden_c)):
                    pairs.append((hidden.at[slot, q, pl.ds(k * tokens, tokens)], target.at[at]))
            outs.append(
                [pltpu.make_async_copy(a, b, out_sem.at[slot, j]) for j, (a, b) in enumerate(pairs)]
            )
            for each in outs[-1]:
                each.start()

        mine.wait()
        arriving[0].wait_recv()
        for each in loads:
            each.wait()
        group(0, fsdp)
        for _ in range(4):
            next(gathering)
        arriving[1].wait_recv()
        arriving[3].wait_recv()
        group(1, first)
        add_up(0, fsdp)
        next(mirroring)
        for _ in range(2):
            next(gathering)
        arriving[2].wait_recv()
        arriving[4].wait_recv()
        group(2, second)
        add_up(1, first)
        for _ in range(3):
            next(mirroring)
        arriving[5].wait_recv()
        arriving[6].wait_recv()
        group(3, corner)
        add_up(2, second)
        next(mirroring)
        add_up(3, corner)
        run_all(mirroring, gathering)
        for each in handed:
            each.wait_send()
        for each in far:
            each.wait_send()
        for each in outs[2] + outs[3] + sums[2:]:
            each.wait()
        for each in summing[2:]:
            each.wait_send()

    act = jax.ShapeDtypeStruct((total, n_own), own.dtype)
    all_rows = jax.ShapeDtypeStruct((2, n_fsdp) + own.shape, own.dtype)
    return pl.pallas_call(
        kernel,
        in_specs=any_specs(2),
        out_specs=any_specs(6),
        out_shape=[all_rows, all_rows, act, act, act, jax.ShapeDtypeStruct((n_fsdp,) + own.shape, own.dtype)],
        scratch_shapes=[
            pltpu.VMEM((2, n_fsdp) + own.shape, own.dtype),
            pltpu.VMEM((3, n_own, features), own.dtype),
            pltpu.VMEM((2, 3, 2 * tokens, n_own), own.dtype),
            pltpu.VMEM((2, 2) + own.shape, own.dtype),
            pltpu.VMEM((n_fsdp,) + own.shape, own.dtype),
            pltpu.SemaphoreType.DMA((4,)),
        ]
        + dma_pair(6)
        + dma_pair(7)
        + dma_pair(2)
        + dma_pair(6)
        + dma_pair(8)
        + dma_pair(4)
        + [pltpu.SemaphoreType.DMA((2, 9))],
        compiler_params=params(6),
        cost_estimate=pl.CostEstimate(
            flops=12 * total * n_own * features, bytes_accessed=50 * 1024 * 1024, transcendentals=total * n_own
        ),
        name="ffn_rows",
    )(own, planes)


def ffn_weights(n_ctx, n_fsdp, partial, rows, rows_mirror, hidden, planes, n_own, chunk=256):
    blocks, _, tokens, features = rows.shape
    total = blocks * tokens
    steps = n_own // chunk
    group = max(1, 256 // tokens)
    half = features // 2
    sides = n_ctx // 4
    wide = half // sides
    fused = partial is not None
    early = 1 if fused else 0
    assert not fused or sides == 2

    def kernel(*refs):
        rows_ref, refs = refs[0], refs[1:]
        mirror_refs, refs = refs[: len(rows_mirror)], refs[len(rows_mirror) :]
        mirror_blocks = [ref.at[b] for ref in mirror_refs for b in range(ref.shape[0])]
        hidden_ref, grad_gate_ref, grad_up_ref, planes_ref, *refs = refs
        if fused:
            partial_ref, weight_ref, out_ref, early_ref, *refs = refs
        else:
            weight_ref, *refs = refs
        mirror, (weights, weight_sems), refs = refs[:3], refs[3:5], refs[5:]
        chip, core, _, length = place(n_ctx)
        side = chip // sides
        step = pl.program_id(0)
        stages = []
        if fused:
            keep, give, take, side_s, side_r, held, square_in, load, sq_s, sq_r = refs
            member = chip % 2
            other = (chip + 1 - 2 * member) * 2 + core
            crossing = [
                send(give.at[j], take.at[j], (side_s, side_r), j, (other, lax.axis_index("fsdp"))) for j in range(early)
            ]
            starts, *stages = corner_sum_stages(n_ctx, partial_ref, out_ref, held, square_in, load, (sq_s, sq_r))

        def fetch(at, slot):
            start = pl.multiple_of((core * steps + at) * chunk, chunk)
            return pltpu.make_async_copy(planes_ref.at[:, pl.ds(start, chunk)], weights.at[slot], weight_sems.at[slot])

        @pl.when(step == 0)
        def _():
            fetch(0, 0).start()
            if fused:
                fsdp = lax.axis_index("fsdp")
                greet(fsdp_peers(4, chip * 2 + core, fsdp) + [(other, fsdp)])
                for start in sum(starts, []):
                    start()

        @pl.when(step + 1 < steps)
        def _():
            fetch(step + 1, (step + 1) % 2).start()

        slot = step % 2
        fetch(step, slot).wait()
        gate_ref, up_ref, down_ref = (weights.at[slot, pl.ds(plane, 1)] for plane in range(3))
        for at in range(0, blocks, group):
            here = jnp.concatenate([ref[0] for ref in mirror_blocks[at : at + group]])
            back = jnp.concatenate([ref[1] for ref in mirror_blocks[at : at + group]])
            span = pl.ds(at * tokens, group * tokens)
            for out, value in zip(mirror, hidden_units(here, back, gate_ref, up_ref, down_ref)):
                out[span] = value

        lefts = ((grad_gate_ref, mirror[1], 0), (grad_up_ref, mirror[2], 0), (hidden_ref, mirror[0], 1))
        for plane, (left, left_mirror, which) in enumerate(lefts):
            left = left[...]
            left_mirror = left_mirror[...]
            for z in range(sides):
                cols = pl.ds(pl.multiple_of(side * half + z * wide, wide), wide)
                right = rows_ref[:, which, :, cols].reshape(total, wide)
                right_mirror = jnp.concatenate([ref[which, :, cols] for ref in mirror_blocks])
                value = mm(left, right, CONTRACT_FIRST) + mm(left_mirror, right_mirror, CONTRACT_FIRST)
                if not fused:
                    weight_ref[z, plane] = low(value)
                    continue

                @pl.when((step < early) & (z == member))
                def _():
                    keep[step % early, plane] = value

                @pl.when((step < early) & (z != member))
                def _():
                    give[step % early, plane] = low(value)

                @pl.when(step >= early)
                def _():
                    weight_ref[z, plane] = low(value)

        for j in range(early):

            @pl.when(step == j)
            def _():
                crossing[j].start()

        for at, stage in ((1, 0), (steps - 1, 1)):
            if stage < len(stages):

                @pl.when(step == min(at, steps - 1))
                def _():
                    stages[stage]()

        if fused:

            @pl.when(step == steps - 1)
            def _():
                for j in range(early):
                    crossing[j].wait()
                    for plane in range(3):
                        early_ref[plane, j * chunk : (j + 1) * chunk] = low(
                            keep[j, plane] + take[j, plane].astype(jnp.float32)
                        )

    act_spec = pl.BlockSpec((total, chunk), lambda j: (0, j))
    once = dict(pipeline_mode=pl.Buffered(1))
    operands = [rows, *rows_mirror, *hidden, planes]
    in_specs = [whole_block(rows.shape, **once)] + [whole_block(part.shape, **once) for part in rows_mirror]
    in_specs += [act_spec] * 3 + any_specs(1)
    out_specs = [pl.BlockSpec((sides, 3, chunk, wide), lambda j: (0, 0, jnp.maximum(j - early, 0), 0))]
    out_shape = [jax.ShapeDtypeStruct((sides, 3, n_own - early * chunk, wide), jnp.bfloat16)]
    scratch = [pltpu.VMEM((total, chunk), jnp.bfloat16)] * 3
    scratch += [pltpu.VMEM((2, 3, chunk, features), jnp.bfloat16), pltpu.SemaphoreType.DMA((2,))]
    if fused:
        operands.append(partial)
        in_specs += any_specs(1)
        out_specs.append(whole_block(partial.shape[-2:], **once))
        out_shape.append(jax.ShapeDtypeStruct(partial.shape[-2:], jnp.float32))
        out_specs.append(whole_block((3, early * chunk, wide), **once))
        out_shape.append(jax.ShapeDtypeStruct((3, early * chunk, wide), jnp.bfloat16))
        scratch.append(pltpu.VMEM((early, 3, chunk, wide), jnp.float32))
        scratch += [pltpu.VMEM((early, 3, chunk, wide), jnp.bfloat16)] * 2 + dma_pair(early)
        scratch += corner_sum_scratch(partial)
    return pl.pallas_call(
        kernel,
        grid=(steps,),
        in_specs=in_specs,
        out_specs=out_specs,
        out_shape=out_shape,
        scratch_shapes=scratch,
        compiler_params=params(3) if fused else params(),
        cost_estimate=pl.CostEstimate(
            flops=12 * total * n_own * features, bytes_accessed=50 * 1024 * 1024, transcendentals=total * n_own
        ),
        name="ffn_weights",
    )(*operands)


def ffn_back(hidden, grad_gate, grad_up, planes, core, blocks, wide=512):
    total, n_own = hidden.shape
    features = planes.shape[2]
    tokens = total // blocks

    def kernel(core_ref, hidden_ref, grad_gate_ref, grad_up_ref, gate_ref, up_ref, down_ref, out_ref):
        out = mm(hidden_ref[...], down_ref[0])
        out_ref[:, 0] = low(out).reshape(blocks, tokens, wide)
        back = mm(grad_gate_ref[...], gate_ref[0]) + mm(grad_up_ref[...], up_ref[0])
        out_ref[:, 1] = low(back).reshape(blocks, tokens, wide)

    def weight_spec(plane):
        return pl.BlockSpec((1, n_own, wide), lambda j, core_ref: (plane, core_ref[0], j))

    act_spec = pl.BlockSpec((total, n_own), lambda j, core_ref: (0, 0), pipeline_mode=pl.Buffered(1))
    return pl.pallas_call(
        kernel,
        grid_spec=pltpu.PrefetchScalarGridSpec(
            num_scalar_prefetch=1,
            grid=(features // wide,),
            in_specs=[act_spec, act_spec, act_spec, weight_spec(0), weight_spec(1), weight_spec(2)],
            out_specs=pl.BlockSpec((blocks, 2, tokens, wide), lambda j, core_ref: (0, 0, 0, j)),
        ),
        out_shape=jax.ShapeDtypeStruct((blocks, 2, tokens, features), jnp.bfloat16),
        compiler_params=params(),
        cost_estimate=pl.CostEstimate(
            flops=6 * total * n_own * features, bytes_accessed=30 * 1024 * 1024, transcendentals=0
        ),
        name="ffn_back",
    )(core, hidden, grad_gate, grad_up, planes, planes, planes)


SPAN = 256


def ctx_peers(n_ctx):
    ctx = lax.axis_index("ctx")
    fsdp = lax.axis_index("fsdp")
    return [((ctx + j) % n_ctx, fsdp) for j in range(1, n_ctx)]


def deal(n_ctx, block, target, landed, sems, own_sem):
    ctx = lax.axis_index("ctx")
    fsdp = lax.axis_index("fsdp")

    @pl.when(target != ctx)
    def _():
        send(block, landed.at[ctx], sems, (target - ctx + n_ctx) % n_ctx, (target, fsdp)).start()

    @pl.when(target == ctx)
    def _():
        pltpu.make_async_copy(block, landed.at[ctx], own_sem).start()


def dealt(n_ctx, block, landed, sems, own_sem):
    ctx = lax.axis_index("ctx")
    pltpu.make_async_copy(block, landed.at[ctx], own_sem).wait()
    for j, peer in enumerate(ctx_peers(n_ctx)):
        copy = send(block, landed.at[(ctx + n_ctx - j - 1) % n_ctx], sems, j + 1, peer)
        copy.wait_send()
        copy.wait_recv()


def turn(values, cosine, sine):
    return values * cosine + pltpu.roll(values, HEAD_DIM // 2, 1) * sine


def attention_forward(n_ctx, rows, w_qkv, cosine, sine, place_column, place_row, heads):
    total, features = rows.shape
    own = heads * HEAD_DIM
    steps = total // SPAN
    length = total // n_ctx
    scale = HEAD_DIM ** (-0.5)

    def kernel(
        rows_ref, w_ref, cosine_ref, sine_ref, column_ref, row_ref,
        query_ref, key_ref, value_ref, out_ref, log_ref, landed, deal_s, deal_r, own_sem,
    ):
        step = pl.program_id(0)

        @pl.when(step == 0)
        def _():
            greet(ctx_peers(n_ctx))

        span = pl.ds(pl.multiple_of(step * SPAN, SPAN), SPAN)
        qkv = mm(rows_ref[...], w_ref[...])
        cosine = cosine_ref[span]
        sine = sine_ref[span]
        for h in range(heads):
            at = slice(h * HEAD_DIM, (h + 1) * HEAD_DIM)
            query_ref[span, at] = low(turn(qkv[:, at], cosine, sine))
            key_ref[span, at] = low(turn(qkv[:, own + h * HEAD_DIM : own + (h + 1) * HEAD_DIM], cosine, sine))
        value_ref[span] = low(qkv[:, 2 * own :])

        @pl.when(step == steps - 1)
        def _():
            @pl.loop(0, steps)
            def _(block):
                here = pl.ds(pl.multiple_of(block * SPAN, SPAN), SPAN)
                for h in range(heads):
                    at = slice(h * HEAD_DIM, (h + 1) * HEAD_DIM)
                    scores = mm(query_ref[here, at], key_ref[:, at], CONTRACT_LAST) * scale
                    scores = jnp.where(column_ref[here] >= row_ref[...], scores, MASKED)
                    highest = jnp.max(scores, axis=-1, keepdims=True)
                    exponent = jnp.exp(scores - highest)
                    sums = jnp.sum(exponent, axis=-1, keepdims=True)
                    out_ref[here, at] = low(mm(low(exponent * (1.0 / sums)), value_ref[:, at]))
                    log_ref[h, here] = highest + jnp.log(sums)
                for r in range(SPAN // length):
                    mine = out_ref.at[pl.ds(pl.multiple_of(block * SPAN + r * length, length), length)]
                    deal(n_ctx, mine, block * (SPAN // length) + r, landed, (deal_s, deal_r), own_sem)

            dealt(n_ctx, out_ref.at[pl.ds(0, length)], landed, (deal_s, deal_r), own_sem)

    act = jax.ShapeDtypeStruct((total, own), jnp.bfloat16)
    return pl.pallas_call(
        kernel,
        grid=(steps,),
        in_specs=[pl.BlockSpec((SPAN, features), lambda r: (r, 0))]
        + [whole_block(a.shape) for a in (w_qkv, cosine, sine, place_column, place_row)],
        out_specs=[whole_block((total, own))] * 4 + [whole_block((heads, total, 1))] + any_specs(1),
        out_shape=[act] * 4
        + [
            jax.ShapeDtypeStruct((heads, total, 1), jnp.float32),
            jax.ShapeDtypeStruct((n_ctx, length, own), jnp.bfloat16),
        ],
        scratch_shapes=dma_pair(n_ctx) + [pltpu.SemaphoreType.DMA],
        compiler_params=params(8),
        name="attention_forward",
    )(rows, w_qkv, cosine, sine, place_column, place_row)


def attention_backward(query, key, value, grad, logs, w_qkv, cosine, sine, place_column, place_row, heads):
    total, own = query.shape
    features = w_qkv.shape[0]
    steps = total // SPAN
    scale = HEAD_DIM ** (-0.5)

    def kernel(
        query_ref, key_ref, value_ref, grad_ref, log_ref, w_ref, cosine_ref, sine_ref, column_ref, row_ref,
        qkv_ref, out_ref, key_sum, value_sum,
    ):
        step = pl.program_id(0)

        @pl.when(step == 0)
        def _():
            for h in range(heads):
                at = slice(h * HEAD_DIM, (h + 1) * HEAD_DIM)
                key_sum[...] = jnp.zeros_like(key_sum)
                value_sum[...] = jnp.zeros_like(value_sum)

                @pl.loop(0, steps)
                def _(block):
                    here = pl.ds(pl.multiple_of(block * SPAN, SPAN), SPAN)
                    queries = query_ref[here, at]
                    grads = grad_ref[here, at]
                    scores = mm(queries, key_ref[:, at], CONTRACT_LAST) * scale
                    scores = jnp.where(column_ref[here] >= row_ref[...], scores, MASKED)
                    probs = jnp.exp(scores - log_ref[h, here])
                    probs_grad = mm(grads, value_ref[:, at], CONTRACT_LAST)
                    centre = jnp.sum(probs * probs_grad, axis=-1, keepdims=True)
                    scores_grad = low(probs * (probs_grad - centre))
                    query_grad = mm(scores_grad, key_ref[:, at]) * scale
                    qkv_ref[here, at] = low(turn(query_grad, cosine_ref[here], -sine_ref[here]))
                    key_sum[...] += mm(scores_grad, queries, CONTRACT_FIRST)
                    value_sum[...] += mm(low(probs), grads, CONTRACT_FIRST)

                qkv_ref[:, own + h * HEAD_DIM : own + (h + 1) * HEAD_DIM] = low(
                    turn(key_sum[...] * scale, cosine_ref[...], -sine_ref[...])
                )
                qkv_ref[:, 2 * own + h * HEAD_DIM : 2 * own + (h + 1) * HEAD_DIM] = low(value_sum[...])

        span = pl.ds(pl.multiple_of(step * SPAN, SPAN), SPAN)
        out_ref[...] = low(mm(qkv_ref[span], w_ref[...], CONTRACT_LAST))

    return pl.pallas_call(
        kernel,
        grid=(steps,),
        in_specs=[
            whole_block(a.shape)
            for a in (query, key, value, grad, logs, w_qkv, cosine, sine, place_column, place_row)
        ],
        out_specs=[whole_block((total, 3 * own)), pl.BlockSpec((SPAN, features), lambda r: (r, 0))],
        out_shape=[
            jax.ShapeDtypeStruct((total, 3 * own), jnp.bfloat16),
            jax.ShapeDtypeStruct((total, features), jnp.bfloat16),
        ],
        scratch_shapes=[pltpu.VMEM((total, HEAD_DIM), jnp.float32)] * 2,
        compiler_params=params(),
        name="attention_backward",
    )(query, key, value, grad, logs, w_qkv, cosine, sine, place_column, place_row)


ROWS = 32


def row_blocks(count, features):
    return pl.BlockSpec((count, ROWS, features), lambda r, *_: (0, r, 0))


def whole_block(shape, **more):
    zeros = (0,) * len(shape)
    return pl.BlockSpec(shape, lambda r, *_: zeros, **more)


def split(values):
    high = low(values)
    return (high, low(values - high.astype(jnp.float32)))


def connect_coefficients(values, dynamic_ref, static_ref, coef_ref, dyn_ref):
    lane = lax.broadcasted_iota(jnp.int32, (values[0].shape[0], 8), 1)
    columns = []
    for i, value in enumerate(values):
        mean = jnp.mean(value, axis=-1, keepdims=True)
        centered = value - mean
        inverse = lax.rsqrt(jnp.mean(centered * centered, axis=-1, keepdims=True) + EPS)
        normed = centered * inverse
        projected = jnp.zeros(lane.shape, jnp.float32)
        for k in range(6):
            part = jnp.sum(normed * dynamic_ref[k : k + 1], axis=-1, keepdims=True)
            projected = jnp.where(lane == k, part, projected)
        coefficient = jnp.tanh(projected) + static_ref[i : i + 1]
        dyn_ref[i] = projected
        coef_ref[i] = jnp.where(lane == 6, mean, jnp.where(lane == 7, inverse, coefficient))
        columns.append(coefficient)
    return columns


def connect_first(streams, dynamic, static):
    number, rows, features = streams.shape

    def kernel(streams_ref, dynamic_ref, static_ref, coef_ref, dyn_ref, low_ref):
        values = [streams_ref[i].astype(jnp.float32) for i in range(number)]
        columns = connect_coefficients(values, dynamic_ref, static_ref, coef_ref, dyn_ref)
        mixed = sum((columns[i][:, 1:2] * values[i] for i in range(number)))
        low_ref[...] = low(normalize(mixed)[0])

    small = jax.ShapeDtypeStruct((number, rows, 8), jnp.float32)
    return pl.pallas_call(
        kernel,
        grid=(rows // ROWS,),
        out_shape=(small, small, jax.ShapeDtypeStruct((rows, features), jnp.bfloat16)),
        in_specs=[row_blocks(number, features), whole_block(dynamic.shape), whole_block(static.shape)],
        out_specs=(
            row_blocks(number, 8),
            row_blocks(number, 8),
            pl.BlockSpec((ROWS, features), lambda r: (r, 0)),
        ),
        compiler_params=params(),
        name="connect_first",
    )(streams, dynamic, static)


def connect_middle(streams, coef, attended, w_mine, w_other, cotangent, dynamic, static, core_fsdp, where, depth):
    number, rows, features = streams.shape
    half = features // 2
    own = attended.shape[2]
    count = len(w_mine)

    def kernel(core_ref, streams_ref, coef_ref, attended_ref, *refs):
        weights, refs = refs[: 2 * count], refs[2 * count :]
        cotangent_ref, dynamic_ref, static_ref = refs[:3]
        first_ref, branch_ref, coef_two_ref, dyn_ref, own_ref, projected = refs[3:]
        step = pl.program_id(0)

        @pl.when(step == 0)
        def _():
            for side in range(2):
                total = 0.0
                for j, (d, offset) in enumerate(where):
                    for q in range(w_mine[j].shape[0] // own):
                        part = attended_ref[(core_ref[1] ^ d) * (depth // own) + offset // own + q]
                        total = total + mm(part, weights[side * count + j][q * own : (q + 1) * own])
                projected[core_ref[0] if side == 0 else 1 - core_ref[0]] = total

        span = pl.ds(pl.multiple_of(step * ROWS, ROWS), ROWS)
        branch = jnp.concatenate([projected[0, span], projected[1, span]], axis=1)
        branch_ref[...] = branch
        inputs = [streams_ref[i].astype(jnp.float32) for i in range(number)]
        outs = []
        for j in range(number):
            out = sum((coef_ref[i][:, 2 + j : 3 + j] * inputs[i] for i in range(number)))
            outs.append(out + coef_ref[j][:, 0:1] * branch)
            first_ref[j] = outs[-1]
        columns = connect_coefficients(outs, dynamic_ref, static_ref, coef_two_ref, dyn_ref)
        mixed = sum((columns[i][:, 1:2] * outs[i] for i in range(number)))
        own_ref[0] = low(normalize(mixed)[0])
        own_ref[1] = low(sum((columns[j][:, 0:1] * cotangent_ref[j].astype(jnp.float32) for j in range(number))))

    small = jax.ShapeDtypeStruct((number, rows, 8), jnp.float32)
    once = dict(pipeline_mode=pl.Buffered(1))
    return pl.pallas_call(
        kernel,
        grid_spec=pltpu.PrefetchScalarGridSpec(
            num_scalar_prefetch=1,
            grid=(rows // ROWS,),
            in_specs=[
                row_blocks(number, features),
                row_blocks(number, 8),
                whole_block(attended.shape, **once),
                *[whole_block(w.shape, **once) for w in w_mine + w_other],
                row_blocks(number, features),
                whole_block(dynamic.shape),
                whole_block(static.shape),
            ],
            out_specs=(
                row_blocks(number, features),
                pl.BlockSpec((ROWS, features), lambda r, *_: (r, 0)),
                row_blocks(number, 8),
                row_blocks(number, 8),
                row_blocks(2, features),
            ),
            scratch_shapes=[pltpu.VMEM((2, rows, half), jnp.float32)],
        ),
        out_shape=(
            jax.ShapeDtypeStruct((number, rows, features), jnp.float32),
            jax.ShapeDtypeStruct((rows, features), jnp.float32),
            small,
            small,
            jax.ShapeDtypeStruct((2, rows, features), jnp.bfloat16),
        ),
        compiler_params=params(),
        name="connect_middle",
    )(core_fsdp, streams, coef, attended, *w_mine, *w_other, cotangent, dynamic, static)


def attention_weights(rows, grads, attended, grad_cols):
    total, features = rows.shape
    parts, _, own = attended.shape
    wide = grads.shape[1]

    def kernel(rows_ref, grads_ref, attended_ref, cols_ref, out_ref):
        out_ref[:, :wide] = low(mm(rows_ref[...], grads_ref[...], CONTRACT_FIRST))
        out_ref[:, wide:] = low(mm(attended_ref[0], cols_ref[...], CONTRACT_FIRST))

    return pl.pallas_call(
        kernel,
        grid=(parts,),
        in_specs=[
            pl.BlockSpec((total, own), lambda k: (0, k)),
            whole_block(grads.shape),
            pl.BlockSpec((1, total, own), lambda k: (k, 0, 0)),
            whole_block(grad_cols.shape),
        ],
        out_specs=pl.BlockSpec((own, wide + own), lambda k: (k, 0)),
        out_shape=jax.ShapeDtypeStruct((features, wide + own), jnp.bfloat16),
        compiler_params=params(),
        cost_estimate=pl.CostEstimate(
            flops=2 * total * features * (wide + own), bytes_accessed=16 * 1024 * 1024, transcendentals=0
        ),
        name="attention_weights",
    )(rows, grads, attended, grad_cols)


def flip(index, bits, count):
    result = index
    bit = 1
    while bit < count:
        if bits & bit:
            result = result + bit - 2 * bit * (index // bit % 2)
        bit *= 2
    return result


def project_back(n_ctx, n_fsdp, grad, w_mine, w_other, where, depth):
    rows, features = grad.shape
    half = features // 2
    count = len(w_mine)
    own = features // n_ctx

    def kernel(grad_ref, *refs):
        weights, refs = refs[: 2 * count], refs[2 * count :]
        landed, cols_ref, outs, deal_s, deal_r, own_sem = refs
        _, core, fsdp, _ = place(n_ctx)
        greet(ctx_peers(n_ctx))
        first = grad_ref[:, pl.ds(pl.multiple_of(core * half, half), half)]
        second = grad_ref[:, pl.ds(pl.multiple_of((1 - core) * half, half), half)]
        for j, (d, offset) in enumerate(where):
            out = low(
                mm(first, weights[j][...], CONTRACT_LAST) + mm(second, weights[count + j][...], CONTRACT_LAST)
            )
            for q in range(w_mine[j].shape[0] // own):
                at = flip(fsdp, d, n_fsdp) * (depth // own) + offset // own + q
                outs[at] = out[:, q * own : (q + 1) * own]
                deal(n_ctx, outs.at[at], at, landed, (deal_s, deal_r), own_sem)
        for index in range(n_ctx):
            cols_ref[index] = grad_ref[:, index * own : (index + 1) * own]
        dealt(n_ctx, outs.at[0], landed, (deal_s, deal_r), own_sem)

    shape = (n_ctx, rows, own)
    return pl.pallas_call(
        kernel,
        in_specs=[pl.BlockSpec(memory_space=pltpu.VMEM)] * (1 + 2 * count),
        out_specs=any_specs(1) + [pl.BlockSpec(memory_space=pltpu.VMEM)],
        out_shape=[jax.ShapeDtypeStruct(shape, grad.dtype)] * 2,
        scratch_shapes=[pltpu.VMEM(shape, grad.dtype)] + dma_pair(n_ctx) + [pltpu.SemaphoreType.DMA],
        compiler_params=params(9),
        name="project_back",
    )(grad, *w_mine, *w_other)


def connect_back(values, coef, dyn, branch, grads, grad_normed, dynamic, means, coef_before=None, offset=0):
    number, rows, features = values.shape
    steps = rows // ROWS
    more = coef_before is not None

    def kernel(*refs):
        values_ref, coef_ref, dyn_ref, branch_ref, grads_ref, normed_ref, dynamic_ref, means_ref = refs[:8]
        refs = refs[8:]
        if more:
            before_ref, refs = refs[0], refs[1:]
        out_ref, dynamic_out, static_out = refs[:3]
        if more:
            forward_ref, grad_low_ref = refs[3:5]
        step = pl.program_id(0)

        @pl.when(step == 0)
        def _():
            dynamic_out[...] = jnp.zeros_like(dynamic_out)
            static_out[...] = jnp.zeros_like(static_out)

        branch = branch_ref[...]
        grads = [grads_ref[j].astype(jnp.float32) for j in range(number)]
        mixed = sum((coef_ref[i][:, 1:2] * values_ref[i].astype(jnp.float32) for i in range(number)))
        normed, inverse = normalize(mixed)
        grad_mixed = normalize_back(normed, inverse, normed_ref[...])
        lane = lax.broadcasted_iota(jnp.int32, (ROWS, 8), 1)
        pre_grads, highs, lows = [], [], []
        for i in range(number):
            value = values_ref[i].astype(jnp.float32)
            columns = [grads[i] * branch, grad_mixed * value] + [grads[j] * value for j in range(number)]
            coef_grad = jnp.zeros((ROWS, 8), jnp.float32)
            for k, column in enumerate(columns):
                coef_grad = jnp.where(lane == k, jnp.sum(column, axis=-1, keepdims=True), coef_grad)
            static_out[i : i + 1] += jnp.sum(coef_grad, axis=0, keepdims=True)
            part = jnp.tanh(dyn_ref[i])
            pre_grads.append(coef_grad * (1.0 - part * part))
            high, rest = split((value - coef_ref[i][:, 6:7]) * coef_ref[i][:, 7:8])
            highs.append(high)
            lows.append(rest)
        pre, pre_rest = split(jnp.concatenate(pre_grads))
        dynamic, dynamic_rest = split(dynamic_ref[...])
        normed_grads = mm(
            jnp.concatenate([pre, pre_rest, pre], axis=1), jnp.concatenate([dynamic, dynamic, dynamic_rest], axis=0)
        )
        highs = jnp.concatenate(highs)
        dynamic_out[...] += (
            mm(pre, highs, CONTRACT_FIRST)
            + mm(pre_rest, highs, CONTRACT_FIRST)
            + mm(pre, jnp.concatenate(lows), CONTRACT_FIRST)
        )
        befores = 0.0
        for i in range(number):
            coef = coef_ref[i]
            mean_grad = jnp.sum(pre_grads[i] * means_ref[...], axis=-1, keepdims=True)
            inner = jnp.sum(pre_grads[i] * dyn_ref[i], axis=-1, keepdims=True) / features
            normed = (values_ref[i].astype(jnp.float32) - coef[:, 6:7]) * coef[:, 7:8]
            out = coef[:, 7:8] * (normed_grads[i * ROWS : (i + 1) * ROWS] - mean_grad - normed * inner)
            out = out + coef[:, 1:2] * grad_mixed
            for j in range(number):
                out = out + coef[:, 2 + j : 3 + j] * grads[j]
            out_ref[i] = out
            if more:
                befores = befores + before_ref[i][:, 0:1] * out
        if more:
            grad_low_ref[...] = low(befores)
            for j in range(number):
                out = coef_ref[j][:, 0:1] * branch
                for i in range(number):
                    out = out + coef_ref[i][:, 2 + j : 3 + j] * values_ref[i].astype(jnp.float32)
                forward_ref[j] = low(out)

    rows_spec = pl.BlockSpec((ROWS, features), lambda r: (r, 0))
    out_shape = [
        jax.ShapeDtypeStruct((number, rows, features), jnp.float32),
        jax.ShapeDtypeStruct((8, features), jnp.float32),
        jax.ShapeDtypeStruct((8, 8), jnp.float32),
    ]
    out_specs = [row_blocks(number, features), whole_block((8, features)), whole_block((8, 8))]
    operands = [values, coef, dyn, branch, grads, grad_normed, dynamic, means]
    in_specs = [
        row_blocks(number, features),
        row_blocks(number, 8),
        row_blocks(number, 8),
        rows_spec,
        row_blocks(number, features),
        pl.BlockSpec((ROWS, features), lambda r: (offset // ROWS + r, 0)),
        whole_block(dynamic.shape),
        whole_block(means.shape),
    ]
    if more:
        operands.append(coef_before)
        in_specs.append(row_blocks(number, 8))
        out_shape.append(jax.ShapeDtypeStruct((number, rows, features), jnp.bfloat16))
        out_specs.append(row_blocks(number, features))
        out_shape.append(jax.ShapeDtypeStruct((rows, features), jnp.bfloat16))
        out_specs.append(rows_spec)
    return pl.pallas_call(
        kernel,
        grid=(steps,),
        in_specs=in_specs,
        out_specs=out_specs,
        out_shape=out_shape,
        compiler_params=params(),
        name="connect_back",
    )(*operands)


def local(n_ctx, n_fsdp, streams, w_attn, w_ffn, hc_dynamic, hc_static, cotangent, pair_order):
    number = streams.shape[1]
    length = streams.shape[2]
    features = streams.shape[3]
    size = HEAD_DIM
    own = features // n_ctx
    heads = own // size
    rows = length * n_ctx
    own_rows = w_attn.shape[0]
    ctx = lax.axis_index("ctx")
    fsdp = lax.axis_index("fsdp")
    core = ctx % 2
    chips = n_ctx // 2
    core_index = jnp.reshape(core, (1,)).astype(jnp.int32)

    def in_order(mine, other, axis):
        return jnp.where(
            core == 0, jnp.concatenate([mine, other], axis=axis), jnp.concatenate([other, mine], axis=axis)
        )


    w_own = lax.dynamic_slice_in_dim(w_attn, ctx * own, own, 2)[:, 0:3].reshape(own_rows, 3 * own)
    w_qkv = gather(w_own, "fsdp")
    half = features // 2
    w_half = lax.dynamic_slice_in_dim(w_attn, core * half, half, 2)[:, 3]
    siblings = [(i, i ^ 1) for i in range(n_ctx)]
    core_fsdp = jnp.stack([core, fsdp]).astype(jnp.int32)

    def exchange(values, most=0):
        return [values] + [
            lax.ppermute(values, "fsdp", [(i, i ^ d) for i in range(n_fsdp)])
            for d in range(1, most + 1 if most else n_fsdp)
        ]

    def swap(blocks):
        return [lax.ppermute(block, "ctx", siblings) for block in blocks]


    positions = block_positions(pair_order, length)
    frequency = THETA ** (-(jnp.arange(size // 2, dtype=jnp.float32) * 2.0) / size)
    angles = positions.astype(jnp.float32)[:, None] * jnp.concatenate([frequency, frequency])[None, :]
    signs = jnp.where(jnp.arange(size) < size // 2, -1.0, 1.0)
    tables = (jnp.cos(angles), jnp.sin(angles) * signs[None, :], positions[:, None], positions[None, :])

    dynamics = jnp.pad(hc_dynamic, ((0, 0), (0, 2), (0, 0)))
    means = jnp.mean(dynamics, axis=-1)
    statics = jnp.pad(hc_static, ((0, 0), (0, 0), (0, 2)))
    coef_one, dyn_one, attn_low = connect_first(streams[0], dynamics[0], statics[0])
    attn_low, w_half = lax.optimization_barrier((attn_low, w_half))
    w_out_mine = exchange(w_half, 2 if n_fsdp == 4 else 0)
    attn_all = line_rows(n_ctx, attn_low).reshape(rows, features)
    w_out_where = [(d, 0) for d in range(len(w_out_mine))]
    attn_all, *w_out_mine = lax.optimization_barrier((attn_all, *w_out_mine))
    w_out_other = swap(w_out_mine)
    if n_fsdp == 4:
        middle = own_rows // 2
        corners = [
            lax.ppermute(w_out_mine[1][:middle], "fsdp", [(i, i ^ 2) for i in range(4)]),
            lax.ppermute(w_out_mine[2][middle:], "fsdp", [(i, i ^ 1) for i in range(4)]),
        ]
        w_out_where += [(3, 0), (3, middle)]
    query, key, value, attended, logs, attended_rows = attention_forward(n_ctx, attn_all, w_qkv, *tables, heads)
    if n_fsdp == 4:
        attended, *corners = lax.optimization_barrier((attended, *corners))
        w_out_mine += corners
        w_out_other += swap(corners)

    first_out, attn_branch, coef_two, dyn_two, ffn_own = connect_middle(
        streams[0], coef_one, attended_rows, w_out_mine, w_out_other, cotangent[0], dynamics[1], statics[1], core_fsdp,
        w_out_where, own_rows,
    )
    ffn_own = ffn_own.reshape(2 * length, features)

    planes = jnp.moveaxis(w_ffn, 1, 0)
    n_own = planes.shape[1] // 2
    blocks = 2 * n_fsdp
    if n_fsdp == 4:
        ffn_all, mirror_rows, *hidden, sums = ffn_rows(n_ctx, ffn_own, planes, n_own)
        ffn_all, mirror_rows = (part.reshape(blocks, 2, length, features) for part in (ffn_all, mirror_rows))
        mirror_rows = [mirror_rows]
        attended, sums = lax.optimization_barrier((attended, sums))
        attended_all = gather(attended, "ctx").reshape(n_ctx, rows, own)
        weight_parts, sums, weight_early = ffn_weights(
            n_ctx, n_fsdp, sums, ffn_all, mirror_rows, hidden, planes, n_own
        )
    else:
        ffn_mirror = lax.ppermute(ffn_own, "ctx", [(i, n_ctx - 2 - i + 2 * (i % 2)) for i in range(n_ctx)])
        ffn_all = square_core_gather(n_ctx, n_fsdp, ffn_own).reshape(blocks, 2, length, features)
        attended_all = gather(attended, "ctx").reshape(n_ctx, rows, own)
        mirror_mine = exchange(ffn_mirror)
        hidden = ffn_forward(ffn_all, planes, core_index, n_own)
        sums = ffn_back(*hidden, planes, core_index, blocks)
        mirror_rows = [part.reshape(1, 2, length, features) for part in mirror_mine + swap(mirror_mine)]
        sums = square_sum(n_ctx, n_fsdp, sums.reshape(2, n_fsdp, 2 * length, features))
        (weight_parts,) = ffn_weights(n_ctx, n_fsdp, None, ffn_all, mirror_rows, hidden, planes, n_own)
    sides = chips // 2
    lines = [[2 * (sides * side + i) + j for i in range(sides)] for side in range(2) for j in range(2)]
    weight_cols = lax.psum_scatter(weight_parts, "ctx", scatter_dimension=0, axis_index_groups=lines)

    grad_first, dynamic_grad_two, static_grad_two, streams_out, grad_attn = connect_back(
        first_out, coef_two, dyn_two, sums, cotangent[0], sums, dynamics[1], means[1:], coef_one, length
    )
    grad_heads, grad_cols = project_back(n_ctx, n_fsdp, grad_attn, w_out_mine, w_out_other, w_out_where, own_rows)
    grad_heads = grad_heads.reshape(rows, own)
    grad_heads, grad_cols = lax.optimization_barrier((grad_heads, grad_cols))
    grad_cols = lax.all_to_all(grad_cols, "ctx", 0, 0, tiled=True).reshape(rows, own)
    qkv_grad, attn_part = attention_backward(query, key, value, grad_heads, logs, w_qkv, *tables, heads)
    attn_part = attn_part.reshape(n_ctx, length, features)
    if n_fsdp == 4:
        grad_attn_normed, attn_grad = attention_sums(n_ctx, attn_part, attn_all, qkv_grad, attended_all, grad_cols)
    else:
        grad_attn_normed = line_sum(n_ctx, attn_part)
        attn_grad = scatter(attention_weights(attn_all, qkv_grad, attended_all, grad_cols), "fsdp").astype(jnp.float32)
    grad_attn_normed, weight_cols = lax.optimization_barrier((grad_attn_normed, weight_cols))
    if n_fsdp == 4:
        weight_cols = jnp.concatenate([weight_early, weight_cols], axis=1)
    mine = lax.dynamic_slice_in_dim(weight_cols, core * own, own, 2)
    other = lax.dynamic_slice_in_dim(weight_cols, (1 - core) * own, own, 2)
    other = lax.ppermute(other, "ctx", siblings)
    ffn_grad = jnp.moveaxis(in_order(mine, other, 1), 0, 1).astype(jnp.float32)
    grad_inputs, dynamic_grad_one, static_grad_one = connect_back(
        streams[0], coef_one, dyn_one, attn_branch, grad_first, grad_attn_normed, dynamics[0], means[:1]
    )
    static_grads = jnp.concatenate([static_grad_one[:number, :6].reshape(1, -1), static_grad_two[:number, :6].reshape(1, -1)])
    small = jnp.concatenate(
        [
            dynamic_grad_one[:6],
            dynamic_grad_two[:6],
            jnp.pad(static_grads, ((0, 2), (0, features - 6 * number))),
        ]
    )
    small = sum_everywhere(n_ctx, n_fsdp, small.reshape(n_ctx, 8, -1))
    small = small.reshape(16, features)
    attn_grad = attn_grad.reshape(own_rows, 4, own)
    dynamic_total = small[:12].reshape(2, 6, features)
    static_total = small[12:14, : 6 * number].reshape(2, number, 6)
    return (streams_out[None], grad_inputs[None], attn_grad, ffn_grad, dynamic_total, static_total)


def solution(mesh):
    return jax.shard_map(
        functools.partial(local, mesh.shape["ctx"], mesh.shape["fsdp"]),
        mesh=mesh,
        in_specs=(
            P("fsdp", None, "ctx", None),
            P("fsdp", None, None),
            P("fsdp", None, None),
            P(),
            P(),
            P("fsdp", None, "ctx", None),
            P(),
        ),
        out_specs=(
            P("fsdp", None, "ctx", None),
            P("fsdp", None, "ctx", None),
            P("fsdp", None, "ctx"),
            P("fsdp", None, "ctx"),
            P(),
            P(),
        ),
        check_vma=False,
    )
```

```python
import functools

import jax
import jax.numpy as jnp
from jax import lax
from jax.experimental import pallas as pl
from jax.experimental.pallas import tpu as pltpu
from jax.sharding import PartitionSpec as P

HEADS = 16
HEAD_DIM = 128


EPS = 1e-05
THETA = 10000.0
HIGH = lax.Precision.HIGHEST
MASKED = -1e30
CONTRACT_LAST = (((1,), (1,)), ((), ()))
CONTRACT_FIRST = (((0,), (0,)), ((), ()))


def normalize(values):
    centered = values - jnp.mean(values, axis=-1, keepdims=True)
    inverse = lax.rsqrt(jnp.mean(centered * centered, axis=-1, keepdims=True) + EPS)
    return (centered * inverse, inverse)


def normalize_back(normed, inverse, gradient):
    inner = jnp.mean(gradient * normed, axis=-1, keepdims=True)
    return inverse * (gradient - jnp.mean(gradient, axis=-1, keepdims=True) - normed * inner)


def block_positions(pair_order, length):
    half_size = length // 2
    offsets = jnp.arange(half_size, dtype=jnp.int32)
    mirror = 2 * pair_order.shape[0] - 1 - pair_order
    first_half = pair_order[:, None] * half_size + offsets[None, :]
    second_half = mirror[:, None] * half_size + offsets[None, :]
    return jnp.concatenate([first_half, second_half], axis=1).reshape(-1)


def low(values):
    return values.astype(jnp.bfloat16)


def mm(a, b, dims=None):
    if dims is None:
        return jnp.dot(a, b, preferred_element_type=jnp.float32)
    return lax.dot_general(a, b, dims, preferred_element_type=jnp.float32)


def gather(values, axis, dim=0):
    return lax.all_gather(values, axis, axis=dim, tiled=True)


def scatter(values, axis, dim=0):
    return lax.psum_scatter(values, axis, scatter_dimension=dim, tiled=True)


MESH = pl.DeviceIdType.MESH
VMEM_LIMIT = 60 * 1024 * 1024


def place(n_ctx):
    ctx = lax.axis_index("ctx")
    return (ctx // 2, ctx % 2, lax.axis_index("fsdp"), n_ctx // 2)


def greet(peers):
    barrier = pltpu.get_barrier_semaphore()
    for peer in peers:
        pl.semaphore_signal(barrier, inc=1, device_id=peer, device_id_type=MESH)
    pl.semaphore_wait(barrier, len(peers))


def send(source, target, sems, index, peer):
    return pltpu.make_async_remote_copy(
        src_ref=source,
        dst_ref=target,
        send_sem=sems[0].at[index],
        recv_sem=sems[1].at[index],
        device_id=peer,
        device_id_type=MESH,
    )


def fsdp_neighbours(fsdp):
    first = fsdp + 1 - 2 * (fsdp % 2)
    second = (fsdp + 2) % 4
    return (first, second, (first + 2) % 4)


def fsdp_peers(n_fsdp, ctx, fsdp):
    if n_fsdp == 4:
        first, second, _ = fsdp_neighbours(fsdp)
        return [(ctx, first), (ctx, second)]
    return [(ctx, (fsdp + j) % n_fsdp) for j in range(1, n_fsdp)]


def line_peers(chip, core, fsdp, length):
    return [
        (chip * 2 + 1 - core, fsdp),
        ((chip + 1) % length * 2 + core, fsdp),
        ((chip + length - 1) % length * 2 + core, fsdp),
    ]


def line_gather(own_ref, all_ref, sems, where):
    chip, core, fsdp, length = where
    right_sems, left_sems, core_sems = sems
    sibling = (chip * 2 + 1 - core, fsdp)
    right = ((chip + 1) % length * 2 + core, fsdp)
    left = ((chip + length - 1) % length * 2 + core, fsdp)

    def block(index):
        return all_ref.at[(index + length) % length * 2 + core]

    def pass_on(index, source):
        return send(source, block(index), core_sems, (index + length) % length, sibling)

    pass_on(chip, own_ref).start()
    for step in range(length - 1):
        for sign, peer, way in ((-1, right, right_sems), (1, left, left_sems)):
            at = chip + sign * step
            held = (at >= 0) & (at < length)
            if step > 0:

                @pl.when(held)
                def _():
                    send(block(at), block(at), way, step - 1, peer).wait_recv()
                    pass_on(at, block(at)).start()

            more = (chip < length - 1) if sign < 0 else (chip > 0)

            @pl.when(held & more)
            def _():
                send(own_ref if step == 0 else block(at), block(at), way, step, peer).start()

        yield
    last = length - 1
    for sign, peer, way in ((-1, right, right_sems), (1, left, left_sems)):
        at = chip + sign * last

        @pl.when((at >= 0) & (at < length))
        def _():
            send(block(at), block(at), way, last - 1, peer).wait_recv()
            pass_on(at, block(at)).start()

    yield
    for step in range(length - 1):
        for sign, peer, way in ((-1, right, right_sems), (1, left, left_sems)):
            at = chip + sign * step
            more = (chip < length - 1) if sign < 0 else (chip > 0)

            @pl.when((at >= 0) & (at < length) & more)
            def _():
                send(block(at), block(at), way, step, peer).wait_send()

    for index in range(length):
        pass_on(index, block(index)).wait_send()
        other = all_ref.at[index * 2 + 1 - core]
        send(other, other, core_sems, index, sibling).wait_recv()


def square_gather(own_ref, all_ref, sems, ctx, fsdp, n_fsdp, passed=None):
    if n_fsdp != 4:
        copies = [
            send(own_ref, all_ref.at[fsdp], sems, j - 1, (ctx, (fsdp + j) % n_fsdp)) for j in range(1, n_fsdp)
        ]
        for copy in copies:
            copy.start()
        yield
        for j, copy in enumerate(copies):
            copy.wait()
            if passed:
                passed(all_ref.at[(fsdp + n_fsdp - j - 1) % n_fsdp], (fsdp + n_fsdp - j - 1) % n_fsdp, None, j)
        return
    first, second, corner = fsdp_neighbours(fsdp)
    half = own_ref.shape[0] // 2
    top, low_half = pl.ds(0, half), pl.ds(half, half)
    to_first, to_second = (ctx, first), (ctx, second)

    def copy(index, owner, part, peer, source=None):
        source = all_ref.at[owner, part] if source is None else source
        return send(source, all_ref.at[owner, part], sems, index, peer)

    starts = [
        copy(0, fsdp, top, to_first, own_ref.at[top]),
        copy(1, fsdp, low_half, to_second, own_ref.at[low_half]),
        copy(2, fsdp, low_half, to_first, own_ref.at[low_half]),
        copy(3, fsdp, top, to_second, own_ref.at[top]),
        copy(4, first, top, to_second),
        copy(5, second, low_half, to_first),
    ]
    arrivals = [
        (0, first, top),
        (1, second, low_half),
        (2, first, low_half),
        (3, second, top),
        (4, corner, top),
        (5, corner, low_half),
    ]
    for each in starts[:4]:
        each.start()
    yield
    for index, owner, part in arrivals:
        copy(index, owner, part, to_first).wait_recv()
        if index < 2:
            starts[4 + index].start()
        if passed:
            passed(all_ref.at[owner, part], owner, part, index)
        yield
    for each in starts:
        each.wait_send()


def run_all(*parts):
    parts = list(parts)
    while parts:
        for part in list(parts):
            try:
                next(part)
            except StopIteration:
                parts.remove(part)


def dma_pair(count):
    return [pltpu.SemaphoreType.DMA((count,)), pltpu.SemaphoreType.DMA((count,))]


def any_specs(count):
    return [pl.BlockSpec(memory_space=pl.ANY)] * count


def params(collective_id=None, **more):
    if collective_id is not None:
        more.update(collective_id=collective_id, has_side_effects=True)
    return pltpu.CompilerParams(vmem_limit_bytes=VMEM_LIMIT, **more)


def passing(own_ref, all_ref, sems, core, fsdp, sibling):
    handed = [send(own_ref, all_ref.at[core, fsdp], sems, 0, sibling)]
    handed[0].start()
    arriving = [send(own_ref, all_ref.at[1 - core, fsdp], sems, 0, sibling)]

    def passed(source, owner, part, index):
        for side, copies in ((core, handed), (1 - core, arriving)):
            target = all_ref.at[side, owner] if part is None else all_ref.at[side, owner, part]
            copies.append(send(source, target, sems, index + 1, sibling))
        handed[-1].start()

    def finish():
        for out, back in zip(handed, arriving):
            out.wait_send()
            back.wait_recv()

    return (passed, finish)


def line_rows(n_ctx, rows):
    def kernel(rows_ref, all_rows, right_s, right_r, left_s, left_r, core_s, core_r, own):
        where = place(n_ctx)
        chip, core, fsdp, length = where
        greet(line_peers(*where))
        mine = pltpu.make_async_copy(rows_ref, all_rows.at[chip * 2 + core], own)
        mine.start()
        run_all(line_gather(rows_ref, all_rows, ((right_s, right_r), (left_s, left_r), (core_s, core_r)), where))
        mine.wait()

    length = n_ctx // 2
    return pl.pallas_call(
        kernel,
        out_shape=jax.ShapeDtypeStruct((n_ctx,) + rows.shape, rows.dtype),
        in_specs=any_specs(1),
        out_specs=pl.BlockSpec(memory_space=pl.ANY),
        scratch_shapes=dma_pair(length) + dma_pair(length) + dma_pair(length) + [pltpu.SemaphoreType.DMA],
        compiler_params=params(0),
        name="line_rows",
    )(rows)


def square_core_gather(n_ctx, n_fsdp, rows):
    def kernel(rows_ref, all_ref, sq_s, sq_r, core_s, core_r, own):
        chip, core, fsdp, _ = place(n_ctx)
        ctx = chip * 2 + core
        sibling = (chip * 2 + 1 - core, fsdp)
        greet([sibling] + fsdp_peers(n_fsdp, ctx, fsdp))
        mine = pltpu.make_async_copy(rows_ref, all_ref.at[core, fsdp], own)
        mine.start()
        passed, finish = passing(rows_ref, all_ref, (core_s, core_r), core, fsdp, sibling)
        run_all(square_gather(rows_ref, all_ref.at[core], (sq_s, sq_r), ctx, fsdp, n_fsdp, passed))
        finish()
        mine.wait()

    return pl.pallas_call(
        kernel,
        out_shape=jax.ShapeDtypeStruct((2, n_fsdp) + rows.shape, rows.dtype),
        in_specs=any_specs(1),
        out_specs=pl.BlockSpec(memory_space=pl.ANY),
        scratch_shapes=dma_pair(max(6, n_fsdp)) + dma_pair(max(7, n_fsdp)) + [pltpu.SemaphoreType.DMA],
        compiler_params=params(1),
        name="square_core_gather",
    )(rows)


def add_into(target, *sources, chunk=64):
    @pl.loop(0, target.shape[0] // chunk)
    def _(step):
        rows = pl.ds(pl.multiple_of(step * chunk, chunk), chunk)
        total = target[rows].astype(jnp.float32)
        for source in sources:
            total = total + source[rows].astype(jnp.float32)
        target[rows] = total.astype(target.dtype)


def square_sum_stages(n_ctx, n_fsdp, partial_ref, out_ref, held, core_in, square_in, load, core_sems, sems):
    rows = partial_ref.shape[-2]
    half = rows // 2
    chip, core, fsdp, _ = place(n_ctx)
    ctx = chip * 2 + core
    sibling = (chip * 2 + 1 - core, fsdp)
    if n_fsdp == 4:
        first, second, corner = fsdp_neighbours(fsdp)
        order = [corner, first, second, fsdp]
    else:
        order = [(fsdp + j) % n_fsdp for j in range(1, n_fsdp + 1)]
    mine = [
        pltpu.make_async_copy(partial_ref.at[core, owner], held.at[owner], load.at[j])
        for j, owner in enumerate(order)
    ]
    others = [
        send(partial_ref.at[1 - core, owner], core_in.at[owner], core_sems, j, sibling)
        for j, owner in enumerate(order)
    ]

    def ready(j):
        mine[j].wait()
        others[j].wait_recv()
        add_into(held.at[order[j]], core_in.at[order[j]])

    def total(parts, sources):
        @pl.loop(0, parts[1] // 64)
        def _(step):
            at = pl.ds(pl.multiple_of(parts[0] + step * 64, 64), 64)
            from_at = pl.ds(pl.multiple_of(step * 64, 64), 64)
            value = held[fsdp, at].astype(jnp.float32)
            for j in sources:
                value = value + square_in[j, from_at].astype(jnp.float32)
            out_ref[at] = value

    def begin():
        greet([sibling] + fsdp_peers(n_fsdp, ctx, fsdp))
        for j in range(n_fsdp):
            others[j].start()
            mine[j].start()

    if n_fsdp != 4:
        copies = [
            send(held.at[order[j]], square_in.at[j], sems, j, (ctx, order[j])) for j in range(n_fsdp - 1)
        ]

        def spread():
            for j in range(n_fsdp):
                ready(j)
                if j < n_fsdp - 1:
                    copies[j].start()

        def finish():
            for copy in copies:
                copy.wait()
            total((0, rows), range(n_fsdp - 1))
            for each in others:
                each.wait_send()

        return [begin, spread, finish]

    top, low_half = pl.ds(0, half), pl.ds(half, half)
    to_first, to_second = (ctx, first), (ctx, second)

    def copy(index, owner, part, peer):
        return send(held.at[owner, part], square_in.at[index], sems, index, peer)

    copies = [
        copy(0, corner, top, to_first),
        copy(1, corner, low_half, to_second),
        copy(2, first, top, to_first),
        copy(3, second, low_half, to_second),
        copy(4, second, top, to_second),
        copy(5, first, low_half, to_first),
    ]

    def spread():
        ready(0)
        copies[0].start()
        copies[1].start()
        ready(1)
        copies[2].start()
        ready(2)
        copies[3].start()
        ready(3)

    def pass_on():
        copies[0].wait_recv()
        add_into(held.at[second, top], square_in.at[0])
        copies[4].start()
        copies[1].wait_recv()
        add_into(held.at[first, low_half], square_in.at[1])
        copies[5].start()

    def finish():
        for j in range(2, 6):
            copies[j].wait_recv()
        total((0, half), (2, 4))
        total((half, half), (3, 5))
        for each in copies:
            each.wait_send()
        for each in others:
            each.wait_send()

    return [begin, spread, pass_on, finish]


def corner_sum_stages(n_ctx, partial_ref, out_ref, held, square_in, load, sems):
    half = partial_ref.shape[1] // 2
    chip, core, fsdp, _ = place(n_ctx)
    ctx = chip * 2 + core
    first, second, corner = fsdp_neighbours(fsdp)
    top, low_half = pl.ds(0, half), pl.ds(half, half)
    to_first, to_second = (ctx, first), (ctx, second)

    def copy(index, source, peer):
        return send(source, square_in.at[index], sems, index, peer)

    copies = [
        copy(0, partial_ref.at[corner, top], to_first),
        copy(1, partial_ref.at[corner, low_half], to_second),
        copy(2, partial_ref.at[first, top], to_first),
        copy(3, partial_ref.at[second, low_half], to_second),
        copy(4, held.at[0], to_second),
        copy(5, held.at[1], to_first),
    ]
    mine = [
        pltpu.make_async_copy(partial_ref.at[second, top], held.at[0], load.at[0]),
        pltpu.make_async_copy(partial_ref.at[first, low_half], held.at[1], load.at[1]),
        pltpu.make_async_copy(partial_ref.at[fsdp, top], held.at[2], load.at[2]),
        pltpu.make_async_copy(partial_ref.at[fsdp, low_half], held.at[3], load.at[3]),
    ]

    starts = [
        [copies[0].start, copies[1].start],
        [copies[2].start, mine[1].start],
        [copies[3].start, mine[0].start],
        [mine[2].start, mine[3].start],
    ]

    def pass_on():
        for index in range(2):
            mine[index].wait()
            copies[index].wait_recv()
            add_into(held.at[index], square_in.at[index])
            copies[4 + index].start()

    def finish():
        for part, sources in ((0, (2, 4)), (1, (3, 5))):
            mine[2 + part].wait()
            for j in sources:
                copies[j].wait_recv()

            @pl.loop(0, half // 64)
            def _(step):
                at = pl.ds(pl.multiple_of(step * 64, 64), 64)
                value = held[2 + part, at].astype(jnp.float32)
                for j in sources:
                    value = value + square_in[j, at].astype(jnp.float32)
                out_ref[pl.ds(pl.multiple_of(part * half + step * 64, 64), 64)] = value

        for each in copies:
            each.wait_send()

    return [starts, pass_on, finish]


def corner_sum_scratch(partial):
    _, rows, columns = partial.shape
    return [
        pltpu.VMEM((4, rows // 2, columns), partial.dtype),
        pltpu.VMEM((6, rows // 2, columns), partial.dtype),
        pltpu.SemaphoreType.DMA((4,)),
    ] + dma_pair(6)


def square_sum_scratch(n_fsdp, partial):
    rows, columns = partial.shape[-2:]
    pieces = (6, rows // 2, columns) if n_fsdp == 4 else (n_fsdp - 1, rows, columns)
    return (
        [
            pltpu.VMEM((n_fsdp, rows, columns), partial.dtype),
            pltpu.VMEM((n_fsdp, rows, columns), partial.dtype),
            pltpu.VMEM(pieces, partial.dtype),
            pltpu.SemaphoreType.DMA((n_fsdp,)),
        ]
        + dma_pair(n_fsdp)
        + dma_pair(max(6, n_fsdp))
    )


def square_sum(n_ctx, n_fsdp, partial):
    def kernel(partial_ref, out_ref, held, core_in, square_in, load, core_s, core_r, sq_s, sq_r):
        for stage in square_sum_stages(
            n_ctx, n_fsdp, partial_ref, out_ref, held, core_in, square_in, load, (core_s, core_r), (sq_s, sq_r)
        ):
            stage()

    return pl.pallas_call(
        kernel,
        out_shape=jax.ShapeDtypeStruct(partial.shape[-2:], jnp.float32),
        in_specs=any_specs(1),
        out_specs=pl.BlockSpec(memory_space=pltpu.VMEM),
        scratch_shapes=square_sum_scratch(n_fsdp, partial),
        compiler_params=params(1),
        name="square_sum",
    )(partial)


def line_sum_steps(n_ctx, partial_ref, out_ref, held, core_in, right_in, left_in, load, core_sems, right_sems, left_sems):
    rows = partial_ref.shape[1]
    where = place(n_ctx)
    chip, core, fsdp, length = where
    sibling, right, left = line_peers(*where)
    order = [(chip + length - 1 - j) % length for j in range(length)]
    mine, others = [], []
    for j, owner in enumerate(order):
        mine.append(pltpu.make_async_copy(partial_ref.at[owner * 2 + core], held.at[owner], load.at[j]))
        others.append(send(partial_ref.at[owner * 2 + 1 - core], core_in.at[owner], core_sems, j, sibling))
        others[-1].start()
        mine[-1].start()
    yield
    for j, owner in enumerate(order):
        mine[j].wait()
        others[j].wait_recv()
        add_into(held.at[owner], core_in.at[owner])
    ways = ((1, right, right_in, right_sems), (-1, left, left_in, left_sems))
    for step in range(length - 1):
        for sign, peer, arrived, sems in ways:
            block = chip + sign * (length - 1 - step)
            inside = (block >= 0) & (block < length)
            came = (chip >= 1) if sign > 0 else (chip < length - 1)
            if step > 0:

                @pl.when(inside & came)
                def _():
                    send(held.at[block], arrived.at[step - 1], sems, step - 1, peer).wait_recv()
                    add_into(held.at[block], arrived.at[step - 1])

            @pl.when(inside)
            def _():
                send(held.at[block], arrived.at[step], sems, step, peer).start()

        yield
    last = length - 2
    for sign, peer, arrived, sems in ways:
        came = (chip >= 1) if sign > 0 else (chip < length - 1)

        @pl.when(came)
        def _():
            send(held.at[chip], arrived.at[last], sems, last, peer).wait_recv()
            add_into(held.at[chip], arrived.at[last])

    @pl.loop(0, rows // 64)
    def _(step):
        at = pl.ds(pl.multiple_of(step * 64, 64), 64)
        out_ref[at] = held[chip, at].astype(jnp.float32)

    for step in range(length - 1):
        for sign, peer, arrived, sems in ways:
            block = chip + sign * (length - 1 - step)

            @pl.when((block >= 0) & (block < length))
            def _():
                send(held.at[block], arrived.at[step], sems, step, peer).wait_send()

    for each in others:
        each.wait_send()


def line_sum_scratch(n_ctx, partial):
    rows, columns = partial.shape[-2:]
    length = n_ctx // 2
    return [
        pltpu.VMEM((length, rows, columns), partial.dtype),
        pltpu.VMEM((length, rows, columns), partial.dtype),
        pltpu.VMEM((length - 1, rows, columns), partial.dtype),
        pltpu.VMEM((length - 1, rows, columns), partial.dtype),
        pltpu.SemaphoreType.DMA((length,)),
    ] + dma_pair(length) * 3


def line_sum(n_ctx, partial):
    def kernel(partial_ref, out_ref, held, core_in, right_in, left_in, load, core_s, core_r, right_s, right_r, left_s, left_r):
        greet(line_peers(*place(n_ctx)))
        run_all(
            line_sum_steps(
                n_ctx, partial_ref, out_ref, held, core_in, right_in, left_in, load,
                (core_s, core_r), (right_s, right_r), (left_s, left_r),
            )
        )

    return pl.pallas_call(
        kernel,
        out_shape=jax.ShapeDtypeStruct(partial.shape[-2:], jnp.float32),
        in_specs=any_specs(1),
        out_specs=pl.BlockSpec(memory_space=pltpu.VMEM),
        scratch_shapes=line_sum_scratch(n_ctx, partial),
        compiler_params=params(5),
        name="line_sum",
    )(partial)


def attention_sums(n_ctx, partial, rows, grads, attended, grad_cols):
    total, features = rows.shape
    parts, _, own = attended.shape
    wide = grads.shape[1]
    depth = features // 4
    weight_shape = jax.ShapeDtypeStruct((4, depth, wide + own), jnp.bfloat16)
    inputs = (rows, grads, attended, grad_cols)

    def kernel(partial_ref, *refs):
        inputs_refs, refs = refs[:4], refs[4:]
        out_ref, weight_ref, rows_v, grads_v, attended_v, cols_v, weights, in_sem, *refs = refs
        line_refs, refs = refs[:5], refs[5:]
        core_s, core_r, right_s, right_r, left_s, left_r, *refs = refs
        held, square_in, load, sq_s, sq_r = refs
        where = place(n_ctx)
        chip, core, fsdp, _ = where
        loads = [
            pltpu.make_async_copy(a, b, in_sem.at[j])
            for j, (a, b) in enumerate(zip(inputs_refs, (rows_v, grads_v, attended_v, cols_v)))
        ]
        for each in loads:
            each.start()
        greet(line_peers(*where) + fsdp_peers(4, chip * 2 + core, fsdp))
        line = line_sum_steps(
            n_ctx, partial_ref, out_ref, *line_refs, (core_s, core_r), (right_s, right_r), (left_s, left_r)
        )
        next(line)
        starts, pass_on, finish = corner_sum_stages(n_ctx, weights, weight_ref, held, square_in, load, (sq_s, sq_r))
        for each in loads:
            each.wait()
        first, second, corner = fsdp_neighbours(fsdp)
        for number, owner in enumerate((corner, first, second, fsdp)):
            at = pl.ds(pl.multiple_of(owner * depth, depth), depth)
            weights[owner, :, :wide] = low(mm(rows_v[:, at], grads_v[...], CONTRACT_FIRST))
            for q in range(depth // own):
                weights[owner, q * own : (q + 1) * own, wide:] = low(
                    mm(attended_v[owner * (depth // own) + q], cols_v[...], CONTRACT_FIRST)
                )
            for start in starts[number]:
                start()
            if number < 2:
                next(line)
        pass_on()
        run_all(line)
        finish()

    return pl.pallas_call(
        kernel,
        out_shape=[
            jax.ShapeDtypeStruct(partial.shape[-2:], jnp.float32),
            jax.ShapeDtypeStruct(weight_shape.shape[1:], jnp.float32),
        ],
        in_specs=any_specs(5),
        out_specs=[pl.BlockSpec(memory_space=pltpu.VMEM)] * 2,
        scratch_shapes=[pltpu.VMEM(a.shape, a.dtype) for a in inputs]
        + [pltpu.VMEM(weight_shape.shape, weight_shape.dtype), pltpu.SemaphoreType.DMA((4,))]
        + line_sum_scratch(n_ctx, partial)
        + corner_sum_scratch(weight_shape),
        compiler_params=params(4),
        cost_estimate=pl.CostEstimate(
            flops=2 * total * features * (wide + own), bytes_accessed=16 * 1024 * 1024, transcendentals=0
        ),
        name="attention_sums",
    )(partial, *inputs)


def sum_everywhere(n_ctx, n_fsdp, values):
    block = values.shape[1:]

    def kernel(values_ref, out_ref, along_ctx, along_fsdp, result, ctx_s, ctx_r, fsdp_s, fsdp_r, back_s, back_r):
        ctx = lax.axis_index("ctx")
        fsdp = lax.axis_index("fsdp")
        ctx_peers = [((ctx + j) % n_ctx, fsdp) for j in range(1, n_ctx)]
        fsdp_peers = [(ctx, (fsdp + j) % n_fsdp) for j in range(1, n_fsdp)]
        greet(ctx_peers + fsdp_peers)

        def exchange(copies):
            for copy in copies:
                copy.start()
            for copy in copies:
                copy.wait()

        def total(slots, count):
            value = slots[0]
            for j in range(1, count):
                value = value + slots[j]
            return value

        along_ctx[ctx] = values_ref[ctx]
        exchange(
            [
                send(values_ref.at[peer[0]], along_ctx.at[ctx], (ctx_s, ctx_r), j, peer)
                for j, peer in enumerate(ctx_peers)
            ]
        )
        along_fsdp[fsdp] = total(along_ctx, n_ctx)
        exchange(
            [
                send(along_fsdp.at[fsdp], along_fsdp.at[fsdp], (fsdp_s, fsdp_r), j, peer)
                for j, peer in enumerate(fsdp_peers)
            ]
        )
        result[ctx] = total(along_fsdp, n_fsdp)
        exchange(
            [send(result.at[ctx], result.at[ctx], (back_s, back_r), j, peer) for j, peer in enumerate(ctx_peers)]
        )
        out_ref[...] = result[...]

    return pl.pallas_call(
        kernel,
        out_shape=jax.ShapeDtypeStruct(values.shape, values.dtype),
        in_specs=[pl.BlockSpec(memory_space=pltpu.VMEM)],
        out_specs=pl.BlockSpec(memory_space=pltpu.VMEM),
        scratch_shapes=[
            pltpu.VMEM((n_ctx,) + block, values.dtype),
            pltpu.VMEM((n_fsdp,) + block, values.dtype),
            pltpu.VMEM((n_ctx,) + block, values.dtype),
        ]
        + dma_pair(n_ctx)
        + dma_pair(n_fsdp)
        + dma_pair(n_ctx),
        compiler_params=params(2),
        name="sum_everywhere",
    )(values)


def hidden_units(here, back, gate_ref, up_ref, down_ref):
    gate = mm(here, gate_ref[0], CONTRACT_LAST)
    up = mm(here, up_ref[0], CONTRACT_LAST)
    grad_hidden = mm(back, down_ref[0], CONTRACT_LAST)
    sigmoid = jax.nn.sigmoid(gate)
    activated = gate * sigmoid
    return (
        low(activated * up),
        low(grad_hidden * up * sigmoid * (1.0 + gate * (1.0 - sigmoid))),
        low(grad_hidden * activated),
    )


def ffn_forward(rows, planes, core, n_own, chunk=256):
    blocks, _, tokens, features = rows.shape
    total = blocks * tokens
    steps = n_own // chunk
    group = max(1, 256 // tokens)

    def kernel(core_ref, rows_ref, gate_ref, up_ref, down_ref, *outs):
        for at in range(0, blocks, group):
            here = rows_ref[at : at + group, 0].reshape(group * tokens, features)
            back = rows_ref[at : at + group, 1].reshape(group * tokens, features)
            span = pl.ds(at * tokens, group * tokens)
            for out, value in zip(outs, hidden_units(here, back, gate_ref, up_ref, down_ref)):
                out[span] = value

    def weight_spec(plane):
        return pl.BlockSpec((1, chunk, features), lambda j, core_ref: (plane, core_ref[0] * steps + j, 0))

    act = jax.ShapeDtypeStruct((total, n_own), jnp.bfloat16)
    act_spec = pl.BlockSpec((total, chunk), lambda j, core_ref: (0, j))
    return pl.pallas_call(
        kernel,
        grid_spec=pltpu.PrefetchScalarGridSpec(
            num_scalar_prefetch=1,
            grid=(steps,),
            in_specs=[
                pl.BlockSpec(rows.shape, lambda j, core_ref: (0, 0, 0, 0), pipeline_mode=pl.Buffered(1)),
                weight_spec(0),
                weight_spec(1),
                weight_spec(2),
            ],
            out_specs=[act_spec, act_spec, act_spec],
        ),
        out_shape=[act, act, act],
        compiler_params=params(),
        cost_estimate=pl.CostEstimate(
            flops=6 * total * n_own * features, bytes_accessed=30 * 1024 * 1024, transcendentals=total * n_own
        ),
        name="ffn_forward",
    )(core, rows, planes, planes, planes)


def mirror_gather(all_ref, arrivals, sems, pass_sems, ctx, core, fsdp, sibling):
    first, second, corner = fsdp_neighbours(fsdp)
    half = all_ref.shape[2] // 2
    parts = [pl.ds(0, half), pl.ds(half, half)]
    to_first, to_second = (ctx, first), (ctx, second)

    def copy(index, owner, part, peer):
        place_ref = all_ref.at[core, owner, parts[part]]
        return send(place_ref, place_ref, sems, index, peer)

    copies = [
        copy(0, fsdp, 0, to_first),
        copy(1, fsdp, 0, to_second),
        copy(2, fsdp, 1, to_first),
        copy(3, fsdp, 1, to_second),
        copy(4, first, 0, to_second),
        copy(5, second, 1, to_first),
    ]
    passes = [(fsdp, 0), (fsdp, 1), (first, 0), (second, 0), (first, 1), (second, 1), (corner, 0), (corner, 1)]

    def passing_copy(number, side):
        owner, part = passes[number]
        place_ref = all_ref.at[side, owner, parts[part]]
        return send(place_ref, place_ref, pass_sems, number, sibling)

    for part in range(2):
        arrivals[part].wait_recv()
        copies[2 * part].start()
        copies[2 * part + 1].start()
        passing_copy(part, core).start()
        yield
    for index, number, then in ((0, 2, 4), (1, 3, None), (2, 4, None), (3, 5, 5), (4, 6, None), (5, 7, None)):
        owner, part = passes[number]
        copy(index, owner, part, to_first).wait_recv()
        if then is not None:
            copies[then].start()
        passing_copy(number, core).start()
        yield
    for each in copies:
        each.wait_send()
    for number in range(8):
        passing_copy(number, core).wait_send()
        passing_copy(number, 1 - core).wait_recv()


def ffn_rows(n_ctx, own, planes, attended, n_own, chunk=256, wide=512):
    n_fsdp = 4
    size, features = own.shape
    tokens = size // 2
    total = 2 * n_fsdp * tokens

    def kernel(
        own_ref, planes_ref, attended_ref, all_ref, mirror_ref, hidden_a, hidden_b, hidden_c, partial_ref, heads_ref,
        rows, weights, hidden, partial, core_in, load, sq_s, sq_r, core_s, core_r, far_s, far_r, mi_s, mi_r, mc_s, mc_r, sum_s, sum_r, out_sem,
        ri_s, ri_r, le_s, le_r, lc_s, lc_r, heads_sem,
    ):
        chip, core, fsdp, length = place(n_ctx)
        ctx = chip * 2 + core
        sibling = (chip * 2 + 1 - core, fsdp)
        mirror = ((length - 1 - chip) * 2 + core, fsdp)
        first, second, corner = fsdp_neighbours(fsdp)
        where = (chip, core, fsdp, length)
        greet([mirror] + line_peers(*where) + fsdp_peers(n_fsdp, ctx, fsdp))
        line = line_gather(attended_ref, heads_ref, ((ri_s, ri_r), (le_s, le_r), (lc_s, lc_r)), where)
        heads_own = pltpu.make_async_copy(attended_ref, heads_ref.at[ctx], heads_sem)
        heads_own.start()
        mine = pltpu.make_async_copy(own_ref, rows.at[core, fsdp], load.at[3])
        mine.start()
        start = pl.multiple_of(core * n_own, n_own)
        loads = [
            pltpu.make_async_copy(planes_ref.at[p, pl.ds(start, n_own)], weights.at[p], load.at[p]) for p in range(3)
        ]
        handed, arriving = [], []

        def hand(source, owner, part, index):
            for side, copies in ((core, handed), (1 - core, arriving)):
                target = rows.at[side, owner] if part is None else rows.at[side, owner, part]
                copies.append(send(source, target, (core_s, core_r), index + 1, sibling))
            handed[-1].start()

        gathering = square_gather(own_ref, rows.at[core], (sq_s, sq_r), ctx, fsdp, n_fsdp, hand)
        next(gathering)
        hand(own_ref, fsdp, None, -1)
        for each in loads:
            each.start()
        far = [
            send(
                own_ref.at[pl.ds(part * tokens, tokens)],
                mirror_ref.at[core, fsdp, pl.ds(part * tokens, tokens)],
                (far_s, far_r),
                part,
                mirror,
            )
            for part in range(2)
        ]
        for each in far:
            each.start()
        mirroring = mirror_gather(mirror_ref, far, (mi_s, mi_r), (mc_s, mc_r), ctx, core, fsdp, sibling)
        outs, summing, sums = [], [], []

        def add_up(number, owner):
            summing[number].wait_recv()
            add_into(partial.at[number % 2, core], core_in.at[number])
            sums.append(
                pltpu.make_async_copy(partial.at[number % 2, core], partial_ref.at[owner], out_sem.at[number % 2, 8])
            )
            sums[-1].start()

        def group(number, owner):
            slot = number % 2
            if number >= 2:
                for each in outs[number - 2]:
                    each.wait()
                summing[number - 2].wait_send()
                sums[number - 2].wait()
            here = jnp.concatenate([rows[0, owner, :tokens], rows[1, owner, :tokens]])
            back = jnp.concatenate([rows[0, owner, tokens:], rows[1, owner, tokens:]])

            @pl.loop(0, n_own // chunk)
            def _(step):
                at = pl.ds(pl.multiple_of(step * chunk, chunk), chunk)
                parts = [weights.at[pl.ds(p, 1), at] for p in range(3)]
                for q, value in enumerate(hidden_units(here, back, *parts)):
                    hidden[slot, q, :, at] = value

            @pl.loop(0, features // wide)
            def _(step):
                at = pl.ds(pl.multiple_of(step * wide, wide), wide)
                out = low(mm(hidden[slot, 0], weights[2, :, at]))
                below = low(mm(hidden[slot, 1], weights[0, :, at]) + mm(hidden[slot, 2], weights[1, :, at]))
                for k in range(2):
                    partial[slot, k, :tokens, at] = out[k * tokens : (k + 1) * tokens]
                    partial[slot, k, tokens:, at] = below[k * tokens : (k + 1) * tokens]

            pairs = []
            summing.append(send(partial.at[slot, 1 - core], core_in.at[number], (sum_s, sum_r), number, sibling))
            summing[-1].start()
            for k in range(2):
                pairs.append((rows.at[k, owner], all_ref.at[k, owner]))
                at = pl.ds(pl.multiple_of((k * n_fsdp + owner) * tokens, tokens), tokens)
                for q, target in enumerate((hidden_a, hidden_b, hidden_c)):
                    pairs.append((hidden.at[slot, q, pl.ds(k * tokens, tokens)], target.at[at]))
            outs.append(
                [pltpu.make_async_copy(a, b, out_sem.at[slot, j]) for j, (a, b) in enumerate(pairs)]
            )
            for each in outs[-1]:
                each.start()

        mine.wait()
        arriving[0].wait_recv()
        for each in loads:
            each.wait()
        group(0, fsdp)
        for _ in range(4):
            next(gathering)
        arriving[1].wait_recv()
        arriving[3].wait_recv()
        group(1, first)
        add_up(0, fsdp)
        next(mirroring)
        for _ in range(2):
            next(gathering)
        arriving[2].wait_recv()
        arriving[4].wait_recv()
        group(2, second)
        add_up(1, first)
        next(mirroring)
        next(line)
        for _ in range(2):
            next(mirroring)
        arriving[5].wait_recv()
        arriving[6].wait_recv()
        group(3, corner)
        next(line)
        add_up(2, second)
        next(mirroring)
        add_up(3, corner)
        run_all(mirroring, line, gathering)
        heads_own.wait()
        for each in handed:
            each.wait_send()
        for each in far:
            each.wait_send()
        for each in outs[2] + outs[3] + sums[2:]:
            each.wait()
        for each in summing[2:]:
            each.wait_send()

    act = jax.ShapeDtypeStruct((total, n_own), own.dtype)
    all_rows = jax.ShapeDtypeStruct((2, n_fsdp) + own.shape, own.dtype)
    return pl.pallas_call(
        kernel,
        in_specs=any_specs(3),
        out_specs=any_specs(7),
        out_shape=[
            all_rows,
            all_rows,
            act,
            act,
            act,
            jax.ShapeDtypeStruct((n_fsdp,) + own.shape, own.dtype),
            jax.ShapeDtypeStruct((n_ctx,) + attended.shape, attended.dtype),
        ],
        scratch_shapes=[
            pltpu.VMEM((2, n_fsdp) + own.shape, own.dtype),
            pltpu.VMEM((3, n_own, features), own.dtype),
            pltpu.VMEM((2, 3, 2 * tokens, n_own), own.dtype),
            pltpu.VMEM((2, 2) + own.shape, own.dtype),
            pltpu.VMEM((n_fsdp,) + own.shape, own.dtype),
            pltpu.SemaphoreType.DMA((4,)),
        ]
        + dma_pair(6)
        + dma_pair(7)
        + dma_pair(2)
        + dma_pair(6)
        + dma_pair(8)
        + dma_pair(4)
        + [pltpu.SemaphoreType.DMA((2, 9))]
        + dma_pair(n_ctx // 2) * 3
        + [pltpu.SemaphoreType.DMA],
        compiler_params=params(6),
        cost_estimate=pl.CostEstimate(
            flops=12 * total * n_own * features, bytes_accessed=50 * 1024 * 1024, transcendentals=total * n_own
        ),
        name="ffn_rows",
    )(own, planes, attended)


def ffn_weights(n_ctx, n_fsdp, partial, rows, rows_mirror, hidden, planes, n_own, chunk=256):
    blocks, _, tokens, features = rows.shape
    total = blocks * tokens
    steps = n_own // chunk
    group = max(1, 256 // tokens)
    half = features // 2
    sides = n_ctx // 4
    wide = half // sides
    fused = partial is not None
    early = steps // 2 if fused else 0
    assert not fused or sides == 2

    def kernel(*refs):
        rows_ref, refs = refs[0], refs[1:]
        mirror_refs, refs = refs[: len(rows_mirror)], refs[len(rows_mirror) :]
        mirror_blocks = [ref.at[b] for ref in mirror_refs for b in range(ref.shape[0])]
        hidden_ref, grad_gate_ref, grad_up_ref, planes_ref, *refs = refs
        if fused:
            partial_ref, weight_ref, out_ref, early_ref, *refs = refs
        else:
            weight_ref, *refs = refs
        mirror, (weights, weight_sems), refs = refs[:3], refs[3:5], refs[5:]
        chip, core, _, length = place(n_ctx)
        side = chip // sides
        step = pl.program_id(0)
        stages = []
        if fused:
            keep, give, take, side_s, side_r, held, square_in, load, sq_s, sq_r = refs
            member = chip % 2
            other = (chip + 1 - 2 * member) * 2 + core
            crossing = [
                send(give.at[j], take.at[j], (side_s, side_r), j, (other, lax.axis_index("fsdp"))) for j in range(early)
            ]
            starts, *stages = corner_sum_stages(n_ctx, partial_ref, out_ref, held, square_in, load, (sq_s, sq_r))

        def fetch(at, slot):
            start = pl.multiple_of((core * steps + at) * chunk, chunk)
            return pltpu.make_async_copy(planes_ref.at[:, pl.ds(start, chunk)], weights.at[slot], weight_sems.at[slot])

        @pl.when(step == 0)
        def _():
            fetch(0, 0).start()
            if fused:
                fsdp = lax.axis_index("fsdp")
                greet(fsdp_peers(4, chip * 2 + core, fsdp) + [(other, fsdp)])
                for start in sum(starts, []):
                    start()

        @pl.when(step + 1 < steps)
        def _():
            fetch(step + 1, (step + 1) % 2).start()

        slot = step % 2
        fetch(step, slot).wait()
        gate_ref, up_ref, down_ref = (weights.at[slot, pl.ds(plane, 1)] for plane in range(3))
        for at in range(0, blocks, group):
            here = jnp.concatenate([ref[0] for ref in mirror_blocks[at : at + group]])
            back = jnp.concatenate([ref[1] for ref in mirror_blocks[at : at + group]])
            span = pl.ds(at * tokens, group * tokens)
            for out, value in zip(mirror, hidden_units(here, back, gate_ref, up_ref, down_ref)):
                out[span] = value

        lefts = ((grad_gate_ref, mirror[1], 0), (grad_up_ref, mirror[2], 0), (hidden_ref, mirror[0], 1))
        for plane, (left, left_mirror, which) in enumerate(lefts):
            left = left[...]
            left_mirror = left_mirror[...]
            for z in range(sides):
                cols = pl.ds(pl.multiple_of(side * half + z * wide, wide), wide)
                right = rows_ref[:, which, :, cols].reshape(total, wide)
                right_mirror = jnp.concatenate([ref[which, :, cols] for ref in mirror_blocks])
                value = mm(left, right, CONTRACT_FIRST) + mm(left_mirror, right_mirror, CONTRACT_FIRST)
                if not fused:
                    weight_ref[z, plane] = low(value)
                    continue

                @pl.when((step < early) & (z == member))
                def _():
                    keep[step % early, plane] = value

                @pl.when((step < early) & (z != member))
                def _():
                    give[step % early, plane] = low(value)

                @pl.when(step >= early)
                def _():
                    weight_ref[z, plane] = low(value)

        for j in range(early):

            @pl.when(step == j)
            def _():
                crossing[j].start()

        for at, stage in ((1, 0), (steps - 1, 1)):
            if stage < len(stages):

                @pl.when(step == min(at, steps - 1))
                def _():
                    stages[stage]()

        if fused:

            @pl.when(step == steps - 1)
            def _():
                for j in range(early):
                    crossing[j].wait()
                    for plane in range(3):
                        early_ref[plane, j * chunk : (j + 1) * chunk] = low(
                            keep[j, plane] + take[j, plane].astype(jnp.float32)
                        )

    act_spec = pl.BlockSpec((total, chunk), lambda j: (0, j))
    once = dict(pipeline_mode=pl.Buffered(1))
    operands = [rows, *rows_mirror, *hidden, planes]
    in_specs = [whole_block(rows.shape, **once)] + [whole_block(part.shape, **once) for part in rows_mirror]
    in_specs += [act_spec] * 3 + any_specs(1)
    out_specs = [pl.BlockSpec((sides, 3, chunk, wide), lambda j: (0, 0, jnp.maximum(j - early, 0), 0))]
    out_shape = [jax.ShapeDtypeStruct((sides, 3, n_own - early * chunk, wide), jnp.bfloat16)]
    scratch = [pltpu.VMEM((total, chunk), jnp.bfloat16)] * 3
    scratch += [pltpu.VMEM((2, 3, chunk, features), jnp.bfloat16), pltpu.SemaphoreType.DMA((2,))]
    if fused:
        operands.append(partial)
        in_specs += any_specs(1)
        out_specs.append(whole_block(partial.shape[-2:], **once))
        out_shape.append(jax.ShapeDtypeStruct(partial.shape[-2:], jnp.float32))
        out_specs.append(whole_block((3, early * chunk, wide), **once))
        out_shape.append(jax.ShapeDtypeStruct((3, early * chunk, wide), jnp.bfloat16))
        scratch.append(pltpu.VMEM((early, 3, chunk, wide), jnp.float32))
        scratch += [pltpu.VMEM((early, 3, chunk, wide), jnp.bfloat16)] * 2 + dma_pair(early)
        scratch += corner_sum_scratch(partial)
    return pl.pallas_call(
        kernel,
        grid=(steps,),
        in_specs=in_specs,
        out_specs=out_specs,
        out_shape=out_shape,
        scratch_shapes=scratch,
        compiler_params=params(3) if fused else params(),
        cost_estimate=pl.CostEstimate(
            flops=12 * total * n_own * features, bytes_accessed=50 * 1024 * 1024, transcendentals=total * n_own
        ),
        name="ffn_weights",
    )(*operands)


def ffn_back(hidden, grad_gate, grad_up, planes, core, blocks, wide=512):
    total, n_own = hidden.shape
    features = planes.shape[2]
    tokens = total // blocks

    def kernel(core_ref, hidden_ref, grad_gate_ref, grad_up_ref, gate_ref, up_ref, down_ref, out_ref):
        out = mm(hidden_ref[...], down_ref[0])
        out_ref[:, 0] = low(out).reshape(blocks, tokens, wide)
        back = mm(grad_gate_ref[...], gate_ref[0]) + mm(grad_up_ref[...], up_ref[0])
        out_ref[:, 1] = low(back).reshape(blocks, tokens, wide)

    def weight_spec(plane):
        return pl.BlockSpec((1, n_own, wide), lambda j, core_ref: (plane, core_ref[0], j))

    act_spec = pl.BlockSpec((total, n_own), lambda j, core_ref: (0, 0), pipeline_mode=pl.Buffered(1))
    return pl.pallas_call(
        kernel,
        grid_spec=pltpu.PrefetchScalarGridSpec(
            num_scalar_prefetch=1,
            grid=(features // wide,),
            in_specs=[act_spec, act_spec, act_spec, weight_spec(0), weight_spec(1), weight_spec(2)],
            out_specs=pl.BlockSpec((blocks, 2, tokens, wide), lambda j, core_ref: (0, 0, 0, j)),
        ),
        out_shape=jax.ShapeDtypeStruct((blocks, 2, tokens, features), jnp.bfloat16),
        compiler_params=params(),
        cost_estimate=pl.CostEstimate(
            flops=6 * total * n_own * features, bytes_accessed=30 * 1024 * 1024, transcendentals=0
        ),
        name="ffn_back",
    )(core, hidden, grad_gate, grad_up, planes, planes, planes)


SPAN = 256


def ctx_peers(n_ctx):
    ctx = lax.axis_index("ctx")
    fsdp = lax.axis_index("fsdp")
    return [((ctx + j) % n_ctx, fsdp) for j in range(1, n_ctx)]


def deal(n_ctx, block, target, landed, sems, own_sem):
    ctx = lax.axis_index("ctx")
    fsdp = lax.axis_index("fsdp")

    @pl.when(target != ctx)
    def _():
        send(block, landed.at[ctx], sems, (target - ctx + n_ctx) % n_ctx, (target, fsdp)).start()

    @pl.when(target == ctx)
    def _():
        pltpu.make_async_copy(block, landed.at[ctx], own_sem).start()


def dealt(n_ctx, block, landed, sems, own_sem):
    ctx = lax.axis_index("ctx")
    pltpu.make_async_copy(block, landed.at[ctx], own_sem).wait()
    for j, peer in enumerate(ctx_peers(n_ctx)):
        copy = send(block, landed.at[(ctx + n_ctx - j - 1) % n_ctx], sems, j + 1, peer)
        copy.wait_send()
        copy.wait_recv()


def turn(values, cosine, sine):
    return values * cosine + pltpu.roll(values, HEAD_DIM // 2, 1) * sine


def attention_forward(n_ctx, rows, w_qkv, cosine, sine, place_column, place_row, heads):
    total, features = rows.shape
    own = heads * HEAD_DIM
    steps = total // SPAN
    length = total // n_ctx
    scale = HEAD_DIM ** (-0.5)

    def kernel(
        rows_ref, w_ref, cosine_ref, sine_ref, column_ref, row_ref,
        query_ref, key_ref, value_ref, out_ref, log_ref, landed, deal_s, deal_r, own_sem,
    ):
        step = pl.program_id(0)

        @pl.when(step == 0)
        def _():
            greet(ctx_peers(n_ctx))

        span = pl.ds(pl.multiple_of(step * SPAN, SPAN), SPAN)
        qkv = mm(rows_ref[...], w_ref[...])
        cosine = cosine_ref[span]
        sine = sine_ref[span]
        for h in range(heads):
            at = slice(h * HEAD_DIM, (h + 1) * HEAD_DIM)
            query_ref[span, at] = low(turn(qkv[:, at], cosine, sine))
            key_ref[span, at] = low(turn(qkv[:, own + h * HEAD_DIM : own + (h + 1) * HEAD_DIM], cosine, sine))
        value_ref[span] = low(qkv[:, 2 * own :])

        @pl.when(step == steps - 1)
        def _():
            @pl.loop(0, steps)
            def _(block):
                here = pl.ds(pl.multiple_of(block * SPAN, SPAN), SPAN)
                for h in range(heads):
                    at = slice(h * HEAD_DIM, (h + 1) * HEAD_DIM)
                    scores = mm(query_ref[here, at], key_ref[:, at], CONTRACT_LAST) * scale
                    scores = jnp.where(column_ref[here] >= row_ref[...], scores, MASKED)
                    highest = jnp.max(scores, axis=-1, keepdims=True)
                    exponent = jnp.exp(scores - highest)
                    sums = jnp.sum(exponent, axis=-1, keepdims=True)
                    out_ref[here, at] = low(mm(low(exponent * (1.0 / sums)), value_ref[:, at]))
                    log_ref[h, here] = highest + jnp.log(sums)
                for r in range(SPAN // length):
                    mine = out_ref.at[pl.ds(pl.multiple_of(block * SPAN + r * length, length), length)]
                    deal(n_ctx, mine, block * (SPAN // length) + r, landed, (deal_s, deal_r), own_sem)

            dealt(n_ctx, out_ref.at[pl.ds(0, length)], landed, (deal_s, deal_r), own_sem)

    act = jax.ShapeDtypeStruct((total, own), jnp.bfloat16)
    return pl.pallas_call(
        kernel,
        grid=(steps,),
        in_specs=[pl.BlockSpec((SPAN, features), lambda r: (r, 0))]
        + [whole_block(a.shape) for a in (w_qkv, cosine, sine, place_column, place_row)],
        out_specs=[whole_block((total, own))] * 4 + [whole_block((heads, total, 1))] + any_specs(1),
        out_shape=[act] * 4
        + [
            jax.ShapeDtypeStruct((heads, total, 1), jnp.float32),
            jax.ShapeDtypeStruct((n_ctx, length, own), jnp.bfloat16),
        ],
        scratch_shapes=dma_pair(n_ctx) + [pltpu.SemaphoreType.DMA],
        compiler_params=params(8),
        name="attention_forward",
    )(rows, w_qkv, cosine, sine, place_column, place_row)


def attention_backward(query, key, value, grad, logs, w_qkv, cosine, sine, place_column, place_row, heads):
    total, own = query.shape
    features = w_qkv.shape[0]
    steps = total // SPAN
    scale = HEAD_DIM ** (-0.5)

    def kernel(
        query_ref, key_ref, value_ref, grad_ref, log_ref, w_ref, cosine_ref, sine_ref, column_ref, row_ref,
        qkv_ref, out_ref, key_sum, value_sum,
    ):
        step = pl.program_id(0)

        @pl.when(step == 0)
        def _():
            for h in range(heads):
                at = slice(h * HEAD_DIM, (h + 1) * HEAD_DIM)
                key_sum[...] = jnp.zeros_like(key_sum)
                value_sum[...] = jnp.zeros_like(value_sum)

                @pl.loop(0, steps)
                def _(block):
                    here = pl.ds(pl.multiple_of(block * SPAN, SPAN), SPAN)
                    queries = query_ref[here, at]
                    grads = grad_ref[here, at]
                    scores = mm(queries, key_ref[:, at], CONTRACT_LAST) * scale
                    scores = jnp.where(column_ref[here] >= row_ref[...], scores, MASKED)
                    probs = jnp.exp(scores - log_ref[h, here])
                    probs_grad = mm(grads, value_ref[:, at], CONTRACT_LAST)
                    centre = jnp.sum(probs * probs_grad, axis=-1, keepdims=True)
                    scores_grad = low(probs * (probs_grad - centre))
                    query_grad = mm(scores_grad, key_ref[:, at]) * scale
                    qkv_ref[here, at] = low(turn(query_grad, cosine_ref[here], -sine_ref[here]))
                    key_sum[...] += mm(scores_grad, queries, CONTRACT_FIRST)
                    value_sum[...] += mm(low(probs), grads, CONTRACT_FIRST)

                qkv_ref[:, own + h * HEAD_DIM : own + (h + 1) * HEAD_DIM] = low(
                    turn(key_sum[...] * scale, cosine_ref[...], -sine_ref[...])
                )
                qkv_ref[:, 2 * own + h * HEAD_DIM : 2 * own + (h + 1) * HEAD_DIM] = low(value_sum[...])

        span = pl.ds(pl.multiple_of(step * SPAN, SPAN), SPAN)
        out_ref[...] = low(mm(qkv_ref[span], w_ref[...], CONTRACT_LAST))

    return pl.pallas_call(
        kernel,
        grid=(steps,),
        in_specs=[
            whole_block(a.shape)
            for a in (query, key, value, grad, logs, w_qkv, cosine, sine, place_column, place_row)
        ],
        out_specs=[whole_block((total, 3 * own)), pl.BlockSpec((SPAN, features), lambda r: (r, 0))],
        out_shape=[
            jax.ShapeDtypeStruct((total, 3 * own), jnp.bfloat16),
            jax.ShapeDtypeStruct((total, features), jnp.bfloat16),
        ],
        scratch_shapes=[pltpu.VMEM((total, HEAD_DIM), jnp.float32)] * 2,
        compiler_params=params(),
        name="attention_backward",
    )(query, key, value, grad, logs, w_qkv, cosine, sine, place_column, place_row)


ROWS = 32


def row_blocks(count, features):
    return pl.BlockSpec((count, ROWS, features), lambda r, *_: (0, r, 0))


def whole_block(shape, **more):
    zeros = (0,) * len(shape)
    return pl.BlockSpec(shape, lambda r, *_: zeros, **more)


def split(values):
    high = low(values)
    return (high, low(values - high.astype(jnp.float32)))


def connect_coefficients(values, dynamic_ref, static_ref, coef_ref, dyn_ref):
    lane = lax.broadcasted_iota(jnp.int32, (values[0].shape[0], 8), 1)
    columns = []
    for i, value in enumerate(values):
        mean = jnp.mean(value, axis=-1, keepdims=True)
        centered = value - mean
        inverse = lax.rsqrt(jnp.mean(centered * centered, axis=-1, keepdims=True) + EPS)
        normed = centered * inverse
        projected = jnp.zeros(lane.shape, jnp.float32)
        for k in range(6):
            part = jnp.sum(normed * dynamic_ref[k : k + 1], axis=-1, keepdims=True)
            projected = jnp.where(lane == k, part, projected)
        coefficient = jnp.tanh(projected) + static_ref[i : i + 1]
        dyn_ref[i] = projected
        coef_ref[i] = jnp.where(lane == 6, mean, jnp.where(lane == 7, inverse, coefficient))
        columns.append(coefficient)
    return columns


def connect_first(streams, dynamic, static):
    number, rows, features = streams.shape

    def kernel(streams_ref, dynamic_ref, static_ref, coef_ref, dyn_ref, low_ref):
        values = [streams_ref[i].astype(jnp.float32) for i in range(number)]
        columns = connect_coefficients(values, dynamic_ref, static_ref, coef_ref, dyn_ref)
        mixed = sum((columns[i][:, 1:2] * values[i] for i in range(number)))
        low_ref[...] = low(normalize(mixed)[0])

    small = jax.ShapeDtypeStruct((number, rows, 8), jnp.float32)
    return pl.pallas_call(
        kernel,
        grid=(rows // ROWS,),
        out_shape=(small, small, jax.ShapeDtypeStruct((rows, features), jnp.bfloat16)),
        in_specs=[row_blocks(number, features), whole_block(dynamic.shape), whole_block(static.shape)],
        out_specs=(
            row_blocks(number, 8),
            row_blocks(number, 8),
            pl.BlockSpec((ROWS, features), lambda r: (r, 0)),
        ),
        compiler_params=params(),
        name="connect_first",
    )(streams, dynamic, static)


def connect_middle(streams, coef, attended, w_mine, w_other, cotangent, dynamic, static, core_fsdp, where, depth):
    number, rows, features = streams.shape
    half = features // 2
    own = attended.shape[2]
    count = len(w_mine)

    def kernel(core_ref, streams_ref, coef_ref, attended_ref, *refs):
        weights, refs = refs[: 2 * count], refs[2 * count :]
        cotangent_ref, dynamic_ref, static_ref = refs[:3]
        first_ref, branch_ref, coef_two_ref, dyn_ref, own_ref, projected = refs[3:]
        step = pl.program_id(0)

        @pl.when(step == 0)
        def _():
            for side in range(2):
                total = 0.0
                for j, (d, offset) in enumerate(where):
                    for q in range(w_mine[j].shape[0] // own):
                        part = attended_ref[(core_ref[1] ^ d) * (depth // own) + offset // own + q]
                        total = total + mm(part, weights[side * count + j][q * own : (q + 1) * own])
                projected[core_ref[0] if side == 0 else 1 - core_ref[0]] = total

        span = pl.ds(pl.multiple_of(step * ROWS, ROWS), ROWS)
        branch = jnp.concatenate([projected[0, span], projected[1, span]], axis=1)
        branch_ref[...] = branch
        inputs = [streams_ref[i].astype(jnp.float32) for i in range(number)]
        outs = []
        for j in range(number):
            out = sum((coef_ref[i][:, 2 + j : 3 + j] * inputs[i] for i in range(number)))
            outs.append(out + coef_ref[j][:, 0:1] * branch)
            first_ref[j] = outs[-1]
        columns = connect_coefficients(outs, dynamic_ref, static_ref, coef_two_ref, dyn_ref)
        mixed = sum((columns[i][:, 1:2] * outs[i] for i in range(number)))
        own_ref[0] = low(normalize(mixed)[0])
        own_ref[1] = low(sum((columns[j][:, 0:1] * cotangent_ref[j].astype(jnp.float32) for j in range(number))))

    small = jax.ShapeDtypeStruct((number, rows, 8), jnp.float32)
    once = dict(pipeline_mode=pl.Buffered(1))
    return pl.pallas_call(
        kernel,
        grid_spec=pltpu.PrefetchScalarGridSpec(
            num_scalar_prefetch=1,
            grid=(rows // ROWS,),
            in_specs=[
                row_blocks(number, features),
                row_blocks(number, 8),
                whole_block(attended.shape, **once),
                *[whole_block(w.shape, **once) for w in w_mine + w_other],
                row_blocks(number, features),
                whole_block(dynamic.shape),
                whole_block(static.shape),
            ],
            out_specs=(
                row_blocks(number, features),
                pl.BlockSpec((ROWS, features), lambda r, *_: (r, 0)),
                row_blocks(number, 8),
                row_blocks(number, 8),
                row_blocks(2, features),
            ),
            scratch_shapes=[pltpu.VMEM((2, rows, half), jnp.float32)],
        ),
        out_shape=(
            jax.ShapeDtypeStruct((number, rows, features), jnp.float32),
            jax.ShapeDtypeStruct((rows, features), jnp.float32),
            small,
            small,
            jax.ShapeDtypeStruct((2, rows, features), jnp.bfloat16),
        ),
        compiler_params=params(),
        name="connect_middle",
    )(core_fsdp, streams, coef, attended, *w_mine, *w_other, cotangent, dynamic, static)


def attention_weights(rows, grads, attended, grad_cols):
    total, features = rows.shape
    parts, _, own = attended.shape
    wide = grads.shape[1]

    def kernel(rows_ref, grads_ref, attended_ref, cols_ref, out_ref):
        out_ref[:, :wide] = low(mm(rows_ref[...], grads_ref[...], CONTRACT_FIRST))
        out_ref[:, wide:] = low(mm(attended_ref[0], cols_ref[...], CONTRACT_FIRST))

    return pl.pallas_call(
        kernel,
        grid=(parts,),
        in_specs=[
            pl.BlockSpec((total, own), lambda k: (0, k)),
            whole_block(grads.shape),
            pl.BlockSpec((1, total, own), lambda k: (k, 0, 0)),
            whole_block(grad_cols.shape),
        ],
        out_specs=pl.BlockSpec((own, wide + own), lambda k: (k, 0)),
        out_shape=jax.ShapeDtypeStruct((features, wide + own), jnp.bfloat16),
        compiler_params=params(),
        cost_estimate=pl.CostEstimate(
            flops=2 * total * features * (wide + own), bytes_accessed=16 * 1024 * 1024, transcendentals=0
        ),
        name="attention_weights",
    )(rows, grads, attended, grad_cols)


def flip(index, bits, count):
    result = index
    bit = 1
    while bit < count:
        if bits & bit:
            result = result + bit - 2 * bit * (index // bit % 2)
        bit *= 2
    return result


def project_back(n_ctx, n_fsdp, grad, w_mine, w_other, where, depth):
    rows, features = grad.shape
    half = features // 2
    count = len(w_mine)
    own = features // n_ctx

    def kernel(grad_ref, *refs):
        weights, refs = refs[: 2 * count], refs[2 * count :]
        landed, cols_ref, outs, deal_s, deal_r, own_sem = refs
        _, core, fsdp, _ = place(n_ctx)
        greet(ctx_peers(n_ctx))
        first = grad_ref[:, pl.ds(pl.multiple_of(core * half, half), half)]
        second = grad_ref[:, pl.ds(pl.multiple_of((1 - core) * half, half), half)]
        for j, (d, offset) in enumerate(where):
            out = low(
                mm(first, weights[j][...], CONTRACT_LAST) + mm(second, weights[count + j][...], CONTRACT_LAST)
            )
            for q in range(w_mine[j].shape[0] // own):
                at = flip(fsdp, d, n_fsdp) * (depth // own) + offset // own + q
                outs[at] = out[:, q * own : (q + 1) * own]
                deal(n_ctx, outs.at[at], at, landed, (deal_s, deal_r), own_sem)
        for index in range(n_ctx):
            cols_ref[index] = grad_ref[:, index * own : (index + 1) * own]
        dealt(n_ctx, outs.at[0], landed, (deal_s, deal_r), own_sem)

    shape = (n_ctx, rows, own)
    return pl.pallas_call(
        kernel,
        in_specs=[pl.BlockSpec(memory_space=pltpu.VMEM)] * (1 + 2 * count),
        out_specs=any_specs(1) + [pl.BlockSpec(memory_space=pltpu.VMEM)],
        out_shape=[jax.ShapeDtypeStruct(shape, grad.dtype)] * 2,
        scratch_shapes=[pltpu.VMEM(shape, grad.dtype)] + dma_pair(n_ctx) + [pltpu.SemaphoreType.DMA],
        compiler_params=params(9),
        name="project_back",
    )(grad, *w_mine, *w_other)


def connect_back(values, coef, dyn, branch, grads, grad_normed, dynamic, means, coef_before=None, offset=0):
    number, rows, features = values.shape
    steps = rows // ROWS
    more = coef_before is not None

    def kernel(*refs):
        values_ref, coef_ref, dyn_ref, branch_ref, grads_ref, normed_ref, dynamic_ref, means_ref = refs[:8]
        refs = refs[8:]
        if more:
            before_ref, refs = refs[0], refs[1:]
        out_ref, dynamic_out, static_out = refs[:3]
        if more:
            forward_ref, grad_low_ref = refs[3:5]
        step = pl.program_id(0)

        @pl.when(step == 0)
        def _():
            dynamic_out[...] = jnp.zeros_like(dynamic_out)
            static_out[...] = jnp.zeros_like(static_out)

        branch = branch_ref[...]
        grads = [grads_ref[j].astype(jnp.float32) for j in range(number)]
        mixed = sum((coef_ref[i][:, 1:2] * values_ref[i].astype(jnp.float32) for i in range(number)))
        normed, inverse = normalize(mixed)
        grad_mixed = normalize_back(normed, inverse, normed_ref[...])
        lane = lax.broadcasted_iota(jnp.int32, (ROWS, 8), 1)
        pre_grads, highs, lows = [], [], []
        for i in range(number):
            value = values_ref[i].astype(jnp.float32)
            columns = [grads[i] * branch, grad_mixed * value] + [grads[j] * value for j in range(number)]
            coef_grad = jnp.zeros((ROWS, 8), jnp.float32)
            for k, column in enumerate(columns):
                coef_grad = jnp.where(lane == k, jnp.sum(column, axis=-1, keepdims=True), coef_grad)
            static_out[i : i + 1] += jnp.sum(coef_grad, axis=0, keepdims=True)
            part = jnp.tanh(dyn_ref[i])
            pre_grads.append(coef_grad * (1.0 - part * part))
            high, rest = split((value - coef_ref[i][:, 6:7]) * coef_ref[i][:, 7:8])
            highs.append(high)
            lows.append(rest)
        pre, pre_rest = split(jnp.concatenate(pre_grads))
        dynamic, dynamic_rest = split(dynamic_ref[...])
        normed_grads = mm(
            jnp.concatenate([pre, pre_rest, pre], axis=1), jnp.concatenate([dynamic, dynamic, dynamic_rest], axis=0)
        )
        highs = jnp.concatenate(highs)
        dynamic_out[...] += (
            mm(pre, highs, CONTRACT_FIRST)
            + mm(pre_rest, highs, CONTRACT_FIRST)
            + mm(pre, jnp.concatenate(lows), CONTRACT_FIRST)
        )
        befores = 0.0
        for i in range(number):
            coef = coef_ref[i]
            mean_grad = jnp.sum(pre_grads[i] * means_ref[...], axis=-1, keepdims=True)
            inner = jnp.sum(pre_grads[i] * dyn_ref[i], axis=-1, keepdims=True) / features
            normed = (values_ref[i].astype(jnp.float32) - coef[:, 6:7]) * coef[:, 7:8]
            out = coef[:, 7:8] * (normed_grads[i * ROWS : (i + 1) * ROWS] - mean_grad - normed * inner)
            out = out + coef[:, 1:2] * grad_mixed
            for j in range(number):
                out = out + coef[:, 2 + j : 3 + j] * grads[j]
            out_ref[i] = out
            if more:
                befores = befores + before_ref[i][:, 0:1] * out
        if more:
            grad_low_ref[...] = low(befores)
            for j in range(number):
                out = coef_ref[j][:, 0:1] * branch
                for i in range(number):
                    out = out + coef_ref[i][:, 2 + j : 3 + j] * values_ref[i].astype(jnp.float32)
                forward_ref[j] = low(out)

    rows_spec = pl.BlockSpec((ROWS, features), lambda r: (r, 0))
    out_shape = [
        jax.ShapeDtypeStruct((number, rows, features), jnp.float32),
        jax.ShapeDtypeStruct((8, features), jnp.float32),
        jax.ShapeDtypeStruct((8, 8), jnp.float32),
    ]
    out_specs = [row_blocks(number, features), whole_block((8, features)), whole_block((8, 8))]
    operands = [values, coef, dyn, branch, grads, grad_normed, dynamic, means]
    in_specs = [
        row_blocks(number, features),
        row_blocks(number, 8),
        row_blocks(number, 8),
        rows_spec,
        row_blocks(number, features),
        pl.BlockSpec((ROWS, features), lambda r: (offset // ROWS + r, 0)),
        whole_block(dynamic.shape),
        whole_block(means.shape),
    ]
    if more:
        operands.append(coef_before)
        in_specs.append(row_blocks(number, 8))
        out_shape.append(jax.ShapeDtypeStruct((number, rows, features), jnp.bfloat16))
        out_specs.append(row_blocks(number, features))
        out_shape.append(jax.ShapeDtypeStruct((rows, features), jnp.bfloat16))
        out_specs.append(rows_spec)
    return pl.pallas_call(
        kernel,
        grid=(steps,),
        in_specs=in_specs,
        out_specs=out_specs,
        out_shape=out_shape,
        compiler_params=params(),
        name="connect_back",
    )(*operands)


def local(n_ctx, n_fsdp, streams, w_attn, w_ffn, hc_dynamic, hc_static, cotangent, pair_order):
    number = streams.shape[1]
    length = streams.shape[2]
    features = streams.shape[3]
    size = HEAD_DIM
    own = features // n_ctx
    heads = own // size
    rows = length * n_ctx
    own_rows = w_attn.shape[0]
    ctx = lax.axis_index("ctx")
    fsdp = lax.axis_index("fsdp")
    core = ctx % 2
    chips = n_ctx // 2
    core_index = jnp.reshape(core, (1,)).astype(jnp.int32)

    def in_order(mine, other, axis):
        return jnp.where(
            core == 0, jnp.concatenate([mine, other], axis=axis), jnp.concatenate([other, mine], axis=axis)
        )


    w_own = lax.dynamic_slice_in_dim(w_attn, ctx * own, own, 2)[:, 0:3].reshape(own_rows, 3 * own)
    w_qkv = gather(w_own, "fsdp")
    half = features // 2
    w_half = lax.dynamic_slice_in_dim(w_attn, core * half, half, 2)[:, 3]
    siblings = [(i, i ^ 1) for i in range(n_ctx)]
    core_fsdp = jnp.stack([core, fsdp]).astype(jnp.int32)

    def exchange(values, most=0):
        return [values] + [
            lax.ppermute(values, "fsdp", [(i, i ^ d) for i in range(n_fsdp)])
            for d in range(1, most + 1 if most else n_fsdp)
        ]

    def swap(blocks):
        return [lax.ppermute(block, "ctx", siblings) for block in blocks]


    positions = block_positions(pair_order, length)
    frequency = THETA ** (-(jnp.arange(size // 2, dtype=jnp.float32) * 2.0) / size)
    angles = positions.astype(jnp.float32)[:, None] * jnp.concatenate([frequency, frequency])[None, :]
    signs = jnp.where(jnp.arange(size) < size // 2, -1.0, 1.0)
    tables = (jnp.cos(angles), jnp.sin(angles) * signs[None, :], positions[:, None], positions[None, :])

    dynamics = jnp.pad(hc_dynamic, ((0, 0), (0, 2), (0, 0)))
    means = jnp.mean(dynamics, axis=-1)
    statics = jnp.pad(hc_static, ((0, 0), (0, 0), (0, 2)))
    coef_one, dyn_one, attn_low = connect_first(streams[0], dynamics[0], statics[0])
    attn_low, w_half = lax.optimization_barrier((attn_low, w_half))
    w_out_mine = exchange(w_half, 2 if n_fsdp == 4 else 0)
    attn_all = line_rows(n_ctx, attn_low).reshape(rows, features)
    w_out_where = [(d, 0) for d in range(len(w_out_mine))]
    attn_all, *w_out_mine = lax.optimization_barrier((attn_all, *w_out_mine))
    w_out_other = swap(w_out_mine)
    if n_fsdp == 4:
        middle = own_rows // 2
        corners = [
            lax.ppermute(w_out_mine[1][:middle], "fsdp", [(i, i ^ 2) for i in range(4)]),
            lax.ppermute(w_out_mine[2][middle:], "fsdp", [(i, i ^ 1) for i in range(4)]),
        ]
        w_out_where += [(3, 0), (3, middle)]
    query, key, value, attended, logs, attended_rows = attention_forward(n_ctx, attn_all, w_qkv, *tables, heads)
    if n_fsdp == 4:
        attended, *corners = lax.optimization_barrier((attended, *corners))
        w_out_mine += corners
        w_out_other += swap(corners)

    first_out, attn_branch, coef_two, dyn_two, ffn_own = connect_middle(
        streams[0], coef_one, attended_rows, w_out_mine, w_out_other, cotangent[0], dynamics[1], statics[1], core_fsdp,
        w_out_where, own_rows,
    )
    ffn_own = ffn_own.reshape(2 * length, features)

    planes = jnp.moveaxis(w_ffn, 1, 0)
    n_own = planes.shape[1] // 2
    blocks = 2 * n_fsdp
    if n_fsdp == 4:
        ffn_all, mirror_rows, *hidden, sums, attended_all = ffn_rows(n_ctx, ffn_own, planes, attended, n_own)
        ffn_all, mirror_rows = (part.reshape(blocks, 2, length, features) for part in (ffn_all, mirror_rows))
        mirror_rows = [mirror_rows]
        weight_parts, sums, weight_early = ffn_weights(
            n_ctx, n_fsdp, sums, ffn_all, mirror_rows, hidden, planes, n_own
        )
    else:
        ffn_mirror = lax.ppermute(ffn_own, "ctx", [(i, n_ctx - 2 - i + 2 * (i % 2)) for i in range(n_ctx)])
        ffn_all = square_core_gather(n_ctx, n_fsdp, ffn_own).reshape(blocks, 2, length, features)
        attended_all = gather(attended, "ctx").reshape(n_ctx, rows, own)
        mirror_mine = exchange(ffn_mirror)
        hidden = ffn_forward(ffn_all, planes, core_index, n_own)
        sums = ffn_back(*hidden, planes, core_index, blocks)
        mirror_rows = [part.reshape(1, 2, length, features) for part in mirror_mine + swap(mirror_mine)]
        sums = square_sum(n_ctx, n_fsdp, sums.reshape(2, n_fsdp, 2 * length, features))
        (weight_parts,) = ffn_weights(n_ctx, n_fsdp, None, ffn_all, mirror_rows, hidden, planes, n_own)
    sides = chips // 2
    lines = [[2 * (sides * side + i) + j for i in range(sides)] for side in range(2) for j in range(2)]
    weight_cols = lax.psum_scatter(weight_parts, "ctx", scatter_dimension=0, axis_index_groups=lines)

    grad_first, dynamic_grad_two, static_grad_two, streams_out, grad_attn = connect_back(
        first_out, coef_two, dyn_two, sums, cotangent[0], sums, dynamics[1], means[1:], coef_one, length
    )
    grad_heads, grad_cols = project_back(n_ctx, n_fsdp, grad_attn, w_out_mine, w_out_other, w_out_where, own_rows)
    grad_heads = grad_heads.reshape(rows, own)
    grad_heads, grad_cols = lax.optimization_barrier((grad_heads, grad_cols))
    grad_cols = lax.all_to_all(grad_cols, "ctx", 0, 0, tiled=True).reshape(rows, own)
    qkv_grad, attn_part = attention_backward(query, key, value, grad_heads, logs, w_qkv, *tables, heads)
    attn_part = attn_part.reshape(n_ctx, length, features)
    if n_fsdp == 4:
        grad_attn_normed, attn_grad = attention_sums(n_ctx, attn_part, attn_all, qkv_grad, attended_all, grad_cols)
    else:
        grad_attn_normed = line_sum(n_ctx, attn_part)
        attn_grad = scatter(attention_weights(attn_all, qkv_grad, attended_all, grad_cols), "fsdp").astype(jnp.float32)
    grad_attn_normed, weight_cols = lax.optimization_barrier((grad_attn_normed, weight_cols))
    if n_fsdp == 4:
        weight_cols = jnp.concatenate([weight_early, weight_cols], axis=1)
    mine = lax.dynamic_slice_in_dim(weight_cols, core * own, own, 2)
    other = lax.dynamic_slice_in_dim(weight_cols, (1 - core) * own, own, 2)
    other = lax.ppermute(other, "ctx", siblings)
    ffn_grad = jnp.moveaxis(in_order(mine, other, 1), 0, 1).astype(jnp.float32)
    grad_inputs, dynamic_grad_one, static_grad_one = connect_back(
        streams[0], coef_one, dyn_one, attn_branch, grad_first, grad_attn_normed, dynamics[0], means[:1]
    )
    static_grads = jnp.concatenate([static_grad_one[:number, :6].reshape(1, -1), static_grad_two[:number, :6].reshape(1, -1)])
    small = jnp.concatenate(
        [
            dynamic_grad_one[:6],
            dynamic_grad_two[:6],
            jnp.pad(static_grads, ((0, 2), (0, features - 6 * number))),
        ]
    )
    small = sum_everywhere(n_ctx, n_fsdp, small.reshape(n_ctx, 8, -1))
    small = small.reshape(16, features)
    attn_grad = attn_grad.reshape(own_rows, 4, own)
    dynamic_total = small[:12].reshape(2, 6, features)
    static_total = small[12:14, : 6 * number].reshape(2, number, 6)
    return (streams_out[None], grad_inputs[None], attn_grad, ffn_grad, dynamic_total, static_total)


def solution(mesh):
    return jax.shard_map(
        functools.partial(local, mesh.shape["ctx"], mesh.shape["fsdp"]),
        mesh=mesh,
        in_specs=(
            P("fsdp", None, "ctx", None),
            P("fsdp", None, None),
            P("fsdp", None, None),
            P(),
            P(),
            P("fsdp", None, "ctx", None),
            P(),
        ),
        out_specs=(
            P("fsdp", None, "ctx", None),
            P("fsdp", None, "ctx", None),
            P("fsdp", None, "ctx"),
            P("fsdp", None, "ctx"),
            P(),
            P(),
        ),
        check_vma=False,
    )
```

```python
import functools

import jax
import jax.numpy as jnp
from jax import lax
from jax.experimental import pallas as pl
from jax.experimental.pallas import tpu as pltpu
from jax.sharding import PartitionSpec as P

HEADS = 16
HEAD_DIM = 128


EPS = 1e-05
THETA = 10000.0
HIGH = lax.Precision.HIGHEST
MASKED = -1e30
CONTRACT_LAST = (((1,), (1,)), ((), ()))
CONTRACT_FIRST = (((0,), (0,)), ((), ()))


def normalize(values):
    centered = values - jnp.mean(values, axis=-1, keepdims=True)
    inverse = lax.rsqrt(jnp.mean(centered * centered, axis=-1, keepdims=True) + EPS)
    return (centered * inverse, inverse)


def normalize_back(normed, inverse, gradient):
    inner = jnp.mean(gradient * normed, axis=-1, keepdims=True)
    return inverse * (gradient - jnp.mean(gradient, axis=-1, keepdims=True) - normed * inner)


def block_positions(pair_order, length):
    half_size = length // 2
    offsets = jnp.arange(half_size, dtype=jnp.int32)
    mirror = 2 * pair_order.shape[0] - 1 - pair_order
    first_half = pair_order[:, None] * half_size + offsets[None, :]
    second_half = mirror[:, None] * half_size + offsets[None, :]
    return jnp.concatenate([first_half, second_half], axis=1).reshape(-1)


def low(values):
    return values.astype(jnp.bfloat16)


def mm(a, b, dims=None):
    if dims is None:
        return jnp.dot(a, b, preferred_element_type=jnp.float32)
    return lax.dot_general(a, b, dims, preferred_element_type=jnp.float32)


def gather(values, axis, dim=0):
    return lax.all_gather(values, axis, axis=dim, tiled=True)


def scatter(values, axis, dim=0):
    return lax.psum_scatter(values, axis, scatter_dimension=dim, tiled=True)


MESH = pl.DeviceIdType.MESH
VMEM_LIMIT = 60 * 1024 * 1024


def place(n_ctx):
    ctx = lax.axis_index("ctx")
    return (ctx // 2, ctx % 2, lax.axis_index("fsdp"), n_ctx // 2)


def greet(peers):
    barrier = pltpu.get_barrier_semaphore()
    for peer in peers:
        pl.semaphore_signal(barrier, inc=1, device_id=peer, device_id_type=MESH)
    pl.semaphore_wait(barrier, len(peers))


def send(source, target, sems, index, peer):
    return pltpu.make_async_remote_copy(
        src_ref=source,
        dst_ref=target,
        send_sem=sems[0].at[index],
        recv_sem=sems[1].at[index],
        device_id=peer,
        device_id_type=MESH,
    )


def fsdp_neighbours(fsdp):
    first = fsdp + 1 - 2 * (fsdp % 2)
    second = (fsdp + 2) % 4
    return (first, second, (first + 2) % 4)


def fsdp_peers(n_fsdp, ctx, fsdp):
    if n_fsdp == 4:
        first, second, _ = fsdp_neighbours(fsdp)
        return [(ctx, first), (ctx, second)]
    return [(ctx, (fsdp + j) % n_fsdp) for j in range(1, n_fsdp)]


def line_peers(chip, core, fsdp, length):
    return [
        (chip * 2 + 1 - core, fsdp),
        ((chip + 1) % length * 2 + core, fsdp),
        ((chip + length - 1) % length * 2 + core, fsdp),
    ]


def line_gather(own_ref, all_ref, sems, where):
    chip, core, fsdp, length = where
    right_sems, left_sems, core_sems = sems
    sibling = (chip * 2 + 1 - core, fsdp)
    right = ((chip + 1) % length * 2 + core, fsdp)
    left = ((chip + length - 1) % length * 2 + core, fsdp)

    def block(index):
        return all_ref.at[(index + length) % length * 2 + core]

    def pass_on(index, source):
        return send(source, block(index), core_sems, (index + length) % length, sibling)

    pass_on(chip, own_ref).start()
    for step in range(length - 1):
        for sign, peer, way in ((-1, right, right_sems), (1, left, left_sems)):
            at = chip + sign * step
            held = (at >= 0) & (at < length)
            if step > 0:

                @pl.when(held)
                def _():
                    send(block(at), block(at), way, step - 1, peer).wait_recv()
                    pass_on(at, block(at)).start()

            more = (chip < length - 1) if sign < 0 else (chip > 0)

            @pl.when(held & more)
            def _():
                send(own_ref if step == 0 else block(at), block(at), way, step, peer).start()

        yield
    last = length - 1
    for sign, peer, way in ((-1, right, right_sems), (1, left, left_sems)):
        at = chip + sign * last

        @pl.when((at >= 0) & (at < length))
        def _():
            send(block(at), block(at), way, last - 1, peer).wait_recv()
            pass_on(at, block(at)).start()

    yield
    for step in range(length - 1):
        for sign, peer, way in ((-1, right, right_sems), (1, left, left_sems)):
            at = chip + sign * step
            more = (chip < length - 1) if sign < 0 else (chip > 0)

            @pl.when((at >= 0) & (at < length) & more)
            def _():
                send(block(at), block(at), way, step, peer).wait_send()

    for index in range(length):
        pass_on(index, block(index)).wait_send()
        other = all_ref.at[index * 2 + 1 - core]
        send(other, other, core_sems, index, sibling).wait_recv()


def square_gather(own_ref, all_ref, sems, ctx, fsdp, n_fsdp, passed=None):
    if n_fsdp != 4:
        copies = [
            send(own_ref, all_ref.at[fsdp], sems, j - 1, (ctx, (fsdp + j) % n_fsdp)) for j in range(1, n_fsdp)
        ]
        for copy in copies:
            copy.start()
        yield
        for j, copy in enumerate(copies):
            copy.wait()
            if passed:
                passed(all_ref.at[(fsdp + n_fsdp - j - 1) % n_fsdp], (fsdp + n_fsdp - j - 1) % n_fsdp, None, j)
        return
    first, second, corner = fsdp_neighbours(fsdp)
    half = own_ref.shape[0] // 2
    top, low_half = pl.ds(0, half), pl.ds(half, half)
    to_first, to_second = (ctx, first), (ctx, second)

    def copy(index, owner, part, peer, source=None):
        source = all_ref.at[owner, part] if source is None else source
        return send(source, all_ref.at[owner, part], sems, index, peer)

    starts = [
        copy(0, fsdp, top, to_first, own_ref.at[top]),
        copy(1, fsdp, low_half, to_second, own_ref.at[low_half]),
        copy(2, fsdp, low_half, to_first, own_ref.at[low_half]),
        copy(3, fsdp, top, to_second, own_ref.at[top]),
        copy(4, first, top, to_second),
        copy(5, second, low_half, to_first),
    ]
    arrivals = [
        (0, first, top),
        (1, second, low_half),
        (2, first, low_half),
        (3, second, top),
        (4, corner, top),
        (5, corner, low_half),
    ]
    for each in starts[:4]:
        each.start()
    yield
    for index, owner, part in arrivals:
        copy(index, owner, part, to_first).wait_recv()
        if index < 2:
            starts[4 + index].start()
        if passed:
            passed(all_ref.at[owner, part], owner, part, index)
        yield
    for each in starts:
        each.wait_send()


def run_all(*parts):
    parts = list(parts)
    while parts:
        for part in list(parts):
            try:
                next(part)
            except StopIteration:
                parts.remove(part)


def dma_pair(count):
    return [pltpu.SemaphoreType.DMA((count,)), pltpu.SemaphoreType.DMA((count,))]


def any_specs(count):
    return [pl.BlockSpec(memory_space=pl.ANY)] * count


def params(collective_id=None, **more):
    if collective_id is not None:
        more.update(collective_id=collective_id, has_side_effects=True)
    return pltpu.CompilerParams(vmem_limit_bytes=VMEM_LIMIT, **more)


def passing(own_ref, all_ref, sems, core, fsdp, sibling):
    handed = [send(own_ref, all_ref.at[core, fsdp], sems, 0, sibling)]
    handed[0].start()
    arriving = [send(own_ref, all_ref.at[1 - core, fsdp], sems, 0, sibling)]

    def passed(source, owner, part, index):
        for side, copies in ((core, handed), (1 - core, arriving)):
            target = all_ref.at[side, owner] if part is None else all_ref.at[side, owner, part]
            copies.append(send(source, target, sems, index + 1, sibling))
        handed[-1].start()

    def finish():
        for out, back in zip(handed, arriving):
            out.wait_send()
            back.wait_recv()

    return (passed, finish)


def line_rows(n_ctx, rows):
    def kernel(rows_ref, all_rows, right_s, right_r, left_s, left_r, core_s, core_r, own):
        where = place(n_ctx)
        chip, core, fsdp, length = where
        greet(line_peers(*where))
        mine = pltpu.make_async_copy(rows_ref, all_rows.at[chip * 2 + core], own)
        mine.start()
        run_all(line_gather(rows_ref, all_rows, ((right_s, right_r), (left_s, left_r), (core_s, core_r)), where))
        mine.wait()

    length = n_ctx // 2
    return pl.pallas_call(
        kernel,
        out_shape=jax.ShapeDtypeStruct((n_ctx,) + rows.shape, rows.dtype),
        in_specs=any_specs(1),
        out_specs=pl.BlockSpec(memory_space=pl.ANY),
        scratch_shapes=dma_pair(length) + dma_pair(length) + dma_pair(length) + [pltpu.SemaphoreType.DMA],
        compiler_params=params(0),
        name="line_rows",
    )(rows)


def square_core_gather(n_ctx, n_fsdp, rows):
    def kernel(rows_ref, all_ref, sq_s, sq_r, core_s, core_r, own):
        chip, core, fsdp, _ = place(n_ctx)
        ctx = chip * 2 + core
        sibling = (chip * 2 + 1 - core, fsdp)
        greet([sibling] + fsdp_peers(n_fsdp, ctx, fsdp))
        mine = pltpu.make_async_copy(rows_ref, all_ref.at[core, fsdp], own)
        mine.start()
        passed, finish = passing(rows_ref, all_ref, (core_s, core_r), core, fsdp, sibling)
        run_all(square_gather(rows_ref, all_ref.at[core], (sq_s, sq_r), ctx, fsdp, n_fsdp, passed))
        finish()
        mine.wait()

    return pl.pallas_call(
        kernel,
        out_shape=jax.ShapeDtypeStruct((2, n_fsdp) + rows.shape, rows.dtype),
        in_specs=any_specs(1),
        out_specs=pl.BlockSpec(memory_space=pl.ANY),
        scratch_shapes=dma_pair(max(6, n_fsdp)) + dma_pair(max(7, n_fsdp)) + [pltpu.SemaphoreType.DMA],
        compiler_params=params(1),
        name="square_core_gather",
    )(rows)


def add_into(target, *sources, chunk=64):
    @pl.loop(0, target.shape[0] // chunk)
    def _(step):
        rows = pl.ds(pl.multiple_of(step * chunk, chunk), chunk)
        total = target[rows].astype(jnp.float32)
        for source in sources:
            total = total + source[rows].astype(jnp.float32)
        target[rows] = total.astype(target.dtype)


def square_sum_stages(n_ctx, n_fsdp, partial_ref, out_ref, held, core_in, square_in, load, core_sems, sems):
    rows = partial_ref.shape[-2]
    half = rows // 2
    chip, core, fsdp, _ = place(n_ctx)
    ctx = chip * 2 + core
    sibling = (chip * 2 + 1 - core, fsdp)
    if n_fsdp == 4:
        first, second, corner = fsdp_neighbours(fsdp)
        order = [corner, first, second, fsdp]
    else:
        order = [(fsdp + j) % n_fsdp for j in range(1, n_fsdp + 1)]
    mine = [
        pltpu.make_async_copy(partial_ref.at[core, owner], held.at[owner], load.at[j])
        for j, owner in enumerate(order)
    ]
    others = [
        send(partial_ref.at[1 - core, owner], core_in.at[owner], core_sems, j, sibling)
        for j, owner in enumerate(order)
    ]

    def ready(j):
        mine[j].wait()
        others[j].wait_recv()
        add_into(held.at[order[j]], core_in.at[order[j]])

    def total(parts, sources):
        @pl.loop(0, parts[1] // 64)
        def _(step):
            at = pl.ds(pl.multiple_of(parts[0] + step * 64, 64), 64)
            from_at = pl.ds(pl.multiple_of(step * 64, 64), 64)
            value = held[fsdp, at].astype(jnp.float32)
            for j in sources:
                value = value + square_in[j, from_at].astype(jnp.float32)
            out_ref[at] = value

    def begin():
        greet([sibling] + fsdp_peers(n_fsdp, ctx, fsdp))
        for j in range(n_fsdp):
            others[j].start()
            mine[j].start()

    if n_fsdp != 4:
        copies = [
            send(held.at[order[j]], square_in.at[j], sems, j, (ctx, order[j])) for j in range(n_fsdp - 1)
        ]

        def spread():
            for j in range(n_fsdp):
                ready(j)
                if j < n_fsdp - 1:
                    copies[j].start()

        def finish():
            for copy in copies:
                copy.wait()
            total((0, rows), range(n_fsdp - 1))
            for each in others:
                each.wait_send()

        return [begin, spread, finish]

    top, low_half = pl.ds(0, half), pl.ds(half, half)
    to_first, to_second = (ctx, first), (ctx, second)

    def copy(index, owner, part, peer):
        return send(held.at[owner, part], square_in.at[index], sems, index, peer)

    copies = [
        copy(0, corner, top, to_first),
        copy(1, corner, low_half, to_second),
        copy(2, first, top, to_first),
        copy(3, second, low_half, to_second),
        copy(4, second, top, to_second),
        copy(5, first, low_half, to_first),
    ]

    def spread():
        ready(0)
        copies[0].start()
        copies[1].start()
        ready(1)
        copies[2].start()
        ready(2)
        copies[3].start()
        ready(3)

    def pass_on():
        copies[0].wait_recv()
        add_into(held.at[second, top], square_in.at[0])
        copies[4].start()
        copies[1].wait_recv()
        add_into(held.at[first, low_half], square_in.at[1])
        copies[5].start()

    def finish():
        for j in range(2, 6):
            copies[j].wait_recv()
        total((0, half), (2, 4))
        total((half, half), (3, 5))
        for each in copies:
            each.wait_send()
        for each in others:
            each.wait_send()

    return [begin, spread, pass_on, finish]


def corner_sum_stages(n_ctx, partial_ref, out_ref, held, square_in, load, sems):
    half = partial_ref.shape[1] // 2
    chip, core, fsdp, _ = place(n_ctx)
    ctx = chip * 2 + core
    first, second, corner = fsdp_neighbours(fsdp)
    top, low_half = pl.ds(0, half), pl.ds(half, half)
    to_first, to_second = (ctx, first), (ctx, second)

    def copy(index, source, peer):
        return send(source, square_in.at[index], sems, index, peer)

    copies = [
        copy(0, partial_ref.at[corner, top], to_first),
        copy(1, partial_ref.at[corner, low_half], to_second),
        copy(2, partial_ref.at[first, top], to_first),
        copy(3, partial_ref.at[second, low_half], to_second),
        copy(4, held.at[0], to_second),
        copy(5, held.at[1], to_first),
    ]
    mine = [
        pltpu.make_async_copy(partial_ref.at[second, top], held.at[0], load.at[0]),
        pltpu.make_async_copy(partial_ref.at[first, low_half], held.at[1], load.at[1]),
        pltpu.make_async_copy(partial_ref.at[fsdp, top], held.at[2], load.at[2]),
        pltpu.make_async_copy(partial_ref.at[fsdp, low_half], held.at[3], load.at[3]),
    ]

    starts = [
        [copies[0].start, copies[1].start],
        [copies[2].start, mine[1].start],
        [copies[3].start, mine[0].start],
        [mine[2].start, mine[3].start],
    ]

    def pass_on():
        for index in range(2):
            mine[index].wait()
            copies[index].wait_recv()
            add_into(held.at[index], square_in.at[index])
            copies[4 + index].start()

    def finish():
        for part, sources in ((0, (2, 4)), (1, (3, 5))):
            mine[2 + part].wait()
            for j in sources:
                copies[j].wait_recv()

            @pl.loop(0, half // 64)
            def _(step):
                at = pl.ds(pl.multiple_of(step * 64, 64), 64)
                value = held[2 + part, at].astype(jnp.float32)
                for j in sources:
                    value = value + square_in[j, at].astype(jnp.float32)
                out_ref[pl.ds(pl.multiple_of(part * half + step * 64, 64), 64)] = value

        for each in copies:
            each.wait_send()

    return [starts, pass_on, finish]


def corner_sum_scratch(partial):
    _, rows, columns = partial.shape
    return [
        pltpu.VMEM((4, rows // 2, columns), partial.dtype),
        pltpu.VMEM((6, rows // 2, columns), partial.dtype),
        pltpu.SemaphoreType.DMA((4,)),
    ] + dma_pair(6)


def square_sum_scratch(n_fsdp, partial):
    rows, columns = partial.shape[-2:]
    pieces = (6, rows // 2, columns) if n_fsdp == 4 else (n_fsdp - 1, rows, columns)
    return (
        [
            pltpu.VMEM((n_fsdp, rows, columns), partial.dtype),
            pltpu.VMEM((n_fsdp, rows, columns), partial.dtype),
            pltpu.VMEM(pieces, partial.dtype),
            pltpu.SemaphoreType.DMA((n_fsdp,)),
        ]
        + dma_pair(n_fsdp)
        + dma_pair(max(6, n_fsdp))
    )


def square_sum(n_ctx, n_fsdp, partial):
    def kernel(partial_ref, out_ref, held, core_in, square_in, load, core_s, core_r, sq_s, sq_r):
        for stage in square_sum_stages(
            n_ctx, n_fsdp, partial_ref, out_ref, held, core_in, square_in, load, (core_s, core_r), (sq_s, sq_r)
        ):
            stage()

    return pl.pallas_call(
        kernel,
        out_shape=jax.ShapeDtypeStruct(partial.shape[-2:], jnp.float32),
        in_specs=any_specs(1),
        out_specs=pl.BlockSpec(memory_space=pltpu.VMEM),
        scratch_shapes=square_sum_scratch(n_fsdp, partial),
        compiler_params=params(1),
        name="square_sum",
    )(partial)


def line_sum_steps(n_ctx, partial_ref, out_ref, held, core_in, right_in, left_in, load, core_sems, right_sems, left_sems):
    rows = partial_ref.shape[1]
    where = place(n_ctx)
    chip, core, fsdp, length = where
    sibling, right, left = line_peers(*where)
    order = [(chip + length - 1 - j) % length for j in range(length)]
    mine, others = [], []
    for j, owner in enumerate(order):
        mine.append(pltpu.make_async_copy(partial_ref.at[owner * 2 + core], held.at[owner], load.at[j]))
        others.append(send(partial_ref.at[owner * 2 + 1 - core], core_in.at[owner], core_sems, j, sibling))
        others[-1].start()
        mine[-1].start()
    yield
    for j, owner in enumerate(order):
        mine[j].wait()
        others[j].wait_recv()
        add_into(held.at[owner], core_in.at[owner])
    ways = ((1, right, right_in, right_sems), (-1, left, left_in, left_sems))
    for step in range(length - 1):
        for sign, peer, arrived, sems in ways:
            block = chip + sign * (length - 1 - step)
            inside = (block >= 0) & (block < length)
            came = (chip >= 1) if sign > 0 else (chip < length - 1)
            if step > 0:

                @pl.when(inside & came)
                def _():
                    send(held.at[block], arrived.at[step - 1], sems, step - 1, peer).wait_recv()
                    add_into(held.at[block], arrived.at[step - 1])

            @pl.when(inside)
            def _():
                send(held.at[block], arrived.at[step], sems, step, peer).start()

        yield
    last = length - 2
    for sign, peer, arrived, sems in ways:
        came = (chip >= 1) if sign > 0 else (chip < length - 1)

        @pl.when(came)
        def _():
            send(held.at[chip], arrived.at[last], sems, last, peer).wait_recv()
            add_into(held.at[chip], arrived.at[last])

    @pl.loop(0, rows // 64)
    def _(step):
        at = pl.ds(pl.multiple_of(step * 64, 64), 64)
        out_ref[at] = held[chip, at].astype(jnp.float32)

    for step in range(length - 1):
        for sign, peer, arrived, sems in ways:
            block = chip + sign * (length - 1 - step)

            @pl.when((block >= 0) & (block < length))
            def _():
                send(held.at[block], arrived.at[step], sems, step, peer).wait_send()

    for each in others:
        each.wait_send()


def line_sum_scratch(n_ctx, partial):
    rows, columns = partial.shape[-2:]
    length = n_ctx // 2
    return [
        pltpu.VMEM((length, rows, columns), partial.dtype),
        pltpu.VMEM((length, rows, columns), partial.dtype),
        pltpu.VMEM((length - 1, rows, columns), partial.dtype),
        pltpu.VMEM((length - 1, rows, columns), partial.dtype),
        pltpu.SemaphoreType.DMA((length,)),
    ] + dma_pair(length) * 3


def line_sum(n_ctx, partial):
    def kernel(partial_ref, out_ref, held, core_in, right_in, left_in, load, core_s, core_r, right_s, right_r, left_s, left_r):
        greet(line_peers(*place(n_ctx)))
        run_all(
            line_sum_steps(
                n_ctx, partial_ref, out_ref, held, core_in, right_in, left_in, load,
                (core_s, core_r), (right_s, right_r), (left_s, left_r),
            )
        )

    return pl.pallas_call(
        kernel,
        out_shape=jax.ShapeDtypeStruct(partial.shape[-2:], jnp.float32),
        in_specs=any_specs(1),
        out_specs=pl.BlockSpec(memory_space=pltpu.VMEM),
        scratch_shapes=line_sum_scratch(n_ctx, partial),
        compiler_params=params(5),
        name="line_sum",
    )(partial)


def attention_sums(n_ctx, partial, rows, grads, attended, grad_cols):
    total, features = rows.shape
    parts, _, own = attended.shape
    wide = grads.shape[1]
    depth = features // 4
    weight_shape = jax.ShapeDtypeStruct((4, depth, wide + own), jnp.bfloat16)
    inputs = (rows, grads, attended, grad_cols)

    def kernel(partial_ref, *refs):
        inputs_refs, refs = refs[:4], refs[4:]
        out_ref, weight_ref, rows_v, grads_v, attended_v, cols_v, weights, in_sem, *refs = refs
        line_refs, refs = refs[:5], refs[5:]
        core_s, core_r, right_s, right_r, left_s, left_r, *refs = refs
        held, square_in, load, sq_s, sq_r = refs
        where = place(n_ctx)
        chip, core, fsdp, _ = where
        loads = [
            pltpu.make_async_copy(a, b, in_sem.at[j])
            for j, (a, b) in enumerate(zip(inputs_refs, (rows_v, grads_v, attended_v, cols_v)))
        ]
        for each in loads:
            each.start()
        greet(line_peers(*where) + fsdp_peers(4, chip * 2 + core, fsdp))
        line = line_sum_steps(
            n_ctx, partial_ref, out_ref, *line_refs, (core_s, core_r), (right_s, right_r), (left_s, left_r)
        )
        next(line)
        starts, pass_on, finish = corner_sum_stages(n_ctx, weights, weight_ref, held, square_in, load, (sq_s, sq_r))
        for each in loads:
            each.wait()
        first, second, corner = fsdp_neighbours(fsdp)
        for number, owner in enumerate((corner, first, second, fsdp)):
            at = pl.ds(pl.multiple_of(owner * depth, depth), depth)
            weights[owner, :, :wide] = low(mm(rows_v[:, at], grads_v[...], CONTRACT_FIRST))
            for q in range(depth // own):
                weights[owner, q * own : (q + 1) * own, wide:] = low(
                    mm(attended_v[owner * (depth // own) + q], cols_v[...], CONTRACT_FIRST)
                )
            for start in starts[number]:
                start()
            if number < 2:
                next(line)
        pass_on()
        run_all(line)
        finish()

    return pl.pallas_call(
        kernel,
        out_shape=[
            jax.ShapeDtypeStruct(partial.shape[-2:], jnp.float32),
            jax.ShapeDtypeStruct(weight_shape.shape[1:], jnp.float32),
        ],
        in_specs=any_specs(5),
        out_specs=[pl.BlockSpec(memory_space=pltpu.VMEM)] * 2,
        scratch_shapes=[pltpu.VMEM(a.shape, a.dtype) for a in inputs]
        + [pltpu.VMEM(weight_shape.shape, weight_shape.dtype), pltpu.SemaphoreType.DMA((4,))]
        + line_sum_scratch(n_ctx, partial)
        + corner_sum_scratch(weight_shape),
        compiler_params=params(4),
        cost_estimate=pl.CostEstimate(
            flops=2 * total * features * (wide + own), bytes_accessed=16 * 1024 * 1024, transcendentals=0
        ),
        name="attention_sums",
    )(partial, *inputs)


def sum_everywhere(n_ctx, n_fsdp, values):
    block = values.shape[1:]

    def kernel(values_ref, out_ref, along_ctx, along_fsdp, result, ctx_s, ctx_r, fsdp_s, fsdp_r, back_s, back_r):
        ctx = lax.axis_index("ctx")
        fsdp = lax.axis_index("fsdp")
        ctx_peers = [((ctx + j) % n_ctx, fsdp) for j in range(1, n_ctx)]
        fsdp_peers = [(ctx, (fsdp + j) % n_fsdp) for j in range(1, n_fsdp)]
        greet(ctx_peers + fsdp_peers)

        def exchange(copies):
            for copy in copies:
                copy.start()
            for copy in copies:
                copy.wait()

        def total(slots, count):
            value = slots[0]
            for j in range(1, count):
                value = value + slots[j]
            return value

        along_ctx[ctx] = values_ref[ctx]
        exchange(
            [
                send(values_ref.at[peer[0]], along_ctx.at[ctx], (ctx_s, ctx_r), j, peer)
                for j, peer in enumerate(ctx_peers)
            ]
        )
        along_fsdp[fsdp] = total(along_ctx, n_ctx)
        exchange(
            [
                send(along_fsdp.at[fsdp], along_fsdp.at[fsdp], (fsdp_s, fsdp_r), j, peer)
                for j, peer in enumerate(fsdp_peers)
            ]
        )
        result[ctx] = total(along_fsdp, n_fsdp)
        exchange(
            [send(result.at[ctx], result.at[ctx], (back_s, back_r), j, peer) for j, peer in enumerate(ctx_peers)]
        )
        out_ref[...] = result[...]

    return pl.pallas_call(
        kernel,
        out_shape=jax.ShapeDtypeStruct(values.shape, values.dtype),
        in_specs=[pl.BlockSpec(memory_space=pltpu.VMEM)],
        out_specs=pl.BlockSpec(memory_space=pltpu.VMEM),
        scratch_shapes=[
            pltpu.VMEM((n_ctx,) + block, values.dtype),
            pltpu.VMEM((n_fsdp,) + block, values.dtype),
            pltpu.VMEM((n_ctx,) + block, values.dtype),
        ]
        + dma_pair(n_ctx)
        + dma_pair(n_fsdp)
        + dma_pair(n_ctx),
        compiler_params=params(2),
        name="sum_everywhere",
    )(values)


def hidden_units(here, back, gate_ref, up_ref, down_ref):
    gate = mm(here, gate_ref[0], CONTRACT_LAST)
    up = mm(here, up_ref[0], CONTRACT_LAST)
    grad_hidden = mm(back, down_ref[0], CONTRACT_LAST)
    sigmoid = jax.nn.sigmoid(gate)
    activated = gate * sigmoid
    return (
        low(activated * up),
        low(grad_hidden * up * sigmoid * (1.0 + gate * (1.0 - sigmoid))),
        low(grad_hidden * activated),
    )


def ffn_forward(rows, planes, core, n_own, chunk=256):
    blocks, _, tokens, features = rows.shape
    total = blocks * tokens
    steps = n_own // chunk
    group = max(1, 256 // tokens)

    def kernel(core_ref, rows_ref, gate_ref, up_ref, down_ref, *outs):
        for at in range(0, blocks, group):
            here = rows_ref[at : at + group, 0].reshape(group * tokens, features)
            back = rows_ref[at : at + group, 1].reshape(group * tokens, features)
            span = pl.ds(at * tokens, group * tokens)
            for out, value in zip(outs, hidden_units(here, back, gate_ref, up_ref, down_ref)):
                out[span] = value

    def weight_spec(plane):
        return pl.BlockSpec((1, chunk, features), lambda j, core_ref: (plane, core_ref[0] * steps + j, 0))

    act = jax.ShapeDtypeStruct((total, n_own), jnp.bfloat16)
    act_spec = pl.BlockSpec((total, chunk), lambda j, core_ref: (0, j))
    return pl.pallas_call(
        kernel,
        grid_spec=pltpu.PrefetchScalarGridSpec(
            num_scalar_prefetch=1,
            grid=(steps,),
            in_specs=[
                pl.BlockSpec(rows.shape, lambda j, core_ref: (0, 0, 0, 0), pipeline_mode=pl.Buffered(1)),
                weight_spec(0),
                weight_spec(1),
                weight_spec(2),
            ],
            out_specs=[act_spec, act_spec, act_spec],
        ),
        out_shape=[act, act, act],
        compiler_params=params(),
        cost_estimate=pl.CostEstimate(
            flops=6 * total * n_own * features, bytes_accessed=30 * 1024 * 1024, transcendentals=total * n_own
        ),
        name="ffn_forward",
    )(core, rows, planes, planes, planes)


def mirror_gather(all_ref, arrivals, sems, pass_sems, ctx, core, fsdp, sibling):
    first, second, corner = fsdp_neighbours(fsdp)
    half = all_ref.shape[2] // 2
    parts = [pl.ds(0, half), pl.ds(half, half)]
    to_first, to_second = (ctx, first), (ctx, second)

    def copy(index, owner, part, peer):
        place_ref = all_ref.at[core, owner, parts[part]]
        return send(place_ref, place_ref, sems, index, peer)

    copies = [
        copy(0, fsdp, 0, to_first),
        copy(1, fsdp, 0, to_second),
        copy(2, fsdp, 1, to_first),
        copy(3, fsdp, 1, to_second),
        copy(4, first, 0, to_second),
        copy(5, second, 1, to_first),
    ]
    passes = [(fsdp, 0), (fsdp, 1), (first, 0), (second, 0), (first, 1), (second, 1), (corner, 0), (corner, 1)]

    def passing_copy(number, side):
        owner, part = passes[number]
        place_ref = all_ref.at[side, owner, parts[part]]
        return send(place_ref, place_ref, pass_sems, number, sibling)

    for part in range(2):
        arrivals[part].wait_recv()
        copies[2 * part].start()
        copies[2 * part + 1].start()
        passing_copy(part, core).start()
        yield
    for index, number, then in ((0, 2, 4), (1, 3, None), (2, 4, None), (3, 5, 5), (4, 6, None), (5, 7, None)):
        owner, part = passes[number]
        copy(index, owner, part, to_first).wait_recv()
        if then is not None:
            copies[then].start()
        passing_copy(number, core).start()
        yield
    for each in copies:
        each.wait_send()
    for number in range(8):
        passing_copy(number, core).wait_send()
        passing_copy(number, 1 - core).wait_recv()


def ffn_rows(n_ctx, own, planes, attended, n_own, chunk=256, wide=512):
    n_fsdp = 4
    size, features = own.shape
    tokens = size // 2
    total = 2 * n_fsdp * tokens

    def kernel(
        own_ref, planes_ref, attended_ref, all_ref, mirror_ref, hidden_a, hidden_b, hidden_c, partial_ref, heads_ref,
        rows, weights, hidden, partial, core_in, load, sq_s, sq_r, core_s, core_r, far_s, far_r, mi_s, mi_r, mc_s, mc_r, sum_s, sum_r, out_sem,
        ri_s, ri_r, le_s, le_r, lc_s, lc_r, heads_sem,
    ):
        chip, core, fsdp, length = place(n_ctx)
        ctx = chip * 2 + core
        sibling = (chip * 2 + 1 - core, fsdp)
        mirror = ((length - 1 - chip) * 2 + core, fsdp)
        first, second, corner = fsdp_neighbours(fsdp)
        where = (chip, core, fsdp, length)
        greet([mirror] + line_peers(*where) + fsdp_peers(n_fsdp, ctx, fsdp))
        line = line_gather(attended_ref, heads_ref, ((ri_s, ri_r), (le_s, le_r), (lc_s, lc_r)), where)
        heads_own = pltpu.make_async_copy(attended_ref, heads_ref.at[ctx], heads_sem)
        heads_own.start()
        mine = pltpu.make_async_copy(own_ref, rows.at[core, fsdp], load.at[3])
        mine.start()
        start = pl.multiple_of(core * n_own, n_own)
        loads = [
            pltpu.make_async_copy(planes_ref.at[p, pl.ds(start, n_own)], weights.at[p], load.at[p]) for p in range(3)
        ]
        handed, arriving = [], []

        def hand(source, owner, part, index):
            for side, copies in ((core, handed), (1 - core, arriving)):
                target = rows.at[side, owner] if part is None else rows.at[side, owner, part]
                copies.append(send(source, target, (core_s, core_r), index + 1, sibling))
            handed[-1].start()

        gathering = square_gather(own_ref, rows.at[core], (sq_s, sq_r), ctx, fsdp, n_fsdp, hand)
        next(gathering)
        hand(own_ref, fsdp, None, -1)
        for each in loads:
            each.start()
        far = [
            send(
                own_ref.at[pl.ds(part * tokens, tokens)],
                mirror_ref.at[core, fsdp, pl.ds(part * tokens, tokens)],
                (far_s, far_r),
                part,
                mirror,
            )
            for part in range(2)
        ]
        for each in far:
            each.start()
        mirroring = mirror_gather(mirror_ref, far, (mi_s, mi_r), (mc_s, mc_r), ctx, core, fsdp, sibling)
        outs, summing, sums = [], [], []

        def add_up(number, owner):
            summing[number].wait_recv()
            add_into(partial.at[number % 2, core], core_in.at[number])
            sums.append(
                pltpu.make_async_copy(partial.at[number % 2, core], partial_ref.at[owner], out_sem.at[number % 2, 8])
            )
            sums[-1].start()

        def group(number, owner):
            slot = number % 2
            if number >= 2:
                for each in outs[number - 2]:
                    each.wait()
                summing[number - 2].wait_send()
                sums[number - 2].wait()
            here = jnp.concatenate([rows[0, owner, :tokens], rows[1, owner, :tokens]])
            back = jnp.concatenate([rows[0, owner, tokens:], rows[1, owner, tokens:]])

            @pl.loop(0, n_own // chunk)
            def _(step):
                at = pl.ds(pl.multiple_of(step * chunk, chunk), chunk)
                parts = [weights.at[pl.ds(p, 1), at] for p in range(3)]
                for q, value in enumerate(hidden_units(here, back, *parts)):
                    hidden[slot, q, :, at] = value

            @pl.loop(0, features // wide)
            def _(step):
                at = pl.ds(pl.multiple_of(step * wide, wide), wide)
                out = low(mm(hidden[slot, 0], weights[2, :, at]))
                below = low(mm(hidden[slot, 1], weights[0, :, at]) + mm(hidden[slot, 2], weights[1, :, at]))
                for k in range(2):
                    partial[slot, k, :tokens, at] = out[k * tokens : (k + 1) * tokens]
                    partial[slot, k, tokens:, at] = below[k * tokens : (k + 1) * tokens]

            pairs = []
            summing.append(send(partial.at[slot, 1 - core], core_in.at[number], (sum_s, sum_r), number, sibling))
            summing[-1].start()
            for k in range(2):
                pairs.append((rows.at[k, owner], all_ref.at[k, owner]))
                at = pl.ds(pl.multiple_of((k * n_fsdp + owner) * tokens, tokens), tokens)
                for q, target in enumerate((hidden_a, hidden_b, hidden_c)):
                    pairs.append((hidden.at[slot, q, pl.ds(k * tokens, tokens)], target.at[at]))
            outs.append(
                [pltpu.make_async_copy(a, b, out_sem.at[slot, j]) for j, (a, b) in enumerate(pairs)]
            )
            for each in outs[-1]:
                each.start()

        mine.wait()
        arriving[0].wait_recv()
        for each in loads:
            each.wait()
        group(0, fsdp)
        for _ in range(4):
            next(gathering)
        arriving[1].wait_recv()
        arriving[3].wait_recv()
        group(1, first)
        add_up(0, fsdp)
        next(mirroring)
        next(line)
        for _ in range(2):
            next(gathering)
        arriving[2].wait_recv()
        arriving[4].wait_recv()
        group(2, second)
        add_up(1, first)
        next(mirroring)
        next(line)
        for _ in range(2):
            next(mirroring)
        arriving[5].wait_recv()
        arriving[6].wait_recv()
        group(3, corner)
        next(line)
        add_up(2, second)
        next(mirroring)
        add_up(3, corner)
        run_all(mirroring, line, gathering)
        heads_own.wait()
        for each in handed:
            each.wait_send()
        for each in far:
            each.wait_send()
        for each in outs[2] + outs[3] + sums[2:]:
            each.wait()
        for each in summing[2:]:
            each.wait_send()

    act = jax.ShapeDtypeStruct((total, n_own), own.dtype)
    all_rows = jax.ShapeDtypeStruct((2, n_fsdp) + own.shape, own.dtype)
    return pl.pallas_call(
        kernel,
        in_specs=any_specs(3),
        out_specs=any_specs(7),
        out_shape=[
            all_rows,
            all_rows,
            act,
            act,
            act,
            jax.ShapeDtypeStruct((n_fsdp,) + own.shape, own.dtype),
            jax.ShapeDtypeStruct((n_ctx,) + attended.shape, attended.dtype),
        ],
        scratch_shapes=[
            pltpu.VMEM((2, n_fsdp) + own.shape, own.dtype),
            pltpu.VMEM((3, n_own, features), own.dtype),
            pltpu.VMEM((2, 3, 2 * tokens, n_own), own.dtype),
            pltpu.VMEM((2, 2) + own.shape, own.dtype),
            pltpu.VMEM((n_fsdp,) + own.shape, own.dtype),
            pltpu.SemaphoreType.DMA((4,)),
        ]
        + dma_pair(6)
        + dma_pair(7)
        + dma_pair(2)
        + dma_pair(6)
        + dma_pair(8)
        + dma_pair(4)
        + [pltpu.SemaphoreType.DMA((2, 9))]
        + dma_pair(n_ctx // 2) * 3
        + [pltpu.SemaphoreType.DMA],
        compiler_params=params(6),
        cost_estimate=pl.CostEstimate(
            flops=12 * total * n_own * features, bytes_accessed=50 * 1024 * 1024, transcendentals=total * n_own
        ),
        name="ffn_rows",
    )(own, planes, attended)


def ffn_weights(n_ctx, n_fsdp, partial, rows, rows_mirror, hidden, planes, n_own, chunk=256):
    blocks, _, tokens, features = rows.shape
    total = blocks * tokens
    steps = n_own // chunk
    group = max(1, 256 // tokens)
    half = features // 2
    sides = n_ctx // 4
    wide = half // sides
    fused = partial is not None
    early = steps // 2 if fused else 0
    assert not fused or sides == 2

    def kernel(*refs):
        rows_ref, refs = refs[0], refs[1:]
        mirror_refs, refs = refs[: len(rows_mirror)], refs[len(rows_mirror) :]
        mirror_blocks = [ref.at[b] for ref in mirror_refs for b in range(ref.shape[0])]
        hidden_ref, grad_gate_ref, grad_up_ref, planes_ref, *refs = refs
        if fused:
            partial_ref, weight_ref, out_ref, early_ref, *refs = refs
        else:
            weight_ref, *refs = refs
        mirror, (weights, weight_sems), refs = refs[:3], refs[3:5], refs[5:]
        chip, core, _, length = place(n_ctx)
        side = chip // sides
        step = pl.program_id(0)
        stages = []
        if fused:
            keep, give, take, side_s, side_r, held, square_in, load, sq_s, sq_r = refs
            member = chip % 2
            other = (chip + 1 - 2 * member) * 2 + core
            crossing = [
                [
                    send(
                        give.at[j, plane],
                        take.at[j, plane],
                        (side_s, side_r),
                        3 * j + plane,
                        (other, lax.axis_index("fsdp")),
                    )
                    for plane in range(3)
                ]
                for j in range(early)
            ]
            starts, *stages = corner_sum_stages(n_ctx, partial_ref, out_ref, held, square_in, load, (sq_s, sq_r))

        def fetch(at, slot):
            start = pl.multiple_of((core * steps + at) * chunk, chunk)
            return pltpu.make_async_copy(planes_ref.at[:, pl.ds(start, chunk)], weights.at[slot], weight_sems.at[slot])

        @pl.when(step == 0)
        def _():
            fetch(0, 0).start()
            if fused:
                fsdp = lax.axis_index("fsdp")
                greet(fsdp_peers(4, chip * 2 + core, fsdp) + [(other, fsdp)])
                for start in sum(starts, []):
                    start()

        @pl.when(step + 1 < steps)
        def _():
            fetch(step + 1, (step + 1) % 2).start()

        slot = step % 2
        fetch(step, slot).wait()
        gate_ref, up_ref, down_ref = (weights.at[slot, pl.ds(plane, 1)] for plane in range(3))
        for at in range(0, blocks, group):
            here = jnp.concatenate([ref[0] for ref in mirror_blocks[at : at + group]])
            back = jnp.concatenate([ref[1] for ref in mirror_blocks[at : at + group]])
            span = pl.ds(at * tokens, group * tokens)
            for out, value in zip(mirror, hidden_units(here, back, gate_ref, up_ref, down_ref)):
                out[span] = value

        lefts = ((grad_gate_ref, mirror[1], 0), (grad_up_ref, mirror[2], 0), (hidden_ref, mirror[0], 1))
        for plane, (left, left_mirror, which) in enumerate(lefts):
            left = left[...]
            left_mirror = left_mirror[...]
            for z in range(sides):
                cols = pl.ds(pl.multiple_of(side * half + z * wide, wide), wide)
                right = rows_ref[:, which, :, cols].reshape(total, wide)
                right_mirror = jnp.concatenate([ref[which, :, cols] for ref in mirror_blocks])
                value = mm(left, right, CONTRACT_FIRST) + mm(left_mirror, right_mirror, CONTRACT_FIRST)
                if not fused:
                    weight_ref[z, plane] = low(value)
                    continue

                @pl.when((step < early) & (z == member))
                def _():
                    keep[step % early, plane] = value

                @pl.when((step < early) & (z != member))
                def _():
                    give[step % early, plane] = low(value)

                @pl.when(step >= early)
                def _():
                    weight_ref[z, plane] = low(value)

            for j in range(early):

                @pl.when(step == j)
                def _():
                    crossing[j][plane].start()

        for at, stage in ((1, 0), (steps - 1, 1)):
            if stage < len(stages):

                @pl.when(step == min(at, steps - 1))
                def _():
                    stages[stage]()

        if fused:

            @pl.when(step == steps - 1)
            def _():
                for j in range(early):
                    for plane in range(3):
                        crossing[j][plane].wait()
                        early_ref[plane, j * chunk : (j + 1) * chunk] = low(
                            keep[j, plane] + take[j, plane].astype(jnp.float32)
                        )

    act_spec = pl.BlockSpec((total, chunk), lambda j: (0, j))
    once = dict(pipeline_mode=pl.Buffered(1))
    operands = [rows, *rows_mirror, *hidden, planes]
    in_specs = [whole_block(rows.shape, **once)] + [whole_block(part.shape, **once) for part in rows_mirror]
    in_specs += [act_spec] * 3 + any_specs(1)
    out_specs = [pl.BlockSpec((sides, 3, chunk, wide), lambda j: (0, 0, jnp.maximum(j - early, 0), 0))]
    out_shape = [jax.ShapeDtypeStruct((sides, 3, n_own - early * chunk, wide), jnp.bfloat16)]
    scratch = [pltpu.VMEM((total, chunk), jnp.bfloat16)] * 3
    scratch += [pltpu.VMEM((2, 3, chunk, features), jnp.bfloat16), pltpu.SemaphoreType.DMA((2,))]
    if fused:
        operands.append(partial)
        in_specs += any_specs(1)
        out_specs.append(whole_block(partial.shape[-2:], **once))
        out_shape.append(jax.ShapeDtypeStruct(partial.shape[-2:], jnp.float32))
        out_specs.append(whole_block((3, early * chunk, wide), **once))
        out_shape.append(jax.ShapeDtypeStruct((3, early * chunk, wide), jnp.bfloat16))
        scratch.append(pltpu.VMEM((early, 3, chunk, wide), jnp.float32))
        scratch += [pltpu.VMEM((early, 3, chunk, wide), jnp.bfloat16)] * 2 + dma_pair(3 * early)
        scratch += corner_sum_scratch(partial)
    return pl.pallas_call(
        kernel,
        grid=(steps,),
        in_specs=in_specs,
        out_specs=out_specs,
        out_shape=out_shape,
        scratch_shapes=scratch,
        compiler_params=params(3) if fused else params(),
        cost_estimate=pl.CostEstimate(
            flops=12 * total * n_own * features, bytes_accessed=50 * 1024 * 1024, transcendentals=total * n_own
        ),
        name="ffn_weights",
    )(*operands)


def ffn_back(hidden, grad_gate, grad_up, planes, core, blocks, wide=512):
    total, n_own = hidden.shape
    features = planes.shape[2]
    tokens = total // blocks

    def kernel(core_ref, hidden_ref, grad_gate_ref, grad_up_ref, gate_ref, up_ref, down_ref, out_ref):
        out = mm(hidden_ref[...], down_ref[0])
        out_ref[:, 0] = low(out).reshape(blocks, tokens, wide)
        back = mm(grad_gate_ref[...], gate_ref[0]) + mm(grad_up_ref[...], up_ref[0])
        out_ref[:, 1] = low(back).reshape(blocks, tokens, wide)

    def weight_spec(plane):
        return pl.BlockSpec((1, n_own, wide), lambda j, core_ref: (plane, core_ref[0], j))

    act_spec = pl.BlockSpec((total, n_own), lambda j, core_ref: (0, 0), pipeline_mode=pl.Buffered(1))
    return pl.pallas_call(
        kernel,
        grid_spec=pltpu.PrefetchScalarGridSpec(
            num_scalar_prefetch=1,
            grid=(features // wide,),
            in_specs=[act_spec, act_spec, act_spec, weight_spec(0), weight_spec(1), weight_spec(2)],
            out_specs=pl.BlockSpec((blocks, 2, tokens, wide), lambda j, core_ref: (0, 0, 0, j)),
        ),
        out_shape=jax.ShapeDtypeStruct((blocks, 2, tokens, features), jnp.bfloat16),
        compiler_params=params(),
        cost_estimate=pl.CostEstimate(
            flops=6 * total * n_own * features, bytes_accessed=30 * 1024 * 1024, transcendentals=0
        ),
        name="ffn_back",
    )(core, hidden, grad_gate, grad_up, planes, planes, planes)


SPAN = 256


def ctx_peers(n_ctx):
    ctx = lax.axis_index("ctx")
    fsdp = lax.axis_index("fsdp")
    return [((ctx + j) % n_ctx, fsdp) for j in range(1, n_ctx)]


def deal(n_ctx, block, target, landed, sems, own_sem):
    ctx = lax.axis_index("ctx")
    fsdp = lax.axis_index("fsdp")

    @pl.when(target != ctx)
    def _():
        send(block, landed.at[ctx], sems, (target - ctx + n_ctx) % n_ctx, (target, fsdp)).start()

    @pl.when(target == ctx)
    def _():
        pltpu.make_async_copy(block, landed.at[ctx], own_sem).start()


def dealt(n_ctx, block, landed, sems, own_sem):
    ctx = lax.axis_index("ctx")
    pltpu.make_async_copy(block, landed.at[ctx], own_sem).wait()
    for j, peer in enumerate(ctx_peers(n_ctx)):
        copy = send(block, landed.at[(ctx + n_ctx - j - 1) % n_ctx], sems, j + 1, peer)
        copy.wait_send()
        copy.wait_recv()


def turn(values, cosine, sine):
    return values * cosine + pltpu.roll(values, HEAD_DIM // 2, 1) * sine


def attention_forward(n_ctx, rows, w_qkv, cosine, sine, place_column, place_row, heads):
    total, features = rows.shape
    own = heads * HEAD_DIM
    steps = total // SPAN
    length = total // n_ctx
    scale = HEAD_DIM ** (-0.5)

    def kernel(
        rows_ref, w_ref, cosine_ref, sine_ref, column_ref, row_ref,
        query_ref, key_ref, value_ref, out_ref, log_ref, landed, deal_s, deal_r, own_sem,
    ):
        step = pl.program_id(0)

        @pl.when(step == 0)
        def _():
            greet(ctx_peers(n_ctx))

        span = pl.ds(pl.multiple_of(step * SPAN, SPAN), SPAN)
        qkv = mm(rows_ref[...], w_ref[...])
        cosine = cosine_ref[span]
        sine = sine_ref[span]
        for h in range(heads):
            at = slice(h * HEAD_DIM, (h + 1) * HEAD_DIM)
            query_ref[span, at] = low(turn(qkv[:, at], cosine, sine))
            key_ref[span, at] = low(turn(qkv[:, own + h * HEAD_DIM : own + (h + 1) * HEAD_DIM], cosine, sine))
        value_ref[span] = low(qkv[:, 2 * own :])

        @pl.when(step == steps - 1)
        def _():
            @pl.loop(0, steps)
            def _(block):
                here = pl.ds(pl.multiple_of(block * SPAN, SPAN), SPAN)
                for h in range(heads):
                    at = slice(h * HEAD_DIM, (h + 1) * HEAD_DIM)
                    scores = mm(query_ref[here, at], key_ref[:, at], CONTRACT_LAST) * scale
                    scores = jnp.where(column_ref[here] >= row_ref[...], scores, MASKED)
                    highest = jnp.max(scores, axis=-1, keepdims=True)
                    exponent = jnp.exp(scores - highest)
                    sums = jnp.sum(exponent, axis=-1, keepdims=True)
                    out_ref[here, at] = low(mm(low(exponent * (1.0 / sums)), value_ref[:, at]))
                    log_ref[h, here] = highest + jnp.log(sums)
                for r in range(SPAN // length):
                    mine = out_ref.at[pl.ds(pl.multiple_of(block * SPAN + r * length, length), length)]
                    deal(n_ctx, mine, block * (SPAN // length) + r, landed, (deal_s, deal_r), own_sem)

            dealt(n_ctx, out_ref.at[pl.ds(0, length)], landed, (deal_s, deal_r), own_sem)

    act = jax.ShapeDtypeStruct((total, own), jnp.bfloat16)
    return pl.pallas_call(
        kernel,
        grid=(steps,),
        in_specs=[pl.BlockSpec((SPAN, features), lambda r: (r, 0))]
        + [whole_block(a.shape) for a in (w_qkv, cosine, sine, place_column, place_row)],
        out_specs=[whole_block((total, own))] * 4 + [whole_block((heads, total, 1))] + any_specs(1),
        out_shape=[act] * 4
        + [
            jax.ShapeDtypeStruct((heads, total, 1), jnp.float32),
            jax.ShapeDtypeStruct((n_ctx, length, own), jnp.bfloat16),
        ],
        scratch_shapes=dma_pair(n_ctx) + [pltpu.SemaphoreType.DMA],
        compiler_params=params(8),
        name="attention_forward",
    )(rows, w_qkv, cosine, sine, place_column, place_row)


def attention_backward(query, key, value, grad, logs, w_qkv, cosine, sine, place_column, place_row, heads):
    total, own = query.shape
    features = w_qkv.shape[0]
    steps = total // SPAN
    scale = HEAD_DIM ** (-0.5)

    def kernel(
        query_ref, key_ref, value_ref, grad_ref, log_ref, w_ref, cosine_ref, sine_ref, column_ref, row_ref,
        qkv_ref, out_ref, key_sum, value_sum,
    ):
        step = pl.program_id(0)

        @pl.when(step == 0)
        def _():
            for h in range(heads):
                at = slice(h * HEAD_DIM, (h + 1) * HEAD_DIM)
                key_sum[...] = jnp.zeros_like(key_sum)
                value_sum[...] = jnp.zeros_like(value_sum)

                @pl.loop(0, steps)
                def _(block):
                    here = pl.ds(pl.multiple_of(block * SPAN, SPAN), SPAN)
                    queries = query_ref[here, at]
                    grads = grad_ref[here, at]
                    scores = mm(queries, key_ref[:, at], CONTRACT_LAST) * scale
                    scores = jnp.where(column_ref[here] >= row_ref[...], scores, MASKED)
                    probs = jnp.exp(scores - log_ref[h, here])
                    probs_grad = mm(grads, value_ref[:, at], CONTRACT_LAST)
                    centre = jnp.sum(probs * probs_grad, axis=-1, keepdims=True)
                    scores_grad = low(probs * (probs_grad - centre))
                    query_grad = mm(scores_grad, key_ref[:, at]) * scale
                    qkv_ref[here, at] = low(turn(query_grad, cosine_ref[here], -sine_ref[here]))
                    key_sum[...] += mm(scores_grad, queries, CONTRACT_FIRST)
                    value_sum[...] += mm(low(probs), grads, CONTRACT_FIRST)

                qkv_ref[:, own + h * HEAD_DIM : own + (h + 1) * HEAD_DIM] = low(
                    turn(key_sum[...] * scale, cosine_ref[...], -sine_ref[...])
                )
                qkv_ref[:, 2 * own + h * HEAD_DIM : 2 * own + (h + 1) * HEAD_DIM] = low(value_sum[...])

        span = pl.ds(pl.multiple_of(step * SPAN, SPAN), SPAN)
        out_ref[...] = low(mm(qkv_ref[span], w_ref[...], CONTRACT_LAST))

    return pl.pallas_call(
        kernel,
        grid=(steps,),
        in_specs=[
            whole_block(a.shape)
            for a in (query, key, value, grad, logs, w_qkv, cosine, sine, place_column, place_row)
        ],
        out_specs=[whole_block((total, 3 * own)), pl.BlockSpec((SPAN, features), lambda r: (r, 0))],
        out_shape=[
            jax.ShapeDtypeStruct((total, 3 * own), jnp.bfloat16),
            jax.ShapeDtypeStruct((total, features), jnp.bfloat16),
        ],
        scratch_shapes=[pltpu.VMEM((total, HEAD_DIM), jnp.float32)] * 2,
        compiler_params=params(),
        name="attention_backward",
    )(query, key, value, grad, logs, w_qkv, cosine, sine, place_column, place_row)


ROWS = 32


def row_blocks(count, features):
    return pl.BlockSpec((count, ROWS, features), lambda r, *_: (0, r, 0))


def whole_block(shape, **more):
    zeros = (0,) * len(shape)
    return pl.BlockSpec(shape, lambda r, *_: zeros, **more)


def split(values):
    high = low(values)
    return (high, low(values - high.astype(jnp.float32)))


def connect_coefficients(values, dynamic_ref, static_ref, coef_ref, dyn_ref):
    lane = lax.broadcasted_iota(jnp.int32, (values[0].shape[0], 8), 1)
    columns = []
    for i, value in enumerate(values):
        mean = jnp.mean(value, axis=-1, keepdims=True)
        centered = value - mean
        inverse = lax.rsqrt(jnp.mean(centered * centered, axis=-1, keepdims=True) + EPS)
        normed = centered * inverse
        projected = jnp.zeros(lane.shape, jnp.float32)
        for k in range(6):
            part = jnp.sum(normed * dynamic_ref[k : k + 1], axis=-1, keepdims=True)
            projected = jnp.where(lane == k, part, projected)
        coefficient = jnp.tanh(projected) + static_ref[i : i + 1]
        dyn_ref[i] = projected
        coef_ref[i] = jnp.where(lane == 6, mean, jnp.where(lane == 7, inverse, coefficient))
        columns.append(coefficient)
    return columns


def connect_first(streams, dynamic, static):
    number, rows, features = streams.shape

    def kernel(streams_ref, dynamic_ref, static_ref, coef_ref, dyn_ref, low_ref):
        values = [streams_ref[i].astype(jnp.float32) for i in range(number)]
        columns = connect_coefficients(values, dynamic_ref, static_ref, coef_ref, dyn_ref)
        mixed = sum((columns[i][:, 1:2] * values[i] for i in range(number)))
        low_ref[...] = low(normalize(mixed)[0])

    small = jax.ShapeDtypeStruct((number, rows, 8), jnp.float32)
    return pl.pallas_call(
        kernel,
        grid=(rows // ROWS,),
        out_shape=(small, small, jax.ShapeDtypeStruct((rows, features), jnp.bfloat16)),
        in_specs=[row_blocks(number, features), whole_block(dynamic.shape), whole_block(static.shape)],
        out_specs=(
            row_blocks(number, 8),
            row_blocks(number, 8),
            pl.BlockSpec((ROWS, features), lambda r: (r, 0)),
        ),
        compiler_params=params(),
        name="connect_first",
    )(streams, dynamic, static)


def connect_middle(streams, coef, attended, w_mine, w_other, cotangent, dynamic, static, core_fsdp, where, depth):
    number, rows, features = streams.shape
    half = features // 2
    own = attended.shape[2]
    count = len(w_mine)

    def kernel(core_ref, streams_ref, coef_ref, attended_ref, *refs):
        weights, refs = refs[: 2 * count], refs[2 * count :]
        cotangent_ref, dynamic_ref, static_ref = refs[:3]
        first_ref, branch_ref, coef_two_ref, dyn_ref, own_ref, projected = refs[3:]
        step = pl.program_id(0)

        @pl.when(step == 0)
        def _():
            for side in range(2):
                total = 0.0
                for j, (d, offset) in enumerate(where):
                    for q in range(w_mine[j].shape[0] // own):
                        part = attended_ref[(core_ref[1] ^ d) * (depth // own) + offset // own + q]
                        total = total + mm(part, weights[side * count + j][q * own : (q + 1) * own])
                projected[core_ref[0] if side == 0 else 1 - core_ref[0]] = total

        span = pl.ds(pl.multiple_of(step * ROWS, ROWS), ROWS)
        branch = jnp.concatenate([projected[0, span], projected[1, span]], axis=1)
        branch_ref[...] = branch
        inputs = [streams_ref[i].astype(jnp.float32) for i in range(number)]
        outs = []
        for j in range(number):
            out = sum((coef_ref[i][:, 2 + j : 3 + j] * inputs[i] for i in range(number)))
            outs.append(out + coef_ref[j][:, 0:1] * branch)
            first_ref[j] = outs[-1]
        columns = connect_coefficients(outs, dynamic_ref, static_ref, coef_two_ref, dyn_ref)
        mixed = sum((columns[i][:, 1:2] * outs[i] for i in range(number)))
        own_ref[0] = low(normalize(mixed)[0])
        own_ref[1] = low(sum((columns[j][:, 0:1] * cotangent_ref[j].astype(jnp.float32) for j in range(number))))

    small = jax.ShapeDtypeStruct((number, rows, 8), jnp.float32)
    once = dict(pipeline_mode=pl.Buffered(1))
    return pl.pallas_call(
        kernel,
        grid_spec=pltpu.PrefetchScalarGridSpec(
            num_scalar_prefetch=1,
            grid=(rows // ROWS,),
            in_specs=[
                row_blocks(number, features),
                row_blocks(number, 8),
                whole_block(attended.shape, **once),
                *[whole_block(w.shape, **once) for w in w_mine + w_other],
                row_blocks(number, features),
                whole_block(dynamic.shape),
                whole_block(static.shape),
            ],
            out_specs=(
                row_blocks(number, features),
                pl.BlockSpec((ROWS, features), lambda r, *_: (r, 0)),
                row_blocks(number, 8),
                row_blocks(number, 8),
                row_blocks(2, features),
            ),
            scratch_shapes=[pltpu.VMEM((2, rows, half), jnp.float32)],
        ),
        out_shape=(
            jax.ShapeDtypeStruct((number, rows, features), jnp.float32),
            jax.ShapeDtypeStruct((rows, features), jnp.float32),
            small,
            small,
            jax.ShapeDtypeStruct((2, rows, features), jnp.bfloat16),
        ),
        compiler_params=params(),
        name="connect_middle",
    )(core_fsdp, streams, coef, attended, *w_mine, *w_other, cotangent, dynamic, static)


def attention_weights(rows, grads, attended, grad_cols):
    total, features = rows.shape
    parts, _, own = attended.shape
    wide = grads.shape[1]

    def kernel(rows_ref, grads_ref, attended_ref, cols_ref, out_ref):
        out_ref[:, :wide] = low(mm(rows_ref[...], grads_ref[...], CONTRACT_FIRST))
        out_ref[:, wide:] = low(mm(attended_ref[0], cols_ref[...], CONTRACT_FIRST))

    return pl.pallas_call(
        kernel,
        grid=(parts,),
        in_specs=[
            pl.BlockSpec((total, own), lambda k: (0, k)),
            whole_block(grads.shape),
            pl.BlockSpec((1, total, own), lambda k: (k, 0, 0)),
            whole_block(grad_cols.shape),
        ],
        out_specs=pl.BlockSpec((own, wide + own), lambda k: (k, 0)),
        out_shape=jax.ShapeDtypeStruct((features, wide + own), jnp.bfloat16),
        compiler_params=params(),
        cost_estimate=pl.CostEstimate(
            flops=2 * total * features * (wide + own), bytes_accessed=16 * 1024 * 1024, transcendentals=0
        ),
        name="attention_weights",
    )(rows, grads, attended, grad_cols)


def flip(index, bits, count):
    result = index
    bit = 1
    while bit < count:
        if bits & bit:
            result = result + bit - 2 * bit * (index // bit % 2)
        bit *= 2
    return result


def project_back(n_ctx, n_fsdp, grad, w_mine, w_other, where, depth):
    rows, features = grad.shape
    half = features // 2
    count = len(w_mine)
    own = features // n_ctx

    def kernel(grad_ref, *refs):
        weights, refs = refs[: 2 * count], refs[2 * count :]
        landed, cols_ref, outs, deal_s, deal_r, own_sem = refs
        _, core, fsdp, _ = place(n_ctx)
        greet(ctx_peers(n_ctx))
        first = grad_ref[:, pl.ds(pl.multiple_of(core * half, half), half)]
        second = grad_ref[:, pl.ds(pl.multiple_of((1 - core) * half, half), half)]
        for j, (d, offset) in enumerate(where):
            out = low(
                mm(first, weights[j][...], CONTRACT_LAST) + mm(second, weights[count + j][...], CONTRACT_LAST)
            )
            for q in range(w_mine[j].shape[0] // own):
                at = flip(fsdp, d, n_fsdp) * (depth // own) + offset // own + q
                outs[at] = out[:, q * own : (q + 1) * own]
                deal(n_ctx, outs.at[at], at, landed, (deal_s, deal_r), own_sem)
        for index in range(n_ctx):
            cols_ref[index] = grad_ref[:, index * own : (index + 1) * own]
        dealt(n_ctx, outs.at[0], landed, (deal_s, deal_r), own_sem)

    shape = (n_ctx, rows, own)
    return pl.pallas_call(
        kernel,
        in_specs=[pl.BlockSpec(memory_space=pltpu.VMEM)] * (1 + 2 * count),
        out_specs=any_specs(1) + [pl.BlockSpec(memory_space=pltpu.VMEM)],
        out_shape=[jax.ShapeDtypeStruct(shape, grad.dtype)] * 2,
        scratch_shapes=[pltpu.VMEM(shape, grad.dtype)] + dma_pair(n_ctx) + [pltpu.SemaphoreType.DMA],
        compiler_params=params(9),
        name="project_back",
    )(grad, *w_mine, *w_other)


def connect_back(values, coef, dyn, branch, grads, grad_normed, dynamic, means, coef_before=None, offset=0):
    number, rows, features = values.shape
    steps = rows // ROWS
    more = coef_before is not None

    def kernel(*refs):
        values_ref, coef_ref, dyn_ref, branch_ref, grads_ref, normed_ref, dynamic_ref, means_ref = refs[:8]
        refs = refs[8:]
        if more:
            before_ref, refs = refs[0], refs[1:]
        out_ref, dynamic_out, static_out = refs[:3]
        if more:
            forward_ref, grad_low_ref = refs[3:5]
        step = pl.program_id(0)

        @pl.when(step == 0)
        def _():
            dynamic_out[...] = jnp.zeros_like(dynamic_out)
            static_out[...] = jnp.zeros_like(static_out)

        branch = branch_ref[...]
        grads = [grads_ref[j].astype(jnp.float32) for j in range(number)]
        mixed = sum((coef_ref[i][:, 1:2] * values_ref[i].astype(jnp.float32) for i in range(number)))
        normed, inverse = normalize(mixed)
        grad_mixed = normalize_back(normed, inverse, normed_ref[...])
        lane = lax.broadcasted_iota(jnp.int32, (ROWS, 8), 1)
        pre_grads, highs, lows = [], [], []
        for i in range(number):
            value = values_ref[i].astype(jnp.float32)
            columns = [grads[i] * branch, grad_mixed * value] + [grads[j] * value for j in range(number)]
            coef_grad = jnp.zeros((ROWS, 8), jnp.float32)
            for k, column in enumerate(columns):
                coef_grad = jnp.where(lane == k, jnp.sum(column, axis=-1, keepdims=True), coef_grad)
            static_out[i : i + 1] += jnp.sum(coef_grad, axis=0, keepdims=True)
            part = jnp.tanh(dyn_ref[i])
            pre_grads.append(coef_grad * (1.0 - part * part))
            high, rest = split((value - coef_ref[i][:, 6:7]) * coef_ref[i][:, 7:8])
            highs.append(high)
            lows.append(rest)
        pre, pre_rest = split(jnp.concatenate(pre_grads))
        dynamic, dynamic_rest = split(dynamic_ref[...])
        normed_grads = mm(
            jnp.concatenate([pre, pre_rest, pre], axis=1), jnp.concatenate([dynamic, dynamic, dynamic_rest], axis=0)
        )
        highs = jnp.concatenate(highs)
        dynamic_out[...] += (
            mm(pre, highs, CONTRACT_FIRST)
            + mm(pre_rest, highs, CONTRACT_FIRST)
            + mm(pre, jnp.concatenate(lows), CONTRACT_FIRST)
        )
        befores = 0.0
        for i in range(number):
            coef = coef_ref[i]
            mean_grad = jnp.sum(pre_grads[i] * means_ref[...], axis=-1, keepdims=True)
            inner = jnp.sum(pre_grads[i] * dyn_ref[i], axis=-1, keepdims=True) / features
            normed = (values_ref[i].astype(jnp.float32) - coef[:, 6:7]) * coef[:, 7:8]
            out = coef[:, 7:8] * (normed_grads[i * ROWS : (i + 1) * ROWS] - mean_grad - normed * inner)
            out = out + coef[:, 1:2] * grad_mixed
            for j in range(number):
                out = out + coef[:, 2 + j : 3 + j] * grads[j]
            out_ref[i] = out
            if more:
                befores = befores + before_ref[i][:, 0:1] * out
        if more:
            grad_low_ref[...] = low(befores)
            for j in range(number):
                out = coef_ref[j][:, 0:1] * branch
                for i in range(number):
                    out = out + coef_ref[i][:, 2 + j : 3 + j] * values_ref[i].astype(jnp.float32)
                forward_ref[j] = low(out)

    rows_spec = pl.BlockSpec((ROWS, features), lambda r: (r, 0))
    out_shape = [
        jax.ShapeDtypeStruct((number, rows, features), jnp.float32),
        jax.ShapeDtypeStruct((8, features), jnp.float32),
        jax.ShapeDtypeStruct((8, 8), jnp.float32),
    ]
    out_specs = [row_blocks(number, features), whole_block((8, features)), whole_block((8, 8))]
    operands = [values, coef, dyn, branch, grads, grad_normed, dynamic, means]
    in_specs = [
        row_blocks(number, features),
        row_blocks(number, 8),
        row_blocks(number, 8),
        rows_spec,
        row_blocks(number, features),
        pl.BlockSpec((ROWS, features), lambda r: (offset // ROWS + r, 0)),
        whole_block(dynamic.shape),
        whole_block(means.shape),
    ]
    if more:
        operands.append(coef_before)
        in_specs.append(row_blocks(number, 8))
        out_shape.append(jax.ShapeDtypeStruct((number, rows, features), jnp.bfloat16))
        out_specs.append(row_blocks(number, features))
        out_shape.append(jax.ShapeDtypeStruct((rows, features), jnp.bfloat16))
        out_specs.append(rows_spec)
    return pl.pallas_call(
        kernel,
        grid=(steps,),
        in_specs=in_specs,
        out_specs=out_specs,
        out_shape=out_shape,
        compiler_params=params(),
        name="connect_back",
    )(*operands)


def local(n_ctx, n_fsdp, streams, w_attn, w_ffn, hc_dynamic, hc_static, cotangent, pair_order):
    number = streams.shape[1]
    length = streams.shape[2]
    features = streams.shape[3]
    size = HEAD_DIM
    own = features // n_ctx
    heads = own // size
    rows = length * n_ctx
    own_rows = w_attn.shape[0]
    ctx = lax.axis_index("ctx")
    fsdp = lax.axis_index("fsdp")
    core = ctx % 2
    chips = n_ctx // 2
    core_index = jnp.reshape(core, (1,)).astype(jnp.int32)

    def in_order(mine, other, axis):
        return jnp.where(
            core == 0, jnp.concatenate([mine, other], axis=axis), jnp.concatenate([other, mine], axis=axis)
        )


    w_own = lax.dynamic_slice_in_dim(w_attn, ctx * own, own, 2)[:, 0:3].reshape(own_rows, 3 * own)
    w_qkv = gather(w_own, "fsdp")
    half = features // 2
    w_half = lax.dynamic_slice_in_dim(w_attn, core * half, half, 2)[:, 3]
    siblings = [(i, i ^ 1) for i in range(n_ctx)]
    core_fsdp = jnp.stack([core, fsdp]).astype(jnp.int32)

    def exchange(values, most=0):
        return [values] + [
            lax.ppermute(values, "fsdp", [(i, i ^ d) for i in range(n_fsdp)])
            for d in range(1, most + 1 if most else n_fsdp)
        ]

    def swap(blocks):
        return [lax.ppermute(block, "ctx", siblings) for block in blocks]


    positions = block_positions(pair_order, length)
    frequency = THETA ** (-(jnp.arange(size // 2, dtype=jnp.float32) * 2.0) / size)
    angles = positions.astype(jnp.float32)[:, None] * jnp.concatenate([frequency, frequency])[None, :]
    signs = jnp.where(jnp.arange(size) < size // 2, -1.0, 1.0)
    tables = (jnp.cos(angles), jnp.sin(angles) * signs[None, :], positions[:, None], positions[None, :])

    dynamics = jnp.pad(hc_dynamic, ((0, 0), (0, 2), (0, 0)))
    means = jnp.mean(dynamics, axis=-1)
    statics = jnp.pad(hc_static, ((0, 0), (0, 0), (0, 2)))
    coef_one, dyn_one, attn_low = connect_first(streams[0], dynamics[0], statics[0])
    attn_low, w_half = lax.optimization_barrier((attn_low, w_half))
    w_out_mine = exchange(w_half, 2 if n_fsdp == 4 else 0)
    attn_all = line_rows(n_ctx, attn_low).reshape(rows, features)
    w_out_where = [(d, 0) for d in range(len(w_out_mine))]
    attn_all, *w_out_mine = lax.optimization_barrier((attn_all, *w_out_mine))
    w_out_other = swap(w_out_mine)
    if n_fsdp == 4:
        middle = own_rows // 2
        corners = [
            lax.ppermute(w_out_mine[1][:middle], "fsdp", [(i, i ^ 2) for i in range(4)]),
            lax.ppermute(w_out_mine[2][middle:], "fsdp", [(i, i ^ 1) for i in range(4)]),
        ]
        w_out_where += [(3, 0), (3, middle)]
    query, key, value, attended, logs, attended_rows = attention_forward(n_ctx, attn_all, w_qkv, *tables, heads)
    if n_fsdp == 4:
        attended, *corners = lax.optimization_barrier((attended, *corners))
        w_out_mine += corners
        w_out_other += swap(corners)

    first_out, attn_branch, coef_two, dyn_two, ffn_own = connect_middle(
        streams[0], coef_one, attended_rows, w_out_mine, w_out_other, cotangent[0], dynamics[1], statics[1], core_fsdp,
        w_out_where, own_rows,
    )
    ffn_own = ffn_own.reshape(2 * length, features)

    planes = jnp.moveaxis(w_ffn, 1, 0)
    n_own = planes.shape[1] // 2
    blocks = 2 * n_fsdp
    if n_fsdp == 4:
        ffn_all, mirror_rows, *hidden, sums, attended_all = ffn_rows(n_ctx, ffn_own, planes, attended, n_own)
        ffn_all, mirror_rows = (part.reshape(blocks, 2, length, features) for part in (ffn_all, mirror_rows))
        mirror_rows = [mirror_rows]
        weight_parts, sums, weight_early = ffn_weights(
            n_ctx, n_fsdp, sums, ffn_all, mirror_rows, hidden, planes, n_own
        )
    else:
        ffn_mirror = lax.ppermute(ffn_own, "ctx", [(i, n_ctx - 2 - i + 2 * (i % 2)) for i in range(n_ctx)])
        ffn_all = square_core_gather(n_ctx, n_fsdp, ffn_own).reshape(blocks, 2, length, features)
        attended_all = gather(attended, "ctx").reshape(n_ctx, rows, own)
        mirror_mine = exchange(ffn_mirror)
        hidden = ffn_forward(ffn_all, planes, core_index, n_own)
        sums = ffn_back(*hidden, planes, core_index, blocks)
        mirror_rows = [part.reshape(1, 2, length, features) for part in mirror_mine + swap(mirror_mine)]
        sums = square_sum(n_ctx, n_fsdp, sums.reshape(2, n_fsdp, 2 * length, features))
        (weight_parts,) = ffn_weights(n_ctx, n_fsdp, None, ffn_all, mirror_rows, hidden, planes, n_own)
    sides = chips // 2
    lines = [[2 * (sides * side + i) + j for i in range(sides)] for side in range(2) for j in range(2)]
    weight_cols = lax.psum_scatter(weight_parts, "ctx", scatter_dimension=0, axis_index_groups=lines)

    grad_first, dynamic_grad_two, static_grad_two, streams_out, grad_attn = connect_back(
        first_out, coef_two, dyn_two, sums, cotangent[0], sums, dynamics[1], means[1:], coef_one, length
    )
    grad_heads, grad_cols = project_back(n_ctx, n_fsdp, grad_attn, w_out_mine, w_out_other, w_out_where, own_rows)
    grad_heads = grad_heads.reshape(rows, own)
    grad_heads, grad_cols = lax.optimization_barrier((grad_heads, grad_cols))
    grad_cols = lax.all_to_all(grad_cols, "ctx", 0, 0, tiled=True).reshape(rows, own)
    qkv_grad, attn_part = attention_backward(query, key, value, grad_heads, logs, w_qkv, *tables, heads)
    attn_part = attn_part.reshape(n_ctx, length, features)
    if n_fsdp == 4:
        grad_attn_normed, attn_grad = attention_sums(n_ctx, attn_part, attn_all, qkv_grad, attended_all, grad_cols)
    else:
        grad_attn_normed = line_sum(n_ctx, attn_part)
        attn_grad = scatter(attention_weights(attn_all, qkv_grad, attended_all, grad_cols), "fsdp").astype(jnp.float32)
    grad_attn_normed, weight_cols = lax.optimization_barrier((grad_attn_normed, weight_cols))
    if n_fsdp == 4:
        weight_cols = jnp.concatenate([weight_early, weight_cols], axis=1)
    mine = lax.dynamic_slice_in_dim(weight_cols, core * own, own, 2)
    other = lax.dynamic_slice_in_dim(weight_cols, (1 - core) * own, own, 2)
    other = lax.ppermute(other, "ctx", siblings)
    ffn_grad = jnp.moveaxis(in_order(mine, other, 1), 0, 1).astype(jnp.float32)
    grad_inputs, dynamic_grad_one, static_grad_one = connect_back(
        streams[0], coef_one, dyn_one, attn_branch, grad_first, grad_attn_normed, dynamics[0], means[:1]
    )
    static_grads = jnp.concatenate([static_grad_one[:number, :6].reshape(1, -1), static_grad_two[:number, :6].reshape(1, -1)])
    small = jnp.concatenate(
        [
            dynamic_grad_one[:6],
            dynamic_grad_two[:6],
            jnp.pad(static_grads, ((0, 2), (0, features - 6 * number))),
        ]
    )
    small = sum_everywhere(n_ctx, n_fsdp, small.reshape(n_ctx, 8, -1))
    small = small.reshape(16, features)
    attn_grad = attn_grad.reshape(own_rows, 4, own)
    dynamic_total = small[:12].reshape(2, 6, features)
    static_total = small[12:14, : 6 * number].reshape(2, number, 6)
    return (streams_out[None], grad_inputs[None], attn_grad, ffn_grad, dynamic_total, static_total)


def solution(mesh):
    return jax.shard_map(
        functools.partial(local, mesh.shape["ctx"], mesh.shape["fsdp"]),
        mesh=mesh,
        in_specs=(
            P("fsdp", None, "ctx", None),
            P("fsdp", None, None),
            P("fsdp", None, None),
            P(),
            P(),
            P("fsdp", None, "ctx", None),
            P(),
        ),
        out_specs=(
            P("fsdp", None, "ctx", None),
            P("fsdp", None, "ctx", None),
            P("fsdp", None, "ctx"),
            P("fsdp", None, "ctx"),
            P(),
            P(),
        ),
        check_vma=False,
    )
```

```python
import functools

import jax
import jax.numpy as jnp
from jax import lax
from jax.experimental import pallas as pl
from jax.experimental.pallas import tpu as pltpu
from jax.sharding import PartitionSpec as P

HEADS = 16
HEAD_DIM = 128


EPS = 1e-05
THETA = 10000.0
HIGH = lax.Precision.HIGHEST
MASKED = -1e30
CONTRACT_LAST = (((1,), (1,)), ((), ()))
CONTRACT_FIRST = (((0,), (0,)), ((), ()))


def normalize(values):
    centered = values - jnp.mean(values, axis=-1, keepdims=True)
    inverse = lax.rsqrt(jnp.mean(centered * centered, axis=-1, keepdims=True) + EPS)
    return (centered * inverse, inverse)


def normalize_back(normed, inverse, gradient):
    inner = jnp.mean(gradient * normed, axis=-1, keepdims=True)
    return inverse * (gradient - jnp.mean(gradient, axis=-1, keepdims=True) - normed * inner)


def block_positions(pair_order, length):
    half_size = length // 2
    offsets = jnp.arange(half_size, dtype=jnp.int32)
    mirror = 2 * pair_order.shape[0] - 1 - pair_order
    first_half = pair_order[:, None] * half_size + offsets[None, :]
    second_half = mirror[:, None] * half_size + offsets[None, :]
    return jnp.concatenate([first_half, second_half], axis=1).reshape(-1)


def low(values):
    return values.astype(jnp.bfloat16)


def mm(a, b, dims=None):
    if dims is None:
        return jnp.dot(a, b, preferred_element_type=jnp.float32)
    return lax.dot_general(a, b, dims, preferred_element_type=jnp.float32)


def gather(values, axis, dim=0):
    return lax.all_gather(values, axis, axis=dim, tiled=True)


def scatter(values, axis, dim=0):
    return lax.psum_scatter(values, axis, scatter_dimension=dim, tiled=True)


MESH = pl.DeviceIdType.MESH
VMEM_LIMIT = 60 * 1024 * 1024


def place(n_ctx):
    ctx = lax.axis_index("ctx")
    return (ctx // 2, ctx % 2, lax.axis_index("fsdp"), n_ctx // 2)


def greet(peers):
    barrier = pltpu.get_barrier_semaphore()
    for peer in peers:
        pl.semaphore_signal(barrier, inc=1, device_id=peer, device_id_type=MESH)
    pl.semaphore_wait(barrier, len(peers))


def send(source, target, sems, index, peer):
    return pltpu.make_async_remote_copy(
        src_ref=source,
        dst_ref=target,
        send_sem=sems[0].at[index],
        recv_sem=sems[1].at[index],
        device_id=peer,
        device_id_type=MESH,
    )


def fsdp_neighbours(fsdp):
    first = fsdp + 1 - 2 * (fsdp % 2)
    second = (fsdp + 2) % 4
    return (first, second, (first + 2) % 4)


def fsdp_peers(n_fsdp, ctx, fsdp):
    if n_fsdp == 4:
        first, second, _ = fsdp_neighbours(fsdp)
        return [(ctx, first), (ctx, second)]
    return [(ctx, (fsdp + j) % n_fsdp) for j in range(1, n_fsdp)]


def line_peers(chip, core, fsdp, length):
    return [
        (chip * 2 + 1 - core, fsdp),
        ((chip + 1) % length * 2 + core, fsdp),
        ((chip + length - 1) % length * 2 + core, fsdp),
    ]


def line_gather(own_ref, all_ref, sems, where):
    chip, core, fsdp, length = where
    right_sems, left_sems, core_sems = sems
    sibling = (chip * 2 + 1 - core, fsdp)
    right = ((chip + 1) % length * 2 + core, fsdp)
    left = ((chip + length - 1) % length * 2 + core, fsdp)

    def block(index):
        return all_ref.at[(index + length) % length * 2 + core]

    def pass_on(index, source):
        return send(source, block(index), core_sems, (index + length) % length, sibling)

    pass_on(chip, own_ref).start()
    for step in range(length - 1):
        for sign, peer, way in ((-1, right, right_sems), (1, left, left_sems)):
            at = chip + sign * step
            held = (at >= 0) & (at < length)
            if step > 0:

                @pl.when(held)
                def _():
                    send(block(at), block(at), way, step - 1, peer).wait_recv()
                    pass_on(at, block(at)).start()

            more = (chip < length - 1) if sign < 0 else (chip > 0)

            @pl.when(held & more)
            def _():
                send(own_ref if step == 0 else block(at), block(at), way, step, peer).start()

        yield
    last = length - 1
    for sign, peer, way in ((-1, right, right_sems), (1, left, left_sems)):
        at = chip + sign * last

        @pl.when((at >= 0) & (at < length))
        def _():
            send(block(at), block(at), way, last - 1, peer).wait_recv()
            pass_on(at, block(at)).start()

    yield
    for step in range(length - 1):
        for sign, peer, way in ((-1, right, right_sems), (1, left, left_sems)):
            at = chip + sign * step
            more = (chip < length - 1) if sign < 0 else (chip > 0)

            @pl.when((at >= 0) & (at < length) & more)
            def _():
                send(block(at), block(at), way, step, peer).wait_send()

    for index in range(length):
        pass_on(index, block(index)).wait_send()
        other = all_ref.at[index * 2 + 1 - core]
        send(other, other, core_sems, index, sibling).wait_recv()


def square_gather(own_ref, all_ref, sems, ctx, fsdp, n_fsdp, passed=None):
    if n_fsdp != 4:
        copies = [
            send(own_ref, all_ref.at[fsdp], sems, j - 1, (ctx, (fsdp + j) % n_fsdp)) for j in range(1, n_fsdp)
        ]
        for copy in copies:
            copy.start()
        yield
        for j, copy in enumerate(copies):
            copy.wait()
            if passed:
                passed(all_ref.at[(fsdp + n_fsdp - j - 1) % n_fsdp], (fsdp + n_fsdp - j - 1) % n_fsdp, None, j)
        return
    first, second, corner = fsdp_neighbours(fsdp)
    half = own_ref.shape[0] // 2
    top, low_half = pl.ds(0, half), pl.ds(half, half)
    to_first, to_second = (ctx, first), (ctx, second)

    def copy(index, owner, part, peer, source=None):
        source = all_ref.at[owner, part] if source is None else source
        return send(source, all_ref.at[owner, part], sems, index, peer)

    starts = [
        copy(0, fsdp, top, to_first, own_ref.at[top]),
        copy(1, fsdp, low_half, to_second, own_ref.at[low_half]),
        copy(2, fsdp, low_half, to_first, own_ref.at[low_half]),
        copy(3, fsdp, top, to_second, own_ref.at[top]),
        copy(4, first, top, to_second),
        copy(5, second, low_half, to_first),
    ]
    arrivals = [
        (0, first, top),
        (1, second, low_half),
        (2, first, low_half),
        (3, second, top),
        (4, corner, top),
        (5, corner, low_half),
    ]
    for each in starts[:4]:
        each.start()
    yield
    for index, owner, part in arrivals:
        copy(index, owner, part, to_first).wait_recv()
        if index < 2:
            starts[4 + index].start()
        if passed:
            passed(all_ref.at[owner, part], owner, part, index)
        yield
    for each in starts:
        each.wait_send()


def run_all(*parts):
    parts = list(parts)
    while parts:
        for part in list(parts):
            try:
                next(part)
            except StopIteration:
                parts.remove(part)


def dma_pair(count):
    return [pltpu.SemaphoreType.DMA((count,)), pltpu.SemaphoreType.DMA((count,))]


def any_specs(count):
    return [pl.BlockSpec(memory_space=pl.ANY)] * count


def params(collective_id=None, **more):
    if collective_id is not None:
        more.update(collective_id=collective_id, has_side_effects=True)
    return pltpu.CompilerParams(vmem_limit_bytes=VMEM_LIMIT, **more)


def passing(own_ref, all_ref, sems, core, fsdp, sibling):
    handed = [send(own_ref, all_ref.at[core, fsdp], sems, 0, sibling)]
    handed[0].start()
    arriving = [send(own_ref, all_ref.at[1 - core, fsdp], sems, 0, sibling)]

    def passed(source, owner, part, index):
        for side, copies in ((core, handed), (1 - core, arriving)):
            target = all_ref.at[side, owner] if part is None else all_ref.at[side, owner, part]
            copies.append(send(source, target, sems, index + 1, sibling))
        handed[-1].start()

    def finish():
        for out, back in zip(handed, arriving):
            out.wait_send()
            back.wait_recv()

    return (passed, finish)


def line_rows(n_ctx, rows):
    def kernel(rows_ref, all_rows, right_s, right_r, left_s, left_r, core_s, core_r, own):
        where = place(n_ctx)
        chip, core, fsdp, length = where
        greet(line_peers(*where))
        mine = pltpu.make_async_copy(rows_ref, all_rows.at[chip * 2 + core], own)
        mine.start()
        run_all(line_gather(rows_ref, all_rows, ((right_s, right_r), (left_s, left_r), (core_s, core_r)), where))
        mine.wait()

    length = n_ctx // 2
    return pl.pallas_call(
        kernel,
        out_shape=jax.ShapeDtypeStruct((n_ctx,) + rows.shape, rows.dtype),
        in_specs=any_specs(1),
        out_specs=pl.BlockSpec(memory_space=pl.ANY),
        scratch_shapes=dma_pair(length) + dma_pair(length) + dma_pair(length) + [pltpu.SemaphoreType.DMA],
        compiler_params=params(0),
        name="line_rows",
    )(rows)


def square_core_gather(n_ctx, n_fsdp, rows):
    def kernel(rows_ref, all_ref, sq_s, sq_r, core_s, core_r, own):
        chip, core, fsdp, _ = place(n_ctx)
        ctx = chip * 2 + core
        sibling = (chip * 2 + 1 - core, fsdp)
        greet([sibling] + fsdp_peers(n_fsdp, ctx, fsdp))
        mine = pltpu.make_async_copy(rows_ref, all_ref.at[core, fsdp], own)
        mine.start()
        passed, finish = passing(rows_ref, all_ref, (core_s, core_r), core, fsdp, sibling)
        run_all(square_gather(rows_ref, all_ref.at[core], (sq_s, sq_r), ctx, fsdp, n_fsdp, passed))
        finish()
        mine.wait()

    return pl.pallas_call(
        kernel,
        out_shape=jax.ShapeDtypeStruct((2, n_fsdp) + rows.shape, rows.dtype),
        in_specs=any_specs(1),
        out_specs=pl.BlockSpec(memory_space=pl.ANY),
        scratch_shapes=dma_pair(max(6, n_fsdp)) + dma_pair(max(7, n_fsdp)) + [pltpu.SemaphoreType.DMA],
        compiler_params=params(1),
        name="square_core_gather",
    )(rows)


def add_into(target, *sources, chunk=64):
    @pl.loop(0, target.shape[0] // chunk)
    def _(step):
        rows = pl.ds(pl.multiple_of(step * chunk, chunk), chunk)
        total = target[rows].astype(jnp.float32)
        for source in sources:
            total = total + source[rows].astype(jnp.float32)
        target[rows] = total.astype(target.dtype)


def square_sum_stages(n_ctx, n_fsdp, partial_ref, out_ref, held, core_in, square_in, load, core_sems, sems):
    rows = partial_ref.shape[-2]
    half = rows // 2
    chip, core, fsdp, _ = place(n_ctx)
    ctx = chip * 2 + core
    sibling = (chip * 2 + 1 - core, fsdp)
    if n_fsdp == 4:
        first, second, corner = fsdp_neighbours(fsdp)
        order = [corner, first, second, fsdp]
    else:
        order = [(fsdp + j) % n_fsdp for j in range(1, n_fsdp + 1)]
    mine = [
        pltpu.make_async_copy(partial_ref.at[core, owner], held.at[owner], load.at[j])
        for j, owner in enumerate(order)
    ]
    others = [
        send(partial_ref.at[1 - core, owner], core_in.at[owner], core_sems, j, sibling)
        for j, owner in enumerate(order)
    ]

    def ready(j):
        mine[j].wait()
        others[j].wait_recv()
        add_into(held.at[order[j]], core_in.at[order[j]])

    def total(parts, sources):
        @pl.loop(0, parts[1] // 64)
        def _(step):
            at = pl.ds(pl.multiple_of(parts[0] + step * 64, 64), 64)
            from_at = pl.ds(pl.multiple_of(step * 64, 64), 64)
            value = held[fsdp, at].astype(jnp.float32)
            for j in sources:
                value = value + square_in[j, from_at].astype(jnp.float32)
            out_ref[at] = value

    def begin():
        greet([sibling] + fsdp_peers(n_fsdp, ctx, fsdp))
        for j in range(n_fsdp):
            others[j].start()
            mine[j].start()

    if n_fsdp != 4:
        copies = [
            send(held.at[order[j]], square_in.at[j], sems, j, (ctx, order[j])) for j in range(n_fsdp - 1)
        ]

        def spread():
            for j in range(n_fsdp):
                ready(j)
                if j < n_fsdp - 1:
                    copies[j].start()

        def finish():
            for copy in copies:
                copy.wait()
            total((0, rows), range(n_fsdp - 1))
            for each in others:
                each.wait_send()

        return [begin, spread, finish]

    top, low_half = pl.ds(0, half), pl.ds(half, half)
    to_first, to_second = (ctx, first), (ctx, second)

    def copy(index, owner, part, peer):
        return send(held.at[owner, part], square_in.at[index], sems, index, peer)

    copies = [
        copy(0, corner, top, to_first),
        copy(1, corner, low_half, to_second),
        copy(2, first, top, to_first),
        copy(3, second, low_half, to_second),
        copy(4, second, top, to_second),
        copy(5, first, low_half, to_first),
    ]

    def spread():
        ready(0)
        copies[0].start()
        copies[1].start()
        ready(1)
        copies[2].start()
        ready(2)
        copies[3].start()
        ready(3)

    def pass_on():
        copies[0].wait_recv()
        add_into(held.at[second, top], square_in.at[0])
        copies[4].start()
        copies[1].wait_recv()
        add_into(held.at[first, low_half], square_in.at[1])
        copies[5].start()

    def finish():
        for j in range(2, 6):
            copies[j].wait_recv()
        total((0, half), (2, 4))
        total((half, half), (3, 5))
        for each in copies:
            each.wait_send()
        for each in others:
            each.wait_send()

    return [begin, spread, pass_on, finish]


def corner_sum_stages(n_ctx, partial_ref, out_ref, held, square_in, load, sems):
    half = partial_ref.shape[1] // 2
    chip, core, fsdp, _ = place(n_ctx)
    ctx = chip * 2 + core
    first, second, corner = fsdp_neighbours(fsdp)
    top, low_half = pl.ds(0, half), pl.ds(half, half)
    to_first, to_second = (ctx, first), (ctx, second)

    def copy(index, source, peer):
        return send(source, square_in.at[index], sems, index, peer)

    copies = [
        copy(0, partial_ref.at[corner, top], to_first),
        copy(1, partial_ref.at[corner, low_half], to_second),
        copy(2, partial_ref.at[first, top], to_first),
        copy(3, partial_ref.at[second, low_half], to_second),
        copy(4, held.at[0], to_second),
        copy(5, held.at[1], to_first),
    ]
    mine = [
        pltpu.make_async_copy(partial_ref.at[second, top], held.at[0], load.at[0]),
        pltpu.make_async_copy(partial_ref.at[first, low_half], held.at[1], load.at[1]),
        pltpu.make_async_copy(partial_ref.at[fsdp, top], held.at[2], load.at[2]),
        pltpu.make_async_copy(partial_ref.at[fsdp, low_half], held.at[3], load.at[3]),
    ]

    starts = [
        [copies[0].start, copies[1].start],
        [copies[2].start, mine[1].start],
        [copies[3].start, mine[0].start],
        [mine[2].start, mine[3].start],
    ]

    def pass_on():
        for index in range(2):
            mine[index].wait()
            copies[index].wait_recv()
            add_into(held.at[index], square_in.at[index])
            copies[4 + index].start()

    def finish():
        for part, sources in ((0, (2, 4)), (1, (3, 5))):
            mine[2 + part].wait()
            for j in sources:
                copies[j].wait_recv()

            @pl.loop(0, half // 64)
            def _(step):
                at = pl.ds(pl.multiple_of(step * 64, 64), 64)
                value = held[2 + part, at].astype(jnp.float32)
                for j in sources:
                    value = value + square_in[j, at].astype(jnp.float32)
                out_ref[pl.ds(pl.multiple_of(part * half + step * 64, 64), 64)] = value

        for each in copies:
            each.wait_send()

    return [starts, pass_on, finish]


def corner_sum_scratch(partial):
    _, rows, columns = partial.shape
    return [
        pltpu.VMEM((4, rows // 2, columns), partial.dtype),
        pltpu.VMEM((6, rows // 2, columns), partial.dtype),
        pltpu.SemaphoreType.DMA((4,)),
    ] + dma_pair(6)


def square_sum_scratch(n_fsdp, partial):
    rows, columns = partial.shape[-2:]
    pieces = (6, rows // 2, columns) if n_fsdp == 4 else (n_fsdp - 1, rows, columns)
    return (
        [
            pltpu.VMEM((n_fsdp, rows, columns), partial.dtype),
            pltpu.VMEM((n_fsdp, rows, columns), partial.dtype),
            pltpu.VMEM(pieces, partial.dtype),
            pltpu.SemaphoreType.DMA((n_fsdp,)),
        ]
        + dma_pair(n_fsdp)
        + dma_pair(max(6, n_fsdp))
    )


def square_sum(n_ctx, n_fsdp, partial):
    def kernel(partial_ref, out_ref, held, core_in, square_in, load, core_s, core_r, sq_s, sq_r):
        for stage in square_sum_stages(
            n_ctx, n_fsdp, partial_ref, out_ref, held, core_in, square_in, load, (core_s, core_r), (sq_s, sq_r)
        ):
            stage()

    return pl.pallas_call(
        kernel,
        out_shape=jax.ShapeDtypeStruct(partial.shape[-2:], jnp.float32),
        in_specs=any_specs(1),
        out_specs=pl.BlockSpec(memory_space=pltpu.VMEM),
        scratch_shapes=square_sum_scratch(n_fsdp, partial),
        compiler_params=params(1),
        name="square_sum",
    )(partial)


def line_sum_steps(n_ctx, partial_ref, out_ref, held, core_in, right_in, left_in, load, core_sems, right_sems, left_sems):
    rows = partial_ref.shape[1]
    where = place(n_ctx)
    chip, core, fsdp, length = where
    sibling, right, left = line_peers(*where)
    order = [(chip + length - 1 - j) % length for j in range(length)]
    mine, others = [], []
    for j, owner in enumerate(order):
        mine.append(pltpu.make_async_copy(partial_ref.at[owner * 2 + core], held.at[owner], load.at[j]))
        others.append(send(partial_ref.at[owner * 2 + 1 - core], core_in.at[owner], core_sems, j, sibling))
        others[-1].start()
        mine[-1].start()
    yield
    for j, owner in enumerate(order):
        mine[j].wait()
        others[j].wait_recv()
        add_into(held.at[owner], core_in.at[owner])
    ways = ((1, right, right_in, right_sems), (-1, left, left_in, left_sems))
    for step in range(length - 1):
        for sign, peer, arrived, sems in ways:
            block = chip + sign * (length - 1 - step)
            inside = (block >= 0) & (block < length)
            came = (chip >= 1) if sign > 0 else (chip < length - 1)
            if step > 0:

                @pl.when(inside & came)
                def _():
                    send(held.at[block], arrived.at[step - 1], sems, step - 1, peer).wait_recv()
                    add_into(held.at[block], arrived.at[step - 1])

            @pl.when(inside)
            def _():
                send(held.at[block], arrived.at[step], sems, step, peer).start()

        yield
    last = length - 2
    for sign, peer, arrived, sems in ways:
        came = (chip >= 1) if sign > 0 else (chip < length - 1)

        @pl.when(came)
        def _():
            send(held.at[chip], arrived.at[last], sems, last, peer).wait_recv()
            add_into(held.at[chip], arrived.at[last])

    @pl.loop(0, rows // 64)
    def _(step):
        at = pl.ds(pl.multiple_of(step * 64, 64), 64)
        out_ref[at] = held[chip, at].astype(jnp.float32)

    for step in range(length - 1):
        for sign, peer, arrived, sems in ways:
            block = chip + sign * (length - 1 - step)

            @pl.when((block >= 0) & (block < length))
            def _():
                send(held.at[block], arrived.at[step], sems, step, peer).wait_send()

    for each in others:
        each.wait_send()


def line_sum_scratch(n_ctx, partial):
    rows, columns = partial.shape[-2:]
    length = n_ctx // 2
    return [
        pltpu.VMEM((length, rows, columns), partial.dtype),
        pltpu.VMEM((length, rows, columns), partial.dtype),
        pltpu.VMEM((length - 1, rows, columns), partial.dtype),
        pltpu.VMEM((length - 1, rows, columns), partial.dtype),
        pltpu.SemaphoreType.DMA((length,)),
    ] + dma_pair(length) * 3


def line_sum(n_ctx, partial):
    def kernel(partial_ref, out_ref, held, core_in, right_in, left_in, load, core_s, core_r, right_s, right_r, left_s, left_r):
        greet(line_peers(*place(n_ctx)))
        run_all(
            line_sum_steps(
                n_ctx, partial_ref, out_ref, held, core_in, right_in, left_in, load,
                (core_s, core_r), (right_s, right_r), (left_s, left_r),
            )
        )

    return pl.pallas_call(
        kernel,
        out_shape=jax.ShapeDtypeStruct(partial.shape[-2:], jnp.float32),
        in_specs=any_specs(1),
        out_specs=pl.BlockSpec(memory_space=pltpu.VMEM),
        scratch_shapes=line_sum_scratch(n_ctx, partial),
        compiler_params=params(5),
        name="line_sum",
    )(partial)


def attention_sums(n_ctx, partial, rows, grads, attended, grad_cols):
    total, features = rows.shape
    parts, _, own = attended.shape
    wide = grads.shape[1]
    depth = features // 4
    weight_shape = jax.ShapeDtypeStruct((4, depth, wide + own), jnp.bfloat16)
    inputs = (rows, grads, attended, grad_cols)

    def kernel(partial_ref, *refs):
        inputs_refs, refs = refs[:4], refs[4:]
        out_ref, weight_ref, rows_v, grads_v, attended_v, cols_v, weights, in_sem, *refs = refs
        line_refs, refs = refs[:5], refs[5:]
        core_s, core_r, right_s, right_r, left_s, left_r, *refs = refs
        held, square_in, load, sq_s, sq_r = refs
        where = place(n_ctx)
        chip, core, fsdp, _ = where
        loads = [
            pltpu.make_async_copy(a, b, in_sem.at[j])
            for j, (a, b) in enumerate(zip(inputs_refs, (rows_v, grads_v, attended_v, cols_v)))
        ]
        for each in loads:
            each.start()
        greet(line_peers(*where) + fsdp_peers(4, chip * 2 + core, fsdp))
        line = line_sum_steps(
            n_ctx, partial_ref, out_ref, *line_refs, (core_s, core_r), (right_s, right_r), (left_s, left_r)
        )
        next(line)
        starts, pass_on, finish = corner_sum_stages(n_ctx, weights, weight_ref, held, square_in, load, (sq_s, sq_r))
        for each in loads:
            each.wait()
        first, second, corner = fsdp_neighbours(fsdp)
        for number, owner in enumerate((corner, first, second, fsdp)):
            at = pl.ds(pl.multiple_of(owner * depth, depth), depth)
            weights[owner, :, :wide] = low(mm(rows_v[:, at], grads_v[...], CONTRACT_FIRST))
            for q in range(depth // own):
                weights[owner, q * own : (q + 1) * own, wide:] = low(
                    mm(attended_v[owner * (depth // own) + q], cols_v[...], CONTRACT_FIRST)
                )
            for start in starts[number]:
                start()
            if number < 2:
                next(line)
        pass_on()
        run_all(line)
        finish()

    return pl.pallas_call(
        kernel,
        out_shape=[
            jax.ShapeDtypeStruct(partial.shape[-2:], jnp.float32),
            jax.ShapeDtypeStruct(weight_shape.shape[1:], jnp.float32),
        ],
        in_specs=any_specs(5),
        out_specs=[pl.BlockSpec(memory_space=pltpu.VMEM)] * 2,
        scratch_shapes=[pltpu.VMEM(a.shape, a.dtype) for a in inputs]
        + [pltpu.VMEM(weight_shape.shape, weight_shape.dtype), pltpu.SemaphoreType.DMA((4,))]
        + line_sum_scratch(n_ctx, partial)
        + corner_sum_scratch(weight_shape),
        compiler_params=params(4),
        cost_estimate=pl.CostEstimate(
            flops=2 * total * features * (wide + own), bytes_accessed=16 * 1024 * 1024, transcendentals=0
        ),
        name="attention_sums",
    )(partial, *inputs)


def sum_everywhere(n_ctx, n_fsdp, values):
    block = values.shape[1:]

    def kernel(values_ref, out_ref, along_ctx, along_fsdp, result, ctx_s, ctx_r, fsdp_s, fsdp_r, back_s, back_r):
        ctx = lax.axis_index("ctx")
        fsdp = lax.axis_index("fsdp")
        ctx_peers = [((ctx + j) % n_ctx, fsdp) for j in range(1, n_ctx)]
        fsdp_peers = [(ctx, (fsdp + j) % n_fsdp) for j in range(1, n_fsdp)]
        greet(ctx_peers + fsdp_peers)

        def exchange(copies):
            for copy in copies:
                copy.start()
            for copy in copies:
                copy.wait()

        def total(slots, count):
            value = slots[0]
            for j in range(1, count):
                value = value + slots[j]
            return value

        along_ctx[ctx] = values_ref[ctx]
        exchange(
            [
                send(values_ref.at[peer[0]], along_ctx.at[ctx], (ctx_s, ctx_r), j, peer)
                for j, peer in enumerate(ctx_peers)
            ]
        )
        along_fsdp[fsdp] = total(along_ctx, n_ctx)
        exchange(
            [
                send(along_fsdp.at[fsdp], along_fsdp.at[fsdp], (fsdp_s, fsdp_r), j, peer)
                for j, peer in enumerate(fsdp_peers)
            ]
        )
        result[ctx] = total(along_fsdp, n_fsdp)
        exchange(
            [send(result.at[ctx], result.at[ctx], (back_s, back_r), j, peer) for j, peer in enumerate(ctx_peers)]
        )
        out_ref[...] = result[...]

    return pl.pallas_call(
        kernel,
        out_shape=jax.ShapeDtypeStruct(values.shape, values.dtype),
        in_specs=[pl.BlockSpec(memory_space=pltpu.VMEM)],
        out_specs=pl.BlockSpec(memory_space=pltpu.VMEM),
        scratch_shapes=[
            pltpu.VMEM((n_ctx,) + block, values.dtype),
            pltpu.VMEM((n_fsdp,) + block, values.dtype),
            pltpu.VMEM((n_ctx,) + block, values.dtype),
        ]
        + dma_pair(n_ctx)
        + dma_pair(n_fsdp)
        + dma_pair(n_ctx),
        compiler_params=params(2),
        name="sum_everywhere",
    )(values)


def hidden_units(here, back, gate_ref, up_ref, down_ref):
    gate = mm(here, gate_ref[0], CONTRACT_LAST)
    up = mm(here, up_ref[0], CONTRACT_LAST)
    grad_hidden = mm(back, down_ref[0], CONTRACT_LAST)
    sigmoid = jax.nn.sigmoid(gate)
    activated = gate * sigmoid
    return (
        low(activated * up),
        low(grad_hidden * up * sigmoid * (1.0 + gate * (1.0 - sigmoid))),
        low(grad_hidden * activated),
    )


def ffn_forward(rows, planes, core, n_own, chunk=256):
    blocks, _, tokens, features = rows.shape
    total = blocks * tokens
    steps = n_own // chunk
    group = max(1, 256 // tokens)

    def kernel(core_ref, rows_ref, gate_ref, up_ref, down_ref, *outs):
        for at in range(0, blocks, group):
            here = rows_ref[at : at + group, 0].reshape(group * tokens, features)
            back = rows_ref[at : at + group, 1].reshape(group * tokens, features)
            span = pl.ds(at * tokens, group * tokens)
            for out, value in zip(outs, hidden_units(here, back, gate_ref, up_ref, down_ref)):
                out[span] = value

    def weight_spec(plane):
        return pl.BlockSpec((1, chunk, features), lambda j, core_ref: (plane, core_ref[0] * steps + j, 0))

    act = jax.ShapeDtypeStruct((total, n_own), jnp.bfloat16)
    act_spec = pl.BlockSpec((total, chunk), lambda j, core_ref: (0, j))
    return pl.pallas_call(
        kernel,
        grid_spec=pltpu.PrefetchScalarGridSpec(
            num_scalar_prefetch=1,
            grid=(steps,),
            in_specs=[
                pl.BlockSpec(rows.shape, lambda j, core_ref: (0, 0, 0, 0), pipeline_mode=pl.Buffered(1)),
                weight_spec(0),
                weight_spec(1),
                weight_spec(2),
            ],
            out_specs=[act_spec, act_spec, act_spec],
        ),
        out_shape=[act, act, act],
        compiler_params=params(),
        cost_estimate=pl.CostEstimate(
            flops=6 * total * n_own * features, bytes_accessed=30 * 1024 * 1024, transcendentals=total * n_own
        ),
        name="ffn_forward",
    )(core, rows, planes, planes, planes)


def mirror_gather(all_ref, arrivals, sems, pass_sems, ctx, core, fsdp, sibling):
    first, second, corner = fsdp_neighbours(fsdp)
    half = all_ref.shape[2] // 2
    parts = [pl.ds(0, half), pl.ds(half, half)]
    to_first, to_second = (ctx, first), (ctx, second)

    def copy(index, owner, part, peer):
        place_ref = all_ref.at[core, owner, parts[part]]
        return send(place_ref, place_ref, sems, index, peer)

    copies = [
        copy(0, fsdp, 0, to_first),
        copy(1, fsdp, 0, to_second),
        copy(2, fsdp, 1, to_first),
        copy(3, fsdp, 1, to_second),
        copy(4, first, 0, to_second),
        copy(5, second, 1, to_first),
    ]
    passes = [(fsdp, 0), (fsdp, 1), (first, 0), (second, 0), (first, 1), (second, 1), (corner, 0), (corner, 1)]

    def passing_copy(number, side):
        owner, part = passes[number]
        place_ref = all_ref.at[side, owner, parts[part]]
        return send(place_ref, place_ref, pass_sems, number, sibling)

    for part in range(2):
        arrivals[part].wait_recv()
        copies[2 * part].start()
        copies[2 * part + 1].start()
        passing_copy(part, core).start()
        yield
    for index, number, then in ((0, 2, 4), (1, 3, None), (2, 4, None), (3, 5, 5), (4, 6, None), (5, 7, None)):
        owner, part = passes[number]
        copy(index, owner, part, to_first).wait_recv()
        if then is not None:
            copies[then].start()
        passing_copy(number, core).start()
        yield
    for each in copies:
        each.wait_send()
    for number in range(8):
        passing_copy(number, core).wait_send()
        passing_copy(number, 1 - core).wait_recv()


def ffn_rows(n_ctx, own, planes, attended, n_own, chunk=256, wide=512):
    n_fsdp = 4
    size, features = own.shape
    tokens = size // 2
    total = 2 * n_fsdp * tokens

    def kernel(
        own_ref, planes_ref, attended_ref, all_ref, mirror_ref, hidden_a, hidden_b, hidden_c, partial_ref, heads_ref,
        rows, weights, hidden, partial, core_in, load, sq_s, sq_r, core_s, core_r, far_s, far_r, mi_s, mi_r, mc_s, mc_r, sum_s, sum_r, out_sem,
        ri_s, ri_r, le_s, le_r, lc_s, lc_r, heads_sem,
    ):
        chip, core, fsdp, length = place(n_ctx)
        ctx = chip * 2 + core
        sibling = (chip * 2 + 1 - core, fsdp)
        mirror = ((length - 1 - chip) * 2 + core, fsdp)
        first, second, corner = fsdp_neighbours(fsdp)
        where = (chip, core, fsdp, length)
        greet([mirror] + line_peers(*where) + fsdp_peers(n_fsdp, ctx, fsdp))
        line = line_gather(attended_ref, heads_ref, ((ri_s, ri_r), (le_s, le_r), (lc_s, lc_r)), where)
        heads_own = pltpu.make_async_copy(attended_ref, heads_ref.at[ctx], heads_sem)
        heads_own.start()
        mine = pltpu.make_async_copy(own_ref, rows.at[core, fsdp], load.at[3])
        mine.start()
        start = pl.multiple_of(core * n_own, n_own)
        loads = [
            pltpu.make_async_copy(planes_ref.at[p, pl.ds(start, n_own)], weights.at[p], load.at[p]) for p in range(3)
        ]
        handed, arriving = [], []

        def hand(source, owner, part, index):
            for side, copies in ((core, handed), (1 - core, arriving)):
                target = rows.at[side, owner] if part is None else rows.at[side, owner, part]
                copies.append(send(source, target, (core_s, core_r), index + 1, sibling))
            handed[-1].start()

        gathering = square_gather(own_ref, rows.at[core], (sq_s, sq_r), ctx, fsdp, n_fsdp, hand)
        next(gathering)
        hand(own_ref, fsdp, None, -1)
        for each in loads:
            each.start()
        far = [
            send(
                own_ref.at[pl.ds(part * tokens, tokens)],
                mirror_ref.at[core, fsdp, pl.ds(part * tokens, tokens)],
                (far_s, far_r),
                part,
                mirror,
            )
            for part in range(2)
        ]
        for each in far:
            each.start()
        mirroring = mirror_gather(mirror_ref, far, (mi_s, mi_r), (mc_s, mc_r), ctx, core, fsdp, sibling)
        outs, summing, sums = [], [], []

        def add_up(number, owner):
            summing[number].wait_recv()
            add_into(partial.at[number % 2, core], core_in.at[number])
            sums.append(
                pltpu.make_async_copy(partial.at[number % 2, core], partial_ref.at[owner], out_sem.at[number % 2, 8])
            )
            sums[-1].start()

        def group(number, owner):
            slot = number % 2
            if number >= 2:
                for each in outs[number - 2]:
                    each.wait()
                summing[number - 2].wait_send()
                sums[number - 2].wait()
            here = jnp.concatenate([rows[0, owner, :tokens], rows[1, owner, :tokens]])
            back = jnp.concatenate([rows[0, owner, tokens:], rows[1, owner, tokens:]])

            @pl.loop(0, n_own // chunk)
            def _(step):
                at = pl.ds(pl.multiple_of(step * chunk, chunk), chunk)
                parts = [weights.at[pl.ds(p, 1), at] for p in range(3)]
                for q, value in enumerate(hidden_units(here, back, *parts)):
                    hidden[slot, q, :, at] = value

            @pl.loop(0, features // wide)
            def _(step):
                at = pl.ds(pl.multiple_of(step * wide, wide), wide)
                out = low(mm(hidden[slot, 0], weights[2, :, at]))
                below = low(mm(hidden[slot, 1], weights[0, :, at]) + mm(hidden[slot, 2], weights[1, :, at]))
                for k in range(2):
                    partial[slot, k, :tokens, at] = out[k * tokens : (k + 1) * tokens]
                    partial[slot, k, tokens:, at] = below[k * tokens : (k + 1) * tokens]

            pairs = []
            summing.append(send(partial.at[slot, 1 - core], core_in.at[number], (sum_s, sum_r), number, sibling))
            summing[-1].start()
            for k in range(2):
                pairs.append((rows.at[k, owner], all_ref.at[k, owner]))
                at = pl.ds(pl.multiple_of((k * n_fsdp + owner) * tokens, tokens), tokens)
                for q, target in enumerate((hidden_a, hidden_b, hidden_c)):
                    pairs.append((hidden.at[slot, q, pl.ds(k * tokens, tokens)], target.at[at]))
            outs.append(
                [pltpu.make_async_copy(a, b, out_sem.at[slot, j]) for j, (a, b) in enumerate(pairs)]
            )
            for each in outs[-1]:
                each.start()

        mine.wait()
        arriving[0].wait_recv()
        for each in loads:
            each.wait()
        group(0, fsdp)
        for _ in range(4):
            next(gathering)
        arriving[1].wait_recv()
        arriving[3].wait_recv()
        group(1, first)
        add_up(0, fsdp)
        next(mirroring)
        next(line)
        for _ in range(2):
            next(gathering)
        arriving[2].wait_recv()
        arriving[4].wait_recv()
        group(2, second)
        add_up(1, first)
        for _ in range(3):
            next(mirroring)
        next(line)
        arriving[5].wait_recv()
        arriving[6].wait_recv()
        group(3, corner)
        next(line)
        add_up(2, second)
        next(mirroring)
        add_up(3, corner)
        run_all(mirroring, line, gathering)
        heads_own.wait()
        for each in handed:
            each.wait_send()
        for each in far:
            each.wait_send()
        for each in outs[2] + outs[3] + sums[2:]:
            each.wait()
        for each in summing[2:]:
            each.wait_send()

    act = jax.ShapeDtypeStruct((total, n_own), own.dtype)
    all_rows = jax.ShapeDtypeStruct((2, n_fsdp) + own.shape, own.dtype)
    return pl.pallas_call(
        kernel,
        in_specs=any_specs(3),
        out_specs=any_specs(7),
        out_shape=[
            all_rows,
            all_rows,
            act,
            act,
            act,
            jax.ShapeDtypeStruct((n_fsdp,) + own.shape, own.dtype),
            jax.ShapeDtypeStruct((n_ctx,) + attended.shape, attended.dtype),
        ],
        scratch_shapes=[
            pltpu.VMEM((2, n_fsdp) + own.shape, own.dtype),
            pltpu.VMEM((3, n_own, features), own.dtype),
            pltpu.VMEM((2, 3, 2 * tokens, n_own), own.dtype),
            pltpu.VMEM((2, 2) + own.shape, own.dtype),
            pltpu.VMEM((n_fsdp,) + own.shape, own.dtype),
            pltpu.SemaphoreType.DMA((4,)),
        ]
        + dma_pair(6)
        + dma_pair(7)
        + dma_pair(2)
        + dma_pair(6)
        + dma_pair(8)
        + dma_pair(4)
        + [pltpu.SemaphoreType.DMA((2, 9))]
        + dma_pair(n_ctx // 2) * 3
        + [pltpu.SemaphoreType.DMA],
        compiler_params=params(6),
        cost_estimate=pl.CostEstimate(
            flops=12 * total * n_own * features, bytes_accessed=50 * 1024 * 1024, transcendentals=total * n_own
        ),
        name="ffn_rows",
    )(own, planes, attended)


def ffn_weights(n_ctx, n_fsdp, partial, rows, rows_mirror, hidden, planes, n_own, chunk=256):
    blocks, _, tokens, features = rows.shape
    total = blocks * tokens
    steps = n_own // chunk
    group = max(1, 256 // tokens)
    half = features // 2
    sides = n_ctx // 4
    wide = half // sides
    fused = partial is not None
    early = steps // 2 if fused else 0
    assert not fused or sides == 2

    def kernel(*refs):
        rows_ref, refs = refs[0], refs[1:]
        mirror_refs, refs = refs[: len(rows_mirror)], refs[len(rows_mirror) :]
        mirror_blocks = [ref.at[b] for ref in mirror_refs for b in range(ref.shape[0])]
        hidden_ref, grad_gate_ref, grad_up_ref, planes_ref, *refs = refs
        if fused:
            partial_ref, weight_ref, out_ref, early_ref, *refs = refs
        else:
            weight_ref, *refs = refs
        mirror, (weights, weight_sems), refs = refs[:3], refs[3:5], refs[5:]
        chip, core, _, length = place(n_ctx)
        side = chip // sides
        step = pl.program_id(0)
        stages = []
        if fused:
            keep, give, take, side_s, side_r, held, square_in, load, sq_s, sq_r = refs
            member = chip % 2
            other = (chip + 1 - 2 * member) * 2 + core
            crossing = [
                [
                    send(
                        give.at[j, plane],
                        take.at[j, plane],
                        (side_s, side_r),
                        3 * j + plane,
                        (other, lax.axis_index("fsdp")),
                    )
                    for plane in range(3)
                ]
                for j in range(early)
            ]
            starts, *stages = corner_sum_stages(n_ctx, partial_ref, out_ref, held, square_in, load, (sq_s, sq_r))

        def fetch(at, slot):
            start = pl.multiple_of((core * steps + at) * chunk, chunk)
            return pltpu.make_async_copy(planes_ref.at[:, pl.ds(start, chunk)], weights.at[slot], weight_sems.at[slot])

        @pl.when(step == 0)
        def _():
            fetch(0, 0).start()
            if fused:
                fsdp = lax.axis_index("fsdp")
                greet(fsdp_peers(4, chip * 2 + core, fsdp) + [(other, fsdp)])
                for start in sum(starts, []):
                    start()

        @pl.when(step + 1 < steps)
        def _():
            fetch(step + 1, (step + 1) % 2).start()

        slot = step % 2
        fetch(step, slot).wait()
        gate_ref, up_ref, down_ref = (weights.at[slot, pl.ds(plane, 1)] for plane in range(3))
        for at in range(0, blocks, group):
            here = jnp.concatenate([ref[0] for ref in mirror_blocks[at : at + group]])
            back = jnp.concatenate([ref[1] for ref in mirror_blocks[at : at + group]])
            span = pl.ds(at * tokens, group * tokens)
            for out, value in zip(mirror, hidden_units(here, back, gate_ref, up_ref, down_ref)):
                out[span] = value

        lefts = ((grad_gate_ref, mirror[1], 0), (grad_up_ref, mirror[2], 0), (hidden_ref, mirror[0], 1))
        for plane, (left, left_mirror, which) in enumerate(lefts):
            left = left[...]
            left_mirror = left_mirror[...]
            for z in range(sides):
                cols = pl.ds(pl.multiple_of(side * half + z * wide, wide), wide)
                right = rows_ref[:, which, :, cols].reshape(total, wide)
                right_mirror = jnp.concatenate([ref[which, :, cols] for ref in mirror_blocks])
                value = mm(left, right, CONTRACT_FIRST) + mm(left_mirror, right_mirror, CONTRACT_FIRST)
                if not fused:
                    weight_ref[z, plane] = low(value)
                    continue

                @pl.when((step < early) & (z == member))
                def _():
                    keep[step % early, plane] = value

                @pl.when((step < early) & (z != member))
                def _():
                    give[step % early, plane] = low(value)

                @pl.when(step >= early)
                def _():
                    weight_ref[z, plane] = low(value)

            for j in range(early):

                @pl.when(step == j)
                def _():
                    crossing[j][plane].start()

        for at, stage in ((1, 0), (steps - 1, 1)):
            if stage < len(stages):

                @pl.when(step == min(at, steps - 1))
                def _():
                    stages[stage]()

        if fused:

            @pl.when(step == steps - 1)
            def _():
                for j in range(early):
                    for plane in range(3):
                        crossing[j][plane].wait()
                        early_ref[plane, j * chunk : (j + 1) * chunk] = low(
                            keep[j, plane] + take[j, plane].astype(jnp.float32)
                        )

    act_spec = pl.BlockSpec((total, chunk), lambda j: (0, j))
    once = dict(pipeline_mode=pl.Buffered(1))
    operands = [rows, *rows_mirror, *hidden, planes]
    in_specs = [whole_block(rows.shape, **once)] + [whole_block(part.shape, **once) for part in rows_mirror]
    in_specs += [act_spec] * 3 + any_specs(1)
    out_specs = [pl.BlockSpec((sides, 3, chunk, wide), lambda j: (0, 0, jnp.maximum(j - early, 0), 0))]
    out_shape = [jax.ShapeDtypeStruct((sides, 3, n_own - early * chunk, wide), jnp.bfloat16)]
    scratch = [pltpu.VMEM((total, chunk), jnp.bfloat16)] * 3
    scratch += [pltpu.VMEM((2, 3, chunk, features), jnp.bfloat16), pltpu.SemaphoreType.DMA((2,))]
    if fused:
        operands.append(partial)
        in_specs += any_specs(1)
        out_specs.append(whole_block(partial.shape[-2:], **once))
        out_shape.append(jax.ShapeDtypeStruct(partial.shape[-2:], jnp.float32))
        out_specs.append(whole_block((3, early * chunk, wide), **once))
        out_shape.append(jax.ShapeDtypeStruct((3, early * chunk, wide), jnp.bfloat16))
        scratch.append(pltpu.VMEM((early, 3, chunk, wide), jnp.float32))
        scratch += [pltpu.VMEM((early, 3, chunk, wide), jnp.bfloat16)] * 2 + dma_pair(3 * early)
        scratch += corner_sum_scratch(partial)
    return pl.pallas_call(
        kernel,
        grid=(steps,),
        in_specs=in_specs,
        out_specs=out_specs,
        out_shape=out_shape,
        scratch_shapes=scratch,
        compiler_params=params(3) if fused else params(),
        cost_estimate=pl.CostEstimate(
            flops=12 * total * n_own * features, bytes_accessed=50 * 1024 * 1024, transcendentals=total * n_own
        ),
        name="ffn_weights",
    )(*operands)


def ffn_back(hidden, grad_gate, grad_up, planes, core, blocks, wide=512):
    total, n_own = hidden.shape
    features = planes.shape[2]
    tokens = total // blocks

    def kernel(core_ref, hidden_ref, grad_gate_ref, grad_up_ref, gate_ref, up_ref, down_ref, out_ref):
        out = mm(hidden_ref[...], down_ref[0])
        out_ref[:, 0] = low(out).reshape(blocks, tokens, wide)
        back = mm(grad_gate_ref[...], gate_ref[0]) + mm(grad_up_ref[...], up_ref[0])
        out_ref[:, 1] = low(back).reshape(blocks, tokens, wide)

    def weight_spec(plane):
        return pl.BlockSpec((1, n_own, wide), lambda j, core_ref: (plane, core_ref[0], j))

    act_spec = pl.BlockSpec((total, n_own), lambda j, core_ref: (0, 0), pipeline_mode=pl.Buffered(1))
    return pl.pallas_call(
        kernel,
        grid_spec=pltpu.PrefetchScalarGridSpec(
            num_scalar_prefetch=1,
            grid=(features // wide,),
            in_specs=[act_spec, act_spec, act_spec, weight_spec(0), weight_spec(1), weight_spec(2)],
            out_specs=pl.BlockSpec((blocks, 2, tokens, wide), lambda j, core_ref: (0, 0, 0, j)),
        ),
        out_shape=jax.ShapeDtypeStruct((blocks, 2, tokens, features), jnp.bfloat16),
        compiler_params=params(),
        cost_estimate=pl.CostEstimate(
            flops=6 * total * n_own * features, bytes_accessed=30 * 1024 * 1024, transcendentals=0
        ),
        name="ffn_back",
    )(core, hidden, grad_gate, grad_up, planes, planes, planes)


SPAN = 256


def ctx_peers(n_ctx):
    ctx = lax.axis_index("ctx")
    fsdp = lax.axis_index("fsdp")
    return [((ctx + j) % n_ctx, fsdp) for j in range(1, n_ctx)]


def deal(n_ctx, block, target, landed, sems, own_sem):
    ctx = lax.axis_index("ctx")
    fsdp = lax.axis_index("fsdp")

    @pl.when(target != ctx)
    def _():
        send(block, landed.at[ctx], sems, (target - ctx + n_ctx) % n_ctx, (target, fsdp)).start()

    @pl.when(target == ctx)
    def _():
        pltpu.make_async_copy(block, landed.at[ctx], own_sem).start()


def dealt(n_ctx, block, landed, sems, own_sem):
    ctx = lax.axis_index("ctx")
    pltpu.make_async_copy(block, landed.at[ctx], own_sem).wait()
    for j, peer in enumerate(ctx_peers(n_ctx)):
        copy = send(block, landed.at[(ctx + n_ctx - j - 1) % n_ctx], sems, j + 1, peer)
        copy.wait_send()
        copy.wait_recv()


def turn(values, cosine, sine):
    return values * cosine + pltpu.roll(values, HEAD_DIM // 2, 1) * sine


def attention_forward(n_ctx, rows, w_qkv, cosine, sine, place_column, place_row, heads):
    total, features = rows.shape
    own = heads * HEAD_DIM
    steps = total // SPAN
    length = total // n_ctx
    scale = HEAD_DIM ** (-0.5)

    def kernel(
        rows_ref, w_ref, cosine_ref, sine_ref, column_ref, row_ref,
        query_ref, key_ref, value_ref, out_ref, log_ref, landed, deal_s, deal_r, own_sem,
    ):
        step = pl.program_id(0)

        @pl.when(step == 0)
        def _():
            greet(ctx_peers(n_ctx))

        span = pl.ds(pl.multiple_of(step * SPAN, SPAN), SPAN)
        qkv = mm(rows_ref[...], w_ref[...])
        cosine = cosine_ref[span]
        sine = sine_ref[span]
        for h in range(heads):
            at = slice(h * HEAD_DIM, (h + 1) * HEAD_DIM)
            query_ref[span, at] = low(turn(qkv[:, at], cosine, sine))
            key_ref[span, at] = low(turn(qkv[:, own + h * HEAD_DIM : own + (h + 1) * HEAD_DIM], cosine, sine))
        value_ref[span] = low(qkv[:, 2 * own :])

        @pl.when(step == steps - 1)
        def _():
            @pl.loop(0, steps)
            def _(block):
                here = pl.ds(pl.multiple_of(block * SPAN, SPAN), SPAN)
                for h in range(heads):
                    at = slice(h * HEAD_DIM, (h + 1) * HEAD_DIM)
                    scores = mm(query_ref[here, at], key_ref[:, at], CONTRACT_LAST) * scale
                    scores = jnp.where(column_ref[here] >= row_ref[...], scores, MASKED)
                    highest = jnp.max(scores, axis=-1, keepdims=True)
                    exponent = jnp.exp(scores - highest)
                    sums = jnp.sum(exponent, axis=-1, keepdims=True)
                    out_ref[here, at] = low(mm(low(exponent * (1.0 / sums)), value_ref[:, at]))
                    log_ref[h, here] = highest + jnp.log(sums)
                for r in range(SPAN // length):
                    mine = out_ref.at[pl.ds(pl.multiple_of(block * SPAN + r * length, length), length)]
                    deal(n_ctx, mine, block * (SPAN // length) + r, landed, (deal_s, deal_r), own_sem)

            dealt(n_ctx, out_ref.at[pl.ds(0, length)], landed, (deal_s, deal_r), own_sem)

    act = jax.ShapeDtypeStruct((total, own), jnp.bfloat16)
    return pl.pallas_call(
        kernel,
        grid=(steps,),
        in_specs=[pl.BlockSpec((SPAN, features), lambda r: (r, 0))]
        + [whole_block(a.shape) for a in (w_qkv, cosine, sine, place_column, place_row)],
        out_specs=[whole_block((total, own))] * 4 + [whole_block((heads, total, 1))] + any_specs(1),
        out_shape=[act] * 4
        + [
            jax.ShapeDtypeStruct((heads, total, 1), jnp.float32),
            jax.ShapeDtypeStruct((n_ctx, length, own), jnp.bfloat16),
        ],
        scratch_shapes=dma_pair(n_ctx) + [pltpu.SemaphoreType.DMA],
        compiler_params=params(8),
        name="attention_forward",
    )(rows, w_qkv, cosine, sine, place_column, place_row)


def attention_backward(query, key, value, grad, logs, w_qkv, cosine, sine, place_column, place_row, heads):
    total, own = query.shape
    features = w_qkv.shape[0]
    steps = total // SPAN
    scale = HEAD_DIM ** (-0.5)

    def kernel(
        query_ref, key_ref, value_ref, grad_ref, log_ref, w_ref, cosine_ref, sine_ref, column_ref, row_ref,
        qkv_ref, out_ref, key_sum, value_sum,
    ):
        step = pl.program_id(0)

        @pl.when(step == 0)
        def _():
            for h in range(heads):
                at = slice(h * HEAD_DIM, (h + 1) * HEAD_DIM)
                key_sum[...] = jnp.zeros_like(key_sum)
                value_sum[...] = jnp.zeros_like(value_sum)

                @pl.loop(0, steps)
                def _(block):
                    here = pl.ds(pl.multiple_of(block * SPAN, SPAN), SPAN)
                    queries = query_ref[here, at]
                    grads = grad_ref[here, at]
                    scores = mm(queries, key_ref[:, at], CONTRACT_LAST) * scale
                    scores = jnp.where(column_ref[here] >= row_ref[...], scores, MASKED)
                    probs = jnp.exp(scores - log_ref[h, here])
                    probs_grad = mm(grads, value_ref[:, at], CONTRACT_LAST)
                    centre = jnp.sum(probs * probs_grad, axis=-1, keepdims=True)
                    scores_grad = low(probs * (probs_grad - centre))
                    query_grad = mm(scores_grad, key_ref[:, at]) * scale
                    qkv_ref[here, at] = low(turn(query_grad, cosine_ref[here], -sine_ref[here]))
                    key_sum[...] += mm(scores_grad, queries, CONTRACT_FIRST)
                    value_sum[...] += mm(low(probs), grads, CONTRACT_FIRST)

                qkv_ref[:, own + h * HEAD_DIM : own + (h + 1) * HEAD_DIM] = low(
                    turn(key_sum[...] * scale, cosine_ref[...], -sine_ref[...])
                )
                qkv_ref[:, 2 * own + h * HEAD_DIM : 2 * own + (h + 1) * HEAD_DIM] = low(value_sum[...])

        span = pl.ds(pl.multiple_of(step * SPAN, SPAN), SPAN)
        out_ref[...] = low(mm(qkv_ref[span], w_ref[...], CONTRACT_LAST))

    return pl.pallas_call(
        kernel,
        grid=(steps,),
        in_specs=[
            whole_block(a.shape)
            for a in (query, key, value, grad, logs, w_qkv, cosine, sine, place_column, place_row)
        ],
        out_specs=[whole_block((total, 3 * own)), pl.BlockSpec((SPAN, features), lambda r: (r, 0))],
        out_shape=[
            jax.ShapeDtypeStruct((total, 3 * own), jnp.bfloat16),
            jax.ShapeDtypeStruct((total, features), jnp.bfloat16),
        ],
        scratch_shapes=[pltpu.VMEM((total, HEAD_DIM), jnp.float32)] * 2,
        compiler_params=params(),
        name="attention_backward",
    )(query, key, value, grad, logs, w_qkv, cosine, sine, place_column, place_row)


ROWS = 32


def row_blocks(count, features):
    return pl.BlockSpec((count, ROWS, features), lambda r, *_: (0, r, 0))


def whole_block(shape, **more):
    zeros = (0,) * len(shape)
    return pl.BlockSpec(shape, lambda r, *_: zeros, **more)


def split(values):
    high = low(values)
    return (high, low(values - high.astype(jnp.float32)))


def connect_coefficients(values, dynamic_ref, static_ref, coef_ref, dyn_ref):
    lane = lax.broadcasted_iota(jnp.int32, (values[0].shape[0], 8), 1)
    columns = []
    for i, value in enumerate(values):
        mean = jnp.mean(value, axis=-1, keepdims=True)
        centered = value - mean
        inverse = lax.rsqrt(jnp.mean(centered * centered, axis=-1, keepdims=True) + EPS)
        normed = centered * inverse
        projected = jnp.zeros(lane.shape, jnp.float32)
        for k in range(6):
            part = jnp.sum(normed * dynamic_ref[k : k + 1], axis=-1, keepdims=True)
            projected = jnp.where(lane == k, part, projected)
        coefficient = jnp.tanh(projected) + static_ref[i : i + 1]
        dyn_ref[i] = projected
        coef_ref[i] = jnp.where(lane == 6, mean, jnp.where(lane == 7, inverse, coefficient))
        columns.append(coefficient)
    return columns


def connect_first(streams, dynamic, static):
    number, rows, features = streams.shape

    def kernel(streams_ref, dynamic_ref, static_ref, coef_ref, dyn_ref, low_ref):
        values = [streams_ref[i].astype(jnp.float32) for i in range(number)]
        columns = connect_coefficients(values, dynamic_ref, static_ref, coef_ref, dyn_ref)
        mixed = sum((columns[i][:, 1:2] * values[i] for i in range(number)))
        low_ref[...] = low(normalize(mixed)[0])

    small = jax.ShapeDtypeStruct((number, rows, 8), jnp.float32)
    return pl.pallas_call(
        kernel,
        grid=(rows // ROWS,),
        out_shape=(small, small, jax.ShapeDtypeStruct((rows, features), jnp.bfloat16)),
        in_specs=[row_blocks(number, features), whole_block(dynamic.shape), whole_block(static.shape)],
        out_specs=(
            row_blocks(number, 8),
            row_blocks(number, 8),
            pl.BlockSpec((ROWS, features), lambda r: (r, 0)),
        ),
        compiler_params=params(),
        name="connect_first",
    )(streams, dynamic, static)


def connect_middle(streams, coef, attended, w_mine, w_other, cotangent, dynamic, static, core_fsdp, where, depth):
    number, rows, features = streams.shape
    half = features // 2
    own = attended.shape[2]
    count = len(w_mine)

    def kernel(core_ref, streams_ref, coef_ref, attended_ref, *refs):
        weights, refs = refs[: 2 * count], refs[2 * count :]
        cotangent_ref, dynamic_ref, static_ref = refs[:3]
        first_ref, branch_ref, coef_two_ref, dyn_ref, own_ref, projected = refs[3:]
        step = pl.program_id(0)

        @pl.when(step == 0)
        def _():
            for side in range(2):
                total = 0.0
                for j, (d, offset) in enumerate(where):
                    for q in range(w_mine[j].shape[0] // own):
                        part = attended_ref[(core_ref[1] ^ d) * (depth // own) + offset // own + q]
                        total = total + mm(part, weights[side * count + j][q * own : (q + 1) * own])
                projected[core_ref[0] if side == 0 else 1 - core_ref[0]] = total

        span = pl.ds(pl.multiple_of(step * ROWS, ROWS), ROWS)
        branch = jnp.concatenate([projected[0, span], projected[1, span]], axis=1)
        branch_ref[...] = branch
        inputs = [streams_ref[i].astype(jnp.float32) for i in range(number)]
        outs = []
        for j in range(number):
            out = sum((coef_ref[i][:, 2 + j : 3 + j] * inputs[i] for i in range(number)))
            outs.append(out + coef_ref[j][:, 0:1] * branch)
            first_ref[j] = outs[-1]
        columns = connect_coefficients(outs, dynamic_ref, static_ref, coef_two_ref, dyn_ref)
        mixed = sum((columns[i][:, 1:2] * outs[i] for i in range(number)))
        own_ref[0] = low(normalize(mixed)[0])
        own_ref[1] = low(sum((columns[j][:, 0:1] * cotangent_ref[j].astype(jnp.float32) for j in range(number))))

    small = jax.ShapeDtypeStruct((number, rows, 8), jnp.float32)
    once = dict(pipeline_mode=pl.Buffered(1))
    return pl.pallas_call(
        kernel,
        grid_spec=pltpu.PrefetchScalarGridSpec(
            num_scalar_prefetch=1,
            grid=(rows // ROWS,),
            in_specs=[
                row_blocks(number, features),
                row_blocks(number, 8),
                whole_block(attended.shape, **once),
                *[whole_block(w.shape, **once) for w in w_mine + w_other],
                row_blocks(number, features),
                whole_block(dynamic.shape),
                whole_block(static.shape),
            ],
            out_specs=(
                row_blocks(number, features),
                pl.BlockSpec((ROWS, features), lambda r, *_: (r, 0)),
                row_blocks(number, 8),
                row_blocks(number, 8),
                row_blocks(2, features),
            ),
            scratch_shapes=[pltpu.VMEM((2, rows, half), jnp.float32)],
        ),
        out_shape=(
            jax.ShapeDtypeStruct((number, rows, features), jnp.float32),
            jax.ShapeDtypeStruct((rows, features), jnp.float32),
            small,
            small,
            jax.ShapeDtypeStruct((2, rows, features), jnp.bfloat16),
        ),
        compiler_params=params(),
        name="connect_middle",
    )(core_fsdp, streams, coef, attended, *w_mine, *w_other, cotangent, dynamic, static)


def attention_weights(rows, grads, attended, grad_cols):
    total, features = rows.shape
    parts, _, own = attended.shape
    wide = grads.shape[1]

    def kernel(rows_ref, grads_ref, attended_ref, cols_ref, out_ref):
        out_ref[:, :wide] = low(mm(rows_ref[...], grads_ref[...], CONTRACT_FIRST))
        out_ref[:, wide:] = low(mm(attended_ref[0], cols_ref[...], CONTRACT_FIRST))

    return pl.pallas_call(
        kernel,
        grid=(parts,),
        in_specs=[
            pl.BlockSpec((total, own), lambda k: (0, k)),
            whole_block(grads.shape),
            pl.BlockSpec((1, total, own), lambda k: (k, 0, 0)),
            whole_block(grad_cols.shape),
        ],
        out_specs=pl.BlockSpec((own, wide + own), lambda k: (k, 0)),
        out_shape=jax.ShapeDtypeStruct((features, wide + own), jnp.bfloat16),
        compiler_params=params(),
        cost_estimate=pl.CostEstimate(
            flops=2 * total * features * (wide + own), bytes_accessed=16 * 1024 * 1024, transcendentals=0
        ),
        name="attention_weights",
    )(rows, grads, attended, grad_cols)


def flip(index, bits, count):
    result = index
    bit = 1
    while bit < count:
        if bits & bit:
            result = result + bit - 2 * bit * (index // bit % 2)
        bit *= 2
    return result


def project_back(n_ctx, n_fsdp, grad, w_mine, w_other, where, depth):
    rows, features = grad.shape
    half = features // 2
    count = len(w_mine)
    own = features // n_ctx

    def kernel(grad_ref, *refs):
        weights, refs = refs[: 2 * count], refs[2 * count :]
        landed, cols_ref, outs, deal_s, deal_r, own_sem = refs
        _, core, fsdp, _ = place(n_ctx)
        greet(ctx_peers(n_ctx))
        first = grad_ref[:, pl.ds(pl.multiple_of(core * half, half), half)]
        second = grad_ref[:, pl.ds(pl.multiple_of((1 - core) * half, half), half)]
        for j, (d, offset) in enumerate(where):
            out = low(
                mm(first, weights[j][...], CONTRACT_LAST) + mm(second, weights[count + j][...], CONTRACT_LAST)
            )
            for q in range(w_mine[j].shape[0] // own):
                at = flip(fsdp, d, n_fsdp) * (depth // own) + offset // own + q
                outs[at] = out[:, q * own : (q + 1) * own]
                deal(n_ctx, outs.at[at], at, landed, (deal_s, deal_r), own_sem)
        for index in range(n_ctx):
            cols_ref[index] = grad_ref[:, index * own : (index + 1) * own]
        dealt(n_ctx, outs.at[0], landed, (deal_s, deal_r), own_sem)

    shape = (n_ctx, rows, own)
    return pl.pallas_call(
        kernel,
        in_specs=[pl.BlockSpec(memory_space=pltpu.VMEM)] * (1 + 2 * count),
        out_specs=any_specs(1) + [pl.BlockSpec(memory_space=pltpu.VMEM)],
        out_shape=[jax.ShapeDtypeStruct(shape, grad.dtype)] * 2,
        scratch_shapes=[pltpu.VMEM(shape, grad.dtype)] + dma_pair(n_ctx) + [pltpu.SemaphoreType.DMA],
        compiler_params=params(9),
        name="project_back",
    )(grad, *w_mine, *w_other)


def connect_back(values, coef, dyn, branch, grads, grad_normed, dynamic, means, coef_before=None, offset=0):
    number, rows, features = values.shape
    steps = rows // ROWS
    more = coef_before is not None

    def kernel(*refs):
        values_ref, coef_ref, dyn_ref, branch_ref, grads_ref, normed_ref, dynamic_ref, means_ref = refs[:8]
        refs = refs[8:]
        if more:
            before_ref, refs = refs[0], refs[1:]
        out_ref, dynamic_out, static_out = refs[:3]
        if more:
            forward_ref, grad_low_ref = refs[3:5]
        step = pl.program_id(0)

        @pl.when(step == 0)
        def _():
            dynamic_out[...] = jnp.zeros_like(dynamic_out)
            static_out[...] = jnp.zeros_like(static_out)

        branch = branch_ref[...]
        grads = [grads_ref[j].astype(jnp.float32) for j in range(number)]
        mixed = sum((coef_ref[i][:, 1:2] * values_ref[i].astype(jnp.float32) for i in range(number)))
        normed, inverse = normalize(mixed)
        grad_mixed = normalize_back(normed, inverse, normed_ref[...])
        lane = lax.broadcasted_iota(jnp.int32, (ROWS, 8), 1)
        pre_grads, highs, lows = [], [], []
        for i in range(number):
            value = values_ref[i].astype(jnp.float32)
            columns = [grads[i] * branch, grad_mixed * value] + [grads[j] * value for j in range(number)]
            coef_grad = jnp.zeros((ROWS, 8), jnp.float32)
            for k, column in enumerate(columns):
                coef_grad = jnp.where(lane == k, jnp.sum(column, axis=-1, keepdims=True), coef_grad)
            static_out[i : i + 1] += jnp.sum(coef_grad, axis=0, keepdims=True)
            part = jnp.tanh(dyn_ref[i])
            pre_grads.append(coef_grad * (1.0 - part * part))
            high, rest = split((value - coef_ref[i][:, 6:7]) * coef_ref[i][:, 7:8])
            highs.append(high)
            lows.append(rest)
        pre, pre_rest = split(jnp.concatenate(pre_grads))
        dynamic, dynamic_rest = split(dynamic_ref[...])
        normed_grads = mm(
            jnp.concatenate([pre, pre_rest, pre], axis=1), jnp.concatenate([dynamic, dynamic, dynamic_rest], axis=0)
        )
        highs = jnp.concatenate(highs)
        dynamic_out[...] += (
            mm(pre, highs, CONTRACT_FIRST)
            + mm(pre_rest, highs, CONTRACT_FIRST)
            + mm(pre, jnp.concatenate(lows), CONTRACT_FIRST)
        )
        befores = 0.0
        for i in range(number):
            coef = coef_ref[i]
            mean_grad = jnp.sum(pre_grads[i] * means_ref[...], axis=-1, keepdims=True)
            inner = jnp.sum(pre_grads[i] * dyn_ref[i], axis=-1, keepdims=True) / features
            normed = (values_ref[i].astype(jnp.float32) - coef[:, 6:7]) * coef[:, 7:8]
            out = coef[:, 7:8] * (normed_grads[i * ROWS : (i + 1) * ROWS] - mean_grad - normed * inner)
            out = out + coef[:, 1:2] * grad_mixed
            for j in range(number):
                out = out + coef[:, 2 + j : 3 + j] * grads[j]
            out_ref[i] = out
            if more:
                befores = befores + before_ref[i][:, 0:1] * out
        if more:
            grad_low_ref[...] = low(befores)
            for j in range(number):
                out = coef_ref[j][:, 0:1] * branch
                for i in range(number):
                    out = out + coef_ref[i][:, 2 + j : 3 + j] * values_ref[i].astype(jnp.float32)
                forward_ref[j] = low(out)

    rows_spec = pl.BlockSpec((ROWS, features), lambda r: (r, 0))
    out_shape = [
        jax.ShapeDtypeStruct((number, rows, features), jnp.float32),
        jax.ShapeDtypeStruct((8, features), jnp.float32),
        jax.ShapeDtypeStruct((8, 8), jnp.float32),
    ]
    out_specs = [row_blocks(number, features), whole_block((8, features)), whole_block((8, 8))]
    operands = [values, coef, dyn, branch, grads, grad_normed, dynamic, means]
    in_specs = [
        row_blocks(number, features),
        row_blocks(number, 8),
        row_blocks(number, 8),
        rows_spec,
        row_blocks(number, features),
        pl.BlockSpec((ROWS, features), lambda r: (offset // ROWS + r, 0)),
        whole_block(dynamic.shape),
        whole_block(means.shape),
    ]
    if more:
        operands.append(coef_before)
        in_specs.append(row_blocks(number, 8))
        out_shape.append(jax.ShapeDtypeStruct((number, rows, features), jnp.bfloat16))
        out_specs.append(row_blocks(number, features))
        out_shape.append(jax.ShapeDtypeStruct((rows, features), jnp.bfloat16))
        out_specs.append(rows_spec)
    return pl.pallas_call(
        kernel,
        grid=(steps,),
        in_specs=in_specs,
        out_specs=out_specs,
        out_shape=out_shape,
        compiler_params=params(),
        name="connect_back",
    )(*operands)


def local(n_ctx, n_fsdp, streams, w_attn, w_ffn, hc_dynamic, hc_static, cotangent, pair_order):
    number = streams.shape[1]
    length = streams.shape[2]
    features = streams.shape[3]
    size = HEAD_DIM
    own = features // n_ctx
    heads = own // size
    rows = length * n_ctx
    own_rows = w_attn.shape[0]
    ctx = lax.axis_index("ctx")
    fsdp = lax.axis_index("fsdp")
    core = ctx % 2
    chips = n_ctx // 2
    core_index = jnp.reshape(core, (1,)).astype(jnp.int32)

    def in_order(mine, other, axis):
        return jnp.where(
            core == 0, jnp.concatenate([mine, other], axis=axis), jnp.concatenate([other, mine], axis=axis)
        )


    w_own = lax.dynamic_slice_in_dim(w_attn, ctx * own, own, 2)[:, 0:3].reshape(own_rows, 3 * own)
    w_qkv = gather(w_own, "fsdp")
    half = features // 2
    w_half = lax.dynamic_slice_in_dim(w_attn, core * half, half, 2)[:, 3]
    siblings = [(i, i ^ 1) for i in range(n_ctx)]
    core_fsdp = jnp.stack([core, fsdp]).astype(jnp.int32)

    def exchange(values, most=0):
        return [values] + [
            lax.ppermute(values, "fsdp", [(i, i ^ d) for i in range(n_fsdp)])
            for d in range(1, most + 1 if most else n_fsdp)
        ]

    def swap(blocks):
        return [lax.ppermute(block, "ctx", siblings) for block in blocks]


    positions = block_positions(pair_order, length)
    frequency = THETA ** (-(jnp.arange(size // 2, dtype=jnp.float32) * 2.0) / size)
    angles = positions.astype(jnp.float32)[:, None] * jnp.concatenate([frequency, frequency])[None, :]
    signs = jnp.where(jnp.arange(size) < size // 2, -1.0, 1.0)
    tables = (jnp.cos(angles), jnp.sin(angles) * signs[None, :], positions[:, None], positions[None, :])

    dynamics = jnp.pad(hc_dynamic, ((0, 0), (0, 2), (0, 0)))
    means = jnp.mean(dynamics, axis=-1)
    statics = jnp.pad(hc_static, ((0, 0), (0, 0), (0, 2)))
    coef_one, dyn_one, attn_low = connect_first(streams[0], dynamics[0], statics[0])
    attn_low, w_half = lax.optimization_barrier((attn_low, w_half))
    w_out_mine = exchange(w_half, 2 if n_fsdp == 4 else 0)
    attn_all = line_rows(n_ctx, attn_low).reshape(rows, features)
    w_out_where = [(d, 0) for d in range(len(w_out_mine))]
    attn_all, *w_out_mine = lax.optimization_barrier((attn_all, *w_out_mine))
    w_out_other = swap(w_out_mine)
    if n_fsdp == 4:
        middle = own_rows // 2
        corners = [
            lax.ppermute(w_out_mine[1][:middle], "fsdp", [(i, i ^ 2) for i in range(4)]),
            lax.ppermute(w_out_mine[2][middle:], "fsdp", [(i, i ^ 1) for i in range(4)]),
        ]
        w_out_where += [(3, 0), (3, middle)]
    query, key, value, attended, logs, attended_rows = attention_forward(n_ctx, attn_all, w_qkv, *tables, heads)
    if n_fsdp == 4:
        attended, *corners = lax.optimization_barrier((attended, *corners))
        w_out_mine += corners
        w_out_other += swap(corners)

    first_out, attn_branch, coef_two, dyn_two, ffn_own = connect_middle(
        streams[0], coef_one, attended_rows, w_out_mine, w_out_other, cotangent[0], dynamics[1], statics[1], core_fsdp,
        w_out_where, own_rows,
    )
    ffn_own = ffn_own.reshape(2 * length, features)

    planes = jnp.moveaxis(w_ffn, 1, 0)
    n_own = planes.shape[1] // 2
    blocks = 2 * n_fsdp
    if n_fsdp == 4:
        ffn_all, mirror_rows, *hidden, sums, attended_all = ffn_rows(n_ctx, ffn_own, planes, attended, n_own)
        ffn_all, mirror_rows = (part.reshape(blocks, 2, length, features) for part in (ffn_all, mirror_rows))
        mirror_rows = [mirror_rows]
        weight_parts, sums, weight_early = ffn_weights(
            n_ctx, n_fsdp, sums, ffn_all, mirror_rows, hidden, planes, n_own
        )
    else:
        ffn_mirror = lax.ppermute(ffn_own, "ctx", [(i, n_ctx - 2 - i + 2 * (i % 2)) for i in range(n_ctx)])
        ffn_all = square_core_gather(n_ctx, n_fsdp, ffn_own).reshape(blocks, 2, length, features)
        attended_all = gather(attended, "ctx").reshape(n_ctx, rows, own)
        mirror_mine = exchange(ffn_mirror)
        hidden = ffn_forward(ffn_all, planes, core_index, n_own)
        sums = ffn_back(*hidden, planes, core_index, blocks)
        mirror_rows = [part.reshape(1, 2, length, features) for part in mirror_mine + swap(mirror_mine)]
        sums = square_sum(n_ctx, n_fsdp, sums.reshape(2, n_fsdp, 2 * length, features))
        (weight_parts,) = ffn_weights(n_ctx, n_fsdp, None, ffn_all, mirror_rows, hidden, planes, n_own)
    sides = chips // 2
    lines = [[2 * (sides * side + i) + j for i in range(sides)] for side in range(2) for j in range(2)]
    weight_cols = lax.psum_scatter(weight_parts, "ctx", scatter_dimension=0, axis_index_groups=lines)

    grad_first, dynamic_grad_two, static_grad_two, streams_out, grad_attn = connect_back(
        first_out, coef_two, dyn_two, sums, cotangent[0], sums, dynamics[1], means[1:], coef_one, length
    )
    grad_heads, grad_cols = project_back(n_ctx, n_fsdp, grad_attn, w_out_mine, w_out_other, w_out_where, own_rows)
    grad_heads = grad_heads.reshape(rows, own)
    grad_heads, grad_cols = lax.optimization_barrier((grad_heads, grad_cols))
    grad_cols = lax.all_to_all(grad_cols, "ctx", 0, 0, tiled=True).reshape(rows, own)
    qkv_grad, attn_part = attention_backward(query, key, value, grad_heads, logs, w_qkv, *tables, heads)
    attn_part = attn_part.reshape(n_ctx, length, features)
    if n_fsdp == 4:
        grad_attn_normed, attn_grad = attention_sums(n_ctx, attn_part, attn_all, qkv_grad, attended_all, grad_cols)
    else:
        grad_attn_normed = line_sum(n_ctx, attn_part)
        attn_grad = scatter(attention_weights(attn_all, qkv_grad, attended_all, grad_cols), "fsdp").astype(jnp.float32)
    grad_attn_normed, weight_cols = lax.optimization_barrier((grad_attn_normed, weight_cols))
    if n_fsdp == 4:
        weight_cols = jnp.concatenate([weight_early, weight_cols], axis=1)
    mine = lax.dynamic_slice_in_dim(weight_cols, core * own, own, 2)
    other = lax.dynamic_slice_in_dim(weight_cols, (1 - core) * own, own, 2)
    other = lax.ppermute(other, "ctx", siblings)
    ffn_grad = jnp.moveaxis(in_order(mine, other, 1), 0, 1).astype(jnp.float32)
    grad_inputs, dynamic_grad_one, static_grad_one = connect_back(
        streams[0], coef_one, dyn_one, attn_branch, grad_first, grad_attn_normed, dynamics[0], means[:1]
    )
    static_grads = jnp.concatenate([static_grad_one[:number, :6].reshape(1, -1), static_grad_two[:number, :6].reshape(1, -1)])
    small = jnp.concatenate(
        [
            dynamic_grad_one[:6],
            dynamic_grad_two[:6],
            jnp.pad(static_grads, ((0, 2), (0, features - 6 * number))),
        ]
    )
    small = sum_everywhere(n_ctx, n_fsdp, small.reshape(n_ctx, 8, -1))
    small = small.reshape(16, features)
    attn_grad = attn_grad.reshape(own_rows, 4, own)
    dynamic_total = small[:12].reshape(2, 6, features)
    static_total = small[12:14, : 6 * number].reshape(2, number, 6)
    return (streams_out[None], grad_inputs[None], attn_grad, ffn_grad, dynamic_total, static_total)


def solution(mesh):
    return jax.shard_map(
        functools.partial(local, mesh.shape["ctx"], mesh.shape["fsdp"]),
        mesh=mesh,
        in_specs=(
            P("fsdp", None, "ctx", None),
            P("fsdp", None, None),
            P("fsdp", None, None),
            P(),
            P(),
            P("fsdp", None, "ctx", None),
            P(),
        ),
        out_specs=(
            P("fsdp", None, "ctx", None),
            P("fsdp", None, "ctx", None),
            P("fsdp", None, "ctx"),
            P("fsdp", None, "ctx"),
            P(),
            P(),
        ),
        check_vma=False,
    )
```

```python
import functools

import jax
import jax.numpy as jnp
from jax import lax
from jax.experimental import pallas as pl
from jax.experimental.pallas import tpu as pltpu
from jax.sharding import PartitionSpec as P

HEADS = 16
HEAD_DIM = 128


EPS = 1e-05
THETA = 10000.0
HIGH = lax.Precision.HIGHEST
MASKED = -1e30
CONTRACT_LAST = (((1,), (1,)), ((), ()))
CONTRACT_FIRST = (((0,), (0,)), ((), ()))


def normalize(values):
    centered = values - jnp.mean(values, axis=-1, keepdims=True)
    inverse = lax.rsqrt(jnp.mean(centered * centered, axis=-1, keepdims=True) + EPS)
    return (centered * inverse, inverse)


def normalize_back(normed, inverse, gradient):
    inner = jnp.mean(gradient * normed, axis=-1, keepdims=True)
    return inverse * (gradient - jnp.mean(gradient, axis=-1, keepdims=True) - normed * inner)


def block_positions(pair_order, length):
    half_size = length // 2
    offsets = jnp.arange(half_size, dtype=jnp.int32)
    mirror = 2 * pair_order.shape[0] - 1 - pair_order
    first_half = pair_order[:, None] * half_size + offsets[None, :]
    second_half = mirror[:, None] * half_size + offsets[None, :]
    return jnp.concatenate([first_half, second_half], axis=1).reshape(-1)


def low(values):
    return values.astype(jnp.bfloat16)


def mm(a, b, dims=None):
    if dims is None:
        return jnp.dot(a, b, preferred_element_type=jnp.float32)
    return lax.dot_general(a, b, dims, preferred_element_type=jnp.float32)


def gather(values, axis, dim=0):
    return lax.all_gather(values, axis, axis=dim, tiled=True)


def scatter(values, axis, dim=0):
    return lax.psum_scatter(values, axis, scatter_dimension=dim, tiled=True)


MESH = pl.DeviceIdType.MESH
VMEM_LIMIT = 60 * 1024 * 1024


def place(n_ctx):
    ctx = lax.axis_index("ctx")
    return (ctx // 2, ctx % 2, lax.axis_index("fsdp"), n_ctx // 2)


def greet(peers):
    barrier = pltpu.get_barrier_semaphore()
    for peer in peers:
        pl.semaphore_signal(barrier, inc=1, device_id=peer, device_id_type=MESH)
    pl.semaphore_wait(barrier, len(peers))


def send(source, target, sems, index, peer):
    return pltpu.make_async_remote_copy(
        src_ref=source,
        dst_ref=target,
        send_sem=sems[0].at[index],
        recv_sem=sems[1].at[index],
        device_id=peer,
        device_id_type=MESH,
    )


def fsdp_neighbours(fsdp):
    first = fsdp + 1 - 2 * (fsdp % 2)
    second = (fsdp + 2) % 4
    return (first, second, (first + 2) % 4)


def fsdp_peers(n_fsdp, ctx, fsdp):
    if n_fsdp == 4:
        first, second, _ = fsdp_neighbours(fsdp)
        return [(ctx, first), (ctx, second)]
    return [(ctx, (fsdp + j) % n_fsdp) for j in range(1, n_fsdp)]


def line_peers(chip, core, fsdp, length):
    return [
        (chip * 2 + 1 - core, fsdp),
        ((chip + 1) % length * 2 + core, fsdp),
        ((chip + length - 1) % length * 2 + core, fsdp),
    ]


def line_gather(own_ref, all_ref, sems, where):
    chip, core, fsdp, length = where
    right_sems, left_sems, core_sems = sems
    sibling = (chip * 2 + 1 - core, fsdp)
    right = ((chip + 1) % length * 2 + core, fsdp)
    left = ((chip + length - 1) % length * 2 + core, fsdp)

    def block(index):
        return all_ref.at[(index + length) % length * 2 + core]

    def pass_on(index, source):
        return send(source, block(index), core_sems, (index + length) % length, sibling)

    pass_on(chip, own_ref).start()
    for step in range(length - 1):
        for sign, peer, way in ((-1, right, right_sems), (1, left, left_sems)):
            at = chip + sign * step
            held = (at >= 0) & (at < length)
            if step > 0:

                @pl.when(held)
                def _():
                    send(block(at), block(at), way, step - 1, peer).wait_recv()
                    pass_on(at, block(at)).start()

            more = (chip < length - 1) if sign < 0 else (chip > 0)

            @pl.when(held & more)
            def _():
                send(own_ref if step == 0 else block(at), block(at), way, step, peer).start()

        yield
    last = length - 1
    for sign, peer, way in ((-1, right, right_sems), (1, left, left_sems)):
        at = chip + sign * last

        @pl.when((at >= 0) & (at < length))
        def _():
            send(block(at), block(at), way, last - 1, peer).wait_recv()
            pass_on(at, block(at)).start()

    yield
    for step in range(length - 1):
        for sign, peer, way in ((-1, right, right_sems), (1, left, left_sems)):
            at = chip + sign * step
            more = (chip < length - 1) if sign < 0 else (chip > 0)

            @pl.when((at >= 0) & (at < length) & more)
            def _():
                send(block(at), block(at), way, step, peer).wait_send()

    for index in range(length):
        pass_on(index, block(index)).wait_send()
        other = all_ref.at[index * 2 + 1 - core]
        send(other, other, core_sems, index, sibling).wait_recv()


def square_gather(own_ref, all_ref, sems, ctx, fsdp, n_fsdp, passed=None):
    if n_fsdp != 4:
        copies = [
            send(own_ref, all_ref.at[fsdp], sems, j - 1, (ctx, (fsdp + j) % n_fsdp)) for j in range(1, n_fsdp)
        ]
        for copy in copies:
            copy.start()
        yield
        for j, copy in enumerate(copies):
            copy.wait()
            if passed:
                passed(all_ref.at[(fsdp + n_fsdp - j - 1) % n_fsdp], (fsdp + n_fsdp - j - 1) % n_fsdp, None, j)
        return
    first, second, corner = fsdp_neighbours(fsdp)
    half = own_ref.shape[0] // 2
    top, low_half = pl.ds(0, half), pl.ds(half, half)
    to_first, to_second = (ctx, first), (ctx, second)

    def copy(index, owner, part, peer, source=None):
        source = all_ref.at[owner, part] if source is None else source
        return send(source, all_ref.at[owner, part], sems, index, peer)

    starts = [
        copy(0, fsdp, top, to_first, own_ref.at[top]),
        copy(1, fsdp, low_half, to_second, own_ref.at[low_half]),
        copy(2, fsdp, low_half, to_first, own_ref.at[low_half]),
        copy(3, fsdp, top, to_second, own_ref.at[top]),
        copy(4, first, top, to_second),
        copy(5, second, low_half, to_first),
    ]
    arrivals = [
        (0, first, top),
        (1, second, low_half),
        (2, first, low_half),
        (3, second, top),
        (4, corner, top),
        (5, corner, low_half),
    ]
    for each in starts[:4]:
        each.start()
    yield
    for index, owner, part in arrivals:
        copy(index, owner, part, to_first).wait_recv()
        if index < 2:
            starts[4 + index].start()
        if passed:
            passed(all_ref.at[owner, part], owner, part, index)
        yield
    for each in starts:
        each.wait_send()


def run_all(*parts):
    parts = list(parts)
    while parts:
        for part in list(parts):
            try:
                next(part)
            except StopIteration:
                parts.remove(part)


def dma_pair(count):
    return [pltpu.SemaphoreType.DMA((count,)), pltpu.SemaphoreType.DMA((count,))]


def any_specs(count):
    return [pl.BlockSpec(memory_space=pl.ANY)] * count


def params(collective_id=None, **more):
    if collective_id is not None:
        more.update(collective_id=collective_id, has_side_effects=True)
    return pltpu.CompilerParams(vmem_limit_bytes=VMEM_LIMIT, **more)


def passing(own_ref, all_ref, sems, core, fsdp, sibling):
    handed = [send(own_ref, all_ref.at[core, fsdp], sems, 0, sibling)]
    handed[0].start()
    arriving = [send(own_ref, all_ref.at[1 - core, fsdp], sems, 0, sibling)]

    def passed(source, owner, part, index):
        for side, copies in ((core, handed), (1 - core, arriving)):
            target = all_ref.at[side, owner] if part is None else all_ref.at[side, owner, part]
            copies.append(send(source, target, sems, index + 1, sibling))
        handed[-1].start()

    def finish():
        for out, back in zip(handed, arriving):
            out.wait_send()
            back.wait_recv()

    return (passed, finish)


def line_rows(n_ctx, rows):
    def kernel(rows_ref, all_rows, right_s, right_r, left_s, left_r, core_s, core_r, own):
        where = place(n_ctx)
        chip, core, fsdp, length = where
        greet(line_peers(*where))
        mine = pltpu.make_async_copy(rows_ref, all_rows.at[chip * 2 + core], own)
        mine.start()
        run_all(line_gather(rows_ref, all_rows, ((right_s, right_r), (left_s, left_r), (core_s, core_r)), where))
        mine.wait()

    length = n_ctx // 2
    return pl.pallas_call(
        kernel,
        out_shape=jax.ShapeDtypeStruct((n_ctx,) + rows.shape, rows.dtype),
        in_specs=any_specs(1),
        out_specs=pl.BlockSpec(memory_space=pl.ANY),
        scratch_shapes=dma_pair(length) + dma_pair(length) + dma_pair(length) + [pltpu.SemaphoreType.DMA],
        compiler_params=params(0),
        name="line_rows",
    )(rows)


def square_core_gather(n_ctx, n_fsdp, rows):
    def kernel(rows_ref, all_ref, sq_s, sq_r, core_s, core_r, own):
        chip, core, fsdp, _ = place(n_ctx)
        ctx = chip * 2 + core
        sibling = (chip * 2 + 1 - core, fsdp)
        greet([sibling] + fsdp_peers(n_fsdp, ctx, fsdp))
        mine = pltpu.make_async_copy(rows_ref, all_ref.at[core, fsdp], own)
        mine.start()
        passed, finish = passing(rows_ref, all_ref, (core_s, core_r), core, fsdp, sibling)
        run_all(square_gather(rows_ref, all_ref.at[core], (sq_s, sq_r), ctx, fsdp, n_fsdp, passed))
        finish()
        mine.wait()

    return pl.pallas_call(
        kernel,
        out_shape=jax.ShapeDtypeStruct((2, n_fsdp) + rows.shape, rows.dtype),
        in_specs=any_specs(1),
        out_specs=pl.BlockSpec(memory_space=pl.ANY),
        scratch_shapes=dma_pair(max(6, n_fsdp)) + dma_pair(max(7, n_fsdp)) + [pltpu.SemaphoreType.DMA],
        compiler_params=params(1),
        name="square_core_gather",
    )(rows)


def add_into(target, *sources, chunk=64):
    @pl.loop(0, target.shape[0] // chunk)
    def _(step):
        rows = pl.ds(pl.multiple_of(step * chunk, chunk), chunk)
        total = target[rows].astype(jnp.float32)
        for source in sources:
            total = total + source[rows].astype(jnp.float32)
        target[rows] = total.astype(target.dtype)


def square_sum_stages(n_ctx, n_fsdp, partial_ref, out_ref, held, core_in, square_in, load, core_sems, sems):
    rows = partial_ref.shape[-2]
    half = rows // 2
    chip, core, fsdp, _ = place(n_ctx)
    ctx = chip * 2 + core
    sibling = (chip * 2 + 1 - core, fsdp)
    if n_fsdp == 4:
        first, second, corner = fsdp_neighbours(fsdp)
        order = [corner, first, second, fsdp]
    else:
        order = [(fsdp + j) % n_fsdp for j in range(1, n_fsdp + 1)]
    mine = [
        pltpu.make_async_copy(partial_ref.at[core, owner], held.at[owner], load.at[j])
        for j, owner in enumerate(order)
    ]
    others = [
        send(partial_ref.at[1 - core, owner], core_in.at[owner], core_sems, j, sibling)
        for j, owner in enumerate(order)
    ]

    def ready(j):
        mine[j].wait()
        others[j].wait_recv()
        add_into(held.at[order[j]], core_in.at[order[j]])

    def total(parts, sources):
        @pl.loop(0, parts[1] // 64)
        def _(step):
            at = pl.ds(pl.multiple_of(parts[0] + step * 64, 64), 64)
            from_at = pl.ds(pl.multiple_of(step * 64, 64), 64)
            value = held[fsdp, at].astype(jnp.float32)
            for j in sources:
                value = value + square_in[j, from_at].astype(jnp.float32)
            out_ref[at] = value

    def begin():
        greet([sibling] + fsdp_peers(n_fsdp, ctx, fsdp))
        for j in range(n_fsdp):
            others[j].start()
            mine[j].start()

    if n_fsdp != 4:
        copies = [
            send(held.at[order[j]], square_in.at[j], sems, j, (ctx, order[j])) for j in range(n_fsdp - 1)
        ]

        def spread():
            for j in range(n_fsdp):
                ready(j)
                if j < n_fsdp - 1:
                    copies[j].start()

        def finish():
            for copy in copies:
                copy.wait()
            total((0, rows), range(n_fsdp - 1))
            for each in others:
                each.wait_send()

        return [begin, spread, finish]

    top, low_half = pl.ds(0, half), pl.ds(half, half)
    to_first, to_second = (ctx, first), (ctx, second)

    def copy(index, owner, part, peer):
        return send(held.at[owner, part], square_in.at[index], sems, index, peer)

    copies = [
        copy(0, corner, top, to_first),
        copy(1, corner, low_half, to_second),
        copy(2, first, top, to_first),
        copy(3, second, low_half, to_second),
        copy(4, second, top, to_second),
        copy(5, first, low_half, to_first),
    ]

    def spread():
        ready(0)
        copies[0].start()
        copies[1].start()
        ready(1)
        copies[2].start()
        ready(2)
        copies[3].start()
        ready(3)

    def pass_on():
        copies[0].wait_recv()
        add_into(held.at[second, top], square_in.at[0])
        copies[4].start()
        copies[1].wait_recv()
        add_into(held.at[first, low_half], square_in.at[1])
        copies[5].start()

    def finish():
        for j in range(2, 6):
            copies[j].wait_recv()
        total((0, half), (2, 4))
        total((half, half), (3, 5))
        for each in copies:
            each.wait_send()
        for each in others:
            each.wait_send()

    return [begin, spread, pass_on, finish]


def corner_sum_stages(n_ctx, partial_ref, out_ref, held, square_in, load, sems):
    half = partial_ref.shape[1] // 2
    chip, core, fsdp, _ = place(n_ctx)
    ctx = chip * 2 + core
    first, second, corner = fsdp_neighbours(fsdp)
    top, low_half = pl.ds(0, half), pl.ds(half, half)
    to_first, to_second = (ctx, first), (ctx, second)

    def copy(index, source, peer):
        return send(source, square_in.at[index], sems, index, peer)

    copies = [
        copy(0, partial_ref.at[corner, top], to_first),
        copy(1, partial_ref.at[corner, low_half], to_second),
        copy(2, partial_ref.at[first, top], to_first),
        copy(3, partial_ref.at[second, low_half], to_second),
        copy(4, held.at[0], to_second),
        copy(5, held.at[1], to_first),
    ]
    mine = [
        pltpu.make_async_copy(partial_ref.at[second, top], held.at[0], load.at[0]),
        pltpu.make_async_copy(partial_ref.at[first, low_half], held.at[1], load.at[1]),
        pltpu.make_async_copy(partial_ref.at[fsdp, top], held.at[2], load.at[2]),
        pltpu.make_async_copy(partial_ref.at[fsdp, low_half], held.at[3], load.at[3]),
    ]

    starts = [
        [copies[0].start, copies[1].start],
        [copies[2].start, mine[1].start],
        [copies[3].start, mine[0].start],
        [mine[2].start, mine[3].start],
    ]

    def pass_on():
        for index in range(2):
            mine[index].wait()
            copies[index].wait_recv()
            add_into(held.at[index], square_in.at[index])
            copies[4 + index].start()

    def finish():
        for part, sources in ((0, (2, 4)), (1, (3, 5))):
            mine[2 + part].wait()
            for j in sources:
                copies[j].wait_recv()

            @pl.loop(0, half // 64)
            def _(step):
                at = pl.ds(pl.multiple_of(step * 64, 64), 64)
                value = held[2 + part, at].astype(jnp.float32)
                for j in sources:
                    value = value + square_in[j, at].astype(jnp.float32)
                out_ref[pl.ds(pl.multiple_of(part * half + step * 64, 64), 64)] = value

        for each in copies:
            each.wait_send()

    return [starts, pass_on, finish]


def corner_sum_scratch(partial):
    _, rows, columns = partial.shape
    return [
        pltpu.VMEM((4, rows // 2, columns), partial.dtype),
        pltpu.VMEM((6, rows // 2, columns), partial.dtype),
        pltpu.SemaphoreType.DMA((4,)),
    ] + dma_pair(6)


def square_sum_scratch(n_fsdp, partial):
    rows, columns = partial.shape[-2:]
    pieces = (6, rows // 2, columns) if n_fsdp == 4 else (n_fsdp - 1, rows, columns)
    return (
        [
            pltpu.VMEM((n_fsdp, rows, columns), partial.dtype),
            pltpu.VMEM((n_fsdp, rows, columns), partial.dtype),
            pltpu.VMEM(pieces, partial.dtype),
            pltpu.SemaphoreType.DMA((n_fsdp,)),
        ]
        + dma_pair(n_fsdp)
        + dma_pair(max(6, n_fsdp))
    )


def square_sum(n_ctx, n_fsdp, partial):
    def kernel(partial_ref, out_ref, held, core_in, square_in, load, core_s, core_r, sq_s, sq_r):
        for stage in square_sum_stages(
            n_ctx, n_fsdp, partial_ref, out_ref, held, core_in, square_in, load, (core_s, core_r), (sq_s, sq_r)
        ):
            stage()

    return pl.pallas_call(
        kernel,
        out_shape=jax.ShapeDtypeStruct(partial.shape[-2:], jnp.float32),
        in_specs=any_specs(1),
        out_specs=pl.BlockSpec(memory_space=pltpu.VMEM),
        scratch_shapes=square_sum_scratch(n_fsdp, partial),
        compiler_params=params(1),
        name="square_sum",
    )(partial)


def line_sum_steps(n_ctx, partial_ref, out_ref, held, core_in, right_in, left_in, load, core_sems, right_sems, left_sems):
    rows = partial_ref.shape[1]
    where = place(n_ctx)
    chip, core, fsdp, length = where
    sibling, right, left = line_peers(*where)
    order = [(chip + length - 1 - j) % length for j in range(length)]
    mine, others = [], []
    for j, owner in enumerate(order):
        mine.append(pltpu.make_async_copy(partial_ref.at[owner * 2 + core], held.at[owner], load.at[j]))
        others.append(send(partial_ref.at[owner * 2 + 1 - core], core_in.at[owner], core_sems, j, sibling))
        others[-1].start()
        mine[-1].start()
    yield
    for j, owner in enumerate(order):
        mine[j].wait()
        others[j].wait_recv()
        add_into(held.at[owner], core_in.at[owner])
    ways = ((1, right, right_in, right_sems), (-1, left, left_in, left_sems))
    for step in range(length - 1):
        for sign, peer, arrived, sems in ways:
            block = chip + sign * (length - 1 - step)
            inside = (block >= 0) & (block < length)
            came = (chip >= 1) if sign > 0 else (chip < length - 1)
            if step > 0:

                @pl.when(inside & came)
                def _():
                    send(held.at[block], arrived.at[step - 1], sems, step - 1, peer).wait_recv()
                    add_into(held.at[block], arrived.at[step - 1])

            @pl.when(inside)
            def _():
                send(held.at[block], arrived.at[step], sems, step, peer).start()

        yield
    last = length - 2
    for sign, peer, arrived, sems in ways:
        came = (chip >= 1) if sign > 0 else (chip < length - 1)

        @pl.when(came)
        def _():
            send(held.at[chip], arrived.at[last], sems, last, peer).wait_recv()
            add_into(held.at[chip], arrived.at[last])

    @pl.loop(0, rows // 64)
    def _(step):
        at = pl.ds(pl.multiple_of(step * 64, 64), 64)
        out_ref[at] = held[chip, at].astype(jnp.float32)

    for step in range(length - 1):
        for sign, peer, arrived, sems in ways:
            block = chip + sign * (length - 1 - step)

            @pl.when((block >= 0) & (block < length))
            def _():
                send(held.at[block], arrived.at[step], sems, step, peer).wait_send()

    for each in others:
        each.wait_send()


def line_sum_scratch(n_ctx, partial):
    rows, columns = partial.shape[-2:]
    length = n_ctx // 2
    return [
        pltpu.VMEM((length, rows, columns), partial.dtype),
        pltpu.VMEM((length, rows, columns), partial.dtype),
        pltpu.VMEM((length - 1, rows, columns), partial.dtype),
        pltpu.VMEM((length - 1, rows, columns), partial.dtype),
        pltpu.SemaphoreType.DMA((length,)),
    ] + dma_pair(length) * 3


def line_sum(n_ctx, partial):
    def kernel(partial_ref, out_ref, held, core_in, right_in, left_in, load, core_s, core_r, right_s, right_r, left_s, left_r):
        greet(line_peers(*place(n_ctx)))
        run_all(
            line_sum_steps(
                n_ctx, partial_ref, out_ref, held, core_in, right_in, left_in, load,
                (core_s, core_r), (right_s, right_r), (left_s, left_r),
            )
        )

    return pl.pallas_call(
        kernel,
        out_shape=jax.ShapeDtypeStruct(partial.shape[-2:], jnp.float32),
        in_specs=any_specs(1),
        out_specs=pl.BlockSpec(memory_space=pltpu.VMEM),
        scratch_shapes=line_sum_scratch(n_ctx, partial),
        compiler_params=params(5),
        name="line_sum",
    )(partial)


def attention_sums(n_ctx, partial, rows, grads, attended, grad_cols):
    total, features = rows.shape
    parts, _, own = attended.shape
    wide = grads.shape[1]
    depth = features // 4
    weight_shape = jax.ShapeDtypeStruct((4, depth, wide + own), jnp.bfloat16)
    inputs = (rows, grads, attended, grad_cols)

    def kernel(partial_ref, *refs):
        inputs_refs, refs = refs[:4], refs[4:]
        out_ref, weight_ref, rows_v, grads_v, attended_v, cols_v, weights, in_sem, *refs = refs
        line_refs, refs = refs[:5], refs[5:]
        core_s, core_r, right_s, right_r, left_s, left_r, *refs = refs
        held, square_in, load, sq_s, sq_r = refs
        where = place(n_ctx)
        chip, core, fsdp, _ = where
        loads = [
            pltpu.make_async_copy(a, b, in_sem.at[j])
            for j, (a, b) in enumerate(zip(inputs_refs, (rows_v, grads_v, attended_v, cols_v)))
        ]
        for each in loads:
            each.start()
        greet(line_peers(*where) + fsdp_peers(4, chip * 2 + core, fsdp))
        line = line_sum_steps(
            n_ctx, partial_ref, out_ref, *line_refs, (core_s, core_r), (right_s, right_r), (left_s, left_r)
        )
        next(line)
        starts, pass_on, finish = corner_sum_stages(n_ctx, weights, weight_ref, held, square_in, load, (sq_s, sq_r))
        for each in loads:
            each.wait()
        first, second, corner = fsdp_neighbours(fsdp)
        for number, owner in enumerate((corner, first, second, fsdp)):
            at = pl.ds(pl.multiple_of(owner * depth, depth), depth)
            weights[owner, :, :wide] = low(mm(rows_v[:, at], grads_v[...], CONTRACT_FIRST))
            for q in range(depth // own):
                weights[owner, q * own : (q + 1) * own, wide:] = low(
                    mm(attended_v[owner * (depth // own) + q], cols_v[...], CONTRACT_FIRST)
                )
            for start in starts[number]:
                start()
            if number < 2:
                next(line)
        pass_on()
        run_all(line)
        finish()

    return pl.pallas_call(
        kernel,
        out_shape=[
            jax.ShapeDtypeStruct(partial.shape[-2:], jnp.float32),
            jax.ShapeDtypeStruct(weight_shape.shape[1:], jnp.float32),
        ],
        in_specs=any_specs(5),
        out_specs=[pl.BlockSpec(memory_space=pltpu.VMEM)] * 2,
        scratch_shapes=[pltpu.VMEM(a.shape, a.dtype) for a in inputs]
        + [pltpu.VMEM(weight_shape.shape, weight_shape.dtype), pltpu.SemaphoreType.DMA((4,))]
        + line_sum_scratch(n_ctx, partial)
        + corner_sum_scratch(weight_shape),
        compiler_params=params(4),
        cost_estimate=pl.CostEstimate(
            flops=2 * total * features * (wide + own), bytes_accessed=16 * 1024 * 1024, transcendentals=0
        ),
        name="attention_sums",
    )(partial, *inputs)


def sum_everywhere(n_ctx, n_fsdp, values):
    block = values.shape[1:]

    def kernel(values_ref, out_ref, along_ctx, along_fsdp, result, ctx_s, ctx_r, fsdp_s, fsdp_r, back_s, back_r):
        ctx = lax.axis_index("ctx")
        fsdp = lax.axis_index("fsdp")
        ctx_peers = [((ctx + j) % n_ctx, fsdp) for j in range(1, n_ctx)]
        fsdp_peers = [(ctx, (fsdp + j) % n_fsdp) for j in range(1, n_fsdp)]
        greet(ctx_peers + fsdp_peers)

        def exchange(copies):
            for copy in copies:
                copy.start()
            for copy in copies:
                copy.wait()

        def total(slots, count):
            value = slots[0]
            for j in range(1, count):
                value = value + slots[j]
            return value

        along_ctx[ctx] = values_ref[ctx]
        exchange(
            [
                send(values_ref.at[peer[0]], along_ctx.at[ctx], (ctx_s, ctx_r), j, peer)
                for j, peer in enumerate(ctx_peers)
            ]
        )
        along_fsdp[fsdp] = total(along_ctx, n_ctx)
        exchange(
            [
                send(along_fsdp.at[fsdp], along_fsdp.at[fsdp], (fsdp_s, fsdp_r), j, peer)
                for j, peer in enumerate(fsdp_peers)
            ]
        )
        result[ctx] = total(along_fsdp, n_fsdp)
        exchange(
            [send(result.at[ctx], result.at[ctx], (back_s, back_r), j, peer) for j, peer in enumerate(ctx_peers)]
        )
        out_ref[...] = result[...]

    return pl.pallas_call(
        kernel,
        out_shape=jax.ShapeDtypeStruct(values.shape, values.dtype),
        in_specs=[pl.BlockSpec(memory_space=pltpu.VMEM)],
        out_specs=pl.BlockSpec(memory_space=pltpu.VMEM),
        scratch_shapes=[
            pltpu.VMEM((n_ctx,) + block, values.dtype),
            pltpu.VMEM((n_fsdp,) + block, values.dtype),
            pltpu.VMEM((n_ctx,) + block, values.dtype),
        ]
        + dma_pair(n_ctx)
        + dma_pair(n_fsdp)
        + dma_pair(n_ctx),
        compiler_params=params(2),
        name="sum_everywhere",
    )(values)


def hidden_units(here, back, gate_ref, up_ref, down_ref):
    gate = mm(here, gate_ref[0], CONTRACT_LAST)
    up = mm(here, up_ref[0], CONTRACT_LAST)
    grad_hidden = mm(back, down_ref[0], CONTRACT_LAST)
    sigmoid = jax.nn.sigmoid(gate)
    activated = gate * sigmoid
    return (
        low(activated * up),
        low(grad_hidden * up * sigmoid * (1.0 + gate * (1.0 - sigmoid))),
        low(grad_hidden * activated),
    )


def ffn_forward(rows, planes, core, n_own, chunk=256):
    blocks, _, tokens, features = rows.shape
    total = blocks * tokens
    steps = n_own // chunk
    group = max(1, 256 // tokens)

    def kernel(core_ref, rows_ref, gate_ref, up_ref, down_ref, *outs):
        for at in range(0, blocks, group):
            here = rows_ref[at : at + group, 0].reshape(group * tokens, features)
            back = rows_ref[at : at + group, 1].reshape(group * tokens, features)
            span = pl.ds(at * tokens, group * tokens)
            for out, value in zip(outs, hidden_units(here, back, gate_ref, up_ref, down_ref)):
                out[span] = value

    def weight_spec(plane):
        return pl.BlockSpec((1, chunk, features), lambda j, core_ref: (plane, core_ref[0] * steps + j, 0))

    act = jax.ShapeDtypeStruct((total, n_own), jnp.bfloat16)
    act_spec = pl.BlockSpec((total, chunk), lambda j, core_ref: (0, j))
    return pl.pallas_call(
        kernel,
        grid_spec=pltpu.PrefetchScalarGridSpec(
            num_scalar_prefetch=1,
            grid=(steps,),
            in_specs=[
                pl.BlockSpec(rows.shape, lambda j, core_ref: (0, 0, 0, 0), pipeline_mode=pl.Buffered(1)),
                weight_spec(0),
                weight_spec(1),
                weight_spec(2),
            ],
            out_specs=[act_spec, act_spec, act_spec],
        ),
        out_shape=[act, act, act],
        compiler_params=params(),
        cost_estimate=pl.CostEstimate(
            flops=6 * total * n_own * features, bytes_accessed=30 * 1024 * 1024, transcendentals=total * n_own
        ),
        name="ffn_forward",
    )(core, rows, planes, planes, planes)


def mirror_gather(all_ref, arrivals, sems, pass_sems, ctx, core, fsdp, sibling):
    first, second, corner = fsdp_neighbours(fsdp)
    half = all_ref.shape[2] // 2
    parts = [pl.ds(0, half), pl.ds(half, half)]
    to_first, to_second = (ctx, first), (ctx, second)

    def copy(index, owner, part, peer):
        place_ref = all_ref.at[core, owner, parts[part]]
        return send(place_ref, place_ref, sems, index, peer)

    copies = [
        copy(0, fsdp, 0, to_first),
        copy(1, fsdp, 0, to_second),
        copy(2, fsdp, 1, to_first),
        copy(3, fsdp, 1, to_second),
        copy(4, first, 0, to_second),
        copy(5, second, 1, to_first),
    ]
    passes = [(fsdp, 0), (fsdp, 1), (first, 0), (second, 0), (first, 1), (second, 1), (corner, 0), (corner, 1)]

    def passing_copy(number, side):
        owner, part = passes[number]
        place_ref = all_ref.at[side, owner, parts[part]]
        return send(place_ref, place_ref, pass_sems, number, sibling)

    for part in range(2):
        arrivals[part].wait_recv()
        copies[2 * part].start()
        copies[2 * part + 1].start()
        passing_copy(part, core).start()
        yield
    for index, number, then in ((0, 2, 4), (1, 3, None), (2, 4, None), (3, 5, 5), (4, 6, None), (5, 7, None)):
        owner, part = passes[number]
        copy(index, owner, part, to_first).wait_recv()
        if then is not None:
            copies[then].start()
        passing_copy(number, core).start()
        yield
    for each in copies:
        each.wait_send()
    for number in range(8):
        passing_copy(number, core).wait_send()
        passing_copy(number, 1 - core).wait_recv()


def ffn_rows(n_ctx, own, planes, attended, n_own, chunk=256, wide=512):
    n_fsdp = 4
    size, features = own.shape
    tokens = size // 2
    total = 2 * n_fsdp * tokens

    def kernel(
        own_ref, planes_ref, attended_ref, all_ref, mirror_ref, hidden_a, hidden_b, hidden_c, partial_ref, heads_ref,
        rows, weights, hidden, partial, core_in, load, sq_s, sq_r, core_s, core_r, far_s, far_r, mi_s, mi_r, mc_s, mc_r, sum_s, sum_r, out_sem,
        ri_s, ri_r, le_s, le_r, lc_s, lc_r, heads_sem,
    ):
        chip, core, fsdp, length = place(n_ctx)
        ctx = chip * 2 + core
        sibling = (chip * 2 + 1 - core, fsdp)
        mirror = ((length - 1 - chip) * 2 + core, fsdp)
        first, second, corner = fsdp_neighbours(fsdp)
        where = (chip, core, fsdp, length)
        greet([mirror] + line_peers(*where) + fsdp_peers(n_fsdp, ctx, fsdp))
        line = line_gather(attended_ref, heads_ref, ((ri_s, ri_r), (le_s, le_r), (lc_s, lc_r)), where)
        heads_own = pltpu.make_async_copy(attended_ref, heads_ref.at[ctx], heads_sem)
        heads_own.start()
        mine = pltpu.make_async_copy(own_ref, rows.at[core, fsdp], load.at[3])
        mine.start()
        start = pl.multiple_of(core * n_own, n_own)
        loads = [
            pltpu.make_async_copy(planes_ref.at[p, pl.ds(start, n_own)], weights.at[p], load.at[p]) for p in range(3)
        ]
        handed, arriving = [], []

        def hand(source, owner, part, index):
            for side, copies in ((core, handed), (1 - core, arriving)):
                target = rows.at[side, owner] if part is None else rows.at[side, owner, part]
                copies.append(send(source, target, (core_s, core_r), index + 1, sibling))
            handed[-1].start()

        gathering = square_gather(own_ref, rows.at[core], (sq_s, sq_r), ctx, fsdp, n_fsdp, hand)
        next(gathering)
        hand(own_ref, fsdp, None, -1)
        for each in loads:
            each.start()
        far = [
            send(
                own_ref.at[pl.ds(part * tokens, tokens)],
                mirror_ref.at[core, fsdp, pl.ds(part * tokens, tokens)],
                (far_s, far_r),
                part,
                mirror,
            )
            for part in range(2)
        ]
        for each in far:
            each.start()
        mirroring = mirror_gather(mirror_ref, far, (mi_s, mi_r), (mc_s, mc_r), ctx, core, fsdp, sibling)
        outs, summing, sums = [], [], []

        def add_up(number, owner):
            summing[number].wait_recv()
            add_into(partial.at[number % 2, core], core_in.at[number])
            sums.append(
                pltpu.make_async_copy(partial.at[number % 2, core], partial_ref.at[owner], out_sem.at[number % 2, 8])
            )
            sums[-1].start()

        def group(number, owner):
            slot = number % 2
            if number >= 2:
                for each in outs[number - 2]:
                    each.wait()
                summing[number - 2].wait_send()
                sums[number - 2].wait()
            here = jnp.concatenate([rows[0, owner, :tokens], rows[1, owner, :tokens]])
            back = jnp.concatenate([rows[0, owner, tokens:], rows[1, owner, tokens:]])

            @pl.loop(0, n_own // chunk)
            def _(step):
                at = pl.ds(pl.multiple_of(step * chunk, chunk), chunk)
                parts = [weights.at[pl.ds(p, 1), at] for p in range(3)]
                for q, value in enumerate(hidden_units(here, back, *parts)):
                    hidden[slot, q, :, at] = value

            @pl.loop(0, features // wide)
            def _(step):
                at = pl.ds(pl.multiple_of(step * wide, wide), wide)
                out = low(mm(hidden[slot, 0], weights[2, :, at]))
                below = low(mm(hidden[slot, 1], weights[0, :, at]) + mm(hidden[slot, 2], weights[1, :, at]))
                for k in range(2):
                    partial[slot, k, :tokens, at] = out[k * tokens : (k + 1) * tokens]
                    partial[slot, k, tokens:, at] = below[k * tokens : (k + 1) * tokens]

            pairs = []
            summing.append(send(partial.at[slot, 1 - core], core_in.at[number], (sum_s, sum_r), number, sibling))
            summing[-1].start()
            for k in range(2):
                pairs.append((rows.at[k, owner], all_ref.at[k, owner]))
                at = pl.ds(pl.multiple_of((k * n_fsdp + owner) * tokens, tokens), tokens)
                for q, target in enumerate((hidden_a, hidden_b, hidden_c)):
                    pairs.append((hidden.at[slot, q, pl.ds(k * tokens, tokens)], target.at[at]))
            outs.append(
                [pltpu.make_async_copy(a, b, out_sem.at[slot, j]) for j, (a, b) in enumerate(pairs)]
            )
            for each in outs[-1]:
                each.start()

        mine.wait()
        arriving[0].wait_recv()
        for each in loads:
            each.wait()
        group(0, fsdp)
        for _ in range(4):
            next(gathering)
        arriving[1].wait_recv()
        arriving[3].wait_recv()
        group(1, first)
        add_up(0, fsdp)
        next(mirroring)
        next(line)
        for _ in range(2):
            next(gathering)
        arriving[2].wait_recv()
        arriving[4].wait_recv()
        group(2, second)
        add_up(1, first)
        for _ in range(3):
            next(mirroring)
        next(line)
        arriving[5].wait_recv()
        arriving[6].wait_recv()
        group(3, corner)
        next(line)
        add_up(2, second)
        next(mirroring)
        add_up(3, corner)
        run_all(mirroring, line, gathering)
        heads_own.wait()
        for each in handed:
            each.wait_send()
        for each in far:
            each.wait_send()
        for each in outs[2] + outs[3] + sums[2:]:
            each.wait()
        for each in summing[2:]:
            each.wait_send()

    act = jax.ShapeDtypeStruct((total, n_own), own.dtype)
    all_rows = jax.ShapeDtypeStruct((2, n_fsdp) + own.shape, own.dtype)
    return pl.pallas_call(
        kernel,
        in_specs=any_specs(3),
        out_specs=any_specs(7),
        out_shape=[
            all_rows,
            all_rows,
            act,
            act,
            act,
            jax.ShapeDtypeStruct((n_fsdp,) + own.shape, own.dtype),
            jax.ShapeDtypeStruct((n_ctx,) + attended.shape, attended.dtype),
        ],
        scratch_shapes=[
            pltpu.VMEM((2, n_fsdp) + own.shape, own.dtype),
            pltpu.VMEM((3, n_own, features), own.dtype),
            pltpu.VMEM((2, 3, 2 * tokens, n_own), own.dtype),
            pltpu.VMEM((2, 2) + own.shape, own.dtype),
            pltpu.VMEM((n_fsdp,) + own.shape, own.dtype),
            pltpu.SemaphoreType.DMA((4,)),
        ]
        + dma_pair(6)
        + dma_pair(7)
        + dma_pair(2)
        + dma_pair(6)
        + dma_pair(8)
        + dma_pair(4)
        + [pltpu.SemaphoreType.DMA((2, 9))]
        + dma_pair(n_ctx // 2) * 3
        + [pltpu.SemaphoreType.DMA],
        compiler_params=params(6),
        cost_estimate=pl.CostEstimate(
            flops=12 * total * n_own * features, bytes_accessed=50 * 1024 * 1024, transcendentals=total * n_own
        ),
        name="ffn_rows",
    )(own, planes, attended)


def ffn_weights(n_ctx, n_fsdp, partial, rows, rows_mirror, hidden, planes, n_own, chunk=256):
    blocks, _, tokens, features = rows.shape
    total = blocks * tokens
    steps = n_own // chunk
    group = max(1, 256 // tokens)
    half = features // 2
    sides = n_ctx // 4
    wide = half // sides
    fused = partial is not None
    early = steps // 2 if fused else 0
    assert not fused or sides == 2

    def kernel(*refs):
        rows_ref, refs = refs[0], refs[1:]
        mirror_refs, refs = refs[: len(rows_mirror)], refs[len(rows_mirror) :]
        mirror_blocks = [ref.at[b] for ref in mirror_refs for b in range(ref.shape[0])]
        hidden_ref, grad_gate_ref, grad_up_ref, planes_ref, *refs = refs
        if fused:
            partial_ref, weight_ref, out_ref, early_ref, *refs = refs
        else:
            weight_ref, *refs = refs
        mirror, (weights, weight_sems), refs = refs[:3], refs[3:5], refs[5:]
        chip, core, _, length = place(n_ctx)
        side = chip // sides
        step = pl.program_id(0)
        stages = []
        if fused:
            keep, give, take, side_s, side_r, held, square_in, load, sq_s, sq_r = refs
            member = chip % 2
            other = (chip + 1 - 2 * member) * 2 + core
            crossing = [
                [
                    send(
                        give.at[j, plane],
                        take.at[j, plane],
                        (side_s, side_r),
                        3 * j + plane,
                        (other, lax.axis_index("fsdp")),
                    )
                    for plane in range(3)
                ]
                for j in range(early)
            ]
            starts, *stages = corner_sum_stages(n_ctx, partial_ref, out_ref, held, square_in, load, (sq_s, sq_r))

        def fetch(at, slot):
            start = pl.multiple_of((core * steps + at) * chunk, chunk)
            return pltpu.make_async_copy(planes_ref.at[:, pl.ds(start, chunk)], weights.at[slot], weight_sems.at[slot])

        @pl.when(step == 0)
        def _():
            fetch(0, 0).start()
            if fused:
                fsdp = lax.axis_index("fsdp")
                greet(fsdp_peers(4, chip * 2 + core, fsdp) + [(other, fsdp)])
                for start in sum(starts, []):
                    start()

        @pl.when(step + 1 < steps)
        def _():
            fetch(step + 1, (step + 1) % 2).start()

        slot = step % 2
        fetch(step, slot).wait()
        gate_ref, up_ref, down_ref = (weights.at[slot, pl.ds(plane, 1)] for plane in range(3))
        for at in range(0, blocks, group):
            here = jnp.concatenate([ref[0] for ref in mirror_blocks[at : at + group]])
            back = jnp.concatenate([ref[1] for ref in mirror_blocks[at : at + group]])
            span = pl.ds(at * tokens, group * tokens)
            for out, value in zip(mirror, hidden_units(here, back, gate_ref, up_ref, down_ref)):
                out[span] = value

        lefts = ((grad_gate_ref, mirror[1], 0), (grad_up_ref, mirror[2], 0), (hidden_ref, mirror[0], 1))
        for plane, (left, left_mirror, which) in enumerate(lefts):
            left = left[...]
            left_mirror = left_mirror[...]
            for z in range(sides):
                cols = pl.ds(pl.multiple_of(side * half + z * wide, wide), wide)
                right = rows_ref[:, which, :, cols].reshape(total, wide)
                right_mirror = jnp.concatenate([ref[which, :, cols] for ref in mirror_blocks])
                value = mm(left, right, CONTRACT_FIRST) + mm(left_mirror, right_mirror, CONTRACT_FIRST)
                if not fused:
                    weight_ref[z, plane] = low(value)
                    continue

                @pl.when((step < early) & (z == member))
                def _():
                    keep[step % early, plane] = value

                @pl.when((step < early) & (z != member))
                def _():
                    give[step % early, plane] = low(value)

                @pl.when(step >= early)
                def _():
                    weight_ref[z, plane] = low(value)

            for j in range(early):

                @pl.when(step == j)
                def _():
                    crossing[j][plane].start()

        for at, stage in ((1, 0), (steps - 1, 1)):
            if stage < len(stages):

                @pl.when(step == min(at, steps - 1))
                def _():
                    stages[stage]()

        if fused:

            @pl.when(step == steps - 1)
            def _():
                for j in range(early):
                    for plane in range(3):
                        crossing[j][plane].wait()
                        early_ref[plane, j * chunk : (j + 1) * chunk] = low(
                            keep[j, plane] + take[j, plane].astype(jnp.float32)
                        )

    act_spec = pl.BlockSpec((total, chunk), lambda j: (0, j))
    once = dict(pipeline_mode=pl.Buffered(1))
    operands = [rows, *rows_mirror, *hidden, planes]
    in_specs = [whole_block(rows.shape, **once)] + [whole_block(part.shape, **once) for part in rows_mirror]
    in_specs += [act_spec] * 3 + any_specs(1)
    out_specs = [pl.BlockSpec((sides, 3, chunk, wide), lambda j: (0, 0, jnp.maximum(j - early, 0), 0))]
    out_shape = [jax.ShapeDtypeStruct((sides, 3, n_own - early * chunk, wide), jnp.bfloat16)]
    scratch = [pltpu.VMEM((total, chunk), jnp.bfloat16)] * 3
    scratch += [pltpu.VMEM((2, 3, chunk, features), jnp.bfloat16), pltpu.SemaphoreType.DMA((2,))]
    if fused:
        operands.append(partial)
        in_specs += any_specs(1)
        out_specs.append(whole_block(partial.shape[-2:], **once))
        out_shape.append(jax.ShapeDtypeStruct(partial.shape[-2:], jnp.float32))
        out_specs.append(whole_block((3, early * chunk, wide), **once))
        out_shape.append(jax.ShapeDtypeStruct((3, early * chunk, wide), jnp.bfloat16))
        scratch.append(pltpu.VMEM((early, 3, chunk, wide), jnp.float32))
        scratch += [pltpu.VMEM((early, 3, chunk, wide), jnp.bfloat16)] * 2 + dma_pair(3 * early)
        scratch += corner_sum_scratch(partial)
    return pl.pallas_call(
        kernel,
        grid=(steps,),
        in_specs=in_specs,
        out_specs=out_specs,
        out_shape=out_shape,
        scratch_shapes=scratch,
        compiler_params=params(3) if fused else params(),
        cost_estimate=pl.CostEstimate(
            flops=12 * total * n_own * features, bytes_accessed=50 * 1024 * 1024, transcendentals=total * n_own
        ),
        name="ffn_weights",
    )(*operands)


def ffn_back(hidden, grad_gate, grad_up, planes, core, blocks, wide=512):
    total, n_own = hidden.shape
    features = planes.shape[2]
    tokens = total // blocks

    def kernel(core_ref, hidden_ref, grad_gate_ref, grad_up_ref, gate_ref, up_ref, down_ref, out_ref):
        out = mm(hidden_ref[...], down_ref[0])
        out_ref[:, 0] = low(out).reshape(blocks, tokens, wide)
        back = mm(grad_gate_ref[...], gate_ref[0]) + mm(grad_up_ref[...], up_ref[0])
        out_ref[:, 1] = low(back).reshape(blocks, tokens, wide)

    def weight_spec(plane):
        return pl.BlockSpec((1, n_own, wide), lambda j, core_ref: (plane, core_ref[0], j))

    act_spec = pl.BlockSpec((total, n_own), lambda j, core_ref: (0, 0), pipeline_mode=pl.Buffered(1))
    return pl.pallas_call(
        kernel,
        grid_spec=pltpu.PrefetchScalarGridSpec(
            num_scalar_prefetch=1,
            grid=(features // wide,),
            in_specs=[act_spec, act_spec, act_spec, weight_spec(0), weight_spec(1), weight_spec(2)],
            out_specs=pl.BlockSpec((blocks, 2, tokens, wide), lambda j, core_ref: (0, 0, 0, j)),
        ),
        out_shape=jax.ShapeDtypeStruct((blocks, 2, tokens, features), jnp.bfloat16),
        compiler_params=params(),
        cost_estimate=pl.CostEstimate(
            flops=6 * total * n_own * features, bytes_accessed=30 * 1024 * 1024, transcendentals=0
        ),
        name="ffn_back",
    )(core, hidden, grad_gate, grad_up, planes, planes, planes)


SPAN = 256


def ctx_peers(n_ctx):
    ctx = lax.axis_index("ctx")
    fsdp = lax.axis_index("fsdp")
    return [((ctx + j) % n_ctx, fsdp) for j in range(1, n_ctx)]


def deal(n_ctx, block, target, landed, sems, own_sem):
    ctx = lax.axis_index("ctx")
    fsdp = lax.axis_index("fsdp")

    @pl.when(target != ctx)
    def _():
        send(block, landed.at[ctx], sems, (target - ctx + n_ctx) % n_ctx, (target, fsdp)).start()

    @pl.when(target == ctx)
    def _():
        pltpu.make_async_copy(block, landed.at[ctx], own_sem).start()


def dealt(n_ctx, block, landed, sems, own_sem):
    ctx = lax.axis_index("ctx")
    pltpu.make_async_copy(block, landed.at[ctx], own_sem).wait()
    for j, peer in enumerate(ctx_peers(n_ctx)):
        copy = send(block, landed.at[(ctx + n_ctx - j - 1) % n_ctx], sems, j + 1, peer)
        copy.wait_send()
        copy.wait_recv()


def turn(values, cosine, sine):
    return values * cosine + pltpu.roll(values, HEAD_DIM // 2, 1) * sine


def attention_forward(n_ctx, rows, w_qkv, cosine, sine, place_column, place_row, heads):
    total, features = rows.shape
    own = heads * HEAD_DIM
    steps = total // SPAN
    length = total // n_ctx
    scale = HEAD_DIM ** (-0.5)

    def kernel(
        rows_ref, w_ref, cosine_ref, sine_ref, column_ref, row_ref,
        query_ref, key_ref, value_ref, out_ref, log_ref, landed, deal_s, deal_r, own_sem,
    ):
        step = pl.program_id(0)

        @pl.when(step == 0)
        def _():
            greet(ctx_peers(n_ctx))

        span = pl.ds(pl.multiple_of(step * SPAN, SPAN), SPAN)
        qkv = mm(rows_ref[...], w_ref[...])
        cosine = cosine_ref[span]
        sine = sine_ref[span]
        for h in range(heads):
            at = slice(h * HEAD_DIM, (h + 1) * HEAD_DIM)
            query_ref[span, at] = low(turn(qkv[:, at], cosine, sine))
            key_ref[span, at] = low(turn(qkv[:, own + h * HEAD_DIM : own + (h + 1) * HEAD_DIM], cosine, sine))
        value_ref[span] = low(qkv[:, 2 * own :])

        @pl.when(step == steps - 1)
        def _():
            @pl.loop(0, steps)
            def _(block):
                here = pl.ds(pl.multiple_of(block * SPAN, SPAN), SPAN)
                for h in range(heads):
                    at = slice(h * HEAD_DIM, (h + 1) * HEAD_DIM)
                    scores = mm(query_ref[here, at], key_ref[:, at], CONTRACT_LAST) * scale
                    scores = jnp.where(column_ref[here] >= row_ref[...], scores, MASKED)
                    highest = jnp.max(scores, axis=-1, keepdims=True)
                    exponent = jnp.exp(scores - highest)
                    sums = jnp.sum(exponent, axis=-1, keepdims=True)
                    out_ref[here, at] = low(mm(low(exponent * (1.0 / sums)), value_ref[:, at]))
                    log_ref[h, here] = highest + jnp.log(sums)
                for r in range(SPAN // length):
                    mine = out_ref.at[pl.ds(pl.multiple_of(block * SPAN + r * length, length), length)]
                    deal(n_ctx, mine, block * (SPAN // length) + r, landed, (deal_s, deal_r), own_sem)

            dealt(n_ctx, out_ref.at[pl.ds(0, length)], landed, (deal_s, deal_r), own_sem)

    act = jax.ShapeDtypeStruct((total, own), jnp.bfloat16)
    return pl.pallas_call(
        kernel,
        grid=(steps,),
        in_specs=[pl.BlockSpec((SPAN, features), lambda r: (r, 0))]
        + [whole_block(a.shape) for a in (w_qkv, cosine, sine, place_column, place_row)],
        out_specs=[whole_block((total, own))] * 4 + [whole_block((heads, total, 1))] + any_specs(1),
        out_shape=[act] * 4
        + [
            jax.ShapeDtypeStruct((heads, total, 1), jnp.float32),
            jax.ShapeDtypeStruct((n_ctx, length, own), jnp.bfloat16),
        ],
        scratch_shapes=dma_pair(n_ctx) + [pltpu.SemaphoreType.DMA],
        compiler_params=params(8),
        name="attention_forward",
    )(rows, w_qkv, cosine, sine, place_column, place_row)


def attention_backward(query, key, value, grad, logs, w_qkv, cosine, sine, place_column, place_row, heads):
    total, own = query.shape
    features = w_qkv.shape[0]
    steps = total // SPAN
    scale = HEAD_DIM ** (-0.5)

    def kernel(
        query_ref, key_ref, value_ref, grad_ref, log_ref, w_ref, cosine_ref, sine_ref, column_ref, row_ref,
        qkv_ref, out_ref, key_sum, value_sum,
    ):
        step = pl.program_id(0)

        @pl.when(step == 0)
        def _():
            for h in range(heads):
                at = slice(h * HEAD_DIM, (h + 1) * HEAD_DIM)
                key_sum[...] = jnp.zeros_like(key_sum)
                value_sum[...] = jnp.zeros_like(value_sum)

                @pl.loop(0, steps)
                def _(block):
                    here = pl.ds(pl.multiple_of(block * SPAN, SPAN), SPAN)
                    queries = query_ref[here, at]
                    grads = grad_ref[here, at]
                    scores = mm(queries, key_ref[:, at], CONTRACT_LAST) * scale
                    scores = jnp.where(column_ref[here] >= row_ref[...], scores, MASKED)
                    probs = jnp.exp(scores - log_ref[h, here])
                    probs_grad = mm(grads, value_ref[:, at], CONTRACT_LAST)
                    centre = jnp.sum(probs * probs_grad, axis=-1, keepdims=True)
                    scores_grad = low(probs * (probs_grad - centre))
                    query_grad = mm(scores_grad, key_ref[:, at]) * scale
                    qkv_ref[here, at] = low(turn(query_grad, cosine_ref[here], -sine_ref[here]))
                    key_sum[...] += mm(scores_grad, queries, CONTRACT_FIRST)
                    value_sum[...] += mm(low(probs), grads, CONTRACT_FIRST)

                qkv_ref[:, own + h * HEAD_DIM : own + (h + 1) * HEAD_DIM] = low(
                    turn(key_sum[...] * scale, cosine_ref[...], -sine_ref[...])
                )
                qkv_ref[:, 2 * own + h * HEAD_DIM : 2 * own + (h + 1) * HEAD_DIM] = low(value_sum[...])

        span = pl.ds(pl.multiple_of(step * SPAN, SPAN), SPAN)
        out_ref[...] = low(mm(qkv_ref[span], w_ref[...], CONTRACT_LAST))

    return pl.pallas_call(
        kernel,
        grid=(steps,),
        in_specs=[
            whole_block(a.shape)
            for a in (query, key, value, grad, logs, w_qkv, cosine, sine, place_column, place_row)
        ],
        out_specs=[whole_block((total, 3 * own)), pl.BlockSpec((SPAN, features), lambda r: (r, 0))],
        out_shape=[
            jax.ShapeDtypeStruct((total, 3 * own), jnp.bfloat16),
            jax.ShapeDtypeStruct((total, features), jnp.bfloat16),
        ],
        scratch_shapes=[pltpu.VMEM((total, HEAD_DIM), jnp.float32)] * 2,
        compiler_params=params(),
        name="attention_backward",
    )(query, key, value, grad, logs, w_qkv, cosine, sine, place_column, place_row)


ROWS = 32


def row_blocks(count, features):
    return pl.BlockSpec((count, ROWS, features), lambda r, *_: (0, r, 0))


def whole_block(shape, **more):
    zeros = (0,) * len(shape)
    return pl.BlockSpec(shape, lambda r, *_: zeros, **more)


def split(values):
    high = low(values)
    return (high, low(values - high.astype(jnp.float32)))


def connect_coefficients(values, dynamic_ref, static_ref, coef_ref, dyn_ref):
    lane = lax.broadcasted_iota(jnp.int32, (values[0].shape[0], 8), 1)
    columns = []
    for i, value in enumerate(values):
        mean = jnp.mean(value, axis=-1, keepdims=True)
        centered = value - mean
        inverse = lax.rsqrt(jnp.mean(centered * centered, axis=-1, keepdims=True) + EPS)
        normed = centered * inverse
        projected = jnp.zeros(lane.shape, jnp.float32)
        for k in range(6):
            part = jnp.sum(normed * dynamic_ref[k : k + 1], axis=-1, keepdims=True)
            projected = jnp.where(lane == k, part, projected)
        coefficient = jnp.tanh(projected) + static_ref[i : i + 1]
        dyn_ref[i] = projected
        coef_ref[i] = jnp.where(lane == 6, mean, jnp.where(lane == 7, inverse, coefficient))
        columns.append(coefficient)
    return columns


def connect_first(streams, dynamic, static):
    number, rows, features = streams.shape

    def kernel(streams_ref, dynamic_ref, static_ref, coef_ref, dyn_ref, low_ref):
        values = [streams_ref[i].astype(jnp.float32) for i in range(number)]
        columns = connect_coefficients(values, dynamic_ref, static_ref, coef_ref, dyn_ref)
        mixed = sum((columns[i][:, 1:2] * values[i] for i in range(number)))
        low_ref[...] = low(normalize(mixed)[0])

    small = jax.ShapeDtypeStruct((number, rows, 8), jnp.float32)
    return pl.pallas_call(
        kernel,
        grid=(rows // ROWS,),
        out_shape=(small, small, jax.ShapeDtypeStruct((rows, features), jnp.bfloat16)),
        in_specs=[row_blocks(number, features), whole_block(dynamic.shape), whole_block(static.shape)],
        out_specs=(
            row_blocks(number, 8),
            row_blocks(number, 8),
            pl.BlockSpec((ROWS, features), lambda r: (r, 0)),
        ),
        compiler_params=params(),
        name="connect_first",
    )(streams, dynamic, static)


def connect_middle(streams, coef, attended, w_mine, w_other, cotangent, dynamic, static, core_fsdp, where, depth):
    number, rows, features = streams.shape
    half = features // 2
    own = attended.shape[2]
    count = len(w_mine)

    def kernel(core_ref, streams_ref, coef_ref, attended_ref, *refs):
        weights, refs = refs[: 2 * count], refs[2 * count :]
        cotangent_ref, dynamic_ref, static_ref = refs[:3]
        first_ref, branch_ref, coef_two_ref, dyn_ref, own_ref, projected = refs[3:]
        step = pl.program_id(0)

        @pl.when(step == 0)
        def _():
            for side in range(2):
                total = 0.0
                for j, (d, offset) in enumerate(where):
                    for q in range(w_mine[j].shape[0] // own):
                        part = attended_ref[(core_ref[1] ^ d) * (depth // own) + offset // own + q]
                        total = total + mm(part, weights[side * count + j][q * own : (q + 1) * own])
                projected[core_ref[0] if side == 0 else 1 - core_ref[0]] = total

        span = pl.ds(pl.multiple_of(step * ROWS, ROWS), ROWS)
        branch = jnp.concatenate([projected[0, span], projected[1, span]], axis=1)
        branch_ref[...] = branch
        inputs = [streams_ref[i].astype(jnp.float32) for i in range(number)]
        outs = []
        for j in range(number):
            out = sum((coef_ref[i][:, 2 + j : 3 + j] * inputs[i] for i in range(number)))
            outs.append(out + coef_ref[j][:, 0:1] * branch)
            first_ref[j] = outs[-1]
        columns = connect_coefficients(outs, dynamic_ref, static_ref, coef_two_ref, dyn_ref)
        mixed = sum((columns[i][:, 1:2] * outs[i] for i in range(number)))
        own_ref[0] = low(normalize(mixed)[0])
        own_ref[1] = low(sum((columns[j][:, 0:1] * cotangent_ref[j].astype(jnp.float32) for j in range(number))))

    small = jax.ShapeDtypeStruct((number, rows, 8), jnp.float32)
    once = dict(pipeline_mode=pl.Buffered(1))
    return pl.pallas_call(
        kernel,
        grid_spec=pltpu.PrefetchScalarGridSpec(
            num_scalar_prefetch=1,
            grid=(rows // ROWS,),
            in_specs=[
                row_blocks(number, features),
                row_blocks(number, 8),
                whole_block(attended.shape, **once),
                *[whole_block(w.shape, **once) for w in w_mine + w_other],
                row_blocks(number, features),
                whole_block(dynamic.shape),
                whole_block(static.shape),
            ],
            out_specs=(
                row_blocks(number, features),
                pl.BlockSpec((ROWS, features), lambda r, *_: (r, 0)),
                row_blocks(number, 8),
                row_blocks(number, 8),
                row_blocks(2, features),
            ),
            scratch_shapes=[pltpu.VMEM((2, rows, half), jnp.float32)],
        ),
        out_shape=(
            jax.ShapeDtypeStruct((number, rows, features), jnp.float32),
            jax.ShapeDtypeStruct((rows, features), jnp.float32),
            small,
            small,
            jax.ShapeDtypeStruct((2, rows, features), jnp.bfloat16),
        ),
        compiler_params=params(),
        name="connect_middle",
    )(core_fsdp, streams, coef, attended, *w_mine, *w_other, cotangent, dynamic, static)


def attention_weights(rows, grads, attended, grad_cols):
    total, features = rows.shape
    parts, _, own = attended.shape
    wide = grads.shape[1]

    def kernel(rows_ref, grads_ref, attended_ref, cols_ref, out_ref):
        out_ref[:, :wide] = low(mm(rows_ref[...], grads_ref[...], CONTRACT_FIRST))
        out_ref[:, wide:] = low(mm(attended_ref[0], cols_ref[...], CONTRACT_FIRST))

    return pl.pallas_call(
        kernel,
        grid=(parts,),
        in_specs=[
            pl.BlockSpec((total, own), lambda k: (0, k)),
            whole_block(grads.shape),
            pl.BlockSpec((1, total, own), lambda k: (k, 0, 0)),
            whole_block(grad_cols.shape),
        ],
        out_specs=pl.BlockSpec((own, wide + own), lambda k: (k, 0)),
        out_shape=jax.ShapeDtypeStruct((features, wide + own), jnp.bfloat16),
        compiler_params=params(),
        cost_estimate=pl.CostEstimate(
            flops=2 * total * features * (wide + own), bytes_accessed=16 * 1024 * 1024, transcendentals=0
        ),
        name="attention_weights",
    )(rows, grads, attended, grad_cols)


def flip(index, bits, count):
    result = index
    bit = 1
    while bit < count:
        if bits & bit:
            result = result + bit - 2 * bit * (index // bit % 2)
        bit *= 2
    return result


def project_back(n_ctx, n_fsdp, grad, w_mine, w_other, where, depth):
    rows, features = grad.shape
    half = features // 2
    count = len(w_mine)
    own = features // n_ctx

    def kernel(grad_ref, *refs):
        weights, refs = refs[: 2 * count], refs[2 * count :]
        landed, cols_ref, outs, deal_s, deal_r, own_sem = refs
        _, core, fsdp, _ = place(n_ctx)
        greet(ctx_peers(n_ctx))
        first = grad_ref[:, pl.ds(pl.multiple_of(core * half, half), half)]
        second = grad_ref[:, pl.ds(pl.multiple_of((1 - core) * half, half), half)]
        for j, (d, offset) in enumerate(where):
            out = low(
                mm(first, weights[j][...], CONTRACT_LAST) + mm(second, weights[count + j][...], CONTRACT_LAST)
            )
            for q in range(w_mine[j].shape[0] // own):
                at = flip(fsdp, d, n_fsdp) * (depth // own) + offset // own + q
                outs[at] = out[:, q * own : (q + 1) * own]
                deal(n_ctx, outs.at[at], at, landed, (deal_s, deal_r), own_sem)
        for index in range(n_ctx):
            cols_ref[index] = grad_ref[:, index * own : (index + 1) * own]
        dealt(n_ctx, outs.at[0], landed, (deal_s, deal_r), own_sem)

    shape = (n_ctx, rows, own)
    return pl.pallas_call(
        kernel,
        in_specs=[pl.BlockSpec(memory_space=pltpu.VMEM)] * (1 + 2 * count),
        out_specs=any_specs(1) + [pl.BlockSpec(memory_space=pltpu.VMEM)],
        out_shape=[jax.ShapeDtypeStruct(shape, grad.dtype)] * 2,
        scratch_shapes=[pltpu.VMEM(shape, grad.dtype)] + dma_pair(n_ctx) + [pltpu.SemaphoreType.DMA],
        compiler_params=params(9),
        name="project_back",
    )(grad, *w_mine, *w_other)


def connect_back(values, coef, dyn, branch, grads, grad_normed, dynamic, means, coef_before=None, offset=0):
    number, rows, features = values.shape
    steps = rows // ROWS
    more = coef_before is not None

    def kernel(*refs):
        values_ref, coef_ref, dyn_ref, branch_ref, grads_ref, normed_ref, dynamic_ref, means_ref = refs[:8]
        refs = refs[8:]
        if more:
            before_ref, refs = refs[0], refs[1:]
        out_ref, dynamic_out, static_out = refs[:3]
        if more:
            forward_ref, grad_low_ref = refs[3:5]
        step = pl.program_id(0)

        @pl.when(step == 0)
        def _():
            dynamic_out[...] = jnp.zeros_like(dynamic_out)
            static_out[...] = jnp.zeros_like(static_out)

        branch = branch_ref[...]
        grads = [grads_ref[j].astype(jnp.float32) for j in range(number)]
        mixed = sum((coef_ref[i][:, 1:2] * values_ref[i].astype(jnp.float32) for i in range(number)))
        normed, inverse = normalize(mixed)
        grad_mixed = normalize_back(normed, inverse, normed_ref[...])
        lane = lax.broadcasted_iota(jnp.int32, (ROWS, 8), 1)
        pre_grads, highs, lows = [], [], []
        for i in range(number):
            value = values_ref[i].astype(jnp.float32)
            columns = [grads[i] * branch, grad_mixed * value] + [grads[j] * value for j in range(number)]
            coef_grad = jnp.zeros((ROWS, 8), jnp.float32)
            for k, column in enumerate(columns):
                coef_grad = jnp.where(lane == k, jnp.sum(column, axis=-1, keepdims=True), coef_grad)
            static_out[i : i + 1] += jnp.sum(coef_grad, axis=0, keepdims=True)
            part = jnp.tanh(dyn_ref[i])
            pre_grads.append(coef_grad * (1.0 - part * part))
            high, rest = split((value - coef_ref[i][:, 6:7]) * coef_ref[i][:, 7:8])
            highs.append(high)
            lows.append(rest)
        pre, pre_rest = split(jnp.concatenate(pre_grads))
        dynamic, dynamic_rest = split(dynamic_ref[...])
        normed_grads = mm(
            jnp.concatenate([pre, pre_rest, pre], axis=1), jnp.concatenate([dynamic, dynamic, dynamic_rest], axis=0)
        )
        highs = jnp.concatenate(highs)
        dynamic_out[...] += (
            mm(pre, highs, CONTRACT_FIRST)
            + mm(pre_rest, highs, CONTRACT_FIRST)
            + mm(pre, jnp.concatenate(lows), CONTRACT_FIRST)
        )
        befores = 0.0
        for i in range(number):
            coef = coef_ref[i]
            mean_grad = jnp.sum(pre_grads[i] * means_ref[...], axis=-1, keepdims=True)
            inner = jnp.sum(pre_grads[i] * dyn_ref[i], axis=-1, keepdims=True) / features
            normed = (values_ref[i].astype(jnp.float32) - coef[:, 6:7]) * coef[:, 7:8]
            out = coef[:, 7:8] * (normed_grads[i * ROWS : (i + 1) * ROWS] - mean_grad - normed * inner)
            out = out + coef[:, 1:2] * grad_mixed
            for j in range(number):
                out = out + coef[:, 2 + j : 3 + j] * grads[j]
            out_ref[i] = out
            if more:
                befores = befores + before_ref[i][:, 0:1] * out
        if more:
            grad_low_ref[...] = low(befores)
            for j in range(number):
                out = coef_ref[j][:, 0:1] * branch
                for i in range(number):
                    out = out + coef_ref[i][:, 2 + j : 3 + j] * values_ref[i].astype(jnp.float32)
                forward_ref[j] = low(out)

    rows_spec = pl.BlockSpec((ROWS, features), lambda r: (r, 0))
    out_shape = [
        jax.ShapeDtypeStruct((number, rows, features), jnp.float32),
        jax.ShapeDtypeStruct((8, features), jnp.float32),
        jax.ShapeDtypeStruct((8, 8), jnp.float32),
    ]
    out_specs = [row_blocks(number, features), whole_block((8, features)), whole_block((8, 8))]
    operands = [values, coef, dyn, branch, grads, grad_normed, dynamic, means]
    in_specs = [
        row_blocks(number, features),
        row_blocks(number, 8),
        row_blocks(number, 8),
        rows_spec,
        row_blocks(number, features),
        pl.BlockSpec((ROWS, features), lambda r: (offset // ROWS + r, 0)),
        whole_block(dynamic.shape),
        whole_block(means.shape),
    ]
    if more:
        operands.append(coef_before)
        in_specs.append(row_blocks(number, 8))
        out_shape.append(jax.ShapeDtypeStruct((number, rows, features), jnp.bfloat16))
        out_specs.append(row_blocks(number, features))
        out_shape.append(jax.ShapeDtypeStruct((rows, features), jnp.bfloat16))
        out_specs.append(rows_spec)
    return pl.pallas_call(
        kernel,
        grid=(steps,),
        in_specs=in_specs,
        out_specs=out_specs,
        out_shape=out_shape,
        compiler_params=params(),
        name="connect_back",
    )(*operands)


def local(n_ctx, n_fsdp, streams, w_attn, w_ffn, hc_dynamic, hc_static, cotangent, pair_order):
    number = streams.shape[1]
    length = streams.shape[2]
    features = streams.shape[3]
    size = HEAD_DIM
    own = features // n_ctx
    heads = own // size
    rows = length * n_ctx
    own_rows = w_attn.shape[0]
    ctx = lax.axis_index("ctx")
    fsdp = lax.axis_index("fsdp")
    core = ctx % 2
    chips = n_ctx // 2
    core_index = jnp.reshape(core, (1,)).astype(jnp.int32)

    def in_order(mine, other, axis):
        return jnp.where(
            core == 0, jnp.concatenate([mine, other], axis=axis), jnp.concatenate([other, mine], axis=axis)
        )


    w_own = lax.dynamic_slice_in_dim(w_attn, ctx * own, own, 2)[:, 0:3].reshape(own_rows, 3 * own)
    w_qkv = gather(w_own, "fsdp")
    half = features // 2
    w_half = lax.dynamic_slice_in_dim(w_attn, core * half, half, 2)[:, 3]
    siblings = [(i, i ^ 1) for i in range(n_ctx)]
    core_fsdp = jnp.stack([core, fsdp]).astype(jnp.int32)

    def exchange(values, most=0):
        return [values] + [
            lax.ppermute(values, "fsdp", [(i, i ^ d) for i in range(n_fsdp)])
            for d in range(1, most + 1 if most else n_fsdp)
        ]

    def swap(blocks):
        return [lax.ppermute(block, "ctx", siblings) for block in blocks]


    positions = block_positions(pair_order, length)
    frequency = THETA ** (-(jnp.arange(size // 2, dtype=jnp.float32) * 2.0) / size)
    angles = positions.astype(jnp.float32)[:, None] * jnp.concatenate([frequency, frequency])[None, :]
    signs = jnp.where(jnp.arange(size) < size // 2, -1.0, 1.0)
    tables = (jnp.cos(angles), jnp.sin(angles) * signs[None, :], positions[:, None], positions[None, :])

    dynamics = jnp.pad(hc_dynamic, ((0, 0), (0, 2), (0, 0)))
    means = jnp.mean(dynamics, axis=-1)
    statics = jnp.pad(hc_static, ((0, 0), (0, 0), (0, 2)))
    coef_one, dyn_one, attn_low = connect_first(streams[0], dynamics[0], statics[0])
    attn_low, w_half = lax.optimization_barrier((attn_low, w_half))
    w_out_mine = exchange(w_half, 2 if n_fsdp == 4 else 0)
    attn_all = line_rows(n_ctx, attn_low).reshape(rows, features)
    w_out_where = [(d, 0) for d in range(len(w_out_mine))]
    attn_all, *w_out_mine = lax.optimization_barrier((attn_all, *w_out_mine))
    w_out_other = swap(w_out_mine)
    if n_fsdp == 4:
        middle = own_rows // 2
        corners = [
            lax.ppermute(w_out_mine[1][:middle], "fsdp", [(i, i ^ 2) for i in range(4)]),
            lax.ppermute(w_out_mine[2][middle:], "fsdp", [(i, i ^ 1) for i in range(4)]),
        ]
        w_out_where += [(3, 0), (3, middle)]
    query, key, value, attended, logs, attended_rows = attention_forward(n_ctx, attn_all, w_qkv, *tables, heads)
    if n_fsdp == 4:
        attended, *corners = lax.optimization_barrier((attended, *corners))
        w_out_mine += corners
        w_out_other += swap(corners)

    first_out, attn_branch, coef_two, dyn_two, ffn_own = connect_middle(
        streams[0], coef_one, attended_rows, w_out_mine, w_out_other, cotangent[0], dynamics[1], statics[1], core_fsdp,
        w_out_where, own_rows,
    )
    ffn_own = ffn_own.reshape(2 * length, features)

    planes = jnp.moveaxis(w_ffn, 1, 0)
    n_own = planes.shape[1] // 2
    blocks = 2 * n_fsdp
    if n_fsdp == 4:
        ffn_all, mirror_rows, *hidden, sums, attended_all = ffn_rows(n_ctx, ffn_own, planes, attended, n_own)
        ffn_all, mirror_rows = (part.reshape(blocks, 2, length, features) for part in (ffn_all, mirror_rows))
        mirror_rows = [mirror_rows]
        weight_parts, sums, weight_early = ffn_weights(
            n_ctx, n_fsdp, sums, ffn_all, mirror_rows, hidden, planes, n_own
        )
    else:
        ffn_mirror = lax.ppermute(ffn_own, "ctx", [(i, n_ctx - 2 - i + 2 * (i % 2)) for i in range(n_ctx)])
        ffn_all = square_core_gather(n_ctx, n_fsdp, ffn_own).reshape(blocks, 2, length, features)
        attended_all = gather(attended, "ctx").reshape(n_ctx, rows, own)
        mirror_mine = exchange(ffn_mirror)
        hidden = ffn_forward(ffn_all, planes, core_index, n_own)
        sums = ffn_back(*hidden, planes, core_index, blocks)
        mirror_rows = [part.reshape(1, 2, length, features) for part in mirror_mine + swap(mirror_mine)]
        sums = square_sum(n_ctx, n_fsdp, sums.reshape(2, n_fsdp, 2 * length, features))
        (weight_parts,) = ffn_weights(n_ctx, n_fsdp, None, ffn_all, mirror_rows, hidden, planes, n_own)
    sides = chips // 2
    lines = [[2 * (sides * side + i) + j for i in range(sides)] for side in range(2) for j in range(2)]

    grad_first, dynamic_grad_two, static_grad_two, streams_out, grad_attn = connect_back(
        first_out, coef_two, dyn_two, sums, cotangent[0], sums, dynamics[1], means[1:], coef_one, length
    )
    grad_heads, grad_cols = project_back(n_ctx, n_fsdp, grad_attn, w_out_mine, w_out_other, w_out_where, own_rows)
    grad_heads, weight_parts = lax.optimization_barrier((grad_heads, weight_parts))
    weight_cols = lax.psum_scatter(weight_parts, "ctx", scatter_dimension=0, axis_index_groups=lines)
    grad_heads = grad_heads.reshape(rows, own)
    grad_heads, grad_cols = lax.optimization_barrier((grad_heads, grad_cols))
    grad_cols = lax.all_to_all(grad_cols, "ctx", 0, 0, tiled=True).reshape(rows, own)
    qkv_grad, attn_part = attention_backward(query, key, value, grad_heads, logs, w_qkv, *tables, heads)
    attn_part = attn_part.reshape(n_ctx, length, features)
    if n_fsdp == 4:
        grad_attn_normed, attn_grad = attention_sums(n_ctx, attn_part, attn_all, qkv_grad, attended_all, grad_cols)
    else:
        grad_attn_normed = line_sum(n_ctx, attn_part)
        attn_grad = scatter(attention_weights(attn_all, qkv_grad, attended_all, grad_cols), "fsdp").astype(jnp.float32)
    grad_attn_normed, weight_cols = lax.optimization_barrier((grad_attn_normed, weight_cols))
    if n_fsdp == 4:
        weight_cols = jnp.concatenate([weight_early, weight_cols], axis=1)
    mine = lax.dynamic_slice_in_dim(weight_cols, core * own, own, 2)
    other = lax.dynamic_slice_in_dim(weight_cols, (1 - core) * own, own, 2)
    other = lax.ppermute(other, "ctx", siblings)
    ffn_grad = jnp.moveaxis(in_order(mine, other, 1), 0, 1).astype(jnp.float32)
    grad_inputs, dynamic_grad_one, static_grad_one = connect_back(
        streams[0], coef_one, dyn_one, attn_branch, grad_first, grad_attn_normed, dynamics[0], means[:1]
    )
    static_grads = jnp.concatenate([static_grad_one[:number, :6].reshape(1, -1), static_grad_two[:number, :6].reshape(1, -1)])
    small = jnp.concatenate(
        [
            dynamic_grad_one[:6],
            dynamic_grad_two[:6],
            jnp.pad(static_grads, ((0, 2), (0, features - 6 * number))),
        ]
    )
    small = sum_everywhere(n_ctx, n_fsdp, small.reshape(n_ctx, 8, -1))
    small = small.reshape(16, features)
    attn_grad = attn_grad.reshape(own_rows, 4, own)
    dynamic_total = small[:12].reshape(2, 6, features)
    static_total = small[12:14, : 6 * number].reshape(2, number, 6)
    return (streams_out[None], grad_inputs[None], attn_grad, ffn_grad, dynamic_total, static_total)


def solution(mesh):
    return jax.shard_map(
        functools.partial(local, mesh.shape["ctx"], mesh.shape["fsdp"]),
        mesh=mesh,
        in_specs=(
            P("fsdp", None, "ctx", None),
            P("fsdp", None, None),
            P("fsdp", None, None),
            P(),
            P(),
            P("fsdp", None, "ctx", None),
            P(),
        ),
        out_specs=(
            P("fsdp", None, "ctx", None),
            P("fsdp", None, "ctx", None),
            P("fsdp", None, "ctx"),
            P("fsdp", None, "ctx"),
            P(),
            P(),
        ),
        check_vma=False,
    )
```
